32 devices in a mesh: rep: 8 (over y, x, core), shard: 4 (over z).
Axes of the slice: x: 2, y: 2, z: 4, core: 2. Of those that a mesh axis runs over, the one named last changes fastest.
Arguments:
- tokens: bfloat16 [8192, 1024], P(('rep', 'shard')), may hold values from -6 to 6
- sequence_start: int32 [8192], P(('rep', 'shard')), may hold values from 0 to 255, as said below
- routes: int32 [8192, 8], P(('rep', 'shard')), may hold values from 0 to 15, all different within a row; in each aligned block of 256 rows (0 to 255, 256 to 511, ...) at most 160 rows name the same one
- route_weights: float32 [8192, 8], P(('rep', 'shard')), may hold values from 0.05 to 0.3
- cotangent: bfloat16 [8192, 1024], P(('rep', 'shard')), may hold values from -6 to 6
- query_proj: bfloat16 [1024, 1024], P('shard'), may hold values from -0.1875 to 0.1875
- key_proj: bfloat16 [1024, 512], P('shard'), may hold values from -0.1875 to 0.1875
- value_proj: bfloat16 [1024, 512], P('shard'), may hold values from -0.1875 to 0.1875
- out_proj: bfloat16 [1024, 1024], P('shard'), may hold values from -1.5 to 1.5
- prenorm: bfloat16 [1024], P('shard'), may hold values from 0.5 to 1.5
- midnorm: bfloat16 [1024], P('shard'), may hold values from 0.5 to 1.5
- gate_proj: bfloat16 [16, 1024, 512], P('shard'), may hold values from -0.1875 to 0.1875
- up_proj: bfloat16 [16, 1024, 512], P('shard'), may hold values from -0.1875 to 0.1875
- down_proj: bfloat16 [16, 512, 1024], P('shard'), may hold values from -0.25 to 0.25
- query_moment: float32 [1024, 1024], P('shard'), may hold values from -640 to 640
- key_moment: float32 [1024, 512], P('shard'), may hold values from -640 to 640
- value_moment: float32 [1024, 512], P('shard'), may hold values from -640 to 640
- out_moment: float32 [1024, 1024], P('shard'), may hold values from -640 to 640
- prenorm_moment: float32 [1024], P('shard'), may hold values from -1792 to 1792
- midnorm_moment: float32 [1024], P('shard'), may hold values from -320 to 320
- gate_moment: float32 [16, 1024, 512], P('shard'), may hold values from -128 to 128
- up_moment: float32 [16, 1024, 512], P('shard'), may hold values from -128 to 128
- down_moment: float32 [16, 512, 1024], P('shard'), may hold values from -128 to 128
Outputs:
- mixed: bfloat16 [8192, 1024], P(('rep', 'shard'))
- grad_tokens: float32 [8192, 1024], P(('rep', 'shard'))
- query_grad: float32 [1024, 1024], P('shard')
- query_next: float32 [1024, 1024], P('shard')
- query_update: float32 [1024, 1024], P('shard')
- key_grad: float32 [1024, 512], P('shard')
- key_next: float32 [1024, 512], P('shard')
- key_update: float32 [1024, 512], P('shard')
- value_grad: float32 [1024, 512], P('shard')
- value_next: float32 [1024, 512], P('shard')
- value_update: float32 [1024, 512], P('shard')
- out_grad: float32 [1024, 1024], P('shard')
- out_next: float32 [1024, 1024], P('shard')
- out_update: float32 [1024, 1024], P('shard')
- prenorm_grad: float32 [1024], P('shard')
- prenorm_next: float32 [1024], P('shard')
- prenorm_update: float32 [1024], P('shard')
- midnorm_grad: float32 [1024], P('shard')
- midnorm_next: float32 [1024], P('shard')
- midnorm_update: float32 [1024], P('shard')
- gate_grad: float32 [16, 1024, 512], P('shard')
- gate_next: float32 [16, 1024, 512], P('shard')
- gate_update: float32 [16, 1024, 512], P('shard')
- up_grad: float32 [16, 1024, 512], P('shard')
- up_next: float32 [16, 1024, 512], P('shard')
- up_update: float32 [16, 1024, 512], P('shard')
- down_grad: float32 [16, 512, 1024], P('shard')
- down_next: float32 [16, 512, 1024], P('shard')
- down_update: float32 [16, 512, 1024], P('shard')
The draws below stay inside these ranges and needn't reach their ends.
Inputs may be any that keep to these rules, and one draw needn't show every extreme that they name: `sequence_start`: within each device's block of 256 tokens, sequences are contiguous runs; every token holds the block-local index of its run's first token, which holds its own index. Some block is one sequence of all 256 tokens. `routes`: each token names 8 different experts. Among the rows of one device no expert is named by more than 160 rows, and in some device one expert is named by exactly 160.
All inputs are finite; a program needn't handle non-finite values.
Results may differ from the reference program's by a relative error of at most 0.011.
The reference program's roundings to bfloat16 on the way count: a program that leaves them out, or rounds other values in their place, can miss the bound.
Values may be sent and summed in bfloat16 or wider, within the bound.
A program may use at most 320 MiB of HBM per device.

```python
import math
import jax
import jax.numpy as jnp
import numpy as np
from jax import lax

D = 1024
NHEADS = 16
KVHEADS = 8
HEAD = 64
FFE = 512
TOPK = 8
EXPERTS = 16
NS_ITERS = 2
TOK_DEV = 256
TOKENS = 8192
CAP = 160
QW = 1024
KW = 512


def draw_sequence_start(key, part):
    row_count = TOKENS // TOK_DEV
    marks = jax.random.randint(jax.random.fold_in(key, 11), (row_count, TOK_DEV), 0, TOK_DEV) < 4
    places = jnp.arange(TOK_DEV, dtype=jnp.int32)
    row_ids = jnp.arange(row_count, dtype=jnp.int32)
    single = jax.random.randint(jax.random.fold_in(key, 12), (), 0, row_count)
    marks = jnp.where(row_ids[:, None] == single, False, marks)
    ending = (single + 1) % row_count
    marks = marks | (row_ids[:, None] == ending) & (places[None, :] == TOK_DEV - 1)
    marks = marks | (places[None, :] == 0)
    starts = lax.cummax(jnp.where(marks, places[None, :], 0), axis=1)
    return starts.reshape(row_count * TOK_DEV).astype(jnp.int32)


def block_levels(own_key, dims, cuts, least, high):
    def one(position, parts):
        heights = jax.random.uniform(jax.random.fold_in(jax.random.fold_in(own_key, 6), position), (parts,), jnp.float32, least / len(cuts), high / len(cuts))
        return jnp.repeat(jnp.exp(heights), dims[position] // parts).reshape((-1,) + (1,) * (len(dims) - position - 1))

    factor_of = one(*cuts[0])
    for cut in cuts[1:]:
        factor_of = factor_of * one(*cut)
    return factor_of


def assign_block(key, own, number, rows, amount, top, limit, slope):
    ranking = jax.random.permutation(key, amount)
    packed, common = portions_of(amount, rows * top, limit, slope, True), portions_of(amount, rows * top, limit, slope, False)
    places = jnp.arange(amount)

    def named(sizes, turn):
        used = int((sizes > 0).sum())
        fixed = max(1, used // 4)
        passed = fixed + (places - fixed + turn * (used - fixed)) % max(1, amount - fixed)
        return jnp.zeros((amount,), jnp.int32).at[ranking[jnp.where(places < fixed, places, passed)]].set(jnp.asarray(sizes, jnp.int32))

    sizes = jnp.where(number % 4 == 0, named(packed, number // 4), named(common, number - number // 4 - 1))
    mixed = jax.random.permutation(jax.random.fold_in(own, 3), amount)
    source_of, taker = mixed[0:amount // 2 * 2:2], mixed[1:amount // 2 * 2:2]
    margin = jnp.minimum(sizes[source_of] - 1, limit - sizes[taker]) // 2
    margin = jnp.where((source_of == ranking[0]) | (taker == ranking[0]) | (sizes[taker] == 0), 0, jnp.maximum(margin, 0))
    passed = jax.random.randint(jax.random.fold_in(own, 4), (amount // 2,), 0, 1 << 20) % (margin + 1)
    sizes = sizes.at[source_of].add(-passed).at[taker].add(passed)
    members = jnp.searchsorted(jnp.cumsum(sizes), jnp.arange(rows * top), side="right").astype(jnp.int32)
    grid = members.reshape(top, rows).T
    grid = grid[jax.random.permutation(jax.random.fold_in(own, 1), rows)]
    turn = jax.random.randint(jax.random.fold_in(own, 2), (rows, 1), 0, top)
    return jnp.take_along_axis(grid, (jnp.arange(top)[None, :] + turn) % top, axis=1)


def portions_of(number_of, total, most, skew, full):
    portions = [(1 << 20) // math.isqrt(standing ** skew) + 1 for standing in range(1, number_of + 1)]
    largest = most if full else min(most, max(-(-total // number_of), total * portions[0] // sum(portions)))
    least = 1 if total - largest >= number_of - 1 else 0
    counts, spare = [largest] + [least] * (number_of - 1), total - largest - least * (number_of - 1)
    while spare > 0:
        candidates = [i for i in range(1, number_of) if counts[i] < largest] or [i for i in range(1, number_of) if counts[i] < most]
        pool, budget = sum([portions[i] for i in candidates]), spare
        for i in candidates:
            addition = min(most - counts[i], max(1, budget * portions[i] // pool), spare)
            counts[i] = counts[i] + addition
            spare = spare - addition
    return np.array(counts)


def gaussian(own_key, shape, spread, reach, shards=(), kind=jnp.bfloat16):
    result = spread * jax.random.normal(own_key, shape, jnp.float32)
    if shards:
        result = result * block_levels(own_key, shape, shards, -0.22, 0.18)
    return jnp.clip(result, -reach, reach).astype(kind)


def setup_inputs(seed: int = 0) -> dict:
    key_of = jax.random.split(jax.random.key(seed), 24)
    tokens = gaussian(key_of[0], (TOKENS, D), 1.0, 6.0, ((0, 32),))
    sequence_start = draw_sequence_start(jax.random.fold_in(key_of[23], 71), 0)
    routes_keys = jax.random.split(jax.random.fold_in(key_of[2], 1), TOKENS // TOK_DEV)
    routes_turns = jax.random.permutation(jax.random.fold_in(key_of[2], 3), TOKENS // TOK_DEV)
    routes = jax.vmap(lambda own, number: assign_block(jax.random.fold_in(key_of[2], 2), own, number, TOK_DEV, EXPERTS, TOPK, CAP, 1))(routes_keys, routes_turns).reshape((TOKENS, TOPK))
    route_weights = jnp.clip(0.05 + 0.25 * jax.random.uniform(key_of[3], (TOKENS, TOPK), jnp.float32) ** block_levels(key_of[3], (TOKENS, TOPK), ((0, 32),), -0.2, 0.2), 0.05, 0.3)
    cotangent = gaussian(key_of[4], (TOKENS, D), 1.0, 6.0, ((0, 32),))
    query_proj = gaussian(key_of[5], (D, QW), D ** -0.5, 0.1875, ((0, 4),))
    key_proj = gaussian(key_of[6], (D, KW), D ** -0.5, 0.1875, ((0, 4),))
    value_proj = gaussian(key_of[7], (D, KW), D ** -0.5, 0.1875, ((0, 4),))
    out_proj = gaussian(key_of[8], (QW, D), (max(1, QW // 64)) ** -0.5, 1.5, ((0, 4),))
    prenorm = jnp.clip(1.0 + 0.1 * jax.random.normal(key_of[9], (D,), jnp.float32), 0.5, 1.5).astype(jnp.bfloat16)
    midnorm = jnp.clip(1.0 + 0.1 * jax.random.normal(key_of[10], (D,), jnp.float32), 0.5, 1.5).astype(jnp.bfloat16)
    gate_proj = gaussian(key_of[11], (EXPERTS, D, FFE), D ** -0.5, 0.1875, ((0, 4),))
    up_proj = gaussian(key_of[12], (EXPERTS, D, FFE), D ** -0.5, 0.1875, ((0, 4),))
    down_proj = gaussian(key_of[13], (EXPERTS, FFE, D), FFE ** -0.5, 0.25, ((0, 4),))
    query_moment = gaussian(key_of[14], (D, QW), 100.0, 640.0, ((0, 4),), jnp.float32)
    key_moment = gaussian(key_of[15], (D, KW), 100.0, 640.0, ((0, 4),), jnp.float32)
    value_moment = gaussian(key_of[16], (D, KW), 100.0, 640.0, ((0, 4),), jnp.float32)
    out_moment = gaussian(key_of[17], (QW, D), 100.0, 640.0, ((0, 4),), jnp.float32)
    prenorm_moment = gaussian(key_of[18], (D,), 300.0, 1792.0, ((0, 4),), jnp.float32)
    midnorm_moment = gaussian(key_of[19], (D,), 50.0, 320.0, ((0, 4),), jnp.float32)
    gate_moment = gaussian(key_of[20], (EXPERTS, D, FFE), 20.0, 128.0, ((0, 4),), jnp.float32)
    up_moment = gaussian(key_of[21], (EXPERTS, D, FFE), 20.0, 128.0, ((0, 4),), jnp.float32)
    down_moment = gaussian(key_of[22], (EXPERTS, FFE, D), 20.0, 128.0, ((0, 4),), jnp.float32)
    return {"tokens": tokens, "sequence_start": sequence_start, "routes": routes, "route_weights": route_weights, "cotangent": cotangent, "query_proj": query_proj, "key_proj": key_proj, "value_proj": value_proj, "out_proj": out_proj, "prenorm": prenorm, "midnorm": midnorm, "gate_proj": gate_proj, "up_proj": up_proj, "down_proj": down_proj, "query_moment": query_moment, "key_moment": key_moment, "value_moment": value_moment, "out_moment": out_moment, "prenorm_moment": prenorm_moment, "midnorm_moment": midnorm_moment, "gate_moment": gate_moment, "up_moment": up_moment, "down_moment": down_moment}


@jax.custom_vjp
def low(v):
    return lax.optimization_barrier(v.astype(jnp.bfloat16)).astype(jnp.float32)

@jax.custom_vjp
def low_back(v):
    return v

def low_keep(v):
    return (low(v), None)

def low_pass(kept, grad):
    return (grad,)

def back_keep(v):
    return (v, None)

def back_low(kept, grad):
    return (low(grad),)
low.defvjp(low_keep, low_pass)
low_back.defvjp(back_keep, back_low)
norm_epsilon = 1e-06
rotary_base = 10000.0
momentum_keep = 0.9
rate_matrix = 0.5
rate_gain = 0.0002
newton_first = 3.4445
newton_second = -4.775
newton_third = 2.0315
masked_score = -1e+30
highest = lax.Precision.HIGHEST

def matmul(left, right):
    return jnp.dot(left, right, precision=highest, preferred_element_type=jnp.float32)

def root_scale(values):
    return values * lax.rsqrt(lax.optimization_barrier(jnp.mean(values * values, axis=-1, keepdims=True)) + norm_epsilon)

def rotary_tables(positions):
    half_size = HEAD // 2
    frequency = rotary_base ** (-(jnp.arange(half_size, dtype=jnp.float32) * 2.0) / HEAD)
    angles = positions.astype(jnp.float32)[:, None] * frequency[None, :]
    angles = jnp.concatenate([angles, angles], axis=-1)
    return (jnp.cos(angles)[:, None, :], jnp.sin(angles)[:, None, :])

def rotate_half(values):
    half_size = values.shape[-1] // 2
    return jnp.concatenate([-values[..., half_size:], values[..., :half_size]], axis=-1)

def attend_device(pieces):
    queries, rotated_keys, values, starts = pieces
    group_size = NHEADS // KVHEADS
    keys_wide = jnp.repeat(rotated_keys, group_size, axis=1)
    values_wide = jnp.repeat(values, group_size, axis=1)
    scores = jnp.einsum('qhd,khd->hqk', queries, keys_wide, precision=highest) * (1.0 / math.sqrt(HEAD))
    scores = low_back(scores)
    places = jnp.arange(TOK_DEV, dtype=jnp.int32)
    allowed = (starts[:, None] == starts[None, :]) & (places[None, :] <= places[:, None])
    scores = jnp.where(allowed[None, :, :], scores, masked_score)
    softmax_low = low(jax.nn.softmax(scores, axis=-1))
    return jnp.einsum('hqk,khd->qhd', softmax_low, values_wide, precision=highest)

def route_tables(routes):
    device_count = TOKENS // TOK_DEV
    per_device = TOK_DEV * TOPK
    flat_routes = routes.reshape(device_count, per_device)
    onehot = (flat_routes[:, :, None] == jnp.arange(EXPERTS, dtype=jnp.int32)[None, None, :]).astype(jnp.int32)
    slot_rank = lax.optimization_barrier(jnp.sum((jnp.cumsum(onehot, axis=1) - onehot) * onehot, axis=2))
    devices = jnp.arange(device_count, dtype=jnp.int32)[:, None]
    slot_place = (flat_routes * device_count + devices) * CAP + slot_rank
    route_ids = devices * per_device + jnp.arange(per_device, dtype=jnp.int32)[None, :]
    empty_slots = jnp.full((EXPERTS * device_count * CAP,), TOKENS * TOPK, jnp.int32)
    return empty_slots.at[slot_place.reshape(-1)].set(route_ids.reshape(-1))

def forward(inputs, query_proj, key_proj, value_proj, out_proj, prenorm, midnorm, gate_proj, up_proj, down_proj, sequence_start, cosine_table, sine_table, slot_route, route_weights):
    device_count = TOKENS // TOK_DEV
    normed_first = low(root_scale(inputs) * prenorm)
    query_linear = low_back(matmul(normed_first, query_proj)).reshape(TOKENS, NHEADS, HEAD)
    key_linear = low_back(matmul(normed_first, key_proj)).reshape(TOKENS, KVHEADS, HEAD)
    values = low(low_back(matmul(normed_first, value_proj))).reshape(TOKENS, KVHEADS, HEAD)
    queries = low(query_linear * cosine_table + rotate_half(query_linear) * sine_table)
    rotated_keys = low(key_linear * cosine_table + rotate_half(key_linear) * sine_table)
    head_out = lax.map(jax.checkpoint(attend_device), (queries.reshape(device_count, TOK_DEV, NHEADS, HEAD), rotated_keys.reshape(device_count, TOK_DEV, KVHEADS, HEAD), values.reshape(device_count, TOK_DEV, KVHEADS, HEAD), sequence_start.reshape(device_count, TOK_DEV)))
    head_low = low_back(low(head_out.reshape(TOKENS, NHEADS * HEAD)))
    middle = inputs + low_back(matmul(head_low, out_proj))
    normed_second = low(root_scale(middle) * midnorm)
    padded = jnp.concatenate([normed_second, jnp.zeros((1, D), jnp.float32)], axis=0)
    weight_pad = jnp.concatenate([route_weights.reshape(TOKENS * TOPK), jnp.zeros((1,), jnp.float32)], axis=0)

    def expert_step(totals, pieces):
        gate_one, up_one, down_one, route_ids = pieces
        token_ids = route_ids // TOPK
        routed = low_back(padded[token_ids])
        gate_linear = low_back(matmul(routed, gate_one))
        up_linear = low_back(matmul(routed, up_one))
        hidden = low(jax.nn.silu(gate_linear) * up_linear)
        expert_out = low_back(low(matmul(hidden, down_one)))
        return (totals.at[token_ids].add(weight_pad[route_ids][:, None] * expert_out), None)
    totals, unused = lax.scan(jax.checkpoint(expert_step), jnp.zeros((TOKENS + 1, D), jnp.float32), (gate_proj, up_proj, down_proj, slot_route.reshape(EXPERTS, device_count * CAP)))
    return middle + totals[:TOKENS]

def orthogonal(matrix):
    is_tall = matrix.shape[0] > matrix.shape[1]
    iterate = matrix.T if is_tall else matrix
    iterate = iterate / (jnp.sqrt(jnp.sum(iterate * iterate)) + 1e-07)
    for iteration in range(NS_ITERS):
        gram_matrix = matmul(iterate, iterate.T)
        polynomial = newton_second * gram_matrix + newton_third * matmul(gram_matrix, gram_matrix)
        iterate = newton_first * iterate + matmul(polynomial, iterate)
    return iterate.T if is_tall else iterate

def matrix_update(moment):
    step_scale = rate_matrix * math.sqrt(max(1.0, moment.shape[-1] / moment.shape[-2]))
    return -step_scale * orthogonal(moment)

def reference(tokens, sequence_start, routes, route_weights, cotangent, query_proj, key_proj, value_proj, out_proj, prenorm, midnorm, gate_proj, up_proj, down_proj, query_moment, key_moment, value_moment, out_moment, prenorm_moment, midnorm_moment, gate_moment, up_moment, down_moment):
    places = jnp.arange(TOKENS, dtype=jnp.int32) % TOK_DEV
    cosine_table, sine_table = rotary_tables(places - sequence_start)
    slot_route = route_tables(routes)

    def runner(inputs, query_weight, key_weight, value_weight, out_weight, pre_gain, mid_gain, gate_weight, up_weight, down_weight):
        return forward(inputs, query_weight, key_weight, value_weight, out_weight, pre_gain, mid_gain, gate_weight, up_weight, down_weight, sequence_start, cosine_table, sine_table, slot_route, route_weights)
    mixed_full, pullback = jax.vjp(runner, tokens.astype(jnp.float32), query_proj.astype(jnp.float32), key_proj.astype(jnp.float32), value_proj.astype(jnp.float32), out_proj.astype(jnp.float32), prenorm.astype(jnp.float32), midnorm.astype(jnp.float32), gate_proj.astype(jnp.float32), up_proj.astype(jnp.float32), down_proj.astype(jnp.float32))
    grads = pullback(cotangent.astype(jnp.float32))
    mixed = mixed_full.astype(jnp.bfloat16)
    grad_tokens = grads[0]
    query_grad = grads[1]
    key_grad = grads[2]
    value_grad = grads[3]
    out_grad = grads[4]
    prenorm_grad = grads[5]
    midnorm_grad = grads[6]
    gate_grad = grads[7]
    up_grad = grads[8]
    down_grad = grads[9]
    query_next = momentum_keep * query_moment + query_grad
    key_next = momentum_keep * key_moment + key_grad
    value_next = momentum_keep * value_moment + value_grad
    out_next = momentum_keep * out_moment + out_grad
    prenorm_next = momentum_keep * prenorm_moment + prenorm_grad
    midnorm_next = momentum_keep * midnorm_moment + midnorm_grad
    gate_next = momentum_keep * gate_moment + gate_grad
    up_next = momentum_keep * up_moment + up_grad
    down_next = momentum_keep * down_moment + down_grad
    query_update = matrix_update(query_next)
    key_update = matrix_update(key_next)
    value_update = matrix_update(value_next)
    out_update = matrix_update(out_next)
    prenorm_update = -rate_gain * prenorm_next
    midnorm_update = -rate_gain * midnorm_next
    gate_update = lax.map(matrix_update, gate_next)
    up_update = lax.map(matrix_update, up_next)
    down_update = lax.map(matrix_update, down_next)
    return (mixed, grad_tokens, query_grad, query_next, query_update, key_grad, key_next, key_update, value_grad, value_next, value_update, out_grad, out_next, out_update, prenorm_grad, prenorm_next, prenorm_update, midnorm_grad, midnorm_next, midnorm_update, gate_grad, gate_next, gate_update, up_grad, up_next, up_update, down_grad, down_next, down_update)
```

```python
import math

import jax
import jax.numpy as jnp
from jax import lax
from jax.sharding import PartitionSpec as P

NHEADS = 16
KVHEADS = 8
HEAD = 64
EXPERTS = 16
NS_ITERS = 2
BLOCK = 256


norm_epsilon = 1e-06
rotary_base = 10000.0
momentum_keep = 0.9
rate_matrix = 0.5
rate_gain = 0.0002
newton_first = 3.4445
newton_second = -4.775
newton_third = 2.0315
masked_score = -1e30


def root_scale(values):
    inverse = lax.rsqrt(jnp.mean(values * values, axis=-1, keepdims=True) + norm_epsilon)
    return (values * inverse, inverse)


def root_back(grad_normed, scaling, scaled, inverse):
    grad_scaled = grad_normed * scaling
    inner_mean = jnp.mean(grad_scaled * scaled, axis=-1, keepdims=True)
    return (inverse * (grad_scaled - scaled * inner_mean), jnp.sum(grad_normed * scaled, axis=0))


def rotary_tables(positions):
    half_size = HEAD // 2
    frequency = rotary_base ** (-(jnp.arange(half_size, dtype=jnp.float32) * 2.0) / HEAD)
    angles = positions.astype(jnp.float32)[:, None] * frequency[None, :]
    angles = jnp.concatenate([angles, angles], axis=-1)
    return (jnp.cos(angles)[:, None, :], jnp.sin(angles)[:, None, :])


def rotate_half(values):
    half_size = values.shape[-1] // 2
    return jnp.concatenate([-values[..., half_size:], values[..., :half_size]], axis=-1)


def rotate_back(values):
    half_size = values.shape[-1] // 2
    return jnp.concatenate([values[..., half_size:], -values[..., :half_size]], axis=-1)


def block_scores(query_block, rotated_keys, start_block, sequence_start, offset):
    scores = jnp.einsum(
        "qkgd,tkd->kgqt", query_block, rotated_keys, preferred_element_type=jnp.float32
    ) * (1.0 / math.sqrt(HEAD))
    key_places = jnp.arange(rotated_keys.shape[0], dtype=jnp.int32)
    query_places = offset + jnp.arange(query_block.shape[0], dtype=jnp.int32)
    allowed = (start_block[:, None] == sequence_start[None, :]) & (
        key_places[None, :] <= query_places[:, None]
    )
    return jnp.where(allowed, scores, masked_score)


def attend_forward(queries, rotated_keys, values, sequence_start):
    block_count = queries.shape[0] // BLOCK

    def one_block(pieces):
        query_block, start_block, offset = pieces
        scores = block_scores(query_block, rotated_keys, start_block, sequence_start, offset)
        row_max = jnp.max(scores, axis=-1, keepdims=True)
        exponents = jnp.exp(scores - row_max)
        totals = jnp.sum(exponents, axis=-1, keepdims=True)
        softmax_low = (exponents / totals).astype(jnp.bfloat16)
        attended = jnp.einsum(
            "kgqt,tkd->qkgd", softmax_low, values, preferred_element_type=jnp.float32
        )
        return (attended, row_max + jnp.log(totals))

    shaped = queries.reshape((block_count, BLOCK) + queries.shape[1:])
    offsets = jnp.arange(block_count, dtype=jnp.int32) * BLOCK
    attended, log_total = lax.map(
        one_block, (shaped, sequence_start.reshape(block_count, BLOCK), offsets)
    )
    return (attended.reshape(queries.shape[0], -1), log_total)


def attend_backward(queries, rotated_keys, values, sequence_start, log_total, grad_heads):
    block_count = queries.shape[0] // BLOCK
    score_scale = 1.0 / math.sqrt(HEAD)

    def one_block(running, pieces):
        grad_keys, grad_values = running
        query_block, start_block, offset, log_block, grad_block = pieces
        scores = block_scores(query_block, rotated_keys, start_block, sequence_start, offset)
        softmax_full = jnp.exp(scores - log_block)
        grad_softmax = jnp.einsum(
            "qkgd,tkd->kgqt", grad_block, values, preferred_element_type=jnp.float32
        )
        inner_sum = jnp.sum(softmax_full * grad_softmax, axis=-1, keepdims=True)
        grad_scores = (softmax_full * (grad_softmax - inner_sum)).astype(jnp.bfloat16)
        grad_query = (
            jnp.einsum(
                "kgqt,tkd->qkgd", grad_scores, rotated_keys, preferred_element_type=jnp.float32
            )
            * score_scale
        )
        grad_keys = (
            grad_keys
            + jnp.einsum(
                "kgqt,qkgd->tkd", grad_scores, query_block, preferred_element_type=jnp.float32
            )
            * score_scale
        )
        grad_values = grad_values + jnp.einsum(
            "kgqt,qkgd->tkd",
            softmax_full.astype(jnp.bfloat16),
            grad_block,
            preferred_element_type=jnp.float32,
        )
        return ((grad_keys, grad_values), grad_query)

    shaped = queries.reshape((block_count, BLOCK) + queries.shape[1:])
    grad_shaped = grad_heads.reshape((block_count, BLOCK) + queries.shape[1:])
    offsets = jnp.arange(block_count, dtype=jnp.int32) * BLOCK
    key_zeros = jnp.zeros(rotated_keys.shape, jnp.float32)
    finals, grad_queries = lax.scan(
        one_block,
        (key_zeros, key_zeros),
        (shaped, sequence_start.reshape(block_count, BLOCK), offsets, log_total, grad_shaped),
    )
    return (grad_queries.reshape(queries.shape), finals[0], finals[1])


def mul(left, right, spec):
    return jnp.einsum(
        spec,
        left.astype(jnp.bfloat16),
        right.astype(jnp.bfloat16),
        preferred_element_type=jnp.float32,
    )


def orthogonal(matrix):
    rows, columns = matrix.shape[-2:]
    squares = jnp.sum(matrix * matrix, axis=(-2, -1), keepdims=True)
    iterate = matrix / (jnp.sqrt(squares) + 1e-07)
    for iteration in range(NS_ITERS):
        if rows > columns:
            gram = mul(iterate, iterate, "...ki,...kj->...ij")
        else:
            gram = mul(iterate, iterate, "...ik,...jk->...ij")
        polynomial = newton_second * gram + newton_third * mul(gram, gram, "...ij,...jk->...ik")
        if rows > columns:
            step = mul(iterate, polynomial, "...ij,...jk->...ik")
        else:
            step = mul(polynomial, iterate, "...ij,...jk->...ik")
        iterate = newton_first * iterate + step
    return iterate


def matrix_update(moment):
    step_scale = rate_matrix * math.sqrt(max(1.0, moment.shape[-1] / moment.shape[-2]))
    return -step_scale * orthogonal(moment)


def local(
    tokens,
    sequence_start,
    routes,
    route_weights,
    cotangent,
    query_proj,
    key_proj,
    value_proj,
    out_proj,
    prenorm,
    midnorm,
    gate_proj,
    up_proj,
    down_proj,
    query_moment,
    key_moment,
    value_moment,
    out_moment,
    prenorm_moment,
    midnorm_moment,
    gate_moment,
    up_moment,
    down_moment,
):
    rep_index = lax.axis_index("rep")
    shard_index = lax.axis_index("shard")
    rep_count = lax.axis_size("rep")
    shard_count = lax.axis_size("shard")
    row_block = query_proj.shape[0]
    piece_rows = row_block // rep_count
    low_rows = jnp.concatenate([query_proj, key_proj, value_proj, out_proj], axis=1)
    low_piece = lax.dynamic_slice_in_dim(low_rows, rep_index * piece_rows, piece_rows, 0)
    low_all = lax.all_gather(low_piece, ("shard", "rep"), axis=0, tiled=True)
    full_query = low_all[:, :1024]
    full_key = low_all[:, 1024:1536]
    full_value = low_all[:, 1536:2048]
    full_out = low_all[:, 2048:]
    gains = lax.all_gather(jnp.stack([prenorm, midnorm]), "shard", axis=1, tiled=True)
    prenorm_low = gains[0]
    midnorm_low = gains[1]
    experts_here = gate_proj.shape[0]
    dense_weights = jnp.sum(
        jnp.where(
            routes[:, :, None] == jnp.arange(EXPERTS, dtype=jnp.int32)[None, None, :],
            route_weights[:, :, None],
            0.0,
        ),
        axis=1,
    )
    dense_all = lax.all_gather(dense_weights, "shard", axis=0, tiled=True)
    expert_weights = lax.dynamic_slice_in_dim(
        dense_all, shard_index * experts_here, experts_here, 1
    ).T[:, :, None]
    cotangent_all = lax.all_gather(cotangent, "shard", axis=0, tiled=True)
    gain_before = prenorm_low.astype(jnp.float32)
    gain_after = midnorm_low.astype(jnp.float32)
    group_size = NHEADS // KVHEADS
    token_count = tokens.shape[0]
    inputs = tokens.astype(jnp.float32)
    scaled_first, inverse_first = root_scale(inputs)
    normed_first = (scaled_first * gain_before).astype(jnp.bfloat16)
    query_linear = jnp.dot(normed_first, full_query, preferred_element_type=jnp.float32).reshape(
        token_count, NHEADS, HEAD
    )
    key_linear = jnp.dot(normed_first, full_key, preferred_element_type=jnp.float32).reshape(
        token_count, KVHEADS, HEAD
    )
    values = (
        jnp.dot(normed_first, full_value, preferred_element_type=jnp.float32)
        .astype(jnp.bfloat16)
        .reshape(token_count, KVHEADS, HEAD)
    )
    cosine_table, sine_table = rotary_tables(
        jnp.arange(token_count, dtype=jnp.int32) - sequence_start
    )
    queries = (
        (query_linear * cosine_table + rotate_half(query_linear) * sine_table)
        .astype(jnp.bfloat16)
        .reshape(token_count, KVHEADS, group_size, HEAD)
    )
    rotated_keys = (key_linear * cosine_table + rotate_half(key_linear) * sine_table).astype(
        jnp.bfloat16
    )
    head_out, log_total = attend_forward(queries, rotated_keys, values, sequence_start)
    head_low = head_out.astype(jnp.bfloat16)
    middle = inputs + jnp.dot(head_low, full_out, preferred_element_type=jnp.float32)
    scaled_second, inverse_second = root_scale(middle)
    normed_second = (scaled_second * gain_after).astype(jnp.bfloat16)
    routed = lax.all_gather(normed_second, "shard", axis=0, tiled=True)
    gate_linear = jnp.einsum("td,xdf->xtf", routed, gate_proj, preferred_element_type=jnp.float32)
    up_linear = jnp.einsum("td,xdf->xtf", routed, up_proj, preferred_element_type=jnp.float32)
    gate_sigmoid = jax.nn.sigmoid(gate_linear)
    hidden = (gate_linear * gate_sigmoid * up_linear).astype(jnp.bfloat16)
    expert_out = jnp.einsum("xtf,xfd->xtd", hidden, down_proj, preferred_element_type=jnp.float32)
    partial_out = jnp.sum(
        expert_weights * expert_out.astype(jnp.bfloat16).astype(jnp.float32), axis=0
    ).astype(jnp.bfloat16)
    grad_out = (expert_weights * cotangent_all.astype(jnp.float32)[None]).astype(jnp.bfloat16)
    grad_hidden = jnp.einsum("xtd,xfd->xtf", grad_out, down_proj, preferred_element_type=jnp.float32)
    gate_delta = (
        grad_hidden * up_linear * gate_sigmoid * (1.0 + gate_linear * (1.0 - gate_sigmoid))
    ).astype(jnp.bfloat16)
    up_delta = (grad_hidden * gate_linear * gate_sigmoid).astype(jnp.bfloat16)
    grad_routed = (
        jnp.einsum("xtf,xdf->xtd", gate_delta, gate_proj, preferred_element_type=jnp.float32)
        + jnp.einsum("xtf,xdf->xtd", up_delta, up_proj, preferred_element_type=jnp.float32)
    )
    partial_grad = jnp.sum(grad_routed, axis=0).astype(jnp.bfloat16)
    down_sum = jnp.einsum("xtf,xtd->xfd", hidden, grad_out, preferred_element_type=jnp.float32)
    gate_sum = jnp.einsum("td,xtf->xdf", routed, gate_delta, preferred_element_type=jnp.float32)
    up_sum = jnp.einsum("td,xtf->xdf", routed, up_delta, preferred_element_type=jnp.float32)
    back = lax.all_to_all(partial_grad, "shard", split_axis=0, concat_axis=0, tiled=True)
    grad_second = jnp.sum(
        back.reshape(shard_count, token_count, -1).astype(jnp.float32), axis=0
    )
    back_out = lax.all_to_all(partial_out, "shard", split_axis=0, concat_axis=0, tiled=True)
    mixed = middle + jnp.sum(
        back_out.reshape(shard_count, token_count, -1).astype(jnp.float32), axis=0
    )
    grad_mixed = cotangent.astype(jnp.float32)
    middle_extra, midnorm_part = root_back(grad_second, gain_after, scaled_second, inverse_second)
    grad_middle = grad_mixed + middle_extra
    grad_branch = grad_middle.astype(jnp.bfloat16)
    out_local = jnp.einsum("tq,td->qd", head_low, grad_branch, preferred_element_type=jnp.float32)
    grad_heads = (
        jnp.einsum("td,qd->tq", grad_branch, full_out, preferred_element_type=jnp.float32)
        .astype(jnp.bfloat16)
        .reshape(queries.shape)
    )
    grad_queries, grad_keys, grad_values = attend_backward(
        queries, rotated_keys, values, sequence_start, log_total, grad_heads
    )
    grad_queries = grad_queries.reshape(token_count, NHEADS, HEAD)
    query_delta = (
        (grad_queries * cosine_table + rotate_back(grad_queries * sine_table))
        .astype(jnp.bfloat16)
        .reshape(token_count, -1)
    )
    key_delta = (
        (grad_keys * cosine_table + rotate_back(grad_keys * sine_table))
        .astype(jnp.bfloat16)
        .reshape(token_count, -1)
    )
    value_delta = grad_values.astype(jnp.bfloat16).reshape(token_count, -1)
    query_local = jnp.einsum(
        "td,tq->dq", normed_first, query_delta, preferred_element_type=jnp.float32
    )
    key_local = jnp.einsum("td,tq->dq", normed_first, key_delta, preferred_element_type=jnp.float32)
    value_local = jnp.einsum(
        "td,tq->dq", normed_first, value_delta, preferred_element_type=jnp.float32
    )
    grad_first = (
        jnp.einsum("tq,dq->td", query_delta, full_query, preferred_element_type=jnp.float32)
        + jnp.einsum("tq,dq->td", key_delta, full_key, preferred_element_type=jnp.float32)
        + jnp.einsum("tq,dq->td", value_delta, full_value, preferred_element_type=jnp.float32)
    )
    input_extra, prenorm_part = root_back(grad_first, gain_before, scaled_first, inverse_first)
    grad_tokens = grad_middle + input_extra
    low_local = jnp.concatenate([query_local, key_local, value_local, out_local], axis=1)
    low_share = lax.psum_scatter(
        low_local.astype(jnp.bfloat16), ("shard", "rep"), scatter_dimension=0, tiled=True
    )
    low_grad = lax.all_gather(low_share, "rep", axis=0, tiled=True).astype(jnp.float32)
    low_moment = jnp.concatenate([query_moment, key_moment, value_moment, out_moment], axis=1)
    low_next = momentum_keep * low_moment + low_grad
    next_piece = lax.dynamic_slice_in_dim(low_next, rep_index * piece_rows, piece_rows, 0)
    next_all = lax.all_gather(
        next_piece.astype(jnp.bfloat16), ("shard", "rep"), axis=0, tiled=True
    ).astype(jnp.float32)
    gains_grad = lax.psum(jnp.stack([prenorm_part, midnorm_part]), ("shard", "rep"))
    gains_here = lax.dynamic_slice_in_dim(gains_grad, shard_index * row_block, row_block, 1)
    prenorm_grad = gains_here[0]
    midnorm_grad = gains_here[1]
    gate_grad, up_grad, down_grad = lax.psum(
        (
            gate_sum.astype(jnp.bfloat16),
            up_sum.astype(jnp.bfloat16),
            down_sum.astype(jnp.bfloat16),
        ),
        "rep",
    )
    gate_grad = gate_grad.astype(jnp.float32)
    up_grad = up_grad.astype(jnp.float32)
    down_grad = down_grad.astype(jnp.float32)
    query_grad, key_grad, value_grad, out_grad = jnp.split(low_grad, (1024, 1536, 2048), axis=1)
    query_next, key_next, value_next, out_next = jnp.split(low_next, (1024, 1536, 2048), axis=1)
    prenorm_next = momentum_keep * prenorm_moment + prenorm_grad
    midnorm_next = momentum_keep * midnorm_moment + midnorm_grad
    gate_next = momentum_keep * gate_moment + gate_grad
    up_next = momentum_keep * up_moment + up_grad
    down_next = momentum_keep * down_moment + down_grad
    prenorm_update = -rate_gain * prenorm_next
    midnorm_update = -rate_gain * midnorm_next
    gate_update = matrix_update(gate_next)
    up_update = matrix_update(up_next)
    down_update = matrix_update(down_next)
    query_update, key_update, value_update, out_update = (
        lax.dynamic_slice_in_dim(matrix_update(whole), shard_index * row_block, row_block, 0)
        for whole in jnp.split(next_all, (1024, 1536, 2048), axis=1)
    )
    return (
        mixed.astype(jnp.bfloat16),
        grad_tokens,
        query_grad,
        query_next,
        query_update,
        key_grad,
        key_next,
        key_update,
        value_grad,
        value_next,
        value_update,
        out_grad,
        out_next,
        out_update,
        prenorm_grad,
        prenorm_next,
        prenorm_update,
        midnorm_grad,
        midnorm_next,
        midnorm_update,
        gate_grad,
        gate_next,
        gate_update,
        up_grad,
        up_next,
        up_update,
        down_grad,
        down_next,
        down_update,
    )


def solution(mesh):
    return jax.shard_map(
        local,
        mesh=mesh,
        in_specs=(
            P(("rep", "shard"), None),
            P(("rep", "shard")),
            P(("rep", "shard"), None),
            P(("rep", "shard"), None),
            P(("rep", "shard"), None),
            P("shard", None),
            P("shard", None),
            P("shard", None),
            P("shard", None),
            P("shard"),
            P("shard"),
            P("shard", None, None),
            P("shard", None, None),
            P("shard", None, None),
            P("shard", None),
            P("shard", None),
            P("shard", None),
            P("shard", None),
            P("shard"),
            P("shard"),
            P("shard", None, None),
            P("shard", None, None),
            P("shard", None, None),
        ),
        out_specs=(
            P(("rep", "shard"), None),
            P(("rep", "shard"), None),
            P("shard", None),
            P("shard", None),
            P("shard", None),
            P("shard", None),
            P("shard", None),
            P("shard", None),
            P("shard", None),
            P("shard", None),
            P("shard", None),
            P("shard", None),
            P("shard", None),
            P("shard", None),
            P("shard"),
            P("shard"),
            P("shard"),
            P("shard"),
            P("shard"),
            P("shard"),
            P("shard", None, None),
            P("shard", None, None),
            P("shard", None, None),
            P("shard", None, None),
            P("shard", None, None),
            P("shard", None, None),
            P("shard", None, None),
            P("shard", None, None),
            P("shard", None, None),
        ),
        check_vma=False,
    )
```

```python
import functools
import math

import jax
import jax.numpy as jnp
from jax import lax
from jax.experimental import pallas as pl
from jax.experimental.pallas import tpu as pltpu
from jax.sharding import PartitionSpec as P

NHEADS = 16
KVHEADS = 8
HEAD = 64
EXPERTS = 16
NS_ITERS = 2
BLOCK = 256


norm_epsilon = 1e-06
rotary_base = 10000.0
momentum_keep = 0.9
rate_matrix = 0.5
rate_gain = 0.0002
newton_first = 3.4445
newton_second = -4.775
newton_third = 2.0315
masked_score = -1e30


def root_scale(values):
    inverse = lax.rsqrt(jnp.mean(values * values, axis=-1, keepdims=True) + norm_epsilon)
    return (values * inverse, inverse)


def root_back(grad_normed, scaling, scaled, inverse):
    grad_scaled = grad_normed * scaling
    inner_mean = jnp.mean(grad_scaled * scaled, axis=-1, keepdims=True)
    return (inverse * (grad_scaled - scaled * inner_mean), jnp.sum(grad_normed * scaled, axis=0))


def rotary_tables(positions):
    half_size = HEAD // 2
    frequency = rotary_base ** (-(jnp.arange(half_size, dtype=jnp.float32) * 2.0) / HEAD)
    angles = positions.astype(jnp.float32)[:, None] * frequency[None, :]
    angles = jnp.concatenate([angles, angles], axis=-1)
    return (jnp.cos(angles)[:, None, :], jnp.sin(angles)[:, None, :])


def rotate_half(values):
    half_size = values.shape[-1] // 2
    return jnp.concatenate([-values[..., half_size:], values[..., :half_size]], axis=-1)


def rotate_back(values):
    half_size = values.shape[-1] // 2
    return jnp.concatenate([values[..., half_size:], -values[..., :half_size]], axis=-1)


def block_scores(query_block, rotated_keys, start_block, sequence_start, offset):
    scores = jnp.einsum(
        "qkgd,tkd->kgqt", query_block, rotated_keys, preferred_element_type=jnp.float32
    ) * (1.0 / math.sqrt(HEAD))
    key_places = jnp.arange(rotated_keys.shape[0], dtype=jnp.int32)
    query_places = offset + jnp.arange(query_block.shape[0], dtype=jnp.int32)
    allowed = (start_block[:, None] == sequence_start[None, :]) & (
        key_places[None, :] <= query_places[:, None]
    )
    return jnp.where(allowed, scores, masked_score)


def attend_forward(queries, rotated_keys, values, sequence_start):
    block_count = queries.shape[0] // BLOCK

    def one_block(pieces):
        query_block, start_block, offset = pieces
        scores = block_scores(query_block, rotated_keys, start_block, sequence_start, offset)
        row_max = jnp.max(scores, axis=-1, keepdims=True)
        exponents = jnp.exp(scores - row_max)
        totals = jnp.sum(exponents, axis=-1, keepdims=True)
        softmax_low = (exponents / totals).astype(jnp.bfloat16)
        attended = jnp.einsum(
            "kgqt,tkd->qkgd", softmax_low, values, preferred_element_type=jnp.float32
        )
        return (attended, row_max + jnp.log(totals))

    shaped = queries.reshape((block_count, BLOCK) + queries.shape[1:])
    offsets = jnp.arange(block_count, dtype=jnp.int32) * BLOCK
    attended, log_total = lax.map(
        one_block, (shaped, sequence_start.reshape(block_count, BLOCK), offsets)
    )
    return (attended.reshape(queries.shape[0], -1), log_total)


def attend_backward(queries, rotated_keys, values, sequence_start, log_total, grad_heads):
    block_count = queries.shape[0] // BLOCK
    score_scale = 1.0 / math.sqrt(HEAD)

    def one_block(running, pieces):
        grad_keys, grad_values = running
        query_block, start_block, offset, log_block, grad_block = pieces
        scores = block_scores(query_block, rotated_keys, start_block, sequence_start, offset)
        softmax_full = jnp.exp(scores - log_block)
        grad_softmax = jnp.einsum(
            "qkgd,tkd->kgqt", grad_block, values, preferred_element_type=jnp.float32
        )
        inner_sum = jnp.sum(softmax_full * grad_softmax, axis=-1, keepdims=True)
        grad_scores = (softmax_full * (grad_softmax - inner_sum)).astype(jnp.bfloat16)
        grad_query = (
            jnp.einsum(
                "kgqt,tkd->qkgd", grad_scores, rotated_keys, preferred_element_type=jnp.float32
            )
            * score_scale
        )
        grad_keys = (
            grad_keys
            + jnp.einsum(
                "kgqt,qkgd->tkd", grad_scores, query_block, preferred_element_type=jnp.float32
            )
            * score_scale
        )
        grad_values = grad_values + jnp.einsum(
            "kgqt,qkgd->tkd",
            softmax_full.astype(jnp.bfloat16),
            grad_block,
            preferred_element_type=jnp.float32,
        )
        return ((grad_keys, grad_values), grad_query)

    shaped = queries.reshape((block_count, BLOCK) + queries.shape[1:])
    grad_shaped = grad_heads.reshape((block_count, BLOCK) + queries.shape[1:])
    offsets = jnp.arange(block_count, dtype=jnp.int32) * BLOCK
    key_zeros = jnp.zeros(rotated_keys.shape, jnp.float32)
    finals, grad_queries = lax.scan(
        one_block,
        (key_zeros, key_zeros),
        (shaped, sequence_start.reshape(block_count, BLOCK), offsets, log_total, grad_shaped),
    )
    return (grad_queries.reshape(queries.shape), finals[0], finals[1])


def newton_parts(gram):
    a, b, c = newton_first, newton_second, newton_third

    def times(left, right):
        return jnp.dot(left, right, preferred_element_type=jnp.float32)

    low = gram.astype(jnp.bfloat16)
    first = b * gram + c * times(low, low)
    first_low = first.astype(jnp.bfloat16)
    mixed_term = times(low, first_low)
    second_gram = (a * a) * gram + (2.0 * a) * mixed_term + times(
        mixed_term.astype(jnp.bfloat16), first_low
    )
    second_low = second_gram.astype(jnp.bfloat16)
    second = b * second_gram + c * times(second_low, second_low)
    return (first, first_low, second, second.astype(jnp.bfloat16))


def expert_update_kernel(tall, scale, grad_ref, moment_ref, grad_out, next_out, update_out):
    a = newton_first
    grad = grad_ref[0].astype(jnp.float32)
    moment = momentum_keep * moment_ref[0] + grad
    grad_out[0] = grad
    next_out[0] = moment
    inverse = 1.0 / (jnp.sqrt(jnp.sum(moment * moment)) + 1e-07)
    low = (moment * inverse).astype(jnp.bfloat16)
    sides = (((0,), (0,)), ((), ())) if tall else (((1,), (1,)), ((), ()))
    gram = lax.dot_general(low, low, sides, preferred_element_type=jnp.float32)
    first, first_low, second, second_low = newton_parts(gram)
    rest = a * (first + second) + jnp.dot(
        first_low, second_low, preferred_element_type=jnp.float32
    )
    rest = rest.astype(jnp.bfloat16)
    if tall:
        step = jnp.dot(low, rest, preferred_element_type=jnp.float32)
    else:
        step = jnp.dot(rest, low, preferred_element_type=jnp.float32)
    update_out[0] = (-scale * a * a * inverse) * next_out[0] - scale * step


def expert_update(grad, moment):
    count, rows, columns = moment.shape
    scale = rate_matrix * math.sqrt(max(1.0, columns / rows))
    block = pl.BlockSpec((1, rows, columns), lambda i: (i, 0, 0))
    shape = jax.ShapeDtypeStruct(moment.shape, jnp.float32)
    return pl.pallas_call(
        functools.partial(expert_update_kernel, rows > columns, scale),
        grid=(count,),
        in_specs=[block, block],
        out_specs=[block, block, block],
        out_shape=[shape, shape, shape],
        compiler_params=pltpu.CompilerParams(vmem_limit_bytes=56 * 1024 * 1024),
        name="expert_update",
        cost_estimate=pl.CostEstimate(
            flops=count * 2500000000, bytes_accessed=moment.size * 18, transcendentals=0
        ),
    )(grad, moment)


def dense_update_kernel(layout, start_ref, whole_ref, *outs):
    a = newton_first
    block_rows = outs[0].shape[0]
    start = pl.multiple_of(start_ref[0] * block_rows, block_rows)
    for (begin, width), out in zip(layout, outs):
        columns = pl.ds(begin, width)
        matrix = whole_ref[:, columns].astype(jnp.float32)
        scale = rate_matrix * math.sqrt(max(1.0, width / matrix.shape[0]))
        inverse = 1.0 / (jnp.sqrt(jnp.sum(matrix * matrix)) + 1e-07)
        low = (matrix * inverse).astype(jnp.bfloat16)
        gram = lax.dot_general(
            low, low, (((0,), (0,)), ((), ())), preferred_element_type=jnp.float32
        )
        first, first_low, second, second_low = newton_parts(gram)
        own = whole_ref[pl.ds(start, block_rows), columns].astype(jnp.float32) * inverse
        once = a * own + jnp.dot(
            own.astype(jnp.bfloat16), first_low, preferred_element_type=jnp.float32
        )
        out[...] = (-scale) * (
            a * once
            + jnp.dot(once.astype(jnp.bfloat16), second_low, preferred_element_type=jnp.float32)
        )


def dense_update(whole, layout, shard_index, block_rows):
    return pl.pallas_call(
        functools.partial(dense_update_kernel, layout),
        in_specs=[
            pl.BlockSpec(memory_space=pltpu.SMEM),
            pl.BlockSpec(memory_space=pltpu.VMEM),
        ],
        out_specs=[pl.BlockSpec(memory_space=pltpu.VMEM)] * len(layout),
        out_shape=[jax.ShapeDtypeStruct((block_rows, width), jnp.float32) for _, width in layout],
        compiler_params=pltpu.CompilerParams(vmem_limit_bytes=60 * 1024 * 1024),
        name="dense_update",
        cost_estimate=pl.CostEstimate(
            flops=28000000000, bytes_accessed=whole.size * 3, transcendentals=0
        ),
    )(shard_index.reshape(1).astype(jnp.int32), whole)


LAYOUT = ((0, 1024), (1024, 512), (1536, 512), (2048, 1024))


def local(
    tokens,
    sequence_start,
    routes,
    route_weights,
    cotangent,
    query_proj,
    key_proj,
    value_proj,
    out_proj,
    prenorm,
    midnorm,
    gate_proj,
    up_proj,
    down_proj,
    query_moment,
    key_moment,
    value_moment,
    out_moment,
    prenorm_moment,
    midnorm_moment,
    gate_moment,
    up_moment,
    down_moment,
):
    rep_index = lax.axis_index("rep")
    shard_index = lax.axis_index("shard")
    rep_count = lax.axis_size("rep")
    shard_count = lax.axis_size("shard")
    row_block = query_proj.shape[0]
    piece_rows = row_block // rep_count
    low_rows = jnp.concatenate([query_proj, key_proj, value_proj, out_proj], axis=1)
    low_piece = lax.dynamic_slice_in_dim(low_rows, rep_index * piece_rows, piece_rows, 0)
    low_all = lax.all_gather(low_piece, ("shard", "rep"), axis=0, tiled=True)
    full_query = low_all[:, :1024]
    full_key = low_all[:, 1024:1536]
    full_value = low_all[:, 1536:2048]
    full_out = low_all[:, 2048:]
    gains = lax.all_gather(jnp.stack([prenorm, midnorm]), "shard", axis=1, tiled=True)
    prenorm_low = gains[0]
    midnorm_low = gains[1]
    experts_here = gate_proj.shape[0]
    dense_weights = jnp.sum(
        jnp.where(
            routes[:, :, None] == jnp.arange(EXPERTS, dtype=jnp.int32)[None, None, :],
            route_weights[:, :, None],
            0.0,
        ),
        axis=1,
    )
    dense_all = lax.all_gather(dense_weights, "shard", axis=0, tiled=True)
    expert_weights = lax.dynamic_slice_in_dim(
        dense_all, shard_index * experts_here, experts_here, 1
    ).T[:, :, None]
    cotangent_all = lax.all_gather(cotangent, "shard", axis=0, tiled=True)
    gain_before = prenorm_low.astype(jnp.float32)
    gain_after = midnorm_low.astype(jnp.float32)
    group_size = NHEADS // KVHEADS
    token_count = tokens.shape[0]
    inputs = tokens.astype(jnp.float32)
    scaled_first, inverse_first = root_scale(inputs)
    normed_first = (scaled_first * gain_before).astype(jnp.bfloat16)
    query_linear = jnp.dot(normed_first, full_query, preferred_element_type=jnp.float32).reshape(
        token_count, NHEADS, HEAD
    )
    key_linear = jnp.dot(normed_first, full_key, preferred_element_type=jnp.float32).reshape(
        token_count, KVHEADS, HEAD
    )
    values = (
        jnp.dot(normed_first, full_value, preferred_element_type=jnp.float32)
        .astype(jnp.bfloat16)
        .reshape(token_count, KVHEADS, HEAD)
    )
    cosine_table, sine_table = rotary_tables(
        jnp.arange(token_count, dtype=jnp.int32) - sequence_start
    )
    queries = (
        (query_linear * cosine_table + rotate_half(query_linear) * sine_table)
        .astype(jnp.bfloat16)
        .reshape(token_count, KVHEADS, group_size, HEAD)
    )
    rotated_keys = (key_linear * cosine_table + rotate_half(key_linear) * sine_table).astype(
        jnp.bfloat16
    )
    head_out, log_total = attend_forward(queries, rotated_keys, values, sequence_start)
    head_low = head_out.astype(jnp.bfloat16)
    middle = inputs + jnp.dot(head_low, full_out, preferred_element_type=jnp.float32)
    scaled_second, inverse_second = root_scale(middle)
    normed_second = (scaled_second * gain_after).astype(jnp.bfloat16)
    routed = lax.all_gather(normed_second, "shard", axis=0, tiled=True)
    gate_linear = jnp.einsum("td,xdf->xtf", routed, gate_proj, preferred_element_type=jnp.float32)
    up_linear = jnp.einsum("td,xdf->xtf", routed, up_proj, preferred_element_type=jnp.float32)
    gate_sigmoid = jax.nn.sigmoid(gate_linear)
    hidden = (gate_linear * gate_sigmoid * up_linear).astype(jnp.bfloat16)
    expert_out = jnp.einsum("xtf,xfd->xtd", hidden, down_proj, preferred_element_type=jnp.float32)
    partial_out = jnp.sum(
        expert_weights * expert_out.astype(jnp.bfloat16).astype(jnp.float32), axis=0
    ).astype(jnp.bfloat16)
    grad_out = (expert_weights * cotangent_all.astype(jnp.float32)[None]).astype(jnp.bfloat16)
    grad_hidden = jnp.einsum("xtd,xfd->xtf", grad_out, down_proj, preferred_element_type=jnp.float32)
    gate_delta = (
        grad_hidden * up_linear * gate_sigmoid * (1.0 + gate_linear * (1.0 - gate_sigmoid))
    ).astype(jnp.bfloat16)
    up_delta = (grad_hidden * gate_linear * gate_sigmoid).astype(jnp.bfloat16)
    grad_routed = (
        jnp.einsum("xtf,xdf->xtd", gate_delta, gate_proj, preferred_element_type=jnp.float32)
        + jnp.einsum("xtf,xdf->xtd", up_delta, up_proj, preferred_element_type=jnp.float32)
    )
    partial_grad = jnp.sum(grad_routed, axis=0).astype(jnp.bfloat16)
    down_sum = jnp.einsum("xtf,xtd->xfd", hidden, grad_out, preferred_element_type=jnp.float32)
    gate_sum = jnp.einsum("td,xtf->xdf", routed, gate_delta, preferred_element_type=jnp.float32)
    up_sum = jnp.einsum("td,xtf->xdf", routed, up_delta, preferred_element_type=jnp.float32)
    back = lax.all_to_all(partial_grad, "shard", split_axis=0, concat_axis=0, tiled=True)
    grad_second = jnp.sum(
        back.reshape(shard_count, token_count, -1).astype(jnp.float32), axis=0
    )
    back_out = lax.all_to_all(partial_out, "shard", split_axis=0, concat_axis=0, tiled=True)
    mixed = middle + jnp.sum(
        back_out.reshape(shard_count, token_count, -1).astype(jnp.float32), axis=0
    )
    grad_mixed = cotangent.astype(jnp.float32)
    middle_extra, midnorm_part = root_back(grad_second, gain_after, scaled_second, inverse_second)
    grad_middle = grad_mixed + middle_extra
    grad_branch = grad_middle.astype(jnp.bfloat16)
    out_local = jnp.einsum("tq,td->qd", head_low, grad_branch, preferred_element_type=jnp.float32)
    grad_heads = (
        jnp.einsum("td,qd->tq", grad_branch, full_out, preferred_element_type=jnp.float32)
        .astype(jnp.bfloat16)
        .reshape(queries.shape)
    )
    grad_queries, grad_keys, grad_values = attend_backward(
        queries, rotated_keys, values, sequence_start, log_total, grad_heads
    )
    grad_queries = grad_queries.reshape(token_count, NHEADS, HEAD)
    query_delta = (
        (grad_queries * cosine_table + rotate_back(grad_queries * sine_table))
        .astype(jnp.bfloat16)
        .reshape(token_count, -1)
    )
    key_delta = (
        (grad_keys * cosine_table + rotate_back(grad_keys * sine_table))
        .astype(jnp.bfloat16)
        .reshape(token_count, -1)
    )
    value_delta = grad_values.astype(jnp.bfloat16).reshape(token_count, -1)
    query_local = jnp.einsum(
        "td,tq->dq", normed_first, query_delta, preferred_element_type=jnp.float32
    )
    key_local = jnp.einsum("td,tq->dq", normed_first, key_delta, preferred_element_type=jnp.float32)
    value_local = jnp.einsum(
        "td,tq->dq", normed_first, value_delta, preferred_element_type=jnp.float32
    )
    grad_first = (
        jnp.einsum("tq,dq->td", query_delta, full_query, preferred_element_type=jnp.float32)
        + jnp.einsum("tq,dq->td", key_delta, full_key, preferred_element_type=jnp.float32)
        + jnp.einsum("tq,dq->td", value_delta, full_value, preferred_element_type=jnp.float32)
    )
    input_extra, prenorm_part = root_back(grad_first, gain_before, scaled_first, inverse_first)
    grad_tokens = grad_middle + input_extra
    low_local = jnp.concatenate([query_local, key_local, value_local, out_local], axis=1)
    low_share = lax.psum_scatter(
        low_local.astype(jnp.bfloat16), ("shard", "rep"), scatter_dimension=0, tiled=True
    )
    low_grad = lax.all_gather(low_share, "rep", axis=0, tiled=True).astype(jnp.float32)
    low_moment = jnp.concatenate([query_moment, key_moment, value_moment, out_moment], axis=1)
    low_next = momentum_keep * low_moment + low_grad
    next_piece = lax.dynamic_slice_in_dim(low_next, rep_index * piece_rows, piece_rows, 0)
    next_all = lax.all_gather(
        next_piece.astype(jnp.bfloat16), ("shard", "rep"), axis=0, tiled=True
    )
    gains_grad = lax.psum(jnp.stack([prenorm_part, midnorm_part]), ("shard", "rep"))
    gains_here = lax.dynamic_slice_in_dim(gains_grad, shard_index * row_block, row_block, 1)
    prenorm_grad = gains_here[0]
    midnorm_grad = gains_here[1]
    gate_grad, up_grad, down_grad = lax.psum(
        (
            gate_sum.astype(jnp.bfloat16),
            up_sum.astype(jnp.bfloat16),
            down_sum.astype(jnp.bfloat16),
        ),
        "rep",
    )
    query_grad, key_grad, value_grad, out_grad = jnp.split(low_grad, (1024, 1536, 2048), axis=1)
    query_next, key_next, value_next, out_next = jnp.split(low_next, (1024, 1536, 2048), axis=1)
    prenorm_next = momentum_keep * prenorm_moment + prenorm_grad
    midnorm_next = momentum_keep * midnorm_moment + midnorm_grad
    prenorm_update = -rate_gain * prenorm_next
    midnorm_update = -rate_gain * midnorm_next
    query_update, key_update, value_update, out_update = dense_update(
        next_all, LAYOUT, shard_index, row_block
    )
    gate_grad, gate_next, gate_update = expert_update(gate_grad, gate_moment)
    up_grad, up_next, up_update = expert_update(up_grad, up_moment)
    down_grad, down_next, down_update = expert_update(down_grad, down_moment)
    return (
        mixed.astype(jnp.bfloat16),
        grad_tokens,
        query_grad,
        query_next,
        query_update,
        key_grad,
        key_next,
        key_update,
        value_grad,
        value_next,
        value_update,
        out_grad,
        out_next,
        out_update,
        prenorm_grad,
        prenorm_next,
        prenorm_update,
        midnorm_grad,
        midnorm_next,
        midnorm_update,
        gate_grad,
        gate_next,
        gate_update,
        up_grad,
        up_next,
        up_update,
        down_grad,
        down_next,
        down_update,
    )


def solution(mesh):
    return jax.shard_map(
        local,
        mesh=mesh,
        in_specs=(
            P(("rep", "shard"), None),
            P(("rep", "shard")),
            P(("rep", "shard"), None),
            P(("rep", "shard"), None),
            P(("rep", "shard"), None),
            P("shard", None),
            P("shard", None),
            P("shard", None),
            P("shard", None),
            P("shard"),
            P("shard"),
            P("shard", None, None),
            P("shard", None, None),
            P("shard", None, None),
            P("shard", None),
            P("shard", None),
            P("shard", None),
            P("shard", None),
            P("shard"),
            P("shard"),
            P("shard", None, None),
            P("shard", None, None),
            P("shard", None, None),
        ),
        out_specs=(
            P(("rep", "shard"), None),
            P(("rep", "shard"), None),
            P("shard", None),
            P("shard", None),
            P("shard", None),
            P("shard", None),
            P("shard", None),
            P("shard", None),
            P("shard", None),
            P("shard", None),
            P("shard", None),
            P("shard", None),
            P("shard", None),
            P("shard", None),
            P("shard"),
            P("shard"),
            P("shard"),
            P("shard"),
            P("shard"),
            P("shard"),
            P("shard", None, None),
            P("shard", None, None),
            P("shard", None, None),
            P("shard", None, None),
            P("shard", None, None),
            P("shard", None, None),
            P("shard", None, None),
            P("shard", None, None),
            P("shard", None, None),
        ),
        check_vma=False,
    )
```

```python
import functools
import math

import jax
import jax.numpy as jnp
from jax import lax
from jax.experimental import pallas as pl
from jax.experimental.pallas import tpu as pltpu
from jax.sharding import PartitionSpec as P

NHEADS = 16
KVHEADS = 8
HEAD = 64
EXPERTS = 16
NS_ITERS = 2
BLOCK = 256


norm_epsilon = 1e-06
rotary_base = 10000.0
momentum_keep = 0.9
rate_matrix = 0.5
rate_gain = 0.0002
newton_first = 3.4445
newton_second = -4.775
newton_third = 2.0315
masked_score = -1e30


def root_scale(values):
    inverse = lax.rsqrt(jnp.mean(values * values, axis=-1, keepdims=True) + norm_epsilon)
    return (values * inverse, inverse)


def root_back(grad_normed, scaling, scaled, inverse):
    grad_scaled = grad_normed * scaling
    inner_mean = jnp.mean(grad_scaled * scaled, axis=-1, keepdims=True)
    return (inverse * (grad_scaled - scaled * inner_mean), jnp.sum(grad_normed * scaled, axis=0))


def rotary_tables(positions):
    half_size = HEAD // 2
    frequency = rotary_base ** (-(jnp.arange(half_size, dtype=jnp.float32) * 2.0) / HEAD)
    angles = positions.astype(jnp.float32)[:, None] * frequency[None, :]
    angles = jnp.concatenate([angles, angles], axis=-1)
    return (jnp.cos(angles)[:, None, :], jnp.sin(angles)[:, None, :])


def rotate_half(values):
    half_size = values.shape[-1] // 2
    return jnp.concatenate([-values[..., half_size:], values[..., :half_size]], axis=-1)


def rotate_back(values):
    half_size = values.shape[-1] // 2
    return jnp.concatenate([values[..., half_size:], -values[..., :half_size]], axis=-1)


def block_scores(query_block, rotated_keys, start_block, sequence_start, offset):
    scores = jnp.einsum(
        "qkgd,tkd->kgqt", query_block, rotated_keys, preferred_element_type=jnp.float32
    ) * (1.0 / math.sqrt(HEAD))
    key_places = jnp.arange(rotated_keys.shape[0], dtype=jnp.int32)
    query_places = offset + jnp.arange(query_block.shape[0], dtype=jnp.int32)
    allowed = (start_block[:, None] == sequence_start[None, :]) & (
        key_places[None, :] <= query_places[:, None]
    )
    return jnp.where(allowed, scores, masked_score)


def attend_forward(queries, rotated_keys, values, sequence_start):
    block_count = queries.shape[0] // BLOCK

    def one_block(pieces):
        query_block, start_block, offset = pieces
        scores = block_scores(query_block, rotated_keys, start_block, sequence_start, offset)
        row_max = jnp.max(scores, axis=-1, keepdims=True)
        exponents = jnp.exp(scores - row_max)
        totals = jnp.sum(exponents, axis=-1, keepdims=True)
        softmax_low = (exponents / totals).astype(jnp.bfloat16)
        attended = jnp.einsum(
            "kgqt,tkd->qkgd", softmax_low, values, preferred_element_type=jnp.float32
        )
        return (attended, row_max + jnp.log(totals))

    shaped = queries.reshape((block_count, BLOCK) + queries.shape[1:])
    offsets = jnp.arange(block_count, dtype=jnp.int32) * BLOCK
    attended, log_total = lax.map(
        one_block, (shaped, sequence_start.reshape(block_count, BLOCK), offsets)
    )
    return (attended.reshape(queries.shape[0], -1), log_total)


def attend_backward(queries, rotated_keys, values, sequence_start, log_total, grad_heads):
    block_count = queries.shape[0] // BLOCK
    score_scale = 1.0 / math.sqrt(HEAD)

    def one_block(running, pieces):
        grad_keys, grad_values = running
        query_block, start_block, offset, log_block, grad_block = pieces
        scores = block_scores(query_block, rotated_keys, start_block, sequence_start, offset)
        softmax_full = jnp.exp(scores - log_block)
        grad_softmax = jnp.einsum(
            "qkgd,tkd->kgqt", grad_block, values, preferred_element_type=jnp.float32
        )
        inner_sum = jnp.sum(softmax_full * grad_softmax, axis=-1, keepdims=True)
        grad_scores = (softmax_full * (grad_softmax - inner_sum)).astype(jnp.bfloat16)
        grad_query = (
            jnp.einsum(
                "kgqt,tkd->qkgd", grad_scores, rotated_keys, preferred_element_type=jnp.float32
            )
            * score_scale
        )
        grad_keys = (
            grad_keys
            + jnp.einsum(
                "kgqt,qkgd->tkd", grad_scores, query_block, preferred_element_type=jnp.float32
            )
            * score_scale
        )
        grad_values = grad_values + jnp.einsum(
            "kgqt,qkgd->tkd",
            softmax_full.astype(jnp.bfloat16),
            grad_block,
            preferred_element_type=jnp.float32,
        )
        return ((grad_keys, grad_values), grad_query)

    shaped = queries.reshape((block_count, BLOCK) + queries.shape[1:])
    grad_shaped = grad_heads.reshape((block_count, BLOCK) + queries.shape[1:])
    offsets = jnp.arange(block_count, dtype=jnp.int32) * BLOCK
    key_zeros = jnp.zeros(rotated_keys.shape, jnp.float32)
    finals, grad_queries = lax.scan(
        one_block,
        (key_zeros, key_zeros),
        (shaped, sequence_start.reshape(block_count, BLOCK), offsets, log_total, grad_shaped),
    )
    return (grad_queries.reshape(queries.shape), finals[0], finals[1])


def newton_parts(gram):
    a, b, c = newton_first, newton_second, newton_third

    def times(left, right):
        return jnp.dot(left, right, preferred_element_type=jnp.float32)

    low = gram.astype(jnp.bfloat16)
    first = b * gram + c * times(low, low)
    first_low = first.astype(jnp.bfloat16)
    mixed_term = times(low, first_low)
    second_gram = (a * a) * gram + (2.0 * a) * mixed_term + times(
        mixed_term.astype(jnp.bfloat16), first_low
    )
    second_low = second_gram.astype(jnp.bfloat16)
    second = b * second_gram + c * times(second_low, second_low)
    return (first, first_low, second, second.astype(jnp.bfloat16))


def expert_update_kernel(kind, scale, grad_ref, moment_ref, grad_out, next_out, update_out):
    a = newton_first
    tall = kind < 2
    half = grad_ref.shape[3]
    if tall:
        grad = grad_ref[0, 0].astype(jnp.float32)
    else:
        grad = jnp.concatenate(
            [grad_ref[0, 0, :half], grad_ref[0, 0, half:]], axis=1
        ).astype(jnp.float32)
    moment = momentum_keep * moment_ref[0] + grad
    grad_out[0] = grad
    next_out[0] = moment
    inverse = 1.0 / (jnp.sqrt(jnp.sum(moment * moment)) + 1e-07)
    low = (moment * inverse).astype(jnp.bfloat16)
    sides = (((0,), (0,)), ((), ())) if tall else (((1,), (1,)), ((), ()))
    gram = lax.dot_general(low, low, sides, preferred_element_type=jnp.float32)
    first, first_low, second, second_low = newton_parts(gram)
    rest = a * (first + second) + jnp.dot(
        first_low, second_low, preferred_element_type=jnp.float32
    )
    rest = rest.astype(jnp.bfloat16)
    if tall:
        step = jnp.dot(low, rest, preferred_element_type=jnp.float32)
    else:
        step = jnp.dot(rest, low, preferred_element_type=jnp.float32)
    update_out[0] = (-scale * a * a * inverse) * next_out[0] - scale * step


def expert_update(grads, kind, moment):
    count, rows, columns = moment.shape
    scale = rate_matrix * math.sqrt(max(1.0, columns / rows))
    block = pl.BlockSpec((1, rows, columns), lambda i: (i, 0, 0))
    taken = pl.BlockSpec((1, 1) + grads.shape[2:], lambda i: (i, kind, 0, 0))
    shape = jax.ShapeDtypeStruct(moment.shape, jnp.float32)
    return pl.pallas_call(
        functools.partial(expert_update_kernel, kind, scale),
        grid=(count,),
        in_specs=[taken, block],
        out_specs=[block, block, block],
        out_shape=[shape, shape, shape],
        compiler_params=pltpu.CompilerParams(vmem_limit_bytes=56 * 1024 * 1024),
        name="expert_update",
        cost_estimate=pl.CostEstimate(
            flops=count * 2500000000, bytes_accessed=moment.size * 18, transcendentals=0
        ),
    )(grads, moment)


def dense_update_kernel(layout, place_ref, grads_ref, moments_ref, *refs):
    a = newton_first
    amount = len(layout)
    own_moments = refs[:amount]
    outs = refs[amount : 4 * amount]
    whole, own_grads = refs[4 * amount :]
    blocks, count, block_rows, width = grads_ref.shape
    me = place_ref[0]
    start = pl.multiple_of(me * block_rows, block_rows)
    for block in range(blocks):
        columns = slice(block * width, (block + 1) * width)
        grads = grads_ref[block].reshape(count * block_rows, width).astype(jnp.float32)
        moments = moments_ref[:, columns].astype(jnp.float32)
        whole[:, columns] = (momentum_keep * moments + grads).astype(jnp.bfloat16)
        own_grads[:, columns] = grads_ref[block, me].astype(jnp.float32)
    for index, (begin, size) in enumerate(layout):
        grad_out, next_out, update_out = outs[3 * index : 3 * index + 3]
        columns = slice(begin, begin + size)
        grad = own_grads[:, columns]
        grad_out[...] = grad
        next_out[...] = momentum_keep * own_moments[index][...] + grad
        matrix = whole[:, columns].astype(jnp.float32)
        scale = rate_matrix * math.sqrt(max(1.0, size / matrix.shape[0]))
        inverse = 1.0 / (jnp.sqrt(jnp.sum(matrix * matrix)) + 1e-07)
        low = (matrix * inverse).astype(jnp.bfloat16)
        gram = lax.dot_general(
            low, low, (((0,), (0,)), ((), ())), preferred_element_type=jnp.float32
        )
        first, first_low, second, second_low = newton_parts(gram)
        own = whole[pl.ds(start, block_rows), columns].astype(jnp.float32) * inverse
        once = a * own + jnp.dot(
            own.astype(jnp.bfloat16), first_low, preferred_element_type=jnp.float32
        )
        update_out[...] = (-scale) * (
            a * once
            + jnp.dot(once.astype(jnp.bfloat16), second_low, preferred_element_type=jnp.float32)
        )


def dense_update(grads, moments, own_moments, layout, shard_index):
    block_rows = grads.shape[2]
    vmem = pl.BlockSpec(memory_space=pltpu.VMEM)
    shapes = []
    for _, width in layout:
        shapes += [jax.ShapeDtypeStruct((block_rows, width), jnp.float32)] * 3
    return pl.pallas_call(
        functools.partial(dense_update_kernel, layout),
        in_specs=[pl.BlockSpec(memory_space=pltpu.SMEM)] + [vmem] * (2 + len(layout)),
        out_specs=[vmem] * len(shapes),
        out_shape=shapes,
        scratch_shapes=[
            pltpu.VMEM(moments.shape, jnp.bfloat16),
            pltpu.VMEM((block_rows, moments.shape[1]), jnp.float32),
        ],
        compiler_params=pltpu.CompilerParams(vmem_limit_bytes=60 * 1024 * 1024),
        name="dense_update",
        cost_estimate=pl.CostEstimate(
            flops=28000000000, bytes_accessed=moments.size * 8, transcendentals=0
        ),
    )(shard_index.reshape(1).astype(jnp.int32), grads, moments, *own_moments)


LAYOUT = ((0, 1024), (1024, 512), (1536, 512), (2048, 1024))


MESH = pl.DeviceIdType.MESH


def flip(index, bit):
    return index + bit - 2 * bit * ((index // bit) % 2)


def greet(peers):
    barrier = pltpu.get_barrier_semaphore()
    for peer in peers:
        pl.semaphore_signal(barrier, inc=1, device_id=peer, device_id_type=MESH)
    pl.semaphore_wait(barrier, len(peers))


def stream_plan(rep, bits, base, size):
    stages = []
    starts = [base, base + size]
    for step in range(len(bits)):
        size = size // 2
        stage = []
        for stream in range(2):
            bit = bits[(step + stream) % len(bits)]
            side = (rep // bit) % 2
            keep = starts[stream] + side * size
            send = starts[stream] + (1 - side) * size
            starts[stream] = keep
            stage.append((bit, stream, keep, send, size))
        stages.append(stage)
    return stages


def rows_of(start, size):
    return pl.ds(pl.multiple_of(start, 16), size)


def moe_kernel(
    count,
    bits,
    own_ref,
    cot_ref,
    weight_ref,
    gate_hbm,
    up_hbm,
    down_hbm,
    out_ref,
    back_ref,
    share_ref,
    tok,
    turned,
    mats,
    hid,
    gate_delta,
    up_delta,
    stage_back,
    stage_out,
    got_back,
    got_out,
    *rest,
):
    landing = rest[: 1 + 2 * len(bits)]
    (
        load_sem,
        right_sem,
        left_sem,
        arrive_sem,
        back_send,
        back_recv,
        out_send,
        out_recv,
        sum_send,
        sum_recv,
    ) = rest[1 + 2 * len(bits) :]
    rep = lax.axis_index("rep")
    me = lax.axis_index("shard")
    experts = mats.shape[0]
    tokens = own_ref.shape[0]
    half = mats.shape[2] // 2
    core = rep % 2

    loads = [
        pltpu.make_async_copy(gate_hbm, mats.at[:, 0], load_sem.at[0]),
        pltpu.make_async_copy(up_hbm, mats.at[:, 1], load_sem.at[1]),
        pltpu.make_async_copy(
            down_hbm.at[:, :, pl.ds(0, half)], mats.at[:, 2, pl.ds(0, half)], load_sem.at[2]
        ),
        pltpu.make_async_copy(
            down_hbm.at[:, :, pl.ds(half, half)], mats.at[:, 2, pl.ds(half, half)], load_sem.at[3]
        ),
    ]
    for load in loads:
        load.start()
    peers = [(rep, lax.rem(me + k, count)) for k in range(1, count)]
    peers += [(flip(rep, bit), me) for bit in (1,) + bits]
    greet(peers)

    right_peer = (rep, jnp.minimum(me + 1, count - 1))
    left_peer = (rep, jnp.maximum(me - 1, 0))

    def hand_on(block, to_right):
        return pltpu.make_async_remote_copy(
            src_ref=tok.at[block],
            dst_ref=tok.at[block],
            send_sem=(right_sem if to_right else left_sem).at[block],
            recv_sem=arrive_sem.at[block],
            device_id=right_peer if to_right else left_peer,
            device_id_type=MESH,
        )

    def returning(stage, got, send_sem, recv_sem, block):
        return pltpu.make_async_remote_copy(
            src_ref=stage.at[block],
            dst_ref=got.at[me],
            send_sem=send_sem.at[block],
            recv_sem=recv_sem.at[me],
            device_id=(rep, block),
            device_id_type=MESH,
        )

    tok[me] = own_ref[...]

    @pl.when(me < count - 1)
    def _():
        hand_on(me, True).start()

    @pl.when(me > 0)
    def _():
        hand_on(me, False).start()

    for load in loads:
        load.wait()

    margin = jnp.minimum(me, count - 1 - me)
    longer = jnp.where(me < count - 1 - me, 1, -1)
    nt = (((1,), (1,)), ((), ()))

    def dot(left, right):
        return jnp.dot(left, right, preferred_element_type=jnp.float32)

    def dot_nt(left, right):
        return lax.dot_general(left, right, nt, preferred_element_type=jnp.float32)

    def visit(j, carry):
        lower = me - j
        upper = me + j

        @pl.when((j > 0) & (lower >= 0))
        def _():
            hand_on(jnp.maximum(lower, 0), True).wait_recv()

            @pl.when(me < count - 1)
            def _():
                hand_on(jnp.maximum(lower, 0), True).start()

        @pl.when((j > 0) & (upper < count))
        def _():
            hand_on(jnp.minimum(upper, count - 1), False).wait_recv()

            @pl.when(me > 0)
            def _():
                hand_on(jnp.minimum(upper, count - 1), False).start()

        near = (j + 1) // 2
        alternating = me + near - 2 * near * (j % 2)
        block = jnp.where(j <= 2 * margin, alternating, me + longer * (j - margin))
        places = pl.ds(pl.multiple_of(block * tokens, tokens), tokens)
        rows = tok[block]
        grads = cot_ref[block]
        turned[:, places] = rows.T
        hiddens = []
        for e in range(experts):
            weight = weight_ref[block, :, e : e + 1]
            u = dot(rows, mats[e, 0])
            w = dot(rows, mats[e, 1])
            gate = 1.0 / (1.0 + jnp.exp(-u))
            act = u * gate
            hidden = (weight * (act * w)).astype(jnp.bfloat16)
            hid[e, :, places] = hidden.T
            hiddens.append(hidden)
            pulled = weight * (
                dot_nt(grads[:, :half], mats[e, 2, :half])
                + dot_nt(grads[:, half:], mats[e, 2, half:])
            )
            gate_delta[e, places] = (pulled * w * (gate + act * (1.0 - gate))).astype(jnp.bfloat16)
            up_delta[e, places] = (pulled * act).astype(jnp.bfloat16)
        for side in range(2):
            part = slice(side * half, (side + 1) * half)
            total_back = None
            total_out = None
            for e in range(experts):
                back = dot_nt(gate_delta[e, places], mats[e, 0, part]) + dot_nt(
                    up_delta[e, places], mats[e, 1, part]
                )
                out = dot(hiddens[e], mats[e, 2, part])
                total_back = back if e == 0 else total_back + back
                total_out = out if e == 0 else total_out + out
            stage_back[block, :, part] = total_back.astype(jnp.bfloat16)
            stage_out[block, :, part] = total_out.astype(jnp.bfloat16)

        @pl.when(j > 0)
        def _():
            returning(stage_back, got_back, back_send, back_recv, block).start()

        return carry

    lax.fori_loop(0, count, visit, 0)
    for k in range(1, count):
        returning(stage_out, got_out, out_send, out_recv, lax.rem(me + k, count)).start()

    plan = stream_plan(rep, bits, core * half, half // 2)

    def sum_copy(stage, slot, e, start, size, bit):
        return pltpu.make_async_remote_copy(
            src_ref=mats.at[e, :, rows_of(start, size)],
            dst_ref=landing[slot].at[e],
            send_sem=sum_send.at[slot, e],
            recv_sem=sum_recv.at[slot, e],
            device_id=(flip(rep, bit), me),
            device_id_type=MESH,
        )

    def copies(stage, e):
        if stage == 0:
            return [(sum_copy(0, 0, e, (1 - core) * half, half, 1), 0, core * half, half)]
        return [
            (
                sum_copy(stage, 1 + 2 * (stage - 1) + stream, e, send, size, bit),
                1 + 2 * (stage - 1) + stream,
                keep,
                size,
            )
            for bit, stream, keep, send, size in plan[stage - 1]
        ]

    def finish(stage, e):
        for copy, slot, keep, size in copies(stage, e):
            copy.wait_recv()
            place = rows_of(keep, size)
            for kind in range(3):
                mats[e, kind, place] = (
                    mats[e, kind, place].astype(jnp.float32)
                    + landing[slot][e, kind].astype(jnp.float32)
                ).astype(jnp.bfloat16)

    stages = 1 + len(bits)
    for turn in range(experts + stages):
        if turn < experts:
            e = turn
            for side in range(2):
                part = slice(side * half, (side + 1) * half)
                mats[e, 0, part] = dot(turned[part], gate_delta[e]).astype(jnp.bfloat16)
                mats[e, 1, part] = dot(turned[part], up_delta[e]).astype(jnp.bfloat16)
                mats[e, 2, part] = dot(hid[e], cot_ref[:, :, part].reshape(count * tokens, half)).astype(jnp.bfloat16)
            copies(0, e)[0][0].start()
        for stage in range(stages):
            e = turn - 1 - stage
            if 0 <= e < experts:
                finish(stage, e)
                if stage + 1 < stages:
                    for copy, _, _, _ in copies(stage + 1, e):
                        copy.start()
                else:
                    for _, stream, keep, _, size in plan[-1]:
                        share_ref[e, :, stream] = mats[e, :, rows_of(keep, size)]

    total = stage_back[me].astype(jnp.float32)
    for k in range(1, count):
        source = lax.rem(me + k, count)
        pltpu.make_async_remote_copy(
            src_ref=stage_back.at[source],
            dst_ref=got_back.at[source],
            send_sem=back_send.at[source],
            recv_sem=back_recv.at[source],
            device_id=(rep, source),
            device_id_type=MESH,
        ).wait_recv()
        total = total + got_back[source].astype(jnp.float32)
    back_ref[...] = total
    total = stage_out[me].astype(jnp.float32)
    for k in range(1, count):
        source = lax.rem(me + k, count)
        pltpu.make_async_remote_copy(
            src_ref=stage_out.at[source],
            dst_ref=got_out.at[source],
            send_sem=out_send.at[source],
            recv_sem=out_recv.at[source],
            device_id=(rep, source),
            device_id_type=MESH,
        ).wait_recv()
        total = total + got_out[source].astype(jnp.float32)
    out_ref[...] = total

    for k in range(1, count):
        block = lax.rem(me + k, count)
        returning(stage_back, got_back, back_send, back_recv, block).wait_send()
        returning(stage_out, got_out, out_send, out_recv, block).wait_send()
    for e in range(experts):
        for stage in range(stages):
            for copy, _, _, _ in copies(stage, e):
                copy.wait_send()
    for block in range(count):

        @pl.when((block <= me) & (me < count - 1))
        def _():
            hand_on(block, True).wait_send()

        @pl.when((block >= me) & (me > 0))
        def _():
            hand_on(block, False).wait_send()


def moe(normed, cotangents, weights, gate_proj, up_proj, down_proj, bits, count):
    tokens, width = normed.shape
    experts, _, hidden = gate_proj.shape
    half = width // 2
    low = jnp.bfloat16
    final = (half // 2) >> len(bits)
    vmem = pl.BlockSpec(memory_space=pltpu.VMEM)
    anywhere = pl.BlockSpec(memory_space=pl.ANY)
    landings = [pltpu.VMEM((experts, 3, half, hidden), low)]
    for step in range(len(bits)):
        size = (half // 2) >> (step + 1)
        landings += [pltpu.VMEM((experts, 3, size, hidden), low)] * 2
    slots = len(landings)
    dma = pltpu.SemaphoreType.DMA
    return pl.pallas_call(
        functools.partial(moe_kernel, count, bits),
        in_specs=[vmem, vmem, vmem, anywhere, anywhere, anywhere],
        out_specs=[vmem, vmem, vmem],
        out_shape=[
            jax.ShapeDtypeStruct((tokens, width), jnp.float32),
            jax.ShapeDtypeStruct((tokens, width), jnp.float32),
            jax.ShapeDtypeStruct((experts, 3, 2, final, hidden), low),
        ],
        scratch_shapes=[
            pltpu.VMEM((count, tokens, width), low),
            pltpu.VMEM((width, count * tokens), low),
            pltpu.VMEM((experts, 3, width, hidden), low),
            pltpu.VMEM((experts, hidden, count * tokens), low),
            pltpu.VMEM((experts, count * tokens, hidden), low),
            pltpu.VMEM((experts, count * tokens, hidden), low),
            pltpu.VMEM((count, tokens, width), low),
            pltpu.VMEM((count, tokens, width), low),
            pltpu.VMEM((count, tokens, width), low),
            pltpu.VMEM((count, tokens, width), low),
        ]
        + landings
        + [
            dma((4,)),
            dma((count,)),
            dma((count,)),
            dma((count,)),
            dma((count,)),
            dma((count,)),
            dma((count,)),
            dma((count,)),
            dma((slots, experts)),
            dma((slots, experts)),
        ],
        compiler_params=pltpu.CompilerParams(
            collective_id=1, has_side_effects=True, vmem_limit_bytes=63 * 1024 * 1024
        ),
        name="moe",
        cost_estimate=pl.CostEstimate(
            flops=39000000000, bytes_accessed=20000000, transcendentals=2000000
        ),
    )(normed, cotangents, weights, gate_proj, up_proj, down_proj)


def rep_bits(rep_count):
    bits = []
    bit = 2
    while bit < rep_count:
        bits.append(bit)
        bit = bit * 2
    return tuple(bits)


def spread_kernel(
    count,
    bits,
    share_ref,
    dense_ref,
    gains_ref,
    experts_out,
    dense_out,
    gains_out,
    total,
    land_core,
    land_first,
    *rest,
):
    later = len(bits) - 1
    land_later = rest[:later]
    (
        piece_send,
        piece_land,
        piece,
        gains_send,
        gains_land,
        gains_all,
        local_sem,
        core_send,
        core_recv,
        half_send,
        half_recv,
        shard_send,
        shard_recv,
        grow_send,
        grow_recv,
        line_send,
        line_recv,
        join_send,
        join_recv,
        expert_send,
        expert_recv,
        gain_send,
        gain_recv,
        gain_line_send,
        gain_line_recv,
    ) = rest[later:]
    rep = lax.axis_index("rep")
    me = lax.axis_index("shard")
    core = rep % 2
    rows = dense_ref.shape[2]
    expert_rows = experts_out.shape[2]
    steps = len(bits)
    streams = range(2)

    def remote(source, target, send_sem, recv_sem, peer):
        return pltpu.make_async_remote_copy(
            src_ref=source,
            dst_ref=target,
            send_sem=send_sem,
            recv_sem=recv_sem,
            device_id=peer,
            device_id_type=MESH,
        )

    def across(bit):
        return (flip(rep, bit), me)

    def order(stream):
        return [bits[(step + stream) % steps] for step in range(steps)]

    def side(bit):
        return (rep // bit) % 2

    plan = stream_plan(rep, bits, core * (expert_rows // 2), expert_rows // 4)
    base = [(core * (expert_rows // 2)) + stream * (expert_rows // 4) for stream in streams]

    def expert_copy(level, stream):
        if level == steps:
            place = rows_of(base[stream], expert_rows // 4)
            peer = across(1)
        else:
            bit, _, keep, _, size = plan[steps - 1 - level][stream]
            place = rows_of(keep, size)
            peer = across(bit)
        source = experts_out.at[:, :, place]
        if level == 0:
            source = share_ref.at[:, :, stream]
        return remote(
            source,
            experts_out.at[:, :, place],
            expert_send.at[level, stream],
            expert_recv.at[level, stream],
            peer,
        )

    def own_copy(stream):
        _, _, keep, _, size = plan[-1][stream]
        return pltpu.make_async_copy(
            share_ref.at[:, :, stream],
            experts_out.at[:, :, rows_of(keep, size)],
            local_sem.at[stream],
        )

    for stream in streams:
        own_copy(stream).start()
    peers = [(rep, lax.rem(me + k, count)) for k in range(1, count)]
    peers += [across(bit) for bit in (1,) + bits]
    greet(peers)

    def core_copy(block):
        return remote(
            dense_ref.at[4 * (1 - core) + block],
            land_core.at[block],
            core_send.at[block],
            core_recv.at[block],
            across(1),
        )

    gain_bits = (1,) + bits

    def gain_copy(stage):
        return remote(
            gains_send.at[stage],
            gains_land.at[stage],
            gain_send.at[stage],
            gain_recv.at[stage],
            across(gain_bits[stage]),
        )

    gains_send[0] = gains_ref[...]
    gain_copy(0).start()
    for block in range(4):
        core_copy(block).start()
    for stream in streams:
        expert_copy(0, stream).start()

    def gain_step(stage):
        gain_copy(stage).wait_recv()
        gains_send[stage + 1] = gains_send[stage] + gains_land[stage]
        if stage + 1 < len(gain_bits):
            gain_copy(stage + 1).start()

    first = [side(order(stream)[0]) for stream in streams]
    held = [2 * stream + first[stream] for stream in streams]
    given = [2 * stream + 1 - first[stream] for stream in streams]

    def first_copy(stream):
        return remote(
            total.at[given[stream]],
            land_first.at[stream],
            half_send.at[0, stream],
            half_recv.at[0, stream],
            across(order(stream)[0]),
        )

    def add_core(block):
        for line in range(count):
            total[block, line] = (
                dense_ref[4 * core + block, line].astype(jnp.float32)
                + land_core[block, line].astype(jnp.float32)
            ).astype(jnp.bfloat16)

    for block in range(4):
        core_copy(block).wait_recv()
    for stream in streams:
        add_core(given[stream])
        first_copy(stream).start()
    for stream in streams:
        add_core(held[stream])
    gain_step(0)

    starts = []
    for stream in streams:
        start, size, line = 0, rows, []
        for step in range(1, steps):
            size = size // 2
            near = side(order(stream)[step])
            line.append((start + near * size, start + (1 - near) * size, size))
            start = start + near * size
        starts.append((start, size, line))

    def later_copy(step, stream):
        keep, send, size = starts[stream][2][step - 1]
        return remote(
            total.at[held[stream], :, rows_of(send, size)],
            land_later[step - 1].at[stream],
            half_send.at[step, stream],
            half_recv.at[step, stream],
            across(order(stream)[step]),
        )

    for stream in streams:
        first_copy(stream).wait_recv()
        for line in range(count):
            total[held[stream], line] = (
                total[held[stream], line].astype(jnp.float32)
                + land_first[stream, line].astype(jnp.float32)
            ).astype(jnp.bfloat16)
        if steps > 1:
            later_copy(1, stream).start()
    gain_step(1)

    for stream in streams:
        own_copy(stream).wait()
        expert_copy(0, stream).wait_recv()
        if steps > 1:
            expert_copy(1, stream).start()

    for step in range(1, steps):
        for stream in streams:
            later_copy(step, stream).wait_recv()
            keep, _, size = starts[stream][2][step - 1]
            for line in range(count):
                place = rows_of(keep, size)
                total[held[stream], line, place] = (
                    total[held[stream], line, place].astype(jnp.float32)
                    + land_later[step - 1][stream, line].astype(jnp.float32)
                ).astype(jnp.bfloat16)
            if step + 1 < steps:
                later_copy(step + 1, stream).start()
        gain_step(step + 1)

    last = starts[0][1]
    places = [rows_of(starts[stream][0], last) for stream in streams]
    for stream in streams:
        for line in range(count):
            piece_send[line, stream] = total[held[stream], line, places[stream]]

    def shard_copy(k):
        target = lax.rem(me + k, count)
        return remote(
            piece_send.at[target],
            piece_land.at[me],
            shard_send.at[target],
            shard_recv.at[me],
            (rep, target),
        )

    def shard_arrival(source):
        return remote(
            piece_send.at[source],
            piece_land.at[source],
            shard_send.at[source],
            shard_recv.at[source],
            (rep, source),
        )

    def gain_line(k):
        target = lax.rem(me + k, count)
        return remote(
            gains_send.at[len(gain_bits)],
            gains_all.at[me],
            gain_line_send.at[target],
            gain_line_recv.at[me],
            (rep, target),
        )

    def gain_arrival(source):
        return remote(
            gains_send.at[len(gain_bits)],
            gains_all.at[source],
            gain_line_send.at[source],
            gain_line_recv.at[source],
            (rep, source),
        )

    for k in range(1, count):
        shard_copy(k).start()
        gain_line(k).start()
    summed = piece_send[me].astype(jnp.float32)
    for k in range(1, count):
        source = lax.rem(me + k, count)
        shard_arrival(source).wait_recv()
        summed = summed + piece_land[source].astype(jnp.float32)
    piece[...] = summed.astype(jnp.bfloat16)

    def line_copy(k, stream):
        target = lax.rem(me + k, count)
        return remote(
            piece.at[stream],
            dense_out.at[4 * core + held[stream], me, places[stream]],
            line_send.at[stream, target],
            line_recv.at[stream, me],
            (rep, target),
        )

    def line_arrival(source, stream):
        return remote(
            piece.at[stream],
            dense_out.at[4 * core + held[stream], source, places[stream]],
            line_send.at[stream, source],
            line_recv.at[stream, source],
            (rep, source),
        )

    def own_piece(stream):
        return pltpu.make_async_copy(
            piece.at[stream],
            dense_out.at[4 * core + held[stream], me, places[stream]],
            local_sem.at[2 + stream],
        )

    for stream in streams:
        own_piece(stream).start()
        for k in range(1, count):
            line_copy(k, stream).start()
    gained = gains_send[len(gain_bits)]
    for k in range(1, count):
        source = lax.rem(me + k, count)
        gain_arrival(source).wait_recv()
        gained = gained + gains_all[source]
    gains_out[...] = gained

    for level in range(1, steps):
        for stream in streams:
            expert_copy(level, stream).wait_recv()
            expert_copy(level + 1, stream).start()
    if steps == 1:
        for stream in streams:
            expert_copy(1, stream).start()

    def grow_copy(step, stream):
        if step == 0:
            place = dense_out.at[4 * core + held[stream]]
        else:
            keep, _, size = starts[stream][2][step - 1]
            place = dense_out.at[4 * core + held[stream], :, rows_of(keep, size)]
        return remote(
            place,
            place,
            grow_send.at[step, stream],
            grow_recv.at[step, stream],
            across(order(stream)[step]),
        )

    for stream in streams:
        own_piece(stream).wait()
        for k in range(1, count):
            line_arrival(lax.rem(me + k, count), stream).wait_recv()
        grow_copy(steps - 1, stream).start()
    for step in reversed(range(steps)):
        for stream in streams:
            grow_copy(step, stream).wait_recv()
            if step > 0:
                grow_copy(step - 1, stream).start()

    def join_copy(stream):
        place = dense_out.at[pl.ds(4 * core + 2 * stream, 2)]
        return remote(place, place, join_send.at[stream], join_recv.at[stream], across(1))

    for stream in streams:
        join_copy(stream).start()
    for stream in streams:
        join_copy(stream).wait()
        expert_copy(steps, stream).wait()
        for level in range(steps):
            expert_copy(level, stream).wait_send()
        first_copy(stream).wait_send()
        for step in range(1, steps):
            later_copy(step, stream).wait_send()
        for k in range(1, count):
            line_copy(k, stream).wait_send()
        for step in range(steps):
            grow_copy(step, stream).wait_send()
    for block in range(4):
        core_copy(block).wait_send()
    for stage in range(len(gain_bits)):
        gain_copy(stage).wait_send()
    for k in range(1, count):
        shard_copy(k).wait_send()
        gain_line(k).wait_send()


def spread(share, dense, gains, bits, count):
    experts, _, _, final, hidden = share.shape
    blocks, _, rows, width = dense.shape
    steps = len(bits)
    last = rows >> (steps - 1)
    low = jnp.bfloat16
    vmem = pl.BlockSpec(memory_space=pltpu.VMEM)
    anywhere = pl.BlockSpec(memory_space=pl.ANY)
    dma = pltpu.SemaphoreType.DMA
    return pl.pallas_call(
        functools.partial(spread_kernel, count, bits),
        in_specs=[vmem, vmem, vmem],
        out_specs=[anywhere, anywhere, vmem],
        out_shape=[
            jax.ShapeDtypeStruct((experts, 3, 4 * (final << steps), hidden), low),
            jax.ShapeDtypeStruct(dense.shape, low),
            jax.ShapeDtypeStruct(gains.shape, jnp.float32),
        ],
        scratch_shapes=[
            pltpu.VMEM((4, count, rows, width), low),
            pltpu.VMEM((4, count, rows, width), low),
            pltpu.VMEM((2, count, rows, width), low),
        ]
        + [pltpu.VMEM((2, count, rows >> step, width), low) for step in range(1, steps)]
        + [
            pltpu.VMEM((count, 2, last, width), low),
            pltpu.VMEM((count, 2, last, width), low),
            pltpu.VMEM((2, last, width), low),
            pltpu.VMEM((steps + 2,) + gains.shape, jnp.float32),
            pltpu.VMEM((steps + 1,) + gains.shape, jnp.float32),
            pltpu.VMEM((count,) + gains.shape, jnp.float32),
            dma((4,)),
            dma((4,)),
            dma((4,)),
            dma((steps, 2)),
            dma((steps, 2)),
            dma((count,)),
            dma((count,)),
            dma((steps, 2)),
            dma((steps, 2)),
            dma((2, count)),
            dma((2, count)),
            dma((2,)),
            dma((2,)),
            dma((steps + 1, 2)),
            dma((steps + 1, 2)),
            dma((steps + 1,)),
            dma((steps + 1,)),
            dma((count,)),
            dma((count,)),
        ],
        compiler_params=pltpu.CompilerParams(
            collective_id=2, has_side_effects=True, vmem_limit_bytes=48 * 1024 * 1024
        ),
        name="spread",
    )(share, dense, gains)


def local(
    tokens,
    sequence_start,
    routes,
    route_weights,
    cotangent,
    query_proj,
    key_proj,
    value_proj,
    out_proj,
    prenorm,
    midnorm,
    gate_proj,
    up_proj,
    down_proj,
    query_moment,
    key_moment,
    value_moment,
    out_moment,
    prenorm_moment,
    midnorm_moment,
    gate_moment,
    up_moment,
    down_moment,
):
    rep_index = lax.axis_index("rep")
    shard_index = lax.axis_index("shard")
    rep_count = lax.axis_size("rep")
    shard_count = lax.axis_size("shard")
    row_block = query_proj.shape[0]
    piece_rows = row_block // rep_count
    low_rows = jnp.concatenate([query_proj, key_proj, value_proj, out_proj], axis=1)
    low_piece = lax.dynamic_slice_in_dim(low_rows, rep_index * piece_rows, piece_rows, 0)
    low_all = lax.all_gather(low_piece, ("shard", "rep"), axis=0, tiled=True)
    full_query = low_all[:, :1024]
    full_key = low_all[:, 1024:1536]
    full_value = low_all[:, 1536:2048]
    full_out = low_all[:, 2048:]
    gains = lax.all_gather(jnp.stack([prenorm, midnorm]), "shard", axis=1, tiled=True)
    prenorm_low = gains[0]
    midnorm_low = gains[1]
    experts_here = gate_proj.shape[0]
    dense_weights = jnp.sum(
        jnp.where(
            routes[:, :, None] == jnp.arange(EXPERTS, dtype=jnp.int32)[None, None, :],
            route_weights[:, :, None],
            0.0,
        ),
        axis=1,
    )
    dense_all = lax.all_gather(dense_weights, "shard", axis=0, tiled=True)
    bits = rep_bits(rep_count)
    expert_weights = lax.dynamic_slice_in_dim(
        dense_all, shard_index * experts_here, experts_here, 1
    ).reshape(shard_count, -1, experts_here)
    cotangent_all = lax.all_gather(cotangent, "shard", axis=0)
    moment_rows = jnp.concatenate(
        [query_moment, key_moment, value_moment, out_moment], axis=1
    ).astype(jnp.bfloat16)
    moment_piece = lax.dynamic_slice_in_dim(moment_rows, rep_index * piece_rows, piece_rows, 0)
    moment_all = lax.all_gather(moment_piece, ("shard", "rep"), axis=0, tiled=True)
    gain_before = prenorm_low.astype(jnp.float32)
    gain_after = midnorm_low.astype(jnp.float32)
    group_size = NHEADS // KVHEADS
    token_count = tokens.shape[0]
    inputs = tokens.astype(jnp.float32)
    scaled_first, inverse_first = root_scale(inputs)
    normed_first = (scaled_first * gain_before).astype(jnp.bfloat16)
    query_linear = jnp.dot(normed_first, full_query, preferred_element_type=jnp.float32).reshape(
        token_count, NHEADS, HEAD
    )
    key_linear = jnp.dot(normed_first, full_key, preferred_element_type=jnp.float32).reshape(
        token_count, KVHEADS, HEAD
    )
    values = (
        jnp.dot(normed_first, full_value, preferred_element_type=jnp.float32)
        .astype(jnp.bfloat16)
        .reshape(token_count, KVHEADS, HEAD)
    )
    cosine_table, sine_table = rotary_tables(
        jnp.arange(token_count, dtype=jnp.int32) - sequence_start
    )
    queries = (
        (query_linear * cosine_table + rotate_half(query_linear) * sine_table)
        .astype(jnp.bfloat16)
        .reshape(token_count, KVHEADS, group_size, HEAD)
    )
    rotated_keys = (key_linear * cosine_table + rotate_half(key_linear) * sine_table).astype(
        jnp.bfloat16
    )
    head_out, log_total = attend_forward(queries, rotated_keys, values, sequence_start)
    head_low = head_out.astype(jnp.bfloat16)
    middle = inputs + jnp.dot(head_low, full_out, preferred_element_type=jnp.float32)
    scaled_second, inverse_second = root_scale(middle)
    normed_second = (scaled_second * gain_after).astype(jnp.bfloat16)
    returned, grad_second, expert_share = moe(
        normed_second,
        cotangent_all,
        expert_weights,
        gate_proj,
        up_proj,
        down_proj,
        bits,
        shard_count,
    )
    mixed = middle + returned
    grad_mixed = cotangent.astype(jnp.float32)
    middle_extra, midnorm_part = root_back(grad_second, gain_after, scaled_second, inverse_second)
    grad_middle = grad_mixed + middle_extra
    grad_branch = grad_middle.astype(jnp.bfloat16)
    out_local = jnp.einsum("tq,td->qd", head_low, grad_branch, preferred_element_type=jnp.float32)
    grad_heads = (
        jnp.einsum("td,qd->tq", grad_branch, full_out, preferred_element_type=jnp.float32)
        .astype(jnp.bfloat16)
        .reshape(queries.shape)
    )
    grad_queries, grad_keys, grad_values = attend_backward(
        queries, rotated_keys, values, sequence_start, log_total, grad_heads
    )
    grad_queries = grad_queries.reshape(token_count, NHEADS, HEAD)
    query_delta = (
        (grad_queries * cosine_table + rotate_back(grad_queries * sine_table))
        .astype(jnp.bfloat16)
        .reshape(token_count, -1)
    )
    key_delta = (
        (grad_keys * cosine_table + rotate_back(grad_keys * sine_table))
        .astype(jnp.bfloat16)
        .reshape(token_count, -1)
    )
    value_delta = grad_values.astype(jnp.bfloat16).reshape(token_count, -1)
    query_local = jnp.einsum(
        "td,tq->dq", normed_first, query_delta, preferred_element_type=jnp.float32
    )
    key_local = jnp.einsum("td,tq->dq", normed_first, key_delta, preferred_element_type=jnp.float32)
    value_local = jnp.einsum(
        "td,tq->dq", normed_first, value_delta, preferred_element_type=jnp.float32
    )
    grad_first = (
        jnp.einsum("tq,dq->td", query_delta, full_query, preferred_element_type=jnp.float32)
        + jnp.einsum("tq,dq->td", key_delta, full_key, preferred_element_type=jnp.float32)
        + jnp.einsum("tq,dq->td", value_delta, full_value, preferred_element_type=jnp.float32)
    )
    input_extra, prenorm_part = root_back(grad_first, gain_before, scaled_first, inverse_first)
    grad_tokens = grad_middle + input_extra
    low_local = jnp.concatenate([query_local, key_local, value_local, out_local], axis=1)
    low_blocks = (
        low_local.astype(jnp.bfloat16)
        .reshape(shard_count, row_block, 8, low_local.shape[1] // 8)
        .transpose(2, 0, 1, 3)
    )
    gains_local = jnp.concatenate(
        [jnp.stack([prenorm_part, midnorm_part]), jnp.zeros((6, prenorm_part.shape[0]))], axis=0
    )
    expert_grads, dense_grads, gains_grad = spread(
        expert_share, low_blocks, gains_local, bits, shard_count
    )
    gains_here = lax.dynamic_slice_in_dim(gains_grad, shard_index * row_block, row_block, 1)
    prenorm_grad = gains_here[0]
    midnorm_grad = gains_here[1]
    prenorm_next = momentum_keep * prenorm_moment + prenorm_grad
    midnorm_next = momentum_keep * midnorm_moment + midnorm_grad
    prenorm_update = -rate_gain * prenorm_next
    midnorm_update = -rate_gain * midnorm_next
    (
        query_grad,
        query_next,
        query_update,
        key_grad,
        key_next,
        key_update,
        value_grad,
        value_next,
        value_update,
        out_grad,
        out_next,
        out_update,
    ) = dense_update(
        dense_grads,
        moment_all,
        (query_moment, key_moment, value_moment, out_moment),
        LAYOUT,
        shard_index,
    )
    gate_grad, gate_next, gate_update = expert_update(expert_grads, 0, gate_moment)
    up_grad, up_next, up_update = expert_update(expert_grads, 1, up_moment)
    down_grad, down_next, down_update = expert_update(expert_grads, 2, down_moment)
    return (
        mixed.astype(jnp.bfloat16),
        grad_tokens,
        query_grad,
        query_next,
        query_update,
        key_grad,
        key_next,
        key_update,
        value_grad,
        value_next,
        value_update,
        out_grad,
        out_next,
        out_update,
        prenorm_grad,
        prenorm_next,
        prenorm_update,
        midnorm_grad,
        midnorm_next,
        midnorm_update,
        gate_grad,
        gate_next,
        gate_update,
        up_grad,
        up_next,
        up_update,
        down_grad,
        down_next,
        down_update,
    )


def solution(mesh):
    return jax.shard_map(
        local,
        mesh=mesh,
        in_specs=(
            P(("rep", "shard"), None),
            P(("rep", "shard")),
            P(("rep", "shard"), None),
            P(("rep", "shard"), None),
            P(("rep", "shard"), None),
            P("shard", None),
            P("shard", None),
            P("shard", None),
            P("shard", None),
            P("shard"),
            P("shard"),
            P("shard", None, None),
            P("shard", None, None),
            P("shard", None, None),
            P("shard", None),
            P("shard", None),
            P("shard", None),
            P("shard", None),
            P("shard"),
            P("shard"),
            P("shard", None, None),
            P("shard", None, None),
            P("shard", None, None),
        ),
        out_specs=(
            P(("rep", "shard"), None),
            P(("rep", "shard"), None),
            P("shard", None),
            P("shard", None),
            P("shard", None),
            P("shard", None),
            P("shard", None),
            P("shard", None),
            P("shard", None),
            P("shard", None),
            P("shard", None),
            P("shard", None),
            P("shard", None),
            P("shard", None),
            P("shard"),
            P("shard"),
            P("shard"),
            P("shard"),
            P("shard"),
            P("shard"),
            P("shard", None, None),
            P("shard", None, None),
            P("shard", None, None),
            P("shard", None, None),
            P("shard", None, None),
            P("shard", None, None),
            P("shard", None, None),
            P("shard", None, None),
            P("shard", None, None),
        ),
        check_vma=False,
    )
```

```python
import functools
import math

import jax
import jax.numpy as jnp
from jax import lax
from jax.experimental import pallas as pl
from jax.experimental.pallas import tpu as pltpu
from jax.sharding import PartitionSpec as P

NHEADS = 16
KVHEADS = 8
HEAD = 64
EXPERTS = 16
NS_ITERS = 2
BLOCK = 256


norm_epsilon = 1e-06
rotary_base = 10000.0
momentum_keep = 0.9
rate_matrix = 0.5
rate_gain = 0.0002
newton_first = 3.4445
newton_second = -4.775
newton_third = 2.0315
masked_score = -1e30


def root_scale(values):
    inverse = lax.rsqrt(jnp.mean(values * values, axis=-1, keepdims=True) + norm_epsilon)
    return (values * inverse, inverse)


def root_back(grad_normed, scaling, scaled, inverse):
    grad_scaled = grad_normed * scaling
    inner_mean = jnp.mean(grad_scaled * scaled, axis=-1, keepdims=True)
    return (inverse * (grad_scaled - scaled * inner_mean), jnp.sum(grad_normed * scaled, axis=0))


def rotary_tables(positions):
    half_size = HEAD // 2
    frequency = rotary_base ** (-(jnp.arange(half_size, dtype=jnp.float32) * 2.0) / HEAD)
    angles = positions.astype(jnp.float32)[:, None] * frequency[None, :]
    angles = jnp.concatenate([angles, angles], axis=-1)
    return (jnp.cos(angles)[:, None, :], jnp.sin(angles)[:, None, :])


def rotate_half(values):
    half_size = values.shape[-1] // 2
    return jnp.concatenate([-values[..., half_size:], values[..., :half_size]], axis=-1)


def rotate_back(values):
    half_size = values.shape[-1] // 2
    return jnp.concatenate([values[..., half_size:], -values[..., :half_size]], axis=-1)


def block_scores(query_block, rotated_keys, start_block, sequence_start, offset):
    scores = jnp.einsum(
        "qkgd,tkd->kgqt", query_block, rotated_keys, preferred_element_type=jnp.float32
    ) * (1.0 / math.sqrt(HEAD))
    key_places = jnp.arange(rotated_keys.shape[0], dtype=jnp.int32)
    query_places = offset + jnp.arange(query_block.shape[0], dtype=jnp.int32)
    allowed = (start_block[:, None] == sequence_start[None, :]) & (
        key_places[None, :] <= query_places[:, None]
    )
    return jnp.where(allowed, scores, masked_score)


def attend_forward(queries, rotated_keys, values, sequence_start):
    block_count = queries.shape[0] // BLOCK

    def one_block(pieces):
        query_block, start_block, offset = pieces
        scores = block_scores(query_block, rotated_keys, start_block, sequence_start, offset)
        row_max = jnp.max(scores, axis=-1, keepdims=True)
        exponents = jnp.exp(scores - row_max)
        totals = jnp.sum(exponents, axis=-1, keepdims=True)
        softmax_low = (exponents / totals).astype(jnp.bfloat16)
        attended = jnp.einsum(
            "kgqt,tkd->qkgd", softmax_low, values, preferred_element_type=jnp.float32
        )
        return (attended, row_max + jnp.log(totals))

    shaped = queries.reshape((block_count, BLOCK) + queries.shape[1:])
    offsets = jnp.arange(block_count, dtype=jnp.int32) * BLOCK
    attended, log_total = lax.map(
        one_block, (shaped, sequence_start.reshape(block_count, BLOCK), offsets)
    )
    return (attended.reshape(queries.shape[0], -1), log_total)


def attend_backward(queries, rotated_keys, values, sequence_start, log_total, grad_heads):
    block_count = queries.shape[0] // BLOCK
    score_scale = 1.0 / math.sqrt(HEAD)

    def one_block(running, pieces):
        grad_keys, grad_values = running
        query_block, start_block, offset, log_block, grad_block = pieces
        scores = block_scores(query_block, rotated_keys, start_block, sequence_start, offset)
        softmax_full = jnp.exp(scores - log_block)
        grad_softmax = jnp.einsum(
            "qkgd,tkd->kgqt", grad_block, values, preferred_element_type=jnp.float32
        )
        inner_sum = jnp.sum(softmax_full * grad_softmax, axis=-1, keepdims=True)
        grad_scores = (softmax_full * (grad_softmax - inner_sum)).astype(jnp.bfloat16)
        grad_query = (
            jnp.einsum(
                "kgqt,tkd->qkgd", grad_scores, rotated_keys, preferred_element_type=jnp.float32
            )
            * score_scale
        )
        grad_keys = (
            grad_keys
            + jnp.einsum(
                "kgqt,qkgd->tkd", grad_scores, query_block, preferred_element_type=jnp.float32
            )
            * score_scale
        )
        grad_values = grad_values + jnp.einsum(
            "kgqt,qkgd->tkd",
            softmax_full.astype(jnp.bfloat16),
            grad_block,
            preferred_element_type=jnp.float32,
        )
        return ((grad_keys, grad_values), grad_query)

    shaped = queries.reshape((block_count, BLOCK) + queries.shape[1:])
    grad_shaped = grad_heads.reshape((block_count, BLOCK) + queries.shape[1:])
    offsets = jnp.arange(block_count, dtype=jnp.int32) * BLOCK
    key_zeros = jnp.zeros(rotated_keys.shape, jnp.float32)
    finals, grad_queries = lax.scan(
        one_block,
        (key_zeros, key_zeros),
        (shaped, sequence_start.reshape(block_count, BLOCK), offsets, log_total, grad_shaped),
    )
    return (grad_queries.reshape(queries.shape), finals[0], finals[1])


def newton_parts(grams):
    a, b, c = newton_first, newton_second, newton_third

    def times(left, right):
        return jnp.dot(left, right, preferred_element_type=jnp.float32)

    lows = [gram.astype(jnp.bfloat16) for gram in grams]
    firsts = [b * gram + c * times(low, low) for gram, low in zip(grams, lows)]
    first_lows = [first.astype(jnp.bfloat16) for first in firsts]
    mixes = [times(low, first) for low, first in zip(lows, first_lows)]
    nexts = [
        (a * a) * gram + (2.0 * a) * mix + times(mix.astype(jnp.bfloat16), first)
        for gram, mix, first in zip(grams, mixes, first_lows)
    ]
    next_lows = [gram.astype(jnp.bfloat16) for gram in nexts]
    seconds = [b * gram + c * times(low, low) for gram, low in zip(nexts, next_lows)]
    second_lows = [second.astype(jnp.bfloat16) for second in seconds]
    return list(zip(firsts, first_lows, seconds, second_lows))


def expert_update_kernel(kinds, scale, *refs):
    a = newton_first
    grads_ref = refs[0]
    moments = refs[1 : 1 + len(kinds)]
    outs = refs[1 + len(kinds) :]
    half = grads_ref.shape[3]
    states = []
    for index in range(len(kinds)):
        for e in range(grads_ref.shape[0]):
            grad = grads_ref[e, index].astype(jnp.float32)
            tall = kinds[index] < 2
            if not tall:
                grad = jnp.concatenate([grad[:half], grad[half:]], axis=1)
            moment = momentum_keep * moments[index][e] + grad
            outs[3 * index][e] = grad
            outs[3 * index + 1][e] = moment
            inverse = 1.0 / (jnp.sqrt(jnp.sum(moment * moment)) + 1e-07)
            low = (moment * inverse).astype(jnp.bfloat16)
            sides = (((0,), (0,)), ((), ())) if tall else (((1,), (1,)), ((), ()))
            gram = lax.dot_general(low, low, sides, preferred_element_type=jnp.float32)
            states.append((index, e, tall, inverse, low, gram))
    parts = newton_parts([state[-1] for state in states])
    for (index, e, tall, inverse, low, _), (first, first_low, second, second_low) in zip(
        states, parts
    ):
        rest = a * (first + second) + jnp.dot(
            first_low, second_low, preferred_element_type=jnp.float32
        )
        rest = (-scale * rest).astype(jnp.bfloat16)
        if tall:
            step = jnp.dot(low, rest, preferred_element_type=jnp.float32)
        else:
            step = jnp.dot(rest, low, preferred_element_type=jnp.float32)
        outs[3 * index + 2][e] = (-scale * a * a * inverse) * outs[3 * index + 1][e] + step


def expert_update(grads, kinds, moments):
    count, rows, columns = moments[0].shape
    group = 2 // len(kinds)
    scale = rate_matrix * math.sqrt(max(1.0, columns / rows))
    block = pl.BlockSpec((group, rows, columns), lambda i: (i, 0, 0))
    place = kinds[0] // len(kinds)
    taken = pl.BlockSpec((group, len(kinds)) + grads.shape[2:], lambda i: (i, place, 0, 0))
    shape = jax.ShapeDtypeStruct(moments[0].shape, jnp.float32)
    return pl.pallas_call(
        functools.partial(expert_update_kernel, kinds, scale),
        grid=(count // group,),
        in_specs=[taken] + [block] * len(kinds),
        out_specs=[block] * (3 * len(kinds)),
        out_shape=[shape] * (3 * len(kinds)),
        compiler_params=pltpu.CompilerParams(vmem_limit_bytes=60 * 1024 * 1024),
        name="expert_update",
        cost_estimate=pl.CostEstimate(
            flops=count * len(kinds) * 2500000000,
            bytes_accessed=moments[0].size * len(kinds) * 18,
            transcendentals=0,
        ),
    )(grads, *moments)


def dense_update_kernel(layout, place_ref, grads_ref, moments_ref, *refs):
    a = newton_first
    amount = len(layout)
    own_moments = refs[:amount]
    outs = refs[amount : 4 * amount]
    whole, own_grads = refs[4 * amount :]
    blocks, count, block_rows, width = grads_ref.shape
    part = width // 3
    me = place_ref[0]
    start = pl.multiple_of(me * block_rows, block_rows)
    for block in range(blocks):
        for index in range(3):
            columns = slice(8 * part * index + block * part, 8 * part * index + (block + 1) * part)
            inner = slice(index * part, (index + 1) * part)
            outer = slice(block * part, (block + 1) * part)
            grads = grads_ref[block, :, :, inner].reshape(count * block_rows, part)
            moments = moments_ref[index, :, :, outer].reshape(count * block_rows, part)
            whole[:, columns] = (
                momentum_keep * moments.astype(jnp.float32) + grads.astype(jnp.float32)
            ).astype(jnp.bfloat16)
            own_grads[:, columns] = grads_ref[block, me, :, inner].astype(jnp.float32)
    for group in ((0, 1), (2, 3)):
        states = []
        for index in group:
            begin, size = layout[index]
            grad_out, next_out, _ = outs[3 * index : 3 * index + 3]
            columns = slice(begin, begin + size)
            grad = own_grads[:, columns]
            grad_out[...] = grad
            next_out[...] = momentum_keep * own_moments[index][...] + grad
            matrix = whole[:, columns].astype(jnp.float32)
            inverse = 1.0 / (jnp.sqrt(jnp.sum(matrix * matrix)) + 1e-07)
            low = (matrix * inverse).astype(jnp.bfloat16)
            gram = lax.dot_general(
                low, low, (((0,), (0,)), ((), ())), preferred_element_type=jnp.float32
            )
            own = whole[pl.ds(start, block_rows), columns].astype(jnp.float32) * inverse
            states.append((index, size, own, gram))
        parts = newton_parts([state[-1] for state in states])
        for (index, size, own, _), (_, first_low, _, second_low) in zip(states, parts):
            scale = rate_matrix * math.sqrt(max(1.0, size / (count * block_rows)))
            once = a * own + jnp.dot(
                own.astype(jnp.bfloat16), first_low, preferred_element_type=jnp.float32
            )
            outs[3 * index + 2][...] = (-scale) * (
                a * once
                + jnp.dot(
                    once.astype(jnp.bfloat16), second_low, preferred_element_type=jnp.float32
                )
            )


def dense_update(grads, gathered, own_moments, layout, shard_index):
    _, count, block_rows, width = gathered.shape
    moments = pl.BlockSpec((3, count, block_rows, width), lambda i: (1, 0, 0, 0))
    whole = lambda shape: pl.BlockSpec(shape, lambda i: (0,) * len(shape))
    shapes = []
    for _, size in layout:
        shapes += [jax.ShapeDtypeStruct((block_rows, size), jnp.float32)] * 3
    return pl.pallas_call(
        functools.partial(dense_update_kernel, layout),
        grid=(1,),
        in_specs=[pl.BlockSpec(memory_space=pltpu.SMEM), whole(grads.shape), moments]
        + [whole(moment.shape) for moment in own_moments],
        out_specs=[whole(shape.shape) for shape in shapes],
        out_shape=shapes,
        scratch_shapes=[
            pltpu.VMEM((count * block_rows, 3 * width), jnp.bfloat16),
            pltpu.VMEM((block_rows, 3 * width), jnp.float32),
        ],
        compiler_params=pltpu.CompilerParams(vmem_limit_bytes=63 * 1024 * 1024),
        name="dense_update",
        cost_estimate=pl.CostEstimate(
            flops=28000000000, bytes_accessed=24 * width * width, transcendentals=0
        ),
    )(shard_index.reshape(1).astype(jnp.int32), grads, gathered, *own_moments)


LAYOUT = ((0, 1024), (1024, 512), (1536, 512), (2048, 1024))


MESH = pl.DeviceIdType.MESH


def flip(index, bit):
    return index + bit - 2 * bit * ((index // bit) % 2)


def greet(peers):
    barrier = pltpu.get_barrier_semaphore()
    for peer in peers:
        pl.semaphore_signal(barrier, inc=1, device_id=peer, device_id_type=MESH)
    pl.semaphore_wait(barrier, len(peers))


def stream_plan(rep, bits, base, size):
    stages = []
    starts = [base, base + size]
    for step in range(len(bits)):
        size = size // 2
        stage = []
        for stream in range(2):
            bit = bits[(step + stream) % len(bits)]
            side = (rep // bit) % 2
            keep = starts[stream] + side * size
            send = starts[stream] + (1 - side) * size
            starts[stream] = keep
            stage.append((bit, stream, keep, send, size))
        stages.append(stage)
    return stages


def rows_of(start, size):
    return pl.ds(pl.multiple_of(start, 16), size)


def moe_kernel(
    count,
    bits,
    own_ref,
    cot_ref,
    weight_ref,
    gate_hbm,
    up_hbm,
    down_hbm,
    out_ref,
    back_ref,
    share_ref,
    tok,
    turned,
    mats,
    hid,
    gate_delta,
    up_delta,
    stage_back,
    stage_out,
    got_back,
    got_out,
    *rest,
):
    landing = rest[: 1 + 2 * len(bits)]
    (
        load_sem,
        right_sem,
        left_sem,
        arrive_sem,
        back_send,
        back_recv,
        out_send,
        out_recv,
        sum_send,
        sum_recv,
    ) = rest[1 + 2 * len(bits) :]
    rep = lax.axis_index("rep")
    me = lax.axis_index("shard")
    experts = mats.shape[0]
    tokens = own_ref.shape[0]
    half = mats.shape[2] // 2
    core = rep % 2

    loads = [
        pltpu.make_async_copy(gate_hbm, mats.at[:, 0], load_sem.at[0]),
        pltpu.make_async_copy(up_hbm, mats.at[:, 1], load_sem.at[1]),
        pltpu.make_async_copy(
            down_hbm.at[:, :, pl.ds(0, half)], mats.at[:, 2, pl.ds(0, half)], load_sem.at[2]
        ),
        pltpu.make_async_copy(
            down_hbm.at[:, :, pl.ds(half, half)], mats.at[:, 2, pl.ds(half, half)], load_sem.at[3]
        ),
    ]
    for load in loads:
        load.start()
    peers = [(rep, lax.rem(me + k, count)) for k in range(1, count)]
    peers += [(flip(rep, bit), me) for bit in (1,) + bits]
    greet(peers)

    right_peer = (rep, jnp.minimum(me + 1, count - 1))
    left_peer = (rep, jnp.maximum(me - 1, 0))

    def hand_on(block, to_right):
        return pltpu.make_async_remote_copy(
            src_ref=tok.at[block],
            dst_ref=tok.at[block],
            send_sem=(right_sem if to_right else left_sem).at[block],
            recv_sem=arrive_sem.at[block],
            device_id=right_peer if to_right else left_peer,
            device_id_type=MESH,
        )

    def returning(stage, got, send_sem, recv_sem, block):
        return pltpu.make_async_remote_copy(
            src_ref=stage.at[block],
            dst_ref=got.at[me],
            send_sem=send_sem.at[block],
            recv_sem=recv_sem.at[me],
            device_id=(rep, block),
            device_id_type=MESH,
        )

    tok[me] = own_ref[...]

    @pl.when(me < count - 1)
    def _():
        hand_on(me, True).start()

    @pl.when(me > 0)
    def _():
        hand_on(me, False).start()

    for load in loads:
        load.wait()

    margin = jnp.minimum(me, count - 1 - me)
    longer = jnp.where(me < count - 1 - me, 1, -1)
    inward = jnp.where(2 * me < count, 1, -1)
    nt = (((1,), (1,)), ((), ()))

    def dot(left, right):
        return jnp.dot(left, right, preferred_element_type=jnp.float32)

    def dot_nt(left, right):
        return lax.dot_general(left, right, nt, preferred_element_type=jnp.float32)

    def visit(j, carry):
        lower = me - j
        upper = me + j

        @pl.when((j > 0) & (lower >= 0))
        def _():
            hand_on(jnp.maximum(lower, 0), True).wait_recv()

            @pl.when(me < count - 1)
            def _():
                hand_on(jnp.maximum(lower, 0), True).start()

        @pl.when((j > 0) & (upper < count))
        def _():
            hand_on(jnp.minimum(upper, count - 1), False).wait_recv()

            @pl.when(me > 0)
            def _():
                hand_on(jnp.minimum(upper, count - 1), False).start()

        near = (j + 1) // 2
        alternating = me + near - 2 * near * (j % 2)
        block = jnp.where(j <= 2 * margin, alternating, me + longer * (j - margin))
        places = pl.ds(pl.multiple_of(block * tokens, tokens), tokens)
        rows = tok[block]
        grads = cot_ref[block]
        turned[:, places] = rows.T
        hiddens = []
        for e in range(experts):
            weight = weight_ref[block, :, e : e + 1]
            u = dot(rows, mats[e, 0])
            w = dot(rows, mats[e, 1])
            gate = 1.0 / (1.0 + jnp.exp(-u))
            act = u * gate
            hidden = (weight * (act * w)).astype(jnp.bfloat16)
            hid[e, :, places] = hidden.T
            hiddens.append(hidden)
            pulled = weight * (
                dot_nt(grads[:, :half], mats[e, 2, :half])
                + dot_nt(grads[:, half:], mats[e, 2, half:])
            )
            gate_delta[e, places] = (pulled * w * (gate + act * (1.0 - gate))).astype(jnp.bfloat16)
            up_delta[e, places] = (pulled * act).astype(jnp.bfloat16)
        for side in range(2):
            part = slice(side * half, (side + 1) * half)
            total_back = None
            total_out = None
            for e in range(experts):
                back = dot_nt(gate_delta[e, places], mats[e, 0, part]) + dot_nt(
                    up_delta[e, places], mats[e, 1, part]
                )
                out = dot(hiddens[e], mats[e, 2, part])
                total_back = back if e == 0 else total_back + back
                total_out = out if e == 0 else total_out + out
            stage_back[block, :, part] = total_back.astype(jnp.bfloat16)
            stage_out[block, :, part] = total_out.astype(jnp.bfloat16)

        @pl.when((j > 0) & ((block - me) * inward > 0))
        def _():
            returning(stage_back, got_back, back_send, back_recv, block).start()

        return carry

    lax.fori_loop(0, count, visit, 0)
    for block in range(count):

        @pl.when((block - me) * inward < 0)
        def _():
            returning(stage_back, got_back, back_send, back_recv, block).start()

    for k in range(1, count):
        returning(stage_out, got_out, out_send, out_recv, lax.rem(me + k, count)).start()

    plan = stream_plan(rep, bits, core * half, half // 2)

    def sum_copy(stage, slot, e, start, size, bit):
        return pltpu.make_async_remote_copy(
            src_ref=mats.at[e, :, rows_of(start, size)],
            dst_ref=landing[slot].at[e],
            send_sem=sum_send.at[slot, e],
            recv_sem=sum_recv.at[slot, e],
            device_id=(flip(rep, bit), me),
            device_id_type=MESH,
        )

    def copies(stage, e):
        if stage == 0:
            return [(sum_copy(0, 0, e, (1 - core) * half, half, 1), 0, core * half, half)]
        return [
            (
                sum_copy(stage, 1 + 2 * (stage - 1) + stream, e, send, size, bit),
                1 + 2 * (stage - 1) + stream,
                keep,
                size,
            )
            for bit, stream, keep, send, size in plan[stage - 1]
        ]

    def finish(stage, e):
        for copy, slot, keep, size in copies(stage, e):
            copy.wait_recv()
            place = rows_of(keep, size)
            for kind in range(3):
                mats[e, kind, place] = (
                    mats[e, kind, place].astype(jnp.float32)
                    + landing[slot][e, kind].astype(jnp.float32)
                ).astype(jnp.bfloat16)

    stages = 1 + len(bits)
    for turn in range(experts + stages):
        if turn < experts:
            e = turn
            for side in range(2):
                part = slice(side * half, (side + 1) * half)
                mats[e, 0, part] = dot(turned[part], gate_delta[e]).astype(jnp.bfloat16)
                mats[e, 1, part] = dot(turned[part], up_delta[e]).astype(jnp.bfloat16)
                mats[e, 2, part] = dot(hid[e], cot_ref[:, :, part].reshape(count * tokens, half)).astype(jnp.bfloat16)
            copies(0, e)[0][0].start()
        for stage in range(stages):
            e = turn - 1 - stage
            if 0 <= e < experts:
                finish(stage, e)
                if stage + 1 < stages:
                    for copy, _, _, _ in copies(stage + 1, e):
                        copy.start()
                else:
                    for _, stream, keep, _, size in plan[-1]:
                        share_ref[e, :, stream] = mats[e, :, rows_of(keep, size)]

    total = stage_back[me].astype(jnp.float32)
    for k in range(1, count):
        source = lax.rem(me + k, count)
        pltpu.make_async_remote_copy(
            src_ref=stage_back.at[source],
            dst_ref=got_back.at[source],
            send_sem=back_send.at[source],
            recv_sem=back_recv.at[source],
            device_id=(rep, source),
            device_id_type=MESH,
        ).wait_recv()
        total = total + got_back[source].astype(jnp.float32)
    back_ref[...] = total
    total = stage_out[me].astype(jnp.float32)
    for k in range(1, count):
        source = lax.rem(me + k, count)
        pltpu.make_async_remote_copy(
            src_ref=stage_out.at[source],
            dst_ref=got_out.at[source],
            send_sem=out_send.at[source],
            recv_sem=out_recv.at[source],
            device_id=(rep, source),
            device_id_type=MESH,
        ).wait_recv()
        total = total + got_out[source].astype(jnp.float32)
    out_ref[...] = total

    for k in range(1, count):
        block = lax.rem(me + k, count)
        returning(stage_back, got_back, back_send, back_recv, block).wait_send()
        returning(stage_out, got_out, out_send, out_recv, block).wait_send()
    for e in range(experts):
        for stage in range(stages):
            for copy, _, _, _ in copies(stage, e):
                copy.wait_send()
    for block in range(count):

        @pl.when((block <= me) & (me < count - 1))
        def _():
            hand_on(block, True).wait_send()

        @pl.when((block >= me) & (me > 0))
        def _():
            hand_on(block, False).wait_send()


def moe(normed, cotangents, weights, gate_proj, up_proj, down_proj, bits, count):
    tokens, width = normed.shape
    experts, _, hidden = gate_proj.shape
    half = width // 2
    low = jnp.bfloat16
    final = (half // 2) >> len(bits)
    vmem = pl.BlockSpec(memory_space=pltpu.VMEM)
    anywhere = pl.BlockSpec(memory_space=pl.ANY)
    landings = [pltpu.VMEM((experts, 3, half, hidden), low)]
    for step in range(len(bits)):
        size = (half // 2) >> (step + 1)
        landings += [pltpu.VMEM((experts, 3, size, hidden), low)] * 2
    slots = len(landings)
    dma = pltpu.SemaphoreType.DMA
    return pl.pallas_call(
        functools.partial(moe_kernel, count, bits),
        in_specs=[vmem, vmem, vmem, anywhere, anywhere, anywhere],
        out_specs=[vmem, vmem, vmem],
        out_shape=[
            jax.ShapeDtypeStruct((tokens, width), jnp.float32),
            jax.ShapeDtypeStruct((tokens, width), jnp.float32),
            jax.ShapeDtypeStruct((experts, 3, 2, final, hidden), low),
        ],
        scratch_shapes=[
            pltpu.VMEM((count, tokens, width), low),
            pltpu.VMEM((width, count * tokens), low),
            pltpu.VMEM((experts, 3, width, hidden), low),
            pltpu.VMEM((experts, hidden, count * tokens), low),
            pltpu.VMEM((experts, count * tokens, hidden), low),
            pltpu.VMEM((experts, count * tokens, hidden), low),
            pltpu.VMEM((count, tokens, width), low),
            pltpu.VMEM((count, tokens, width), low),
            pltpu.VMEM((count, tokens, width), low),
            pltpu.VMEM((count, tokens, width), low),
        ]
        + landings
        + [
            dma((4,)),
            dma((count,)),
            dma((count,)),
            dma((count,)),
            dma((count,)),
            dma((count,)),
            dma((count,)),
            dma((count,)),
            dma((slots, experts)),
            dma((slots, experts)),
        ],
        compiler_params=pltpu.CompilerParams(
            collective_id=1, has_side_effects=True, vmem_limit_bytes=63 * 1024 * 1024
        ),
        name="moe",
        cost_estimate=pl.CostEstimate(
            flops=39000000000, bytes_accessed=20000000, transcendentals=2000000
        ),
    )(normed, cotangents, weights, gate_proj, up_proj, down_proj)


def rep_bits(rep_count):
    bits = []
    bit = 2
    while bit < rep_count:
        bits.append(bit)
        bit = bit * 2
    return tuple(bits)


def spread_kernel(
    count,
    bits,
    share_ref,
    normed_ref,
    delta_ref,
    head_ref,
    branch_ref,
    gains_ref,
    experts_out,
    dense_out,
    gains_out,
    dense_ref,
    total,
    land_core,
    land_first,
    *rest,
):
    later = len(bits) - 1
    land_later = rest[:later]
    (
        piece_send,
        piece_land,
        piece,
        gains_send,
        gains_land,
        gains_all,
        local_sem,
        core_send,
        core_recv,
        half_send,
        half_recv,
        shard_send,
        shard_recv,
        grow_send,
        grow_recv,
        line_send,
        line_recv,
        join_send,
        join_recv,
        expert_send,
        expert_recv,
        gain_send,
        gain_recv,
        gain_line_send,
        gain_line_recv,
    ) = rest[later:]
    rep = lax.axis_index("rep")
    me = lax.axis_index("shard")
    core = rep % 2
    rows = dense_ref.shape[2]
    expert_rows = experts_out.shape[2]
    steps = len(bits)
    streams = range(2)

    def remote(source, target, send_sem, recv_sem, peer):
        return pltpu.make_async_remote_copy(
            src_ref=source,
            dst_ref=target,
            send_sem=send_sem,
            recv_sem=recv_sem,
            device_id=peer,
            device_id_type=MESH,
        )

    def across(bit):
        return (flip(rep, bit), me)

    def order(stream):
        return [bits[(step + stream) % steps] for step in range(steps)]

    def side(bit):
        return (rep // bit) % 2

    plan = stream_plan(rep, bits, core * (expert_rows // 2), expert_rows // 4)
    base = [(core * (expert_rows // 2)) + stream * (expert_rows // 4) for stream in streams]

    def expert_copy(level, stream):
        if level == steps:
            place = rows_of(base[stream], expert_rows // 4)
            peer = across(1)
        else:
            bit, _, keep, _, size = plan[steps - 1 - level][stream]
            place = rows_of(keep, size)
            peer = across(bit)
        source = experts_out.at[:, :, place]
        if level == 0:
            source = share_ref.at[:, :, stream]
        return remote(
            source,
            experts_out.at[:, :, place],
            expert_send.at[level, stream],
            expert_recv.at[level, stream],
            peer,
        )

    def own_copy(stream):
        _, _, keep, _, size = plan[-1][stream]
        return pltpu.make_async_copy(
            share_ref.at[:, :, stream],
            experts_out.at[:, :, rows_of(keep, size)],
            local_sem.at[stream],
        )

    for stream in streams:
        own_copy(stream).start()
    peers = [(rep, lax.rem(me + k, count)) for k in range(1, count)]
    peers += [across(bit) for bit in (1,) + bits]
    greet(peers)

    def core_copy(block):
        return remote(
            dense_ref.at[4 * (1 - core) + block],
            land_core.at[block],
            core_send.at[block],
            core_recv.at[block],
            across(1),
        )

    gain_bits = (1,) + bits

    def gain_copy(stage):
        return remote(
            gains_send.at[stage],
            gains_land.at[stage],
            gain_send.at[stage],
            gain_recv.at[stage],
            across(gain_bits[stage]),
        )

    gains_send[0] = gains_ref[...]
    gain_copy(0).start()
    for stream in streams:
        expert_copy(0, stream).start()

    part = dense_ref.shape[3] // 3
    normed_turned = normed_ref[...].T
    head_turned = head_ref[...].T

    def make_block(block):
        def columns(ref, offset):
            return ref[:, pl.ds(pl.multiple_of(offset + block * part, part), part)]

        pair = jnp.concatenate([columns(delta_ref, 0), columns(delta_ref, 8 * part)], axis=1)
        left = jnp.dot(normed_turned, pair, preferred_element_type=jnp.float32)
        right = jnp.dot(head_turned, columns(branch_ref, 0), preferred_element_type=jnp.float32)
        for line in range(count):
            place = slice(line * rows, (line + 1) * rows)
            dense_ref[block, line, :, : 2 * part] = left[place].astype(jnp.bfloat16)
            dense_ref[block, line, :, 2 * part :] = right[place].astype(jnp.bfloat16)

    for block in range(4):
        make_block(4 * (1 - core) + block)
        core_copy(block).start()
    for block in range(4):
        make_block(4 * core + block)

    def gain_step(stage):
        gain_copy(stage).wait_recv()
        gains_send[stage + 1] = gains_send[stage] + gains_land[stage]
        if stage + 1 < len(gain_bits):
            gain_copy(stage + 1).start()

    first = [side(order(stream)[0]) for stream in streams]
    held = [2 * stream + first[stream] for stream in streams]
    given = [2 * stream + 1 - first[stream] for stream in streams]

    def first_copy(stream):
        return remote(
            total.at[given[stream]],
            land_first.at[stream],
            half_send.at[0, stream],
            half_recv.at[0, stream],
            across(order(stream)[0]),
        )

    def add_core(block):
        for line in range(count):
            total[block, line] = (
                dense_ref[4 * core + block, line].astype(jnp.float32)
                + land_core[block, line].astype(jnp.float32)
            ).astype(jnp.bfloat16)

    for block in range(4):
        core_copy(block).wait_recv()
    for stream in streams:
        add_core(given[stream])
        first_copy(stream).start()
    for stream in streams:
        add_core(held[stream])
    gain_step(0)

    starts = []
    for stream in streams:
        start, size, line = 0, rows, []
        for step in range(1, steps):
            size = size // 2
            near = side(order(stream)[step])
            line.append((start + near * size, start + (1 - near) * size, size))
            start = start + near * size
        starts.append((start, size, line))

    def later_copy(step, stream):
        keep, send, size = starts[stream][2][step - 1]
        return remote(
            total.at[held[stream], :, rows_of(send, size)],
            land_later[step - 1].at[stream],
            half_send.at[step, stream],
            half_recv.at[step, stream],
            across(order(stream)[step]),
        )

    for stream in streams:
        first_copy(stream).wait_recv()
        for line in range(count):
            total[held[stream], line] = (
                total[held[stream], line].astype(jnp.float32)
                + land_first[stream, line].astype(jnp.float32)
            ).astype(jnp.bfloat16)
        if steps > 1:
            later_copy(1, stream).start()
    gain_step(1)

    for stream in streams:
        own_copy(stream).wait()
        expert_copy(0, stream).wait_recv()
        if steps > 1:
            expert_copy(1, stream).start()

    for step in range(1, steps):
        for stream in streams:
            later_copy(step, stream).wait_recv()
            keep, _, size = starts[stream][2][step - 1]
            for line in range(count):
                place = rows_of(keep, size)
                total[held[stream], line, place] = (
                    total[held[stream], line, place].astype(jnp.float32)
                    + land_later[step - 1][stream, line].astype(jnp.float32)
                ).astype(jnp.bfloat16)
            if step + 1 < steps:
                later_copy(step + 1, stream).start()
        gain_step(step + 1)

    last = starts[0][1]
    places = [rows_of(starts[stream][0], last) for stream in streams]
    for stream in streams:
        for line in range(count):
            piece_send[line, stream] = total[held[stream], line, places[stream]]

    def shard_copy(k):
        target = lax.rem(me + k, count)
        return remote(
            piece_send.at[target],
            piece_land.at[me],
            shard_send.at[target],
            shard_recv.at[me],
            (rep, target),
        )

    def shard_arrival(source):
        return remote(
            piece_send.at[source],
            piece_land.at[source],
            shard_send.at[source],
            shard_recv.at[source],
            (rep, source),
        )

    def gain_line(k):
        target = lax.rem(me + k, count)
        return remote(
            gains_send.at[len(gain_bits)],
            gains_all.at[me],
            gain_line_send.at[target],
            gain_line_recv.at[me],
            (rep, target),
        )

    def gain_arrival(source):
        return remote(
            gains_send.at[len(gain_bits)],
            gains_all.at[source],
            gain_line_send.at[source],
            gain_line_recv.at[source],
            (rep, source),
        )

    for k in range(1, count):
        shard_copy(k).start()
        gain_line(k).start()
    summed = piece_send[me].astype(jnp.float32)
    for k in range(1, count):
        source = lax.rem(me + k, count)
        shard_arrival(source).wait_recv()
        summed = summed + piece_land[source].astype(jnp.float32)
    piece[...] = summed.astype(jnp.bfloat16)

    def line_copy(k, stream):
        target = lax.rem(me + k, count)
        return remote(
            piece.at[stream],
            dense_out.at[4 * core + held[stream], me, places[stream]],
            line_send.at[stream, target],
            line_recv.at[stream, me],
            (rep, target),
        )

    def line_arrival(source, stream):
        return remote(
            piece.at[stream],
            dense_out.at[4 * core + held[stream], source, places[stream]],
            line_send.at[stream, source],
            line_recv.at[stream, source],
            (rep, source),
        )

    def own_piece(stream):
        return pltpu.make_async_copy(
            piece.at[stream],
            dense_out.at[4 * core + held[stream], me, places[stream]],
            local_sem.at[2 + stream],
        )

    for stream in streams:
        own_piece(stream).start()
        for k in range(1, count):
            line_copy(k, stream).start()
    gained = gains_send[len(gain_bits)]
    for k in range(1, count):
        source = lax.rem(me + k, count)
        gain_arrival(source).wait_recv()
        gained = gained + gains_all[source]
    gains_out[...] = gained

    for level in range(1, steps):
        for stream in streams:
            expert_copy(level, stream).wait_recv()
            expert_copy(level + 1, stream).start()
    if steps == 1:
        for stream in streams:
            expert_copy(1, stream).start()

    def grow_copy(step, stream):
        if step == 0:
            place = dense_out.at[4 * core + held[stream]]
        else:
            keep, _, size = starts[stream][2][step - 1]
            place = dense_out.at[4 * core + held[stream], :, rows_of(keep, size)]
        return remote(
            place,
            place,
            grow_send.at[step, stream],
            grow_recv.at[step, stream],
            across(order(stream)[step]),
        )

    for stream in streams:
        own_piece(stream).wait()
        for k in range(1, count):
            line_arrival(lax.rem(me + k, count), stream).wait_recv()
        grow_copy(steps - 1, stream).start()
    for step in reversed(range(steps)):
        for stream in streams:
            grow_copy(step, stream).wait_recv()
            if step > 0:
                grow_copy(step - 1, stream).start()

    def join_copy(stream):
        place = dense_out.at[pl.ds(4 * core + 2 * stream, 2)]
        return remote(place, place, join_send.at[stream], join_recv.at[stream], across(1))

    for stream in streams:
        join_copy(stream).start()
    for stream in streams:
        join_copy(stream).wait()
        expert_copy(steps, stream).wait()
        for level in range(steps):
            expert_copy(level, stream).wait_send()
        first_copy(stream).wait_send()
        for step in range(1, steps):
            later_copy(step, stream).wait_send()
        for k in range(1, count):
            line_copy(k, stream).wait_send()
        for step in range(steps):
            grow_copy(step, stream).wait_send()
    for block in range(4):
        core_copy(block).wait_send()
    for stage in range(len(gain_bits)):
        gain_copy(stage).wait_send()
    for k in range(1, count):
        shard_copy(k).wait_send()
        gain_line(k).wait_send()


def spread(share, normed, deltas, head_low, branch, gains, bits, count):
    experts, _, _, final, hidden = share.shape
    rows = normed.shape[1] // count
    width = 3 * normed.shape[1] // 8
    dense_shape = (8, count, rows, width)
    steps = len(bits)
    last = rows >> (steps - 1)
    low = jnp.bfloat16
    vmem = pl.BlockSpec(memory_space=pltpu.VMEM)
    dma = pltpu.SemaphoreType.DMA
    return pl.pallas_call(
        functools.partial(spread_kernel, count, bits),
        in_specs=[vmem] * 6,
        out_specs=[vmem, vmem, vmem],
        out_shape=[
            jax.ShapeDtypeStruct((experts, 3, 4 * (final << steps), hidden), low),
            jax.ShapeDtypeStruct(dense_shape, low),
            jax.ShapeDtypeStruct(gains.shape, jnp.float32),
        ],
        scratch_shapes=[
            pltpu.VMEM(dense_shape, low),
            pltpu.VMEM((4, count, rows, width), low),
            pltpu.VMEM((4, count, rows, width), low),
            pltpu.VMEM((2, count, rows, width), low),
        ]
        + [pltpu.VMEM((2, count, rows >> step, width), low) for step in range(1, steps)]
        + [
            pltpu.VMEM((count, 2, last, width), low),
            pltpu.VMEM((count, 2, last, width), low),
            pltpu.VMEM((2, last, width), low),
            pltpu.VMEM((steps + 2,) + gains.shape, jnp.float32),
            pltpu.VMEM((steps + 1,) + gains.shape, jnp.float32),
            pltpu.VMEM((count,) + gains.shape, jnp.float32),
            dma((4,)),
            dma((4,)),
            dma((4,)),
            dma((steps, 2)),
            dma((steps, 2)),
            dma((count,)),
            dma((count,)),
            dma((steps, 2)),
            dma((steps, 2)),
            dma((2, count)),
            dma((2, count)),
            dma((2,)),
            dma((2,)),
            dma((steps + 1, 2)),
            dma((steps + 1, 2)),
            dma((steps + 1,)),
            dma((steps + 1,)),
            dma((count,)),
            dma((count,)),
        ],
        compiler_params=pltpu.CompilerParams(
            collective_id=2, has_side_effects=True, vmem_limit_bytes=60 * 1024 * 1024
        ),
        name="spread",
    )(share, normed, deltas, head_low, branch, gains)


def gather_kernel(
    count,
    bits,
    own_ref,
    small_ref,
    full_out,
    small_out,
    local_sem,
    line_send,
    line_recv,
    grow_send,
    grow_recv,
    join_send,
    join_recv,
    small_send,
    small_recv,
):
    rep = lax.axis_index("rep")
    me = lax.axis_index("shard")
    core = rep % 2
    steps = len(bits)
    streams = range(2)
    rows = own_ref.shape[1]
    half = own_ref.shape[2] // 2
    fine = half // 4
    groups = 2
    depth = own_ref.shape[0] // groups
    others = [lax.rem(me + k, count) for k in range(1, count)]

    def columns_of(start, size):
        return pl.ds(pl.multiple_of(start, 128), size)

    def order(stream):
        return [bits[(step + stream) % steps] for step in range(steps)]

    def side(bit):
        return (rep // bit) % 2

    own_copy = pltpu.make_async_copy(own_ref, full_out.at[:, me], local_sem.at[0])
    own_copy.start()
    own_small = pltpu.make_async_copy(small_ref, small_out.at[me], local_sem.at[1])
    own_small.start()
    peers = [(rep, other) for other in others]
    peers += [(flip(rep, bit), me) for bit in (1,) + bits]
    greet(peers)

    regions = []
    for stream in streams:
        column = core * half + stream * 2 * fine
        narrow = columns_of(column + side(order(stream)[0]) * fine, fine)
        start, size = 0, rows
        held = [(pl.ds(0, rows), narrow)]
        for step in range(1, steps):
            size = size // 2
            start = start + side(order(stream)[step]) * size
            held.append((rows_of(start, size), narrow))
        regions.append((held, columns_of(column, 2 * fine)))

    def remote(source, target, send_sem, recv_sem, peer):
        return pltpu.make_async_remote_copy(
            src_ref=source,
            dst_ref=target,
            send_sem=send_sem,
            recv_sem=recv_sem,
            device_id=peer,
            device_id_type=MESH,
        )

    def slab(group):
        return pl.ds(group * depth, depth)

    def line_copy(group, stream, source, peer):
        place, columns = regions[stream][0][-1]
        return remote(
            own_ref.at[slab(group), place, columns],
            full_out.at[slab(group), source, place, columns],
            line_send.at[group, stream, peer],
            line_recv.at[group, stream, source],
            (rep, peer),
        )

    def grow_copy(step, group, stream, source):
        place, columns = regions[stream][0][step]
        part = full_out.at[slab(group), source, place, columns]
        return remote(
            part,
            part,
            grow_send.at[step, group, stream, source],
            grow_recv.at[step, group, stream, source],
            (flip(rep, order(stream)[step]), me),
        )

    def join_copy(group, stream, source):
        part = full_out.at[slab(group), source, :, regions[stream][1]]
        return remote(
            part,
            part,
            join_send.at[group, stream, source],
            join_recv.at[group, stream, source],
            (flip(rep, 1), me),
        )

    def small_copy(source, peer):
        return remote(
            small_ref,
            small_out.at[source],
            small_send.at[peer],
            small_recv.at[source],
            (rep, peer),
        )

    for other in others:
        small_copy(me, other).start()
    for group in range(groups):
        for other in others:
            for stream in streams:
                line_copy(group, stream, me, other).start()

    def advance(level, group):
        for other in others:
            for stream in streams:
                if level == 0:
                    line_copy(group, stream, other, other).wait_recv()
                else:
                    grow_copy(steps - level, group, stream, other).wait_recv()
                if level < steps:
                    grow_copy(steps - 1 - level, group, stream, other).start()
                else:
                    join_copy(group, stream, other).start()

    for level in range(steps + 2):
        if level <= steps:
            advance(level, 0)
        if level > 0:
            advance(level - 1, 1)
    for group in range(groups):
        for other in others:
            for stream in streams:
                join_copy(group, stream, other).wait()
                line_copy(group, stream, me, other).wait_send()
                for step in range(steps):
                    grow_copy(step, group, stream, other).wait_send()
    for other in others:
        small_copy(other, other).wait_recv()
        small_copy(me, other).wait_send()
    own_copy.wait()
    own_small.wait()


def gather(own, small, bits, count):
    depth, rows, columns = own.shape
    steps = len(bits)
    vmem = pl.BlockSpec(memory_space=pltpu.VMEM)
    dma = pltpu.SemaphoreType.DMA
    return pl.pallas_call(
        functools.partial(gather_kernel, count, bits),
        in_specs=[vmem, vmem],
        out_specs=[vmem, vmem],
        out_shape=[
            jax.ShapeDtypeStruct((depth, count, rows, columns), own.dtype),
            jax.ShapeDtypeStruct((count,) + small.shape, small.dtype),
        ],
        scratch_shapes=[
            dma((2,)),
            dma((2, 2, count)),
            dma((2, 2, count)),
            dma((steps, 2, 2, count)),
            dma((steps, 2, 2, count)),
            dma((2, 2, count)),
            dma((2, 2, count)),
            dma((count,)),
            dma((count,)),
        ],
        compiler_params=pltpu.CompilerParams(
            collective_id=3, has_side_effects=True, vmem_limit_bytes=32 * 1024 * 1024
        ),
        name="gather",
    )(own, small)


def local(
    tokens,
    sequence_start,
    routes,
    route_weights,
    cotangent,
    query_proj,
    key_proj,
    value_proj,
    out_proj,
    prenorm,
    midnorm,
    gate_proj,
    up_proj,
    down_proj,
    query_moment,
    key_moment,
    value_moment,
    out_moment,
    prenorm_moment,
    midnorm_moment,
    gate_moment,
    up_moment,
    down_moment,
):
    shard_index = lax.axis_index("shard")
    rep_count = lax.axis_size("rep")
    shard_count = lax.axis_size("shard")
    row_block, width = query_proj.shape
    bits = rep_bits(rep_count)
    experts_here = gate_proj.shape[0]
    low = jnp.bfloat16
    own_rows = jnp.stack(
        [
            query_proj,
            jnp.concatenate([key_proj, value_proj], axis=1),
            out_proj,
            query_moment.astype(low),
            jnp.concatenate([key_moment.astype(low), value_moment.astype(low)], axis=1),
            out_moment.astype(low),
        ]
    )
    dense_weights = jnp.sum(
        jnp.where(
            routes.T[None, :, :] == jnp.arange(EXPERTS, dtype=jnp.int32)[:, None, None],
            route_weights.T[None, :, :],
            0.0,
        ),
        axis=1,
    )
    gain_rows = jnp.pad(
        jnp.stack([prenorm, midnorm]).astype(jnp.float32),
        ((0, 6), (0, tokens.shape[0] - row_block)),
    )
    cotangent_all = lax.all_gather(cotangent, "shard", axis=0)
    gathered, small = gather(
        own_rows, jnp.concatenate([dense_weights, gain_rows], axis=0), bits, shard_count
    )
    full_query = gathered[0].reshape(width, width)
    full_pair = gathered[1].reshape(width, width)
    full_out = gathered[2].reshape(width, width)
    full_key = full_pair[:, : width // 2]
    full_value = full_pair[:, width // 2 :]
    gain_before = small[:, EXPERTS, :row_block].reshape(width)
    gain_after = small[:, EXPERTS + 1, :row_block].reshape(width)
    expert_weights = lax.dynamic_slice_in_dim(
        small, shard_index * experts_here, experts_here, 1
    ).transpose(0, 2, 1)
    group_size = NHEADS // KVHEADS
    token_count = tokens.shape[0]
    inputs = tokens.astype(jnp.float32)
    scaled_first, inverse_first = root_scale(inputs)
    normed_first = (scaled_first * gain_before).astype(jnp.bfloat16)
    query_linear = jnp.dot(normed_first, full_query, preferred_element_type=jnp.float32).reshape(
        token_count, NHEADS, HEAD
    )
    key_linear = jnp.dot(normed_first, full_key, preferred_element_type=jnp.float32).reshape(
        token_count, KVHEADS, HEAD
    )
    values = (
        jnp.dot(normed_first, full_value, preferred_element_type=jnp.float32)
        .astype(jnp.bfloat16)
        .reshape(token_count, KVHEADS, HEAD)
    )
    cosine_table, sine_table = rotary_tables(
        jnp.arange(token_count, dtype=jnp.int32) - sequence_start
    )
    queries = (
        (query_linear * cosine_table + rotate_half(query_linear) * sine_table)
        .astype(jnp.bfloat16)
        .reshape(token_count, KVHEADS, group_size, HEAD)
    )
    rotated_keys = (key_linear * cosine_table + rotate_half(key_linear) * sine_table).astype(
        jnp.bfloat16
    )
    head_out, log_total = attend_forward(queries, rotated_keys, values, sequence_start)
    head_low = head_out.astype(jnp.bfloat16)
    middle = inputs + jnp.dot(head_low, full_out, preferred_element_type=jnp.float32)
    scaled_second, inverse_second = root_scale(middle)
    normed_second = (scaled_second * gain_after).astype(jnp.bfloat16)
    returned, grad_second, expert_share = moe(
        normed_second,
        cotangent_all,
        expert_weights,
        gate_proj,
        up_proj,
        down_proj,
        bits,
        shard_count,
    )
    mixed = middle + returned
    grad_mixed = cotangent.astype(jnp.float32)
    middle_extra, midnorm_part = root_back(grad_second, gain_after, scaled_second, inverse_second)
    grad_middle = grad_mixed + middle_extra
    grad_branch = grad_middle.astype(jnp.bfloat16)
    grad_heads = (
        jnp.einsum("td,qd->tq", grad_branch, full_out, preferred_element_type=jnp.float32)
        .astype(jnp.bfloat16)
        .reshape(queries.shape)
    )
    grad_queries, grad_keys, grad_values = attend_backward(
        queries, rotated_keys, values, sequence_start, log_total, grad_heads
    )
    grad_queries = grad_queries.reshape(token_count, NHEADS, HEAD)
    query_delta = (
        (grad_queries * cosine_table + rotate_back(grad_queries * sine_table))
        .astype(jnp.bfloat16)
        .reshape(token_count, -1)
    )
    key_delta = (
        (grad_keys * cosine_table + rotate_back(grad_keys * sine_table))
        .astype(jnp.bfloat16)
        .reshape(token_count, -1)
    )
    value_delta = grad_values.astype(jnp.bfloat16).reshape(token_count, -1)
    grad_first = (
        jnp.einsum("tq,dq->td", query_delta, full_query, preferred_element_type=jnp.float32)
        + jnp.einsum("tq,dq->td", key_delta, full_key, preferred_element_type=jnp.float32)
        + jnp.einsum("tq,dq->td", value_delta, full_value, preferred_element_type=jnp.float32)
    )
    input_extra, prenorm_part = root_back(grad_first, gain_before, scaled_first, inverse_first)
    grad_tokens = grad_middle + input_extra
    deltas = jnp.concatenate([query_delta, key_delta, value_delta], axis=1)
    gains_local = jnp.concatenate(
        [jnp.stack([prenorm_part, midnorm_part]), jnp.zeros((6, prenorm_part.shape[0]))], axis=0
    )
    expert_grads, dense_grads, gains_grad = spread(
        expert_share,
        normed_first,
        deltas,
        head_low,
        grad_branch,
        gains_local,
        bits,
        shard_count,
    )
    gains_here = lax.dynamic_slice_in_dim(gains_grad, shard_index * row_block, row_block, 1)
    prenorm_grad = gains_here[0]
    midnorm_grad = gains_here[1]
    prenorm_next = momentum_keep * prenorm_moment + prenorm_grad
    midnorm_next = momentum_keep * midnorm_moment + midnorm_grad
    prenorm_update = -rate_gain * prenorm_next
    midnorm_update = -rate_gain * midnorm_next
    (
        query_grad,
        query_next,
        query_update,
        key_grad,
        key_next,
        key_update,
        value_grad,
        value_next,
        value_update,
        out_grad,
        out_next,
        out_update,
    ) = dense_update(
        dense_grads,
        gathered,
        (query_moment, key_moment, value_moment, out_moment),
        LAYOUT,
        shard_index,
    )
    gate_grad, gate_next, gate_update, up_grad, up_next, up_update = expert_update(
        expert_grads, (0, 1), (gate_moment, up_moment)
    )
    down_grad, down_next, down_update = expert_update(expert_grads, (2,), (down_moment,))
    return (
        mixed.astype(jnp.bfloat16),
        grad_tokens,
        query_grad,
        query_next,
        query_update,
        key_grad,
        key_next,
        key_update,
        value_grad,
        value_next,
        value_update,
        out_grad,
        out_next,
        out_update,
        prenorm_grad,
        prenorm_next,
        prenorm_update,
        midnorm_grad,
        midnorm_next,
        midnorm_update,
        gate_grad,
        gate_next,
        gate_update,
        up_grad,
        up_next,
        up_update,
        down_grad,
        down_next,
        down_update,
    )


def solution(mesh):
    return jax.shard_map(
        local,
        mesh=mesh,
        in_specs=(
            P(("rep", "shard"), None),
            P(("rep", "shard")),
            P(("rep", "shard"), None),
            P(("rep", "shard"), None),
            P(("rep", "shard"), None),
            P("shard", None),
            P("shard", None),
            P("shard", None),
            P("shard", None),
            P("shard"),
            P("shard"),
            P("shard", None, None),
            P("shard", None, None),
            P("shard", None, None),
            P("shard", None),
            P("shard", None),
            P("shard", None),
            P("shard", None),
            P("shard"),
            P("shard"),
            P("shard", None, None),
            P("shard", None, None),
            P("shard", None, None),
        ),
        out_specs=(
            P(("rep", "shard"), None),
            P(("rep", "shard"), None),
            P("shard", None),
            P("shard", None),
            P("shard", None),
            P("shard", None),
            P("shard", None),
            P("shard", None),
            P("shard", None),
            P("shard", None),
            P("shard", None),
            P("shard", None),
            P("shard", None),
            P("shard", None),
            P("shard"),
            P("shard"),
            P("shard"),
            P("shard"),
            P("shard"),
            P("shard"),
            P("shard", None, None),
            P("shard", None, None),
            P("shard", None, None),
            P("shard", None, None),
            P("shard", None, None),
            P("shard", None, None),
            P("shard", None, None),
            P("shard", None, None),
            P("shard", None, None),
        ),
        check_vma=False,
    )
```

```python
import functools
import math

import jax
import jax.numpy as jnp
from jax import lax
from jax.experimental import pallas as pl
from jax.experimental.pallas import tpu as pltpu
from jax.sharding import PartitionSpec as P

NHEADS = 16
KVHEADS = 8
HEAD = 64
EXPERTS = 16
NS_ITERS = 2


norm_epsilon = 1e-06
rotary_base = 10000.0
momentum_keep = 0.9
rate_matrix = 0.5
rate_gain = 0.0002
newton_first = 3.4445
newton_second = -4.775
newton_third = 2.0315
masked_score = -1e30


def normalize(values):
    inverse = lax.rsqrt(jnp.mean(values * values, axis=-1, keepdims=True) + norm_epsilon)
    return (values * inverse, inverse)


def normalize_back(grad_normed, scaling, scaled, inverse):
    grad_scaled = grad_normed * scaling
    inner_mean = jnp.mean(grad_scaled * scaled, axis=-1, keepdims=True)
    return (
        inverse * (grad_scaled - scaled * inner_mean),
        jnp.sum(grad_normed * scaled, axis=0, keepdims=True),
    )


def dot_nn(left, right):
    return jnp.dot(left, right, preferred_element_type=jnp.float32)


def dot_nt(left, right):
    return lax.dot_general(
        left, right, (((1,), (1,)), ((), ())), preferred_element_type=jnp.float32
    )


def dot_tn(left, right):
    return lax.dot_general(
        left, right, (((0,), (0,)), ((), ())), preferred_element_type=jnp.float32
    )


def rotate(values, table_ref, sign):
    return (
        values * table_ref[0]
        + sign * pltpu.roll(values, 96, 1) * table_ref[1]
        + sign * pltpu.roll(values, 32, 1) * table_ref[2]
    )


def lane_low(shape):
    return lax.broadcasted_iota(jnp.int32, shape, 1) < HEAD


def twice(pair, upper):
    wide = pair.astype(jnp.float32)
    turned = pltpu.roll(wide, HEAD, 1)
    first = lane_low(pair.shape)
    return jnp.where(first != upper, wide, turned).astype(pair.dtype)


def stacked(pair):
    first = lane_low(pair.shape)
    zero = jnp.zeros_like(pair)
    return jnp.concatenate([jnp.where(first, pair, zero), jnp.where(first, zero, pair)], axis=0)


def unstacked(rows):
    half = rows.shape[0] // 2
    return jnp.where(lane_low((half, rows.shape[1])), rows[:half], rows[half:])


def allowed_pairs(start_column, start_row):
    shape = (start_column.shape[0], start_row.shape[1])
    query_places = lax.broadcasted_iota(jnp.int32, shape, 0)
    key_places = lax.broadcasted_iota(jnp.int32, shape, 1)
    one = (start_column == start_row) & (key_places <= query_places)
    return jnp.where(jnp.concatenate([one, one], axis=0), 0.0, masked_score)


def block_lanes(ref, block):
    return ref[:, block * 2 * HEAD : (block + 1) * 2 * HEAD]


def attend_pair(block, query_ref, pair_ref, bias):
    key = twice(block_lanes(pair_ref, block // 2), block % 2 == 1)
    value = twice(block_lanes(pair_ref, KVHEADS // 2 + block // 2), block % 2 == 1)
    queries = stacked(block_lanes(query_ref, block))
    scores = dot_nt(queries, key) * (1.0 / math.sqrt(HEAD)) + bias
    return (queries, key, value, scores)


def project_inputs(normed, weights, query_ref, pair_ref, table_ref):
    queries = dot_nn(normed, weights(0))
    for block in range(NHEADS // 2):
        lanes = slice(block * 2 * HEAD, (block + 1) * 2 * HEAD)
        query_ref[:, lanes] = rotate(queries[:, lanes], table_ref, 1.0).astype(jnp.bfloat16)
    pairs = dot_nn(normed, weights(1))
    for block in range(KVHEADS):
        lanes = slice(block * 2 * HEAD, (block + 1) * 2 * HEAD)
        value = pairs[:, lanes]
        if block < KVHEADS // 2:
            value = rotate(value, table_ref, 1.0)
        pair_ref[:, lanes] = value.astype(jnp.bfloat16)


def attend_forward(blocks, query_ref, pair_ref, bias, head_ref, total_ref):
    for block in blocks:
        _, _, value, scores = attend_pair(block, query_ref, pair_ref, bias)
        row_max = jnp.max(scores, axis=-1, keepdims=True)
        exponents = jnp.exp(scores - row_max)
        totals = jnp.sum(exponents, axis=-1, keepdims=True)
        softmax_low = (exponents * (1.0 / totals)).astype(jnp.bfloat16)
        head_ref[:, block * 2 * HEAD : (block + 1) * 2 * HEAD] = unstacked(
            dot_nn(softmax_low, value)
        ).astype(jnp.bfloat16)
        total_ref[:, block : block + 1] = row_max + jnp.log(totals)


def attend_backward(query_ref, pair_ref, bias, total_ref, grad_ref, table_ref, delta_ref):
    folded = []
    for block in range(KVHEADS):
        queries, key, value, scores = attend_pair(block, query_ref, pair_ref, bias)
        grads = stacked(block_lanes(grad_ref, block))
        softmax_full = jnp.exp(scores - total_ref[:, block : block + 1])
        grad_softmax = dot_nt(grads, value)
        inner = jnp.sum(softmax_full * grad_softmax, axis=-1, keepdims=True)
        grad_scores = (softmax_full * (grad_softmax - inner)).astype(jnp.bfloat16)
        scale = 1.0 / math.sqrt(HEAD)
        grad_query = unstacked(dot_nn(grad_scores, key)) * scale
        lanes = slice(block * 2 * HEAD, (block + 1) * 2 * HEAD)
        delta_ref[:, lanes] = rotate(grad_query, table_ref, -1.0).astype(jnp.bfloat16)
        grad_key = dot_tn(grad_scores, queries) * scale
        grad_value = dot_tn(softmax_full.astype(jnp.bfloat16), grads)
        folded.append(
            (
                grad_key + pltpu.roll(grad_key, HEAD, 1),
                grad_value + pltpu.roll(grad_value, HEAD, 1),
            )
        )
        if block % 2 == 1:
            first = lane_low(grad_key.shape)
            both = [jnp.where(first, low, high) for low, high in zip(*folded)]
            folded = []
            base = NHEADS * HEAD + (block // 2) * 2 * HEAD
            delta_ref[:, base : base + 2 * HEAD] = rotate(both[0], table_ref, -1.0).astype(
                jnp.bfloat16
            )
            base = base + KVHEADS * HEAD
            delta_ref[:, base : base + 2 * HEAD] = both[1].astype(jnp.bfloat16)


def rotary_tables(positions):
    half_size = HEAD // 2
    frequency = rotary_base ** (-(jnp.arange(half_size, dtype=jnp.float32) * 2.0) / HEAD)
    angles = positions.astype(jnp.float32)[:, None] * frequency[None, :]
    cosine, sine = (jnp.cos(angles), jnp.sin(angles))
    zero = jnp.zeros_like(sine)
    return jnp.stack(
        [
            jnp.concatenate([cosine] * 4, axis=1),
            jnp.concatenate([-sine, zero] * 2, axis=1),
            jnp.concatenate([zero, sine] * 2, axis=1),
        ]
    )


def newton_parts(grams):
    a, b, c = newton_first, newton_second, newton_third

    def times(left, right):
        return jnp.dot(left, right, preferred_element_type=jnp.float32)

    lows = [gram.astype(jnp.bfloat16) for gram in grams]
    firsts = [b * gram + c * times(low, low) for gram, low in zip(grams, lows)]
    first_lows = [first.astype(jnp.bfloat16) for first in firsts]
    mixes = [times(low, first) for low, first in zip(lows, first_lows)]
    nexts = [
        (a * a) * gram + (2.0 * a) * mix + times(mix.astype(jnp.bfloat16), first)
        for gram, mix, first in zip(grams, mixes, first_lows)
    ]
    next_lows = [gram.astype(jnp.bfloat16) for gram in nexts]
    seconds = [b * gram + c * times(low, low) for gram, low in zip(nexts, next_lows)]
    second_lows = [second.astype(jnp.bfloat16) for second in seconds]
    return list(zip(firsts, first_lows, seconds, second_lows))


def expert_update_kernel(kinds, scale, *refs):
    a = newton_first
    grads_ref = refs[0]
    moments = refs[1 : 1 + len(kinds)]
    outs = refs[1 + len(kinds) :]
    half = grads_ref.shape[3]
    states = []
    for index in range(len(kinds)):
        for e in range(grads_ref.shape[0]):
            grad = grads_ref[e, index].astype(jnp.float32)
            tall = kinds[index] < 2
            if not tall:
                grad = jnp.concatenate([grad[:half], grad[half:]], axis=1)
            moment = momentum_keep * moments[index][e] + grad
            outs[3 * index][e] = grad
            outs[3 * index + 1][e] = moment
            inverse = 1.0 / (jnp.sqrt(jnp.sum(moment * moment)) + 1e-07)
            low = (moment * inverse).astype(jnp.bfloat16)
            sides = (((0,), (0,)), ((), ())) if tall else (((1,), (1,)), ((), ()))
            gram = lax.dot_general(low, low, sides, preferred_element_type=jnp.float32)
            states.append((index, e, tall, inverse, low, gram))
    parts = newton_parts([state[-1] for state in states])
    for (index, e, tall, inverse, low, _), (first, first_low, second, second_low) in zip(
        states, parts
    ):
        rest = a * (first + second) + jnp.dot(
            first_low, second_low, preferred_element_type=jnp.float32
        )
        rest = (-scale * rest).astype(jnp.bfloat16)
        if tall:
            step = jnp.dot(low, rest, preferred_element_type=jnp.float32)
        else:
            step = jnp.dot(rest, low, preferred_element_type=jnp.float32)
        outs[3 * index + 2][e] = (-scale * a * a * inverse) * outs[3 * index + 1][e] + step


def expert_update(grads, kinds, moments):
    count, rows, columns = moments[0].shape
    group = 2 // len(kinds)
    scale = rate_matrix * math.sqrt(max(1.0, columns / rows))
    block = pl.BlockSpec((group, rows, columns), lambda i: (i, 0, 0))
    place = kinds[0] // len(kinds)
    taken = pl.BlockSpec((group, len(kinds)) + grads.shape[2:], lambda i: (i, place, 0, 0))
    shape = jax.ShapeDtypeStruct(moments[0].shape, jnp.float32)
    return pl.pallas_call(
        functools.partial(expert_update_kernel, kinds, scale),
        grid=(count // group,),
        in_specs=[taken] + [block] * len(kinds),
        out_specs=[block] * (3 * len(kinds)),
        out_shape=[shape] * (3 * len(kinds)),
        compiler_params=pltpu.CompilerParams(vmem_limit_bytes=60 * 1024 * 1024),
        name="expert_update",
        cost_estimate=pl.CostEstimate(
            flops=count * len(kinds) * 2500000000,
            bytes_accessed=moments[0].size * len(kinds) * 18,
            transcendentals=0,
        ),
    )(grads, *moments)


def dense_update_kernel(layout, place_ref, grads_ref, moments_ref, *refs):
    a = newton_first
    amount = len(layout)
    own_moments = refs[:amount]
    outs = refs[amount : 4 * amount]
    whole, own_grads = refs[4 * amount :]
    blocks, count, block_rows, width = grads_ref.shape
    part = width // 3
    me = place_ref[0]
    start = pl.multiple_of(me * block_rows, block_rows)
    for block in range(blocks):
        for index in range(3):
            columns = slice(8 * part * index + block * part, 8 * part * index + (block + 1) * part)
            inner = slice(index * part, (index + 1) * part)
            outer = slice(block * part, (block + 1) * part)
            grads = grads_ref[block, :, :, inner].reshape(count * block_rows, part)
            moments = moments_ref[index, :, :, outer].reshape(count * block_rows, part)
            whole[:, columns] = (
                momentum_keep * moments.astype(jnp.float32) + grads.astype(jnp.float32)
            ).astype(jnp.bfloat16)
            own_grads[:, columns] = grads_ref[block, me, :, inner].astype(jnp.float32)
    for group in ((0, 1), (2, 3)):
        states = []
        for index in group:
            begin, size = layout[index]
            grad_out, next_out, _ = outs[3 * index : 3 * index + 3]
            columns = slice(begin, begin + size)
            grad = own_grads[:, columns]
            grad_out[...] = grad
            next_out[...] = momentum_keep * own_moments[index][...] + grad
            matrix = whole[:, columns].astype(jnp.float32)
            inverse = 1.0 / (jnp.sqrt(jnp.sum(matrix * matrix)) + 1e-07)
            low = (matrix * inverse).astype(jnp.bfloat16)
            gram = lax.dot_general(
                low, low, (((0,), (0,)), ((), ())), preferred_element_type=jnp.float32
            )
            own = whole[pl.ds(start, block_rows), columns].astype(jnp.float32) * inverse
            states.append((index, size, own, gram))
        parts = newton_parts([state[-1] for state in states])
        for (index, size, own, _), (_, first_low, _, second_low) in zip(states, parts):
            scale = rate_matrix * math.sqrt(max(1.0, size / (count * block_rows)))
            once = a * own + jnp.dot(
                own.astype(jnp.bfloat16), first_low, preferred_element_type=jnp.float32
            )
            outs[3 * index + 2][...] = (-scale) * (
                a * once
                + jnp.dot(
                    once.astype(jnp.bfloat16), second_low, preferred_element_type=jnp.float32
                )
            )


def dense_update(grads, moments, own_moments, layout, shard_index):
    _, count, block_rows, width = moments.shape
    whole = lambda shape: pl.BlockSpec(shape, lambda i: (0,) * len(shape))
    shapes = []
    for _, size in layout:
        shapes += [jax.ShapeDtypeStruct((block_rows, size), jnp.float32)] * 3
    return pl.pallas_call(
        functools.partial(dense_update_kernel, layout),
        grid=(1,),
        in_specs=[pl.BlockSpec(memory_space=pltpu.SMEM), whole(grads.shape), whole(moments.shape)]
        + [whole(moment.shape) for moment in own_moments],
        out_specs=[whole(shape.shape) for shape in shapes],
        out_shape=shapes,
        scratch_shapes=[
            pltpu.VMEM((count * block_rows, 3 * width), jnp.bfloat16),
            pltpu.VMEM((block_rows, 3 * width), jnp.float32),
        ],
        compiler_params=pltpu.CompilerParams(vmem_limit_bytes=63 * 1024 * 1024),
        name="dense_update",
        cost_estimate=pl.CostEstimate(
            flops=28000000000, bytes_accessed=24 * width * width, transcendentals=0
        ),
    )(shard_index.reshape(1).astype(jnp.int32), grads, moments, *own_moments)


LAYOUT = ((0, 1024), (1024, 512), (1536, 512), (2048, 1024))


MESH = pl.DeviceIdType.MESH


def flip(index, bit):
    return index + bit - 2 * bit * ((index // bit) % 2)


def greet(peers):
    barrier = pltpu.get_barrier_semaphore()
    for peer in peers:
        pl.semaphore_signal(barrier, inc=1, device_id=peer, device_id_type=MESH)
    pl.semaphore_wait(barrier, len(peers))


def stream_plan(rep, bits, base, size):
    stages = []
    starts = [base, base + size]
    for step in range(len(bits)):
        size = size // 2
        stage = []
        for stream in range(2):
            bit = bits[(step + stream) % len(bits)]
            side = (rep // bit) % 2
            keep = starts[stream] + side * size
            send = starts[stream] + (1 - side) * size
            starts[stream] = keep
            stage.append((bit, stream, keep, send, size))
        stages.append(stage)
    return stages


def rows_of(start, size):
    return pl.ds(pl.multiple_of(start, 16), size)


def moe_kernel(
    count,
    bits,
    own_ref,
    middle_ref,
    cot_ref,
    weight_ref,
    gate_hbm,
    up_hbm,
    down_hbm,
    out_ref,
    back_ref,
    share_ref,
    tok,
    turned,
    mats,
    hid,
    gate_delta,
    up_delta,
    stage_back,
    stage_out,
    got_back,
    got_out,
    *rest,
):
    landing = rest[: 1 + 2 * len(bits)]
    (
        load_sem,
        right_sem,
        left_sem,
        arrive_sem,
        back_send,
        back_recv,
        out_send,
        out_recv,
        sum_send,
        sum_recv,
    ) = rest[1 + 2 * len(bits) :]
    rep = lax.axis_index("rep")
    me = lax.axis_index("shard")
    experts = mats.shape[0]
    tokens = own_ref.shape[0]
    half = mats.shape[2] // 2
    core = rep % 2

    loads = [
        pltpu.make_async_copy(gate_hbm, mats.at[:, 0], load_sem.at[0]),
        pltpu.make_async_copy(up_hbm, mats.at[:, 1], load_sem.at[1]),
        pltpu.make_async_copy(
            down_hbm.at[:, :, pl.ds(0, half)], mats.at[:, 2, pl.ds(0, half)], load_sem.at[2]
        ),
        pltpu.make_async_copy(
            down_hbm.at[:, :, pl.ds(half, half)], mats.at[:, 2, pl.ds(half, half)], load_sem.at[3]
        ),
    ]
    for load in loads:
        load.start()
    peers = [(rep, lax.rem(me + k, count)) for k in range(1, count)]
    peers += [(flip(rep, bit), me) for bit in (1,) + bits]
    greet(peers)

    right_peer = (rep, jnp.minimum(me + 1, count - 1))
    left_peer = (rep, jnp.maximum(me - 1, 0))

    def hand_on(block, to_right):
        return pltpu.make_async_remote_copy(
            src_ref=tok.at[block],
            dst_ref=tok.at[block],
            send_sem=(right_sem if to_right else left_sem).at[block],
            recv_sem=arrive_sem.at[block],
            device_id=right_peer if to_right else left_peer,
            device_id_type=MESH,
        )

    def returning(stage, got, send_sem, recv_sem, block):
        return pltpu.make_async_remote_copy(
            src_ref=stage.at[block],
            dst_ref=got.at[me],
            send_sem=send_sem.at[block],
            recv_sem=recv_sem.at[me],
            device_id=(rep, block),
            device_id_type=MESH,
        )

    tok[me] = own_ref[...]

    @pl.when(me < count - 1)
    def _():
        hand_on(me, True).start()

    @pl.when(me > 0)
    def _():
        hand_on(me, False).start()

    for load in loads:
        load.wait()

    margin = jnp.minimum(me, count - 1 - me)
    longer = jnp.where(me < count - 1 - me, 1, -1)
    inward = jnp.where(2 * me < count, 1, -1)
    nt = (((1,), (1,)), ((), ()))

    def dot(left, right):
        return jnp.dot(left, right, preferred_element_type=jnp.float32)

    def dot_nt(left, right):
        return lax.dot_general(left, right, nt, preferred_element_type=jnp.float32)

    def visit(j, carry):
        lower = me - j
        upper = me + j

        @pl.when((j > 0) & (lower >= 0))
        def _():
            hand_on(jnp.maximum(lower, 0), True).wait_recv()

            @pl.when(me < count - 1)
            def _():
                hand_on(jnp.maximum(lower, 0), True).start()

        @pl.when((j > 0) & (upper < count))
        def _():
            hand_on(jnp.minimum(upper, count - 1), False).wait_recv()

            @pl.when(me > 0)
            def _():
                hand_on(jnp.minimum(upper, count - 1), False).start()

        near = (j + 1) // 2
        alternating = me + near - 2 * near * (j % 2)
        block = jnp.where(j <= 2 * margin, alternating, me + longer * (j - margin))
        places = pl.ds(pl.multiple_of(block * tokens, tokens), tokens)
        rows = tok[block]
        grads = cot_ref[block]
        turned[:, places] = rows.T
        hiddens = []
        for e in range(experts):
            weight = weight_ref[block, :, e : e + 1]
            u = dot(rows, mats[e, 0])
            w = dot(rows, mats[e, 1])
            gate = 1.0 / (1.0 + jnp.exp(-u))
            act = u * gate
            hidden = (weight * (act * w)).astype(jnp.bfloat16)
            hid[e, :, places] = hidden.T
            hiddens.append(hidden)
            pulled = weight * (
                dot_nt(grads[:, :half], mats[e, 2, :half])
                + dot_nt(grads[:, half:], mats[e, 2, half:])
            )
            gate_delta[e, places] = (pulled * w * (gate + act * (1.0 - gate))).astype(jnp.bfloat16)
            up_delta[e, places] = (pulled * act).astype(jnp.bfloat16)
        for side in range(2):
            part = slice(side * half, (side + 1) * half)
            total_back = None
            total_out = None
            for e in range(experts):
                back = dot_nt(gate_delta[e, places], mats[e, 0, part]) + dot_nt(
                    up_delta[e, places], mats[e, 1, part]
                )
                out = dot(hiddens[e], mats[e, 2, part])
                total_back = back if e == 0 else total_back + back
                total_out = out if e == 0 else total_out + out
            stage_back[block, :, part] = total_back.astype(jnp.bfloat16)
            stage_out[block, :, part] = total_out.astype(jnp.bfloat16)

        @pl.when((j > 0) & ((block - me) * inward > 0))
        def _():
            returning(stage_back, got_back, back_send, back_recv, block).start()

        return carry

    lax.fori_loop(0, count, visit, 0)
    for block in range(count):

        @pl.when((block - me) * inward < 0)
        def _():
            returning(stage_back, got_back, back_send, back_recv, block).start()

    for k in range(1, count):
        returning(stage_out, got_out, out_send, out_recv, lax.rem(me + k, count)).start()

    plan = stream_plan(rep, bits, core * half, half // 2)

    def sum_copy(stage, slot, e, start, size, bit):
        return pltpu.make_async_remote_copy(
            src_ref=mats.at[e, :, rows_of(start, size)],
            dst_ref=landing[slot].at[e],
            send_sem=sum_send.at[slot, e],
            recv_sem=sum_recv.at[slot, e],
            device_id=(flip(rep, bit), me),
            device_id_type=MESH,
        )

    def copies(stage, e):
        if stage == 0:
            return [(sum_copy(0, 0, e, (1 - core) * half, half, 1), 0, core * half, half)]
        return [
            (
                sum_copy(stage, 1 + 2 * (stage - 1) + stream, e, send, size, bit),
                1 + 2 * (stage - 1) + stream,
                keep,
                size,
            )
            for bit, stream, keep, send, size in plan[stage - 1]
        ]

    def finish(stage, e):
        for copy, slot, keep, size in copies(stage, e):
            copy.wait_recv()
            place = rows_of(keep, size)
            for kind in range(3):
                mats[e, kind, place] = (
                    mats[e, kind, place].astype(jnp.float32)
                    + landing[slot][e, kind].astype(jnp.float32)
                ).astype(jnp.bfloat16)

    stages = 1 + len(bits)
    for turn in range(experts + stages):
        if turn < experts:
            e = turn
            for side in range(2):
                part = slice(side * half, (side + 1) * half)
                mats[e, 0, part] = dot(turned[part], gate_delta[e]).astype(jnp.bfloat16)
                mats[e, 1, part] = dot(turned[part], up_delta[e]).astype(jnp.bfloat16)
                mats[e, 2, part] = dot(hid[e], cot_ref[:, :, part].reshape(count * tokens, half)).astype(jnp.bfloat16)
            copies(0, e)[0][0].start()
        for stage in range(stages):
            e = turn - 1 - stage
            if 0 <= e < experts:
                finish(stage, e)
                if stage + 1 < stages:
                    for copy, _, _, _ in copies(stage + 1, e):
                        copy.start()
                else:
                    for _, stream, keep, _, size in plan[-1]:
                        share_ref[e, :, stream] = mats[e, :, rows_of(keep, size)]

    total = stage_back[me].astype(jnp.float32)
    for k in range(1, count):
        source = lax.rem(me + k, count)
        pltpu.make_async_remote_copy(
            src_ref=stage_back.at[source],
            dst_ref=got_back.at[source],
            send_sem=back_send.at[source],
            recv_sem=back_recv.at[source],
            device_id=(rep, source),
            device_id_type=MESH,
        ).wait_recv()
        total = total + got_back[source].astype(jnp.float32)
    back_ref[...] = total
    total = stage_out[me].astype(jnp.float32)
    for k in range(1, count):
        source = lax.rem(me + k, count)
        pltpu.make_async_remote_copy(
            src_ref=stage_out.at[source],
            dst_ref=got_out.at[source],
            send_sem=out_send.at[source],
            recv_sem=out_recv.at[source],
            device_id=(rep, source),
            device_id_type=MESH,
        ).wait_recv()
        total = total + got_out[source].astype(jnp.float32)
    out_ref[...] = (middle_ref[...] + total).astype(out_ref.dtype)

    for k in range(1, count):
        block = lax.rem(me + k, count)
        returning(stage_back, got_back, back_send, back_recv, block).wait_send()
        returning(stage_out, got_out, out_send, out_recv, block).wait_send()
    for e in range(experts):
        for stage in range(stages):
            for copy, _, _, _ in copies(stage, e):
                copy.wait_send()
    for block in range(count):

        @pl.when((block <= me) & (me < count - 1))
        def _():
            hand_on(block, True).wait_send()

        @pl.when((block >= me) & (me > 0))
        def _():
            hand_on(block, False).wait_send()


def moe(normed, middle, cotangents, weights, gate_proj, up_proj, down_proj, bits, count):
    tokens, width = normed.shape
    experts, _, hidden = gate_proj.shape
    half = width // 2
    low = jnp.bfloat16
    final = (half // 2) >> len(bits)
    vmem = pl.BlockSpec(memory_space=pltpu.VMEM)
    anywhere = pl.BlockSpec(memory_space=pl.ANY)
    landings = [pltpu.VMEM((experts, 3, half, hidden), low)]
    for step in range(len(bits)):
        size = (half // 2) >> (step + 1)
        landings += [pltpu.VMEM((experts, 3, size, hidden), low)] * 2
    slots = len(landings)
    dma = pltpu.SemaphoreType.DMA
    return pl.pallas_call(
        functools.partial(moe_kernel, count, bits),
        in_specs=[vmem, vmem, vmem, vmem, anywhere, anywhere, anywhere],
        out_specs=[vmem, vmem, vmem],
        out_shape=[
            jax.ShapeDtypeStruct((tokens, width), low),
            jax.ShapeDtypeStruct((tokens, width), jnp.float32),
            jax.ShapeDtypeStruct((experts, 3, 2, final, hidden), low),
        ],
        scratch_shapes=[
            pltpu.VMEM((count, tokens, width), low),
            pltpu.VMEM((width, count * tokens), low),
            pltpu.VMEM((experts, 3, width, hidden), low),
            pltpu.VMEM((experts, hidden, count * tokens), low),
            pltpu.VMEM((experts, count * tokens, hidden), low),
            pltpu.VMEM((experts, count * tokens, hidden), low),
            pltpu.VMEM((count, tokens, width), low),
            pltpu.VMEM((count, tokens, width), low),
            pltpu.VMEM((count, tokens, width), low),
            pltpu.VMEM((count, tokens, width), low),
        ]
        + landings
        + [
            dma((4,)),
            dma((count,)),
            dma((count,)),
            dma((count,)),
            dma((count,)),
            dma((count,)),
            dma((count,)),
            dma((count,)),
            dma((slots, experts)),
            dma((slots, experts)),
        ],
        compiler_params=pltpu.CompilerParams(
            collective_id=1, has_side_effects=True, vmem_limit_bytes=63 * 1024 * 1024
        ),
        name="moe",
        cost_estimate=pl.CostEstimate(
            flops=39000000000, bytes_accessed=20000000, transcendentals=2000000
        ),
    )(normed, middle, cotangents, weights, gate_proj, up_proj, down_proj)


def rep_bits(rep_count):
    bits = []
    bit = 2
    while bit < rep_count:
        bits.append(bit)
        bit = bit * 2
    return tuple(bits)


def spread_kernel(
    count,
    bits,
    share_ref,
    normed_ref,
    head_ref,
    weights_ref,
    small_ref,
    tokens_ref,
    cot_ref,
    second_ref,
    middle_ref,
    query_ref,
    pair_ref,
    total_ref,
    table_ref,
    column_ref,
    row_ref,
    experts_out,
    dense_out,
    gains_out,
    tokens_out,
    delta_ref,
    branch_ref,
    heads_ref,
    dense_ref,
    total,
    land_core,
    land_first,
    *rest,
):
    later = len(bits) - 1
    land_later = rest[:later]
    (
        piece_send,
        piece_land,
        piece,
        gains_send,
        gains_land,
        gains_all,
        local_sem,
        core_send,
        core_recv,
        half_send,
        half_recv,
        shard_send,
        shard_recv,
        grow_send,
        grow_recv,
        line_send,
        line_recv,
        join_send,
        join_recv,
        expert_send,
        expert_recv,
        gain_send,
        gain_recv,
        gain_line_send,
        gain_line_recv,
    ) = rest[later:]
    rep = lax.axis_index("rep")
    me = lax.axis_index("shard")
    core = rep % 2
    rows = dense_ref.shape[2]
    expert_rows = experts_out.shape[2]
    steps = len(bits)
    streams = range(2)

    def remote(source, target, send_sem, recv_sem, peer):
        return pltpu.make_async_remote_copy(
            src_ref=source,
            dst_ref=target,
            send_sem=send_sem,
            recv_sem=recv_sem,
            device_id=peer,
            device_id_type=MESH,
        )

    def across(bit):
        return (flip(rep, bit), me)

    def order(stream):
        return [bits[(step + stream) % steps] for step in range(steps)]

    def side(bit):
        return (rep // bit) % 2

    plan = stream_plan(rep, bits, core * (expert_rows // 2), expert_rows // 4)
    base = [(core * (expert_rows // 2)) + stream * (expert_rows // 4) for stream in streams]

    def expert_copy(level, stream):
        if level == steps:
            place = rows_of(base[stream], expert_rows // 4)
            peer = across(1)
        else:
            bit, _, keep, _, size = plan[steps - 1 - level][stream]
            place = rows_of(keep, size)
            peer = across(bit)
        source = experts_out.at[:, :, place]
        if level == 0:
            source = share_ref.at[:, :, stream]
        return remote(
            source,
            experts_out.at[:, :, place],
            expert_send.at[level, stream],
            expert_recv.at[level, stream],
            peer,
        )

    def own_copy(stream):
        _, _, keep, _, size = plan[-1][stream]
        return pltpu.make_async_copy(
            share_ref.at[:, :, stream],
            experts_out.at[:, :, rows_of(keep, size)],
            local_sem.at[stream],
        )

    for stream in streams:
        own_copy(stream).start()
    peers = [(rep, lax.rem(me + k, count)) for k in range(1, count)]
    peers += [across(bit) for bit in (1,) + bits]
    greet(peers)

    def core_copy(block):
        return remote(
            dense_ref.at[4 * (1 - core) + block],
            land_core.at[block],
            core_send.at[block],
            core_recv.at[block],
            across(1),
        )

    gain_bits = (1,) + bits

    def gain_copy(stage):
        return remote(
            gains_send.at[stage],
            gains_land.at[stage],
            gain_send.at[stage],
            gain_recv.at[stage],
            across(gain_bits[stage]),
        )

    for stream in streams:
        expert_copy(0, stream).start()

    def whole(index):
        return weights_ref[index].reshape(count * rows, -1)

    def gain(index):
        at = EXPERTS + index
        return jnp.concatenate([small_ref[z, at : at + 1, :rows] for z in range(count)], axis=1)

    scaled, inverse = normalize(middle_ref[...])
    middle_extra, midnorm_part = normalize_back(second_ref[...], gain(1), scaled, inverse)
    grad_middle = cot_ref[...].astype(jnp.float32) + middle_extra
    tokens_out[...] = grad_middle
    branch_ref[...] = grad_middle.astype(jnp.bfloat16)
    heads_ref[...] = dot_nt(branch_ref[...], whole(2)).astype(jnp.bfloat16)
    bias = allowed_pairs(column_ref[...], row_ref[...])
    attend_backward(query_ref, pair_ref, bias, total_ref, heads_ref, table_ref, delta_ref)

    part = dense_ref.shape[3] // 3
    normed_turned = normed_ref[...].T
    head_turned = head_ref[...].T

    def make_block(block):
        def columns(ref, offset):
            return ref[:, pl.ds(pl.multiple_of(offset + block * part, part), part)]

        pair = jnp.concatenate([columns(delta_ref, 0), columns(delta_ref, 8 * part)], axis=1)
        left = jnp.dot(normed_turned, pair, preferred_element_type=jnp.float32)
        right = jnp.dot(head_turned, columns(branch_ref, 0), preferred_element_type=jnp.float32)
        for line in range(count):
            place = slice(line * rows, (line + 1) * rows)
            dense_ref[block, line, :, : 2 * part] = left[place].astype(jnp.bfloat16)
            dense_ref[block, line, :, 2 * part :] = right[place].astype(jnp.bfloat16)

    for block in range(4):
        make_block(4 * (1 - core) + block)
        core_copy(block).start()
    for block in range(4):
        make_block(4 * core + block)

    def gain_step(stage):
        gain_copy(stage).wait_recv()
        gains_send[stage + 1] = gains_send[stage] + gains_land[stage]
        if stage + 1 < len(gain_bits):
            gain_copy(stage + 1).start()

    first = [side(order(stream)[0]) for stream in streams]
    held = [2 * stream + first[stream] for stream in streams]
    given = [2 * stream + 1 - first[stream] for stream in streams]

    def first_copy(stream):
        return remote(
            total.at[given[stream]],
            land_first.at[stream],
            half_send.at[0, stream],
            half_recv.at[0, stream],
            across(order(stream)[0]),
        )

    def add_core(block):
        for line in range(count):
            total[block, line] = (
                dense_ref[4 * core + block, line].astype(jnp.float32)
                + land_core[block, line].astype(jnp.float32)
            ).astype(jnp.bfloat16)

    for block in range(4):
        core_copy(block).wait_recv()
    for stream in streams:
        add_core(given[stream])
        first_copy(stream).start()
    for stream in streams:
        add_core(held[stream])
    grad_first = dot_nt(delta_ref[:, : NHEADS * HEAD], whole(0)) + dot_nt(
        delta_ref[:, NHEADS * HEAD :], whole(1)
    )
    scaled, inverse = normalize(tokens_ref[...].astype(jnp.float32))
    input_extra, prenorm_part = normalize_back(grad_first, gain(0), scaled, inverse)
    tokens_out[...] = tokens_out[...] + input_extra
    gains_send[0] = jnp.concatenate(
        [prenorm_part, midnorm_part, jnp.zeros((6, prenorm_part.shape[1]), jnp.float32)], axis=0
    )
    gain_copy(0).start()
    gain_step(0)

    starts = []
    for stream in streams:
        start, size, line = 0, rows, []
        for step in range(1, steps):
            size = size // 2
            near = side(order(stream)[step])
            line.append((start + near * size, start + (1 - near) * size, size))
            start = start + near * size
        starts.append((start, size, line))

    def later_copy(step, stream):
        keep, send, size = starts[stream][2][step - 1]
        return remote(
            total.at[held[stream], :, rows_of(send, size)],
            land_later[step - 1].at[stream],
            half_send.at[step, stream],
            half_recv.at[step, stream],
            across(order(stream)[step]),
        )

    for stream in streams:
        first_copy(stream).wait_recv()
        for line in range(count):
            total[held[stream], line] = (
                total[held[stream], line].astype(jnp.float32)
                + land_first[stream, line].astype(jnp.float32)
            ).astype(jnp.bfloat16)
        if steps > 1:
            later_copy(1, stream).start()
    gain_step(1)

    for stream in streams:
        own_copy(stream).wait()
        expert_copy(0, stream).wait_recv()
        if steps > 1:
            expert_copy(1, stream).start()

    for step in range(1, steps):
        for stream in streams:
            later_copy(step, stream).wait_recv()
            keep, _, size = starts[stream][2][step - 1]
            for line in range(count):
                place = rows_of(keep, size)
                total[held[stream], line, place] = (
                    total[held[stream], line, place].astype(jnp.float32)
                    + land_later[step - 1][stream, line].astype(jnp.float32)
                ).astype(jnp.bfloat16)
            if step + 1 < steps:
                later_copy(step + 1, stream).start()
        gain_step(step + 1)

    last = starts[0][1]
    places = [rows_of(starts[stream][0], last) for stream in streams]
    for stream in streams:
        for line in range(count):
            piece_send[line, stream] = total[held[stream], line, places[stream]]

    def shard_copy(k):
        target = lax.rem(me + k, count)
        return remote(
            piece_send.at[target],
            piece_land.at[me],
            shard_send.at[target],
            shard_recv.at[me],
            (rep, target),
        )

    def shard_arrival(source):
        return remote(
            piece_send.at[source],
            piece_land.at[source],
            shard_send.at[source],
            shard_recv.at[source],
            (rep, source),
        )

    def gain_line(k):
        target = lax.rem(me + k, count)
        return remote(
            gains_send.at[len(gain_bits)],
            gains_all.at[me],
            gain_line_send.at[target],
            gain_line_recv.at[me],
            (rep, target),
        )

    def gain_arrival(source):
        return remote(
            gains_send.at[len(gain_bits)],
            gains_all.at[source],
            gain_line_send.at[source],
            gain_line_recv.at[source],
            (rep, source),
        )

    for k in range(1, count):
        shard_copy(k).start()
        gain_line(k).start()
    summed = piece_send[me].astype(jnp.float32)
    for k in range(1, count):
        source = lax.rem(me + k, count)
        shard_arrival(source).wait_recv()
        summed = summed + piece_land[source].astype(jnp.float32)
    piece[...] = summed.astype(jnp.bfloat16)

    def line_copy(k, stream):
        target = lax.rem(me + k, count)
        return remote(
            piece.at[stream],
            dense_out.at[4 * core + held[stream], me, places[stream]],
            line_send.at[stream, target],
            line_recv.at[stream, me],
            (rep, target),
        )

    def line_arrival(source, stream):
        return remote(
            piece.at[stream],
            dense_out.at[4 * core + held[stream], source, places[stream]],
            line_send.at[stream, source],
            line_recv.at[stream, source],
            (rep, source),
        )

    def own_piece(stream):
        return pltpu.make_async_copy(
            piece.at[stream],
            dense_out.at[4 * core + held[stream], me, places[stream]],
            local_sem.at[2 + stream],
        )

    for stream in streams:
        own_piece(stream).start()
        for k in range(1, count):
            line_copy(k, stream).start()
    gained = gains_send[len(gain_bits)]
    for k in range(1, count):
        source = lax.rem(me + k, count)
        gain_arrival(source).wait_recv()
        gained = gained + gains_all[source]
    gains_out[...] = gained

    for level in range(1, steps):
        for stream in streams:
            expert_copy(level, stream).wait_recv()
            expert_copy(level + 1, stream).start()
    if steps == 1:
        for stream in streams:
            expert_copy(1, stream).start()

    def grow_copy(step, stream):
        if step == 0:
            place = dense_out.at[4 * core + held[stream]]
        else:
            keep, _, size = starts[stream][2][step - 1]
            place = dense_out.at[4 * core + held[stream], :, rows_of(keep, size)]
        return remote(
            place,
            place,
            grow_send.at[step, stream],
            grow_recv.at[step, stream],
            across(order(stream)[step]),
        )

    for stream in streams:
        own_piece(stream).wait()
        for k in range(1, count):
            line_arrival(lax.rem(me + k, count), stream).wait_recv()
        grow_copy(steps - 1, stream).start()
    for step in reversed(range(steps)):
        for stream in streams:
            grow_copy(step, stream).wait_recv()
            if step > 0:
                grow_copy(step - 1, stream).start()

    def join_copy(stream):
        place = dense_out.at[pl.ds(4 * core + 2 * stream, 2)]
        return remote(place, place, join_send.at[stream], join_recv.at[stream], across(1))

    for stream in streams:
        join_copy(stream).start()
    for stream in streams:
        join_copy(stream).wait()
        expert_copy(steps, stream).wait()
        for level in range(steps):
            expert_copy(level, stream).wait_send()
        first_copy(stream).wait_send()
        for step in range(1, steps):
            later_copy(step, stream).wait_send()
        for k in range(1, count):
            line_copy(k, stream).wait_send()
        for step in range(steps):
            grow_copy(step, stream).wait_send()
    for block in range(4):
        core_copy(block).wait_send()
    for stage in range(len(gain_bits)):
        gain_copy(stage).wait_send()
    for k in range(1, count):
        shard_copy(k).wait_send()
        gain_line(k).wait_send()


def spread(
    share, normed, head_low, weights, small, tokens, cotangent, second, middle, *rest, bits, count
):
    query, pair, log_total, tables, starts = rest
    experts, _, _, final, hidden = share.shape
    token_count, features = normed.shape
    rows = features // count
    width = 3 * features // 8
    dense_shape = (8, count, rows, width)
    gains_shape = (8, features)
    steps = len(bits)
    last = rows >> (steps - 1)
    low = jnp.bfloat16
    vmem = pl.BlockSpec(memory_space=pltpu.VMEM)
    dma = pltpu.SemaphoreType.DMA
    return pl.pallas_call(
        functools.partial(spread_kernel, count, bits),
        in_specs=[vmem] * 15,
        out_specs=[vmem] * 4,
        out_shape=[
            jax.ShapeDtypeStruct((experts, 3, 4 * (final << steps), hidden), low),
            jax.ShapeDtypeStruct(dense_shape, low),
            jax.ShapeDtypeStruct(gains_shape, jnp.float32),
            jax.ShapeDtypeStruct((token_count, features), jnp.float32),
        ],
        scratch_shapes=[
            pltpu.VMEM((token_count, 2 * features), low),
            pltpu.VMEM((token_count, features), low),
            pltpu.VMEM((token_count, features), low),
            pltpu.VMEM(dense_shape, low),
            pltpu.VMEM((4, count, rows, width), low),
            pltpu.VMEM((4, count, rows, width), low),
            pltpu.VMEM((2, count, rows, width), low),
        ]
        + [pltpu.VMEM((2, count, rows >> step, width), low) for step in range(1, steps)]
        + [
            pltpu.VMEM((count, 2, last, width), low),
            pltpu.VMEM((count, 2, last, width), low),
            pltpu.VMEM((2, last, width), low),
            pltpu.VMEM((steps + 2,) + gains_shape, jnp.float32),
            pltpu.VMEM((steps + 1,) + gains_shape, jnp.float32),
            pltpu.VMEM((count,) + gains_shape, jnp.float32),
            dma((4,)),
            dma((4,)),
            dma((4,)),
            dma((steps, 2)),
            dma((steps, 2)),
            dma((count,)),
            dma((count,)),
            dma((steps, 2)),
            dma((steps, 2)),
            dma((2, count)),
            dma((2, count)),
            dma((2,)),
            dma((2,)),
            dma((steps + 1, 2)),
            dma((steps + 1, 2)),
            dma((steps + 1,)),
            dma((steps + 1,)),
            dma((count,)),
            dma((count,)),
        ],
        compiler_params=pltpu.CompilerParams(
            collective_id=2, has_side_effects=True, vmem_limit_bytes=63 * 1024 * 1024
        ),
        name="spread",
    )(
        share,
        normed,
        head_low,
        weights,
        small,
        tokens,
        cotangent,
        second,
        middle,
        query,
        pair,
        log_total,
        tables,
        starts[:, None],
        starts[None, :],
    )


def gather_kernel(
    count,
    bits,
    weights_ref,
    moments_ref,
    small_ref,
    tokens_ref,
    cot_ref,
    table_ref,
    column_ref,
    row_ref,
    weights_out,
    moments_out,
    small_out,
    cot_out,
    middle_out,
    first_out,
    second_out,
    query_out,
    pair_out,
    head_out,
    total_out,
    local_sem,
    line_send,
    line_recv,
    grow_send,
    grow_recv,
    join_send,
    join_recv,
    small_send,
    small_recv,
    right_sem,
    left_sem,
    arrive_sem,
):
    rep = lax.axis_index("rep")
    me = lax.axis_index("shard")
    core = rep % 2
    steps = len(bits)
    streams = range(2)
    owns = (weights_ref, moments_ref)
    fulls = (weights_out, moments_out)
    rows, width = weights_ref.shape[1:]
    half = width // 2
    fine = half // 4
    groups = 2
    others = [lax.rem(me + k, count) for k in range(1, count)]

    def columns_of(start, size):
        return pl.ds(pl.multiple_of(start, 128), size)

    def order(stream):
        return [bits[(step + stream) % steps] for step in range(steps)]

    def side(bit):
        return (rep // bit) % 2

    own_copies = [
        pltpu.make_async_copy(weights_ref, weights_out.at[:, me], local_sem.at[0]),
        pltpu.make_async_copy(moments_ref, moments_out.at[:, me], local_sem.at[1]),
    ]
    for own_copy in own_copies:
        own_copy.start()
    small_out[me] = small_ref[...]
    cot_out[me] = cot_ref[...]
    peers = [(rep, other) for other in others]
    peers += [(flip(rep, bit), me) for bit in (1,) + bits]
    greet(peers)

    regions = []
    for stream in streams:
        column = core * half + stream * 2 * fine
        narrow = columns_of(column + side(order(stream)[0]) * fine, fine)
        start, size = 0, rows
        held = [(pl.ds(0, rows), narrow)]
        for step in range(1, steps):
            size = size // 2
            start = start + side(order(stream)[step]) * size
            held.append((rows_of(start, size), narrow))
        regions.append((held, columns_of(column, 2 * fine)))

    def remote(source, target, send_sem, recv_sem, peer):
        return pltpu.make_async_remote_copy(
            src_ref=source,
            dst_ref=target,
            send_sem=send_sem,
            recv_sem=recv_sem,
            device_id=peer,
            device_id_type=MESH,
        )

    def line_copy(group, stream, source, peer):
        place, columns = regions[stream][0][-1]
        return remote(
            owns[group].at[:, place, columns],
            fulls[group].at[:, source, place, columns],
            line_send.at[group, stream, peer],
            line_recv.at[group, stream, source],
            (rep, peer),
        )

    def grow_copy(step, group, stream, source):
        place, columns = regions[stream][0][step]
        part = fulls[group].at[:, source, place, columns]
        return remote(
            part,
            part,
            grow_send.at[step, group, stream, source],
            grow_recv.at[step, group, stream, source],
            (flip(rep, order(stream)[step]), me),
        )

    def join_copy(group, stream, source):
        part = fulls[group].at[:, source, :, regions[stream][1]]
        return remote(
            part,
            part,
            join_send.at[group, stream, source],
            join_recv.at[group, stream, source],
            (flip(rep, 1), me),
        )

    def small_copy(source, peer):
        return remote(
            small_ref,
            small_out.at[source],
            small_send.at[peer],
            small_recv.at[source],
            (rep, peer),
        )

    def hand_on(block, to_right):
        peer = jnp.minimum(me + 1, count - 1) if to_right else jnp.maximum(me - 1, 0)
        return remote(
            cot_out.at[block],
            cot_out.at[block],
            (right_sem if to_right else left_sem).at[block],
            arrive_sem.at[block],
            (rep, peer),
        )

    def line_start():
        @pl.when(me < count - 1)
        def _():
            hand_on(me, True).start()

        @pl.when(me > 0)
        def _():
            hand_on(me, False).start()

    def line_step(step):
        lower = me - step
        upper = me + step

        @pl.when(lower >= 0)
        def _():
            hand_on(jnp.maximum(lower, 0), True).wait_recv()

            @pl.when(me < count - 1)
            def _():
                hand_on(jnp.maximum(lower, 0), True).start()

        @pl.when(upper < count)
        def _():
            hand_on(jnp.minimum(upper, count - 1), False).wait_recv()

            @pl.when(me > 0)
            def _():
                hand_on(jnp.minimum(upper, count - 1), False).start()

    def line_send_group(group):
        for other in others:
            for stream in streams:
                line_copy(group, stream, me, other).start()

    def advance(level, group):
        for other in others:
            for stream in streams:
                if level == 0:
                    line_copy(group, stream, other, other).wait_recv()
                else:
                    grow_copy(steps - level, group, stream, other).wait_recv()
                if level < steps:
                    grow_copy(steps - 1 - level, group, stream, other).start()
                else:
                    join_copy(group, stream, other).start()

    for other in others:
        small_copy(me, other).start()
    line_send_group(0)
    for other in others:
        small_copy(other, other).wait_recv()

    def gain(index):
        at = EXPERTS + index
        return jnp.concatenate([small_out[z, at : at + 1, :rows] for z in range(count)], axis=1)

    inputs = tokens_ref[...].astype(jnp.float32)
    first_out[...] = (normalize(inputs)[0] * gain(0)).astype(jnp.bfloat16)
    advance(0, 0)
    line_start()
    line_send_group(1)
    for level in range(1, steps + 1):
        advance(level, 0)
        if level == 1:
            line_step(1)
    for other in others:
        for stream in streams:
            join_copy(0, stream, other).wait_recv()
    own_copies[0].wait()

    def whole(index):
        return weights_out[index].reshape(count * rows, width)

    project_inputs(first_out[...], whole, query_out, pair_out, table_ref)
    advance(0, 1)
    if count > 2:
        line_step(2)
    bias = allowed_pairs(column_ref[...], row_ref[...])
    quarter = KVHEADS // 4
    attend_forward(range(quarter), query_out, pair_out, bias, head_out, total_out)
    advance(1, 1)
    for step in range(3, count):
        line_step(step)
    attend_forward(range(quarter, KVHEADS), query_out, pair_out, bias, head_out, total_out)
    for level in range(2, steps + 1):
        advance(level, 1)
    middle = inputs + dot_nn(head_out[...], whole(2))
    middle_out[...] = middle
    second_out[...] = (normalize(middle)[0] * gain(1)).astype(jnp.bfloat16)
    for group in range(groups):
        for other in others:
            for stream in streams:
                join_copy(group, stream, other).wait_send()
                if group == 1:
                    join_copy(group, stream, other).wait_recv()
                line_copy(group, stream, me, other).wait_send()
                for step in range(steps):
                    grow_copy(step, group, stream, other).wait_send()
    for other in others:
        small_copy(me, other).wait_send()
    for block in range(count):

        @pl.when((block <= me) & (me < count - 1))
        def _():
            hand_on(block, True).wait_send()

        @pl.when((block >= me) & (me > 0))
        def _():
            hand_on(block, False).wait_send()

    own_copies[1].wait()


def gather(weights, moments, small, tokens, cotangent, tables, starts, bits, count):
    depth, rows, width = weights.shape
    token_count = tokens.shape[0]
    steps = len(bits)
    low = jnp.bfloat16
    vmem = pl.BlockSpec(memory_space=pltpu.VMEM)
    dma = pltpu.SemaphoreType.DMA
    whole = jax.ShapeDtypeStruct((depth, count, rows, width), low)
    features = jax.ShapeDtypeStruct((token_count, width), low)
    return pl.pallas_call(
        functools.partial(gather_kernel, count, bits),
        in_specs=[vmem] * 8,
        out_specs=[vmem] * 11,
        out_shape=[
            whole,
            whole,
            jax.ShapeDtypeStruct((count,) + small.shape, small.dtype),
            jax.ShapeDtypeStruct((count, token_count, width), low),
            jax.ShapeDtypeStruct((token_count, width), jnp.float32),
            features,
            features,
            features,
            features,
            features,
            jax.ShapeDtypeStruct((2 * token_count, KVHEADS), jnp.float32),
        ],
        scratch_shapes=[
            dma((2,)),
            dma((2, 2, count)),
            dma((2, 2, count)),
            dma((steps, 2, 2, count)),
            dma((steps, 2, 2, count)),
            dma((2, 2, count)),
            dma((2, 2, count)),
            dma((count,)),
            dma((count,)),
            dma((count,)),
            dma((count,)),
            dma((count,)),
        ],
        compiler_params=pltpu.CompilerParams(
            collective_id=3, has_side_effects=True, vmem_limit_bytes=56 * 1024 * 1024
        ),
        name="gather",
    )(weights, moments, small, tokens, cotangent, tables, starts[:, None], starts[None, :])


def local(
    tokens,
    sequence_start,
    routes,
    route_weights,
    cotangent,
    query_proj,
    key_proj,
    value_proj,
    out_proj,
    prenorm,
    midnorm,
    gate_proj,
    up_proj,
    down_proj,
    query_moment,
    key_moment,
    value_moment,
    out_moment,
    prenorm_moment,
    midnorm_moment,
    gate_moment,
    up_moment,
    down_moment,
):
    shard_index = lax.axis_index("shard")
    rep_count = lax.axis_size("rep")
    shard_count = lax.axis_size("shard")
    row_block = query_proj.shape[0]
    bits = rep_bits(rep_count)
    experts_here = gate_proj.shape[0]
    low = jnp.bfloat16
    own_weights = jnp.stack(
        [query_proj, jnp.concatenate([key_proj, value_proj], axis=1), out_proj]
    )
    own_moments = jnp.stack(
        [
            query_moment.astype(low),
            jnp.concatenate([key_moment.astype(low), value_moment.astype(low)], axis=1),
            out_moment.astype(low),
        ]
    )
    dense_weights = jnp.sum(
        jnp.where(
            routes.T[None, :, :] == jnp.arange(EXPERTS, dtype=jnp.int32)[:, None, None],
            route_weights.T[None, :, :],
            0.0,
        ),
        axis=1,
    )
    gain_rows = jnp.pad(
        jnp.stack([prenorm, midnorm]).astype(jnp.float32),
        ((0, 6), (0, tokens.shape[0] - row_block)),
    )
    tables = rotary_tables(jnp.arange(tokens.shape[0], dtype=jnp.int32) - sequence_start)
    (
        weights,
        moments,
        small,
        cotangent_all,
        middle,
        normed_first,
        normed_second,
        query,
        pair,
        head_low,
        log_total,
    ) = gather(
        own_weights,
        own_moments,
        jnp.concatenate([dense_weights, gain_rows], axis=0),
        tokens,
        cotangent,
        tables,
        sequence_start,
        bits,
        shard_count,
    )
    expert_weights = lax.dynamic_slice_in_dim(
        small, shard_index * experts_here, experts_here, 1
    ).transpose(0, 2, 1)
    mixed, grad_second, expert_share = moe(
        normed_second,
        middle,
        cotangent_all,
        expert_weights,
        gate_proj,
        up_proj,
        down_proj,
        bits,
        shard_count,
    )
    expert_grads, dense_grads, gains_grad, grad_tokens = spread(
        expert_share,
        normed_first,
        head_low,
        weights,
        small,
        tokens,
        cotangent,
        grad_second,
        middle,
        query,
        pair,
        log_total,
        tables,
        sequence_start,
        bits=bits,
        count=shard_count,
    )
    gains_here = lax.dynamic_slice_in_dim(gains_grad, shard_index * row_block, row_block, 1)
    prenorm_grad = gains_here[0]
    midnorm_grad = gains_here[1]
    prenorm_next = momentum_keep * prenorm_moment + prenorm_grad
    midnorm_next = momentum_keep * midnorm_moment + midnorm_grad
    prenorm_update = -rate_gain * prenorm_next
    midnorm_update = -rate_gain * midnorm_next
    (
        query_grad,
        query_next,
        query_update,
        key_grad,
        key_next,
        key_update,
        value_grad,
        value_next,
        value_update,
        out_grad,
        out_next,
        out_update,
    ) = dense_update(
        dense_grads,
        moments,
        (query_moment, key_moment, value_moment, out_moment),
        LAYOUT,
        shard_index,
    )
    gate_grad, gate_next, gate_update, up_grad, up_next, up_update = expert_update(
        expert_grads, (0, 1), (gate_moment, up_moment)
    )
    down_grad, down_next, down_update = expert_update(expert_grads, (2,), (down_moment,))
    return (
        mixed,
        grad_tokens,
        query_grad,
        query_next,
        query_update,
        key_grad,
        key_next,
        key_update,
        value_grad,
        value_next,
        value_update,
        out_grad,
        out_next,
        out_update,
        prenorm_grad,
        prenorm_next,
        prenorm_update,
        midnorm_grad,
        midnorm_next,
        midnorm_update,
        gate_grad,
        gate_next,
        gate_update,
        up_grad,
        up_next,
        up_update,
        down_grad,
        down_next,
        down_update,
    )


def solution(mesh):
    return jax.shard_map(
        local,
        mesh=mesh,
        in_specs=(
            P(("rep", "shard"), None),
            P(("rep", "shard")),
            P(("rep", "shard"), None),
            P(("rep", "shard"), None),
            P(("rep", "shard"), None),
            P("shard", None),
            P("shard", None),
            P("shard", None),
            P("shard", None),
            P("shard"),
            P("shard"),
            P("shard", None, None),
            P("shard", None, None),
            P("shard", None, None),
            P("shard", None),
            P("shard", None),
            P("shard", None),
            P("shard", None),
            P("shard"),
            P("shard"),
            P("shard", None, None),
            P("shard", None, None),
            P("shard", None, None),
        ),
        out_specs=(
            P(("rep", "shard"), None),
            P(("rep", "shard"), None),
            P("shard", None),
            P("shard", None),
            P("shard", None),
            P("shard", None),
            P("shard", None),
            P("shard", None),
            P("shard", None),
            P("shard", None),
            P("shard", None),
            P("shard", None),
            P("shard", None),
            P("shard", None),
            P("shard"),
            P("shard"),
            P("shard"),
            P("shard"),
            P("shard"),
            P("shard"),
            P("shard", None, None),
            P("shard", None, None),
            P("shard", None, None),
            P("shard", None, None),
            P("shard", None, None),
            P("shard", None, None),
            P("shard", None, None),
            P("shard", None, None),
            P("shard", None, None),
        ),
        check_vma=False,
    )
```

```python
import functools
import math

import jax
import jax.numpy as jnp
from jax import lax
from jax.experimental import pallas as pl
from jax.experimental.pallas import tpu as pltpu
from jax.sharding import PartitionSpec as P

NHEADS = 16
KVHEADS = 8
HEAD = 64
EXPERTS = 16
NS_ITERS = 2


norm_epsilon = 1e-06
rotary_base = 10000.0
momentum_keep = 0.9
rate_matrix = 0.5
rate_gain = 0.0002
newton_first = 3.4445
newton_second = -4.775
newton_third = 2.0315
masked_score = -1e30


def normalize(values):
    inverse = lax.rsqrt(jnp.mean(values * values, axis=-1, keepdims=True) + norm_epsilon)
    return (values * inverse, inverse)


def normalize_back(grad_normed, scaling, scaled, inverse):
    grad_scaled = grad_normed * scaling
    inner_mean = jnp.mean(grad_scaled * scaled, axis=-1, keepdims=True)
    return (
        inverse * (grad_scaled - scaled * inner_mean),
        jnp.sum(grad_normed * scaled, axis=0, keepdims=True),
    )


def dot_nn(left, right):
    return jnp.dot(left, right, preferred_element_type=jnp.float32)


def dot_nt(left, right):
    return lax.dot_general(
        left, right, (((1,), (1,)), ((), ())), preferred_element_type=jnp.float32
    )


def dot_tn(left, right):
    return lax.dot_general(
        left, right, (((0,), (0,)), ((), ())), preferred_element_type=jnp.float32
    )


def rotate(values, table_ref, sign):
    return (
        values * table_ref[0]
        + sign * pltpu.roll(values, 96, 1) * table_ref[1]
        + sign * pltpu.roll(values, 32, 1) * table_ref[2]
    )


def lane_low(shape):
    return lax.broadcasted_iota(jnp.int32, shape, 1) < HEAD


def twice(pair, upper):
    wide = pair.astype(jnp.float32)
    turned = pltpu.roll(wide, HEAD, 1)
    first = lane_low(pair.shape)
    return jnp.where(first != upper, wide, turned).astype(pair.dtype)


def stacked(pair):
    first = lane_low(pair.shape)
    zero = jnp.zeros_like(pair)
    return jnp.concatenate([jnp.where(first, pair, zero), jnp.where(first, zero, pair)], axis=0)


def unstacked(rows):
    half = rows.shape[0] // 2
    return jnp.where(lane_low((half, rows.shape[1])), rows[:half], rows[half:])


def allowed_pairs(start_column, start_row):
    shape = (start_column.shape[0], start_row.shape[1])
    query_places = lax.broadcasted_iota(jnp.int32, shape, 0)
    key_places = lax.broadcasted_iota(jnp.int32, shape, 1)
    one = (start_column == start_row) & (key_places <= query_places)
    return jnp.where(jnp.concatenate([one, one], axis=0), 0.0, masked_score)


def block_lanes(ref, block):
    return ref[:, block * 2 * HEAD : (block + 1) * 2 * HEAD]


def attend_pair(block, query_ref, pair_ref, bias):
    key = twice(block_lanes(pair_ref, block // 2), block % 2 == 1)
    value = twice(block_lanes(pair_ref, KVHEADS // 2 + block // 2), block % 2 == 1)
    queries = stacked(block_lanes(query_ref, block))
    scores = dot_nt(queries, key) * (1.0 / math.sqrt(HEAD)) + bias
    return (queries, key, value, scores)


def project_inputs(normed, weights, query_ref, pair_ref, table_ref):
    queries = dot_nn(normed, weights(0))
    for block in range(NHEADS // 2):
        lanes = slice(block * 2 * HEAD, (block + 1) * 2 * HEAD)
        query_ref[:, lanes] = rotate(queries[:, lanes], table_ref, 1.0).astype(jnp.bfloat16)
    pairs = dot_nn(normed, weights(1))
    for block in range(KVHEADS):
        lanes = slice(block * 2 * HEAD, (block + 1) * 2 * HEAD)
        value = pairs[:, lanes]
        if block < KVHEADS // 2:
            value = rotate(value, table_ref, 1.0)
        pair_ref[:, lanes] = value.astype(jnp.bfloat16)


def attend_forward(blocks, query_ref, pair_ref, bias, head_ref, total_ref):
    for block in blocks:
        _, _, value, scores = attend_pair(block, query_ref, pair_ref, bias)
        row_max = jnp.max(scores, axis=-1, keepdims=True)
        exponents = jnp.exp(scores - row_max)
        totals = jnp.sum(exponents, axis=-1, keepdims=True)
        softmax_low = (exponents * (1.0 / totals)).astype(jnp.bfloat16)
        head_ref[:, block * 2 * HEAD : (block + 1) * 2 * HEAD] = unstacked(
            dot_nn(softmax_low, value)
        ).astype(jnp.bfloat16)
        total_ref[:, block : block + 1] = row_max + jnp.log(totals)


def attend_backward(query_ref, pair_ref, bias, total_ref, grad_ref, table_ref, delta_ref):
    folded = []
    for block in range(KVHEADS):
        queries, key, value, scores = attend_pair(block, query_ref, pair_ref, bias)
        grads = stacked(block_lanes(grad_ref, block))
        softmax_full = jnp.exp(scores - total_ref[:, block : block + 1])
        grad_softmax = dot_nt(grads, value)
        inner = jnp.sum(softmax_full * grad_softmax, axis=-1, keepdims=True)
        grad_scores = (softmax_full * (grad_softmax - inner)).astype(jnp.bfloat16)
        scale = 1.0 / math.sqrt(HEAD)
        grad_query = unstacked(dot_nn(grad_scores, key)) * scale
        lanes = slice(block * 2 * HEAD, (block + 1) * 2 * HEAD)
        delta_ref[:, lanes] = rotate(grad_query, table_ref, -1.0).astype(jnp.bfloat16)
        grad_key = dot_tn(grad_scores, queries) * scale
        grad_value = dot_tn(softmax_full.astype(jnp.bfloat16), grads)
        folded.append(
            (
                grad_key + pltpu.roll(grad_key, HEAD, 1),
                grad_value + pltpu.roll(grad_value, HEAD, 1),
            )
        )
        if block % 2 == 1:
            first = lane_low(grad_key.shape)
            both = [jnp.where(first, low, high) for low, high in zip(*folded)]
            folded = []
            base = NHEADS * HEAD + (block // 2) * 2 * HEAD
            delta_ref[:, base : base + 2 * HEAD] = rotate(both[0], table_ref, -1.0).astype(
                jnp.bfloat16
            )
            base = base + KVHEADS * HEAD
            delta_ref[:, base : base + 2 * HEAD] = both[1].astype(jnp.bfloat16)


def rotary_tables(positions):
    half_size = HEAD // 2
    frequency = rotary_base ** (-(jnp.arange(half_size, dtype=jnp.float32) * 2.0) / HEAD)
    angles = positions.astype(jnp.float32)[:, None] * frequency[None, :]
    cosine, sine = (jnp.cos(angles), jnp.sin(angles))
    zero = jnp.zeros_like(sine)
    return jnp.stack(
        [
            jnp.concatenate([cosine] * 4, axis=1),
            jnp.concatenate([-sine, zero] * 2, axis=1),
            jnp.concatenate([zero, sine] * 2, axis=1),
        ]
    )


def newton_parts(grams):
    a, b, c = newton_first, newton_second, newton_third

    def times(left, right):
        return jnp.dot(left, right, preferred_element_type=jnp.float32)

    lows = [gram.astype(jnp.bfloat16) for gram in grams]
    firsts = [b * gram + c * times(low, low) for gram, low in zip(grams, lows)]
    first_lows = [first.astype(jnp.bfloat16) for first in firsts]
    mixes = [times(low, first) for low, first in zip(lows, first_lows)]
    nexts = [
        (a * a) * gram + (2.0 * a) * mix + times(mix.astype(jnp.bfloat16), first)
        for gram, mix, first in zip(grams, mixes, first_lows)
    ]
    next_lows = [gram.astype(jnp.bfloat16) for gram in nexts]
    seconds = [b * gram + c * times(low, low) for gram, low in zip(nexts, next_lows)]
    second_lows = [second.astype(jnp.bfloat16) for second in seconds]
    return list(zip(firsts, first_lows, seconds, second_lows))


def scaled_gram(gram):
    shape = gram.shape
    rows = lax.broadcasted_iota(jnp.int32, shape, 0)
    diagonal = rows == lax.broadcasted_iota(jnp.int32, shape, 1)
    inverse = 1.0 / (jnp.sqrt(jnp.sum(jnp.where(diagonal, gram, 0.0))) + 1e-07)
    return (gram * (inverse * inverse), inverse)


def expert_update_kernel(kinds, scale, *refs):
    a = newton_first
    grads_ref = refs[0]
    moments = refs[1 : 1 + len(kinds)]
    outs = refs[1 + len(kinds) :]
    half = grads_ref.shape[3]
    tall = kinds[0] < 2
    states = []
    for index in range(len(kinds)):
        for e in range(grads_ref.shape[0]):
            grad = grads_ref[e, index].astype(jnp.float32)
            if not tall:
                grad = jnp.concatenate([grad[:half], grad[half:]], axis=1)
            moment = momentum_keep * moments[index][e] + grad
            outs[3 * index][e] = grad
            outs[3 * index + 1][e] = moment
            low = moment.astype(jnp.bfloat16)
            sides = (((0,), (0,)), ((), ())) if tall else (((1,), (1,)), ((), ()))
            gram, inverse = scaled_gram(
                lax.dot_general(low, low, sides, preferred_element_type=jnp.float32)
            )
            states.append((index, e, inverse, low, gram))
    parts = newton_parts([state[-1] for state in states])
    for (index, e, inverse, low, _), (first, first_low, second, second_low) in zip(states, parts):
        rest = a * (first + second) + jnp.dot(
            first_low, second_low, preferred_element_type=jnp.float32
        )
        rest = ((-scale * inverse) * rest).astype(jnp.bfloat16)
        if tall:
            step = jnp.dot(low, rest, preferred_element_type=jnp.float32)
        else:
            step = jnp.dot(rest, low, preferred_element_type=jnp.float32)
        outs[3 * index + 2][e] = (-scale * a * a * inverse) * outs[3 * index + 1][e] + step


def expert_update(grads, kinds, moments):
    count, rows, columns = moments[0].shape
    group = 2 // len(kinds)
    scale = rate_matrix * math.sqrt(max(1.0, columns / rows))
    block = pl.BlockSpec((group, rows, columns), lambda i: (i, 0, 0))
    place = kinds[0] // len(kinds)
    taken = pl.BlockSpec((group, len(kinds)) + grads.shape[2:], lambda i: (i, place, 0, 0))
    shape = jax.ShapeDtypeStruct(moments[0].shape, jnp.float32)
    return pl.pallas_call(
        functools.partial(expert_update_kernel, kinds, scale),
        grid=(count // group,),
        in_specs=[taken] + [block] * len(kinds),
        out_specs=[block] * (3 * len(kinds)),
        out_shape=[shape] * (3 * len(kinds)),
        compiler_params=pltpu.CompilerParams(vmem_limit_bytes=60 * 1024 * 1024),
        name="expert_update",
        cost_estimate=pl.CostEstimate(
            flops=count * len(kinds) * 2500000000,
            bytes_accessed=moments[0].size * len(kinds) * 18,
            transcendentals=0,
        ),
    )(grads, *moments)


def dense_update_kernel(layout, place_ref, grads_ref, moments_ref, *refs):
    a = newton_first
    amount = len(layout)
    own_moments = refs[:amount]
    outs = refs[amount : 3 * amount]
    updates = refs[3 * amount : 3 * amount + 2]
    matrices = refs[3 * amount + 2 : 3 * amount + 4]
    own_grads = refs[3 * amount + 4]
    blocks, count, block_rows, width = grads_ref.shape
    part = width // 3
    me = place_ref[0]
    core = place_ref[1]
    start = pl.multiple_of(me * block_rows, block_rows)

    def momentum(moments, grads):
        return (
            (momentum_keep * moments.astype(jnp.float32) + grads.astype(jnp.float32))
            .astype(jnp.bfloat16)
            .reshape(count * block_rows, part)
        )

    for block in range(blocks):
        outer = slice(block * part, (block + 1) * part)
        lanes = pl.ds(pl.multiple_of(2 * core * part, part), part)
        matrices[0][:, outer] = momentum(
            moments_ref[2 * core, :, :, outer], grads_ref[block, :, :, lanes]
        )
        for index in range(3):
            columns = slice(8 * part * index + block * part, 8 * part * index + (block + 1) * part)
            inner = slice(index * part, (index + 1) * part)
            own_grads[:, columns] = grads_ref[block, me, :, inner].astype(jnp.float32)
    for block in range(blocks // 2):
        outer = slice(block * part, (block + 1) * part)
        lanes = pl.ds(pl.multiple_of((core * (blocks // 2) + block) * part, part), part)
        matrices[1][:, outer] = momentum(
            moments_ref[1, :, :, lanes],
            grads_ref[core * (blocks // 2) + block, :, :, part : 2 * part],
        )
    for index, (begin, size) in enumerate(layout):
        grad = own_grads[:, begin : begin + size]
        outs[2 * index][...] = grad
        outs[2 * index + 1][...] = momentum_keep * own_moments[index][...] + grad
    states = []
    for matrix in matrices:
        low = matrix[...]
        states.append(
            scaled_gram(
                lax.dot_general(
                    low, low, (((0,), (0,)), ((), ())), preferred_element_type=jnp.float32
                )
            )
        )
    parts = newton_parts([state[0] for state in states])
    for matrix, update, (_, inverse), (_, first_low, _, second_low) in zip(
        matrices, updates, states, parts
    ):
        rows, columns = matrix.shape
        scale = rate_matrix * math.sqrt(max(1.0, columns / rows))
        own = matrix[pl.ds(start, block_rows)]
        once = a * own.astype(jnp.float32) + jnp.dot(
            own, first_low, preferred_element_type=jnp.float32
        )
        update[...] = (-scale * inverse) * (
            a * once
            + jnp.dot(once.astype(jnp.bfloat16), second_low, preferred_element_type=jnp.float32)
        )


def dense_update(grads, moments, own_moments, layout, shard_index, rep_index):
    _, count, block_rows, width = moments.shape
    whole = lambda shape: pl.BlockSpec(shape, lambda i: (0,) * len(shape))
    shapes = []
    for _, size in layout:
        shapes += [jax.ShapeDtypeStruct((block_rows, size), jnp.float32)] * 2
    shapes += [
        jax.ShapeDtypeStruct((block_rows, width), jnp.float32),
        jax.ShapeDtypeStruct((block_rows, width // 2), jnp.float32),
    ]
    place = jnp.stack([shard_index, rep_index % 2]).astype(jnp.int32)
    return pl.pallas_call(
        functools.partial(dense_update_kernel, layout),
        grid=(1,),
        in_specs=[pl.BlockSpec(memory_space=pltpu.SMEM), whole(grads.shape), whole(moments.shape)]
        + [whole(moment.shape) for moment in own_moments],
        out_specs=[whole(shape.shape) for shape in shapes],
        out_shape=shapes,
        scratch_shapes=[
            pltpu.VMEM((count * block_rows, width), jnp.bfloat16),
            pltpu.VMEM((count * block_rows, width // 2), jnp.bfloat16),
            pltpu.VMEM((block_rows, 3 * width), jnp.float32),
        ],
        compiler_params=pltpu.CompilerParams(vmem_limit_bytes=63 * 1024 * 1024),
        name="dense_update",
        cost_estimate=pl.CostEstimate(
            flops=14000000000, bytes_accessed=24 * width * width, transcendentals=0
        ),
    )(place, grads, moments, *own_moments)


LAYOUT = ((0, 1024), (1024, 512), (1536, 512), (2048, 1024))


MESH = pl.DeviceIdType.MESH


def flip(index, bit):
    return index + bit - 2 * bit * ((index // bit) % 2)


def greet(peers):
    barrier = pltpu.get_barrier_semaphore()
    for peer in peers:
        pl.semaphore_signal(barrier, inc=1, device_id=peer, device_id_type=MESH)
    pl.semaphore_wait(barrier, len(peers))


def stream_plan(rep, bits, base, size):
    stages = []
    starts = [base, base + size]
    for step in range(len(bits)):
        size = size // 2
        stage = []
        for stream in range(2):
            bit = bits[(step + stream) % len(bits)]
            side = (rep // bit) % 2
            keep = starts[stream] + side * size
            send = starts[stream] + (1 - side) * size
            starts[stream] = keep
            stage.append((bit, stream, keep, send, size))
        stages.append(stage)
    return stages


def rows_of(start, size):
    return pl.ds(pl.multiple_of(start, 16), size)


def moe_kernel(
    count,
    bits,
    own_ref,
    middle_ref,
    cot_ref,
    weight_ref,
    gate_hbm,
    up_hbm,
    down_hbm,
    out_ref,
    back_ref,
    share_ref,
    tok,
    turned,
    mats,
    hid,
    gate_delta,
    up_delta,
    stage_back,
    stage_out,
    got_back,
    got_out,
    *rest,
):
    landing = rest[: 1 + 2 * len(bits)]
    (
        load_sem,
        right_sem,
        left_sem,
        arrive_sem,
        back_send,
        back_recv,
        out_send,
        out_recv,
        sum_send,
        sum_recv,
    ) = rest[1 + 2 * len(bits) :]
    rep = lax.axis_index("rep")
    me = lax.axis_index("shard")
    experts = mats.shape[0]
    tokens = own_ref.shape[0]
    half = mats.shape[2] // 2
    core = rep % 2

    loads = [
        pltpu.make_async_copy(gate_hbm, mats.at[:, 0], load_sem.at[0]),
        pltpu.make_async_copy(up_hbm, mats.at[:, 1], load_sem.at[1]),
        pltpu.make_async_copy(
            down_hbm.at[:, :, pl.ds(0, half)], mats.at[:, 2, pl.ds(0, half)], load_sem.at[2]
        ),
        pltpu.make_async_copy(
            down_hbm.at[:, :, pl.ds(half, half)], mats.at[:, 2, pl.ds(half, half)], load_sem.at[3]
        ),
    ]
    for load in loads:
        load.start()
    peers = [(rep, lax.rem(me + k, count)) for k in range(1, count)]
    peers += [(flip(rep, bit), me) for bit in (1,) + bits]
    greet(peers)

    right_peer = (rep, jnp.minimum(me + 1, count - 1))
    left_peer = (rep, jnp.maximum(me - 1, 0))

    def hand_on(block, to_right):
        return pltpu.make_async_remote_copy(
            src_ref=tok.at[block],
            dst_ref=tok.at[block],
            send_sem=(right_sem if to_right else left_sem).at[block],
            recv_sem=arrive_sem.at[block],
            device_id=right_peer if to_right else left_peer,
            device_id_type=MESH,
        )

    def returning(stage, got, send_sem, recv_sem, block):
        return pltpu.make_async_remote_copy(
            src_ref=stage.at[block],
            dst_ref=got.at[me],
            send_sem=send_sem.at[block],
            recv_sem=recv_sem.at[me],
            device_id=(rep, block),
            device_id_type=MESH,
        )

    tok[me] = own_ref[...]

    @pl.when(me < count - 1)
    def _():
        hand_on(me, True).start()

    @pl.when(me > 0)
    def _():
        hand_on(me, False).start()

    for load in loads:
        load.wait()

    margin = jnp.minimum(me, count - 1 - me)
    longer = jnp.where(me < count - 1 - me, 1, -1)
    inward = jnp.where(2 * me < count, 1, -1)
    nt = (((1,), (1,)), ((), ()))

    def dot(left, right):
        return jnp.dot(left, right, preferred_element_type=jnp.float32)

    def dot_nt(left, right):
        return lax.dot_general(left, right, nt, preferred_element_type=jnp.float32)

    def visit(j, carry):
        lower = me - j
        upper = me + j

        @pl.when((j > 0) & (lower >= 0))
        def _():
            hand_on(jnp.maximum(lower, 0), True).wait_recv()

            @pl.when(me < count - 1)
            def _():
                hand_on(jnp.maximum(lower, 0), True).start()

        @pl.when((j > 0) & (upper < count))
        def _():
            hand_on(jnp.minimum(upper, count - 1), False).wait_recv()

            @pl.when(me > 0)
            def _():
                hand_on(jnp.minimum(upper, count - 1), False).start()

        near = (j + 1) // 2
        alternating = me + near - 2 * near * (j % 2)
        block = jnp.where(j <= 2 * margin, alternating, me + longer * (j - margin))
        places = pl.ds(pl.multiple_of(block * tokens, tokens), tokens)
        rows = tok[block]
        grads = cot_ref[block]
        turned[:, places] = rows.T
        hiddens = []
        for e in range(experts):
            weight = weight_ref[block, :, e : e + 1]
            u = dot(rows, mats[e, 0])
            w = dot(rows, mats[e, 1])
            gate = 1.0 / (1.0 + jnp.exp(-u))
            act = u * gate
            hidden = (weight * (act * w)).astype(jnp.bfloat16)
            hid[e, :, places] = hidden.T
            hiddens.append(hidden)
            pulled = weight * (
                dot_nt(grads[:, :half], mats[e, 2, :half])
                + dot_nt(grads[:, half:], mats[e, 2, half:])
            )
            gate_delta[e, places] = (pulled * w * (gate + act * (1.0 - gate))).astype(jnp.bfloat16)
            up_delta[e, places] = (pulled * act).astype(jnp.bfloat16)
        for side in range(2):
            part = slice(side * half, (side + 1) * half)
            total_back = None
            total_out = None
            for e in range(experts):
                back = dot_nt(gate_delta[e, places], mats[e, 0, part]) + dot_nt(
                    up_delta[e, places], mats[e, 1, part]
                )
                out = dot(hiddens[e], mats[e, 2, part])
                total_back = back if e == 0 else total_back + back
                total_out = out if e == 0 else total_out + out
            stage_back[block, :, part] = total_back.astype(jnp.bfloat16)
            stage_out[block, :, part] = total_out.astype(jnp.bfloat16)

        @pl.when((j > 0) & ((block - me) * inward > 0))
        def _():
            returning(stage_back, got_back, back_send, back_recv, block).start()

        return carry

    lax.fori_loop(0, count, visit, 0)
    for block in range(count):

        @pl.when((block - me) * inward < 0)
        def _():
            returning(stage_back, got_back, back_send, back_recv, block).start()

    for k in range(1, count):
        returning(stage_out, got_out, out_send, out_recv, lax.rem(me + k, count)).start()

    plan = stream_plan(rep, bits, core * half, half // 2)

    def sum_copy(stage, slot, e, start, size, bit):
        return pltpu.make_async_remote_copy(
            src_ref=mats.at[e, :, rows_of(start, size)],
            dst_ref=landing[slot].at[e],
            send_sem=sum_send.at[slot, e],
            recv_sem=sum_recv.at[slot, e],
            device_id=(flip(rep, bit), me),
            device_id_type=MESH,
        )

    def copies(stage, e):
        if stage == 0:
            return [(sum_copy(0, 0, e, (1 - core) * half, half, 1), 0, core * half, half)]
        return [
            (
                sum_copy(stage, 1 + 2 * (stage - 1) + stream, e, send, size, bit),
                1 + 2 * (stage - 1) + stream,
                keep,
                size,
            )
            for bit, stream, keep, send, size in plan[stage - 1]
        ]

    def finish(stage, e):
        for copy, slot, keep, size in copies(stage, e):
            copy.wait_recv()
            place = rows_of(keep, size)
            for kind in range(3):
                mats[e, kind, place] = (
                    mats[e, kind, place].astype(jnp.float32)
                    + landing[slot][e, kind].astype(jnp.float32)
                ).astype(jnp.bfloat16)

    stages = 1 + len(bits)
    for turn in range(experts + stages):
        if turn < experts:
            e = turn
            for side in range(2):
                part = slice(side * half, (side + 1) * half)
                mats[e, 0, part] = dot(turned[part], gate_delta[e]).astype(jnp.bfloat16)
                mats[e, 1, part] = dot(turned[part], up_delta[e]).astype(jnp.bfloat16)
                mats[e, 2, part] = dot(hid[e], cot_ref[:, :, part].reshape(count * tokens, half)).astype(jnp.bfloat16)
            copies(0, e)[0][0].start()
        for stage in range(stages):
            e = turn - 1 - stage
            if 0 <= e < experts:
                finish(stage, e)
                if stage + 1 < stages:
                    for copy, _, _, _ in copies(stage + 1, e):
                        copy.start()
                else:
                    for _, stream, keep, _, size in plan[-1]:
                        share_ref[e, :, stream] = mats[e, :, rows_of(keep, size)]

    total = stage_back[me].astype(jnp.float32)
    for k in range(1, count):
        source = lax.rem(me + k, count)
        pltpu.make_async_remote_copy(
            src_ref=stage_back.at[source],
            dst_ref=got_back.at[source],
            send_sem=back_send.at[source],
            recv_sem=back_recv.at[source],
            device_id=(rep, source),
            device_id_type=MESH,
        ).wait_recv()
        total = total + got_back[source].astype(jnp.float32)
    back_ref[...] = total
    total = stage_out[me].astype(jnp.float32)
    for k in range(1, count):
        source = lax.rem(me + k, count)
        pltpu.make_async_remote_copy(
            src_ref=stage_out.at[source],
            dst_ref=got_out.at[source],
            send_sem=out_send.at[source],
            recv_sem=out_recv.at[source],
            device_id=(rep, source),
            device_id_type=MESH,
        ).wait_recv()
        total = total + got_out[source].astype(jnp.float32)
    out_ref[...] = (middle_ref[...] + total).astype(out_ref.dtype)

    for k in range(1, count):
        block = lax.rem(me + k, count)
        returning(stage_back, got_back, back_send, back_recv, block).wait_send()
        returning(stage_out, got_out, out_send, out_recv, block).wait_send()
    for e in range(experts):
        for stage in range(stages):
            for copy, _, _, _ in copies(stage, e):
                copy.wait_send()
    for block in range(count):

        @pl.when((block <= me) & (me < count - 1))
        def _():
            hand_on(block, True).wait_send()

        @pl.when((block >= me) & (me > 0))
        def _():
            hand_on(block, False).wait_send()


def moe(normed, middle, cotangents, weights, gate_proj, up_proj, down_proj, bits, count):
    tokens, width = normed.shape
    experts, _, hidden = gate_proj.shape
    half = width // 2
    low = jnp.bfloat16
    final = (half // 2) >> len(bits)
    vmem = pl.BlockSpec(memory_space=pltpu.VMEM)
    anywhere = pl.BlockSpec(memory_space=pl.ANY)
    landings = [pltpu.VMEM((experts, 3, half, hidden), low)]
    for step in range(len(bits)):
        size = (half // 2) >> (step + 1)
        landings += [pltpu.VMEM((experts, 3, size, hidden), low)] * 2
    slots = len(landings)
    dma = pltpu.SemaphoreType.DMA
    return pl.pallas_call(
        functools.partial(moe_kernel, count, bits),
        in_specs=[vmem, vmem, vmem, vmem, anywhere, anywhere, anywhere],
        out_specs=[vmem, vmem, vmem],
        out_shape=[
            jax.ShapeDtypeStruct((tokens, width), low),
            jax.ShapeDtypeStruct((tokens, width), jnp.float32),
            jax.ShapeDtypeStruct((experts, 3, 2, final, hidden), low),
        ],
        scratch_shapes=[
            pltpu.VMEM((count, tokens, width), low),
            pltpu.VMEM((width, count * tokens), low),
            pltpu.VMEM((experts, 3, width, hidden), low),
            pltpu.VMEM((experts, hidden, count * tokens), low),
            pltpu.VMEM((experts, count * tokens, hidden), low),
            pltpu.VMEM((experts, count * tokens, hidden), low),
            pltpu.VMEM((count, tokens, width), low),
            pltpu.VMEM((count, tokens, width), low),
            pltpu.VMEM((count, tokens, width), low),
            pltpu.VMEM((count, tokens, width), low),
        ]
        + landings
        + [
            dma((4,)),
            dma((count,)),
            dma((count,)),
            dma((count,)),
            dma((count,)),
            dma((count,)),
            dma((count,)),
            dma((count,)),
            dma((slots, experts)),
            dma((slots, experts)),
        ],
        compiler_params=pltpu.CompilerParams(
            collective_id=1, has_side_effects=True, vmem_limit_bytes=63 * 1024 * 1024
        ),
        name="moe",
        cost_estimate=pl.CostEstimate(
            flops=39000000000, bytes_accessed=20000000, transcendentals=2000000
        ),
    )(normed, middle, cotangents, weights, gate_proj, up_proj, down_proj)


def rep_bits(rep_count):
    bits = []
    bit = 2
    while bit < rep_count:
        bits.append(bit)
        bit = bit * 2
    return tuple(bits)


def spread_kernel(
    count,
    bits,
    share_ref,
    normed_ref,
    head_ref,
    weights_ref,
    small_ref,
    tokens_ref,
    cot_ref,
    second_ref,
    middle_ref,
    query_ref,
    pair_ref,
    total_ref,
    table_ref,
    column_ref,
    row_ref,
    experts_hbm,
    dense_out,
    gains_out,
    tokens_out,
    experts_out,
    delta_ref,
    branch_ref,
    heads_ref,
    dense_ref,
    total,
    land_core,
    land_first,
    *rest,
):
    later = len(bits) - 1
    land_later = rest[:later]
    (
        piece_send,
        piece_land,
        piece,
        gains_send,
        gains_land,
        gains_all,
        local_sem,
        core_send,
        core_recv,
        half_send,
        half_recv,
        shard_send,
        shard_recv,
        grow_send,
        grow_recv,
        line_send,
        line_recv,
        join_send,
        join_recv,
        expert_send,
        expert_recv,
        gain_send,
        gain_recv,
        gain_line_send,
        gain_line_recv,
    ) = rest[later:]
    rep = lax.axis_index("rep")
    me = lax.axis_index("shard")
    core = rep % 2
    rows = dense_ref.shape[2]
    expert_rows = experts_out.shape[2]
    steps = len(bits)
    streams = range(2)

    def remote(source, target, send_sem, recv_sem, peer):
        return pltpu.make_async_remote_copy(
            src_ref=source,
            dst_ref=target,
            send_sem=send_sem,
            recv_sem=recv_sem,
            device_id=peer,
            device_id_type=MESH,
        )

    def across(bit):
        return (flip(rep, bit), me)

    def order(stream):
        return [bits[(step + stream) % steps] for step in range(steps)]

    def side(bit):
        return (rep // bit) % 2

    plan = stream_plan(rep, bits, core * (expert_rows // 2), expert_rows // 4)
    base = [(core * (expert_rows // 2)) + stream * (expert_rows // 4) for stream in streams]

    def expert_copy(level, stream):
        if level == steps:
            place = rows_of(base[stream], expert_rows // 4)
            peer = across(1)
        else:
            bit, _, keep, _, size = plan[steps - 1 - level][stream]
            place = rows_of(keep, size)
            peer = across(bit)
        source = experts_out.at[:, :, place]
        if level == 0:
            source = share_ref.at[:, :, stream]
        return remote(
            source,
            experts_out.at[:, :, place],
            expert_send.at[level, stream],
            expert_recv.at[level, stream],
            peer,
        )

    def own_copy(stream):
        _, _, keep, _, size = plan[-1][stream]
        return pltpu.make_async_copy(
            share_ref.at[:, :, stream],
            experts_out.at[:, :, rows_of(keep, size)],
            local_sem.at[stream],
        )

    for stream in streams:
        own_copy(stream).start()
    peers = [(rep, lax.rem(me + k, count)) for k in range(1, count)]
    peers += [across(bit) for bit in (1,) + bits]
    greet(peers)

    def core_copy(block):
        return remote(
            dense_ref.at[4 * (1 - core) + block],
            land_core.at[block],
            core_send.at[block],
            core_recv.at[block],
            across(1),
        )

    gain_bits = (1,) + bits

    def gain_copy(stage):
        return remote(
            gains_send.at[stage],
            gains_land.at[stage],
            gain_send.at[stage],
            gain_recv.at[stage],
            across(gain_bits[stage]),
        )

    for stream in streams:
        expert_copy(0, stream).start()

    def whole(index):
        return weights_ref[index].reshape(count * rows, -1)

    def gain(index):
        at = EXPERTS + index
        return jnp.concatenate([small_ref[z, at : at + 1, :rows] for z in range(count)], axis=1)

    scaled, inverse = normalize(middle_ref[...])
    middle_extra, midnorm_part = normalize_back(second_ref[...], gain(1), scaled, inverse)
    grad_middle = cot_ref[...].astype(jnp.float32) + middle_extra
    tokens_out[...] = grad_middle
    branch_ref[...] = grad_middle.astype(jnp.bfloat16)
    heads_ref[...] = dot_nt(branch_ref[...], whole(2)).astype(jnp.bfloat16)
    bias = allowed_pairs(column_ref[...], row_ref[...])
    attend_backward(query_ref, pair_ref, bias, total_ref, heads_ref, table_ref, delta_ref)

    part = dense_ref.shape[3] // 3
    normed_turned = normed_ref[...].T
    head_turned = head_ref[...].T

    def make_block(block):
        def columns(ref, offset):
            return ref[:, pl.ds(pl.multiple_of(offset + block * part, part), part)]

        pair = jnp.concatenate([columns(delta_ref, 0), columns(delta_ref, 8 * part)], axis=1)
        left = jnp.dot(normed_turned, pair, preferred_element_type=jnp.float32)
        right = jnp.dot(head_turned, columns(branch_ref, 0), preferred_element_type=jnp.float32)
        for line in range(count):
            place = slice(line * rows, (line + 1) * rows)
            dense_ref[block, line, :, : 2 * part] = left[place].astype(jnp.bfloat16)
            dense_ref[block, line, :, 2 * part :] = right[place].astype(jnp.bfloat16)

    for block in range(4):
        make_block(4 * (1 - core) + block)
        core_copy(block).start()
    for block in range(4):
        make_block(4 * core + block)

    def gain_step(stage):
        gain_copy(stage).wait_recv()
        gains_send[stage + 1] = gains_send[stage] + gains_land[stage]
        if stage + 1 < len(gain_bits):
            gain_copy(stage + 1).start()

    first = [side(order(stream)[0]) for stream in streams]
    held = [2 * stream + first[stream] for stream in streams]
    given = [2 * stream + 1 - first[stream] for stream in streams]

    def first_copy(stream):
        return remote(
            total.at[given[stream]],
            land_first.at[stream],
            half_send.at[0, stream],
            half_recv.at[0, stream],
            across(order(stream)[0]),
        )

    def add_core(block):
        for line in range(count):
            total[block, line] = (
                dense_ref[4 * core + block, line].astype(jnp.float32)
                + land_core[block, line].astype(jnp.float32)
            ).astype(jnp.bfloat16)

    for block in range(4):
        core_copy(block).wait_recv()
    for stream in streams:
        add_core(given[stream])
        first_copy(stream).start()
    for stream in streams:
        add_core(held[stream])
    grad_first = dot_nt(delta_ref[:, : NHEADS * HEAD], whole(0)) + dot_nt(
        delta_ref[:, NHEADS * HEAD :], whole(1)
    )
    scaled, inverse = normalize(tokens_ref[...].astype(jnp.float32))
    input_extra, prenorm_part = normalize_back(grad_first, gain(0), scaled, inverse)
    tokens_out[...] = tokens_out[...] + input_extra
    gains_send[0] = jnp.concatenate(
        [prenorm_part, midnorm_part, jnp.zeros((6, prenorm_part.shape[1]), jnp.float32)], axis=0
    )
    gain_copy(0).start()
    gain_step(0)

    starts = []
    for stream in streams:
        start, size, line = 0, rows, []
        for step in range(1, steps):
            size = size // 2
            near = side(order(stream)[step])
            line.append((start + near * size, start + (1 - near) * size, size))
            start = start + near * size
        starts.append((start, size, line))

    def later_copy(step, stream):
        keep, send, size = starts[stream][2][step - 1]
        return remote(
            total.at[held[stream], :, rows_of(send, size)],
            land_later[step - 1].at[stream],
            half_send.at[step, stream],
            half_recv.at[step, stream],
            across(order(stream)[step]),
        )

    for stream in streams:
        first_copy(stream).wait_recv()
        for line in range(count):
            total[held[stream], line] = (
                total[held[stream], line].astype(jnp.float32)
                + land_first[stream, line].astype(jnp.float32)
            ).astype(jnp.bfloat16)
        if steps > 1:
            later_copy(1, stream).start()
    gain_step(1)

    for step in range(1, steps):
        for stream in streams:
            later_copy(step, stream).wait_recv()
            keep, _, size = starts[stream][2][step - 1]
            for line in range(count):
                place = rows_of(keep, size)
                total[held[stream], line, place] = (
                    total[held[stream], line, place].astype(jnp.float32)
                    + land_later[step - 1][stream, line].astype(jnp.float32)
                ).astype(jnp.bfloat16)
            if step + 1 < steps:
                later_copy(step + 1, stream).start()
        gain_step(step + 1)

    for stream in streams:
        own_copy(stream).wait()
        expert_copy(0, stream).wait_recv()
        if steps > 1:
            expert_copy(1, stream).start()

    last = starts[0][1]
    places = [rows_of(starts[stream][0], last) for stream in streams]
    for stream in streams:
        for line in range(count):
            piece_send[line, stream] = total[held[stream], line, places[stream]]

    def shard_copy(k):
        target = lax.rem(me + k, count)
        return remote(
            piece_send.at[target],
            piece_land.at[me],
            shard_send.at[target],
            shard_recv.at[me],
            (rep, target),
        )

    def shard_arrival(source):
        return remote(
            piece_send.at[source],
            piece_land.at[source],
            shard_send.at[source],
            shard_recv.at[source],
            (rep, source),
        )

    def gain_line(k):
        target = lax.rem(me + k, count)
        return remote(
            gains_send.at[len(gain_bits)],
            gains_all.at[me],
            gain_line_send.at[target],
            gain_line_recv.at[me],
            (rep, target),
        )

    def gain_arrival(source):
        return remote(
            gains_send.at[len(gain_bits)],
            gains_all.at[source],
            gain_line_send.at[source],
            gain_line_recv.at[source],
            (rep, source),
        )

    for k in range(1, count):
        shard_copy(k).start()
        gain_line(k).start()
    summed = piece_send[me].astype(jnp.float32)
    for k in range(1, count):
        source = lax.rem(me + k, count)
        shard_arrival(source).wait_recv()
        summed = summed + piece_land[source].astype(jnp.float32)
    piece[...] = summed.astype(jnp.bfloat16)

    def line_copy(k, stream):
        target = lax.rem(me + k, count)
        return remote(
            piece.at[stream],
            dense_out.at[4 * core + held[stream], me, places[stream]],
            line_send.at[stream, target],
            line_recv.at[stream, me],
            (rep, target),
        )

    def line_arrival(source, stream):
        return remote(
            piece.at[stream],
            dense_out.at[4 * core + held[stream], source, places[stream]],
            line_send.at[stream, source],
            line_recv.at[stream, source],
            (rep, source),
        )

    def own_piece(stream):
        return pltpu.make_async_copy(
            piece.at[stream],
            dense_out.at[4 * core + held[stream], me, places[stream]],
            local_sem.at[2 + stream],
        )

    for stream in streams:
        own_piece(stream).start()
        for k in range(1, count):
            line_copy(k, stream).start()
    gained = gains_send[len(gain_bits)]
    for k in range(1, count):
        source = lax.rem(me + k, count)
        gain_arrival(source).wait_recv()
        gained = gained + gains_all[source]
    gains_out[...] = gained

    for level in range(1, steps):
        for stream in streams:
            expert_copy(level, stream).wait_recv()
            expert_copy(level + 1, stream).start()
    if steps == 1:
        for stream in streams:
            expert_copy(1, stream).start()

    def grow_copy(step, stream):
        if step == 0:
            place = dense_out.at[4 * core + held[stream]]
        else:
            keep, _, size = starts[stream][2][step - 1]
            place = dense_out.at[4 * core + held[stream], :, rows_of(keep, size)]
        return remote(
            place,
            place,
            grow_send.at[step, stream],
            grow_recv.at[step, stream],
            across(order(stream)[step]),
        )

    for stream in streams:
        own_piece(stream).wait()
        for k in range(1, count):
            line_arrival(lax.rem(me + k, count), stream).wait_recv()
        grow_copy(steps - 1, stream).start()
    for stream in streams:
        expert_copy(steps, stream).wait()
    leave = pltpu.make_async_copy(experts_out, experts_hbm, local_sem.at[0])
    leave.start()
    for step in reversed(range(steps)):
        for stream in streams:
            grow_copy(step, stream).wait_recv()
            if step > 0:
                grow_copy(step - 1, stream).start()

    def join_copy(stream):
        place = dense_out.at[pl.ds(4 * core + 2 * stream, 2)]
        return remote(place, place, join_send.at[stream], join_recv.at[stream], across(1))

    for stream in streams:
        join_copy(stream).start()
    for stream in streams:
        join_copy(stream).wait()
        for level in range(steps):
            expert_copy(level, stream).wait_send()
        first_copy(stream).wait_send()
        for step in range(1, steps):
            later_copy(step, stream).wait_send()
        for k in range(1, count):
            line_copy(k, stream).wait_send()
        for step in range(steps):
            grow_copy(step, stream).wait_send()
    for block in range(4):
        core_copy(block).wait_send()
    for stage in range(len(gain_bits)):
        gain_copy(stage).wait_send()
    for k in range(1, count):
        shard_copy(k).wait_send()
        gain_line(k).wait_send()
    leave.wait()


def spread(
    share, normed, head_low, weights, small, tokens, cotangent, second, middle, *rest, bits, count
):
    query, pair, log_total, tables, starts = rest
    experts, _, _, final, hidden = share.shape
    token_count, features = normed.shape
    rows = features // count
    width = 3 * features // 8
    dense_shape = (8, count, rows, width)
    gains_shape = (8, features)
    steps = len(bits)
    last = rows >> (steps - 1)
    low = jnp.bfloat16
    vmem = pl.BlockSpec(memory_space=pltpu.VMEM)
    dma = pltpu.SemaphoreType.DMA
    return pl.pallas_call(
        functools.partial(spread_kernel, count, bits),
        in_specs=[vmem] * 15,
        out_specs=[pl.BlockSpec(memory_space=pl.ANY)] + [vmem] * 3,
        out_shape=[
            jax.ShapeDtypeStruct((experts, 3, 4 * (final << steps), hidden), low),
            jax.ShapeDtypeStruct(dense_shape, low),
            jax.ShapeDtypeStruct(gains_shape, jnp.float32),
            jax.ShapeDtypeStruct((token_count, features), jnp.float32),
        ],
        scratch_shapes=[
            pltpu.VMEM((experts, 3, 4 * (final << steps), hidden), low),
            pltpu.VMEM((token_count, 2 * features), low),
            pltpu.VMEM((token_count, features), low),
            pltpu.VMEM((token_count, features), low),
            pltpu.VMEM(dense_shape, low),
            pltpu.VMEM((4, count, rows, width), low),
            pltpu.VMEM((4, count, rows, width), low),
            pltpu.VMEM((2, count, rows, width), low),
        ]
        + [pltpu.VMEM((2, count, rows >> step, width), low) for step in range(1, steps)]
        + [
            pltpu.VMEM((count, 2, last, width), low),
            pltpu.VMEM((count, 2, last, width), low),
            pltpu.VMEM((2, last, width), low),
            pltpu.VMEM((steps + 2,) + gains_shape, jnp.float32),
            pltpu.VMEM((steps + 1,) + gains_shape, jnp.float32),
            pltpu.VMEM((count,) + gains_shape, jnp.float32),
            dma((4,)),
            dma((4,)),
            dma((4,)),
            dma((steps, 2)),
            dma((steps, 2)),
            dma((count,)),
            dma((count,)),
            dma((steps, 2)),
            dma((steps, 2)),
            dma((2, count)),
            dma((2, count)),
            dma((2,)),
            dma((2,)),
            dma((steps + 1, 2)),
            dma((steps + 1, 2)),
            dma((steps + 1,)),
            dma((steps + 1,)),
            dma((count,)),
            dma((count,)),
        ],
        compiler_params=pltpu.CompilerParams(
            collective_id=2, has_side_effects=True, vmem_limit_bytes=63 * 1024 * 1024
        ),
        name="spread",
    )(
        share,
        normed,
        head_low,
        weights,
        small,
        tokens,
        cotangent,
        second,
        middle,
        query,
        pair,
        log_total,
        tables,
        starts[:, None],
        starts[None, :],
    )


def gather_kernel(
    count,
    bits,
    weights_ref,
    moments_ref,
    small_ref,
    tokens_ref,
    cot_ref,
    table_ref,
    column_ref,
    row_ref,
    weights_hbm,
    moments_out,
    small_out,
    cot_out,
    middle_out,
    first_out,
    second_out,
    query_out,
    pair_out,
    head_out,
    total_out,
    weights_out,
    local_sem,
    line_send,
    line_recv,
    grow_send,
    grow_recv,
    join_send,
    join_recv,
    small_send,
    small_recv,
    right_sem,
    left_sem,
    arrive_sem,
):
    rep = lax.axis_index("rep")
    me = lax.axis_index("shard")
    core = rep % 2
    steps = len(bits)
    streams = range(2)
    owns = (weights_ref, moments_ref)
    fulls = (weights_out, moments_out)
    rows, width = weights_ref.shape[1:]
    half = width // 2
    fine = half // 4
    groups = 2
    others = [lax.rem(me + k, count) for k in range(1, count)]

    def columns_of(start, size):
        return pl.ds(pl.multiple_of(start, 128), size)

    def order(stream):
        return [bits[(step + stream) % steps] for step in range(steps)]

    def side(bit):
        return (rep // bit) % 2

    own_copies = [
        pltpu.make_async_copy(weights_ref, weights_out.at[:, me], local_sem.at[0]),
        pltpu.make_async_copy(moments_ref, moments_out.at[:, me], local_sem.at[1]),
    ]
    for own_copy in own_copies:
        own_copy.start()
    small_out[me] = small_ref[...]
    cot_out[me] = cot_ref[...]
    peers = [(rep, other) for other in others]
    peers += [(flip(rep, bit), me) for bit in (1,) + bits]
    greet(peers)

    regions = []
    for stream in streams:
        column = core * half + stream * 2 * fine
        narrow = columns_of(column + side(order(stream)[0]) * fine, fine)
        start, size = 0, rows
        held = [(pl.ds(0, rows), narrow)]
        for step in range(1, steps):
            size = size // 2
            start = start + side(order(stream)[step]) * size
            held.append((rows_of(start, size), narrow))
        regions.append((held, columns_of(column, 2 * fine)))

    def remote(source, target, send_sem, recv_sem, peer):
        return pltpu.make_async_remote_copy(
            src_ref=source,
            dst_ref=target,
            send_sem=send_sem,
            recv_sem=recv_sem,
            device_id=peer,
            device_id_type=MESH,
        )

    def line_copy(group, stream, source, peer):
        place, columns = regions[stream][0][-1]
        return remote(
            owns[group].at[:, place, columns],
            fulls[group].at[:, source, place, columns],
            line_send.at[group, stream, peer],
            line_recv.at[group, stream, source],
            (rep, peer),
        )

    def grow_copy(step, group, stream, source):
        place, columns = regions[stream][0][step]
        part = fulls[group].at[:, source, place, columns]
        return remote(
            part,
            part,
            grow_send.at[step, group, stream, source],
            grow_recv.at[step, group, stream, source],
            (flip(rep, order(stream)[step]), me),
        )

    def join_copy(group, stream, source):
        part = fulls[group].at[:, source, :, regions[stream][1]]
        return remote(
            part,
            part,
            join_send.at[group, stream, source],
            join_recv.at[group, stream, source],
            (flip(rep, 1), me),
        )

    def small_copy(source, peer):
        return remote(
            small_ref,
            small_out.at[source],
            small_send.at[peer],
            small_recv.at[source],
            (rep, peer),
        )

    def hand_on(block, to_right):
        peer = jnp.minimum(me + 1, count - 1) if to_right else jnp.maximum(me - 1, 0)
        return remote(
            cot_out.at[block],
            cot_out.at[block],
            (right_sem if to_right else left_sem).at[block],
            arrive_sem.at[block],
            (rep, peer),
        )

    def line_start():
        @pl.when(me < count - 1)
        def _():
            hand_on(me, True).start()

        @pl.when(me > 0)
        def _():
            hand_on(me, False).start()

    def line_step(step):
        lower = me - step
        upper = me + step

        @pl.when(lower >= 0)
        def _():
            hand_on(jnp.maximum(lower, 0), True).wait_recv()

            @pl.when(me < count - 1)
            def _():
                hand_on(jnp.maximum(lower, 0), True).start()

        @pl.when(upper < count)
        def _():
            hand_on(jnp.minimum(upper, count - 1), False).wait_recv()

            @pl.when(me > 0)
            def _():
                hand_on(jnp.minimum(upper, count - 1), False).start()

    def line_send_group(group):
        for other in others:
            for stream in streams:
                line_copy(group, stream, me, other).start()

    def advance(level, group):
        for other in others:
            for stream in streams:
                if level == 0:
                    line_copy(group, stream, other, other).wait_recv()
                else:
                    grow_copy(steps - level, group, stream, other).wait_recv()
                if level < steps:
                    grow_copy(steps - 1 - level, group, stream, other).start()
                else:
                    join_copy(group, stream, other).start()

    for other in others:
        small_copy(me, other).start()
    line_send_group(0)
    for other in others:
        small_copy(other, other).wait_recv()

    def gain(index):
        at = EXPERTS + index
        return jnp.concatenate([small_out[z, at : at + 1, :rows] for z in range(count)], axis=1)

    inputs = tokens_ref[...].astype(jnp.float32)
    first_out[...] = (normalize(inputs)[0] * gain(0)).astype(jnp.bfloat16)
    advance(0, 0)
    line_send_group(1)
    for level in range(1, steps + 1):
        advance(level, 0)
    for other in others:
        for stream in streams:
            join_copy(0, stream, other).wait_recv()
    own_copies[0].wait()
    leave = pltpu.make_async_copy(weights_out, weights_hbm, local_sem.at[2])
    leave.start()

    def whole(index):
        return weights_out[index].reshape(count * rows, width)

    project_inputs(first_out[...], whole, query_out, pair_out, table_ref)
    advance(0, 1)
    line_start()
    bias = allowed_pairs(column_ref[...], row_ref[...])
    quarter = KVHEADS // 4
    attend_forward(range(quarter), query_out, pair_out, bias, head_out, total_out)
    advance(1, 1)
    attend_forward(range(quarter, 2 * quarter), query_out, pair_out, bias, head_out, total_out)
    line_step(1)
    attend_forward(range(2 * quarter, KVHEADS), query_out, pair_out, bias, head_out, total_out)
    for level in range(2, steps + 1):
        advance(level, 1)
    middle = inputs + dot_nn(head_out[...], whole(2))
    middle_out[...] = middle
    second_out[...] = (normalize(middle)[0] * gain(1)).astype(jnp.bfloat16)
    for step in range(2, count):
        line_step(step)
    for group in range(groups):
        for other in others:
            for stream in streams:
                join_copy(group, stream, other).wait_send()
                if group == 1:
                    join_copy(group, stream, other).wait_recv()
                line_copy(group, stream, me, other).wait_send()
                for step in range(steps):
                    grow_copy(step, group, stream, other).wait_send()
    for other in others:
        small_copy(me, other).wait_send()
    for block in range(count):

        @pl.when((block <= me) & (me < count - 1))
        def _():
            hand_on(block, True).wait_send()

        @pl.when((block >= me) & (me > 0))
        def _():
            hand_on(block, False).wait_send()

    own_copies[1].wait()
    leave.wait()


def gather(weights, moments, small, tokens, cotangent, tables, starts, bits, count):
    depth, rows, width = weights.shape
    token_count = tokens.shape[0]
    steps = len(bits)
    low = jnp.bfloat16
    vmem = pl.BlockSpec(memory_space=pltpu.VMEM)
    dma = pltpu.SemaphoreType.DMA
    whole = jax.ShapeDtypeStruct((depth, count, rows, width), low)
    features = jax.ShapeDtypeStruct((token_count, width), low)
    return pl.pallas_call(
        functools.partial(gather_kernel, count, bits),
        in_specs=[vmem] * 8,
        out_specs=[pl.BlockSpec(memory_space=pl.ANY)] + [vmem] * 10,
        out_shape=[
            whole,
            whole,
            jax.ShapeDtypeStruct((count,) + small.shape, small.dtype),
            jax.ShapeDtypeStruct((count, token_count, width), low),
            jax.ShapeDtypeStruct((token_count, width), jnp.float32),
            features,
            features,
            features,
            features,
            features,
            jax.ShapeDtypeStruct((2 * token_count, KVHEADS), jnp.float32),
        ],
        scratch_shapes=[
            pltpu.VMEM(whole.shape, low),
            dma((3,)),
            dma((2, 2, count)),
            dma((2, 2, count)),
            dma((steps, 2, 2, count)),
            dma((steps, 2, 2, count)),
            dma((2, 2, count)),
            dma((2, 2, count)),
            dma((count,)),
            dma((count,)),
            dma((count,)),
            dma((count,)),
            dma((count,)),
        ],
        compiler_params=pltpu.CompilerParams(
            collective_id=3, has_side_effects=True, vmem_limit_bytes=56 * 1024 * 1024
        ),
        name="gather",
    )(weights, moments, small, tokens, cotangent, tables, starts[:, None], starts[None, :])


def local(
    tokens,
    sequence_start,
    routes,
    route_weights,
    cotangent,
    query_proj,
    key_proj,
    value_proj,
    out_proj,
    prenorm,
    midnorm,
    gate_proj,
    up_proj,
    down_proj,
    query_moment,
    key_moment,
    value_moment,
    out_moment,
    prenorm_moment,
    midnorm_moment,
    gate_moment,
    up_moment,
    down_moment,
):
    shard_index = lax.axis_index("shard")
    rep_count = lax.axis_size("rep")
    shard_count = lax.axis_size("shard")
    row_block = query_proj.shape[0]
    bits = rep_bits(rep_count)
    experts_here = gate_proj.shape[0]
    low = jnp.bfloat16
    own_weights = jnp.stack(
        [query_proj, jnp.concatenate([key_proj, value_proj], axis=1), out_proj]
    )
    own_moments = jnp.stack(
        [
            query_moment.astype(low),
            jnp.concatenate([key_moment.astype(low), value_moment.astype(low)], axis=1),
            out_moment.astype(low),
        ]
    )
    dense_weights = jnp.sum(
        jnp.where(
            routes.T[None, :, :] == jnp.arange(EXPERTS, dtype=jnp.int32)[:, None, None],
            route_weights.T[None, :, :],
            0.0,
        ),
        axis=1,
    )
    gain_rows = jnp.pad(
        jnp.stack([prenorm, midnorm]).astype(jnp.float32),
        ((0, 6), (0, tokens.shape[0] - row_block)),
    )
    tables = rotary_tables(jnp.arange(tokens.shape[0], dtype=jnp.int32) - sequence_start)
    (
        weights,
        moments,
        small,
        cotangent_all,
        middle,
        normed_first,
        normed_second,
        query,
        pair,
        head_low,
        log_total,
    ) = gather(
        own_weights,
        own_moments,
        jnp.concatenate([dense_weights, gain_rows], axis=0),
        tokens,
        cotangent,
        tables,
        sequence_start,
        bits,
        shard_count,
    )
    expert_weights = lax.dynamic_slice_in_dim(
        small, shard_index * experts_here, experts_here, 1
    ).transpose(0, 2, 1)
    mixed, grad_second, expert_share = moe(
        normed_second,
        middle,
        cotangent_all,
        expert_weights,
        gate_proj,
        up_proj,
        down_proj,
        bits,
        shard_count,
    )
    expert_grads, dense_grads, gains_grad, grad_tokens = spread(
        expert_share,
        normed_first,
        head_low,
        weights,
        small,
        tokens,
        cotangent,
        grad_second,
        middle,
        query,
        pair,
        log_total,
        tables,
        sequence_start,
        bits=bits,
        count=shard_count,
    )
    gains_here = lax.dynamic_slice_in_dim(gains_grad, shard_index * row_block, row_block, 1)
    prenorm_grad = gains_here[0]
    midnorm_grad = gains_here[1]
    prenorm_next = momentum_keep * prenorm_moment + prenorm_grad
    midnorm_next = momentum_keep * midnorm_moment + midnorm_grad
    prenorm_update = -rate_gain * prenorm_next
    midnorm_update = -rate_gain * midnorm_next
    rep_index = lax.axis_index("rep")
    (
        query_grad,
        query_next,
        key_grad,
        key_next,
        value_grad,
        value_next,
        out_grad,
        out_next,
        own_wide,
        own_narrow,
    ) = dense_update(
        dense_grads,
        moments,
        (query_moment, key_moment, value_moment, out_moment),
        LAYOUT,
        shard_index,
        rep_index,
    )
    pairs = [(index, index + 1 - 2 * (index % 2)) for index in range(rep_count)]
    other_wide = lax.ppermute(own_wide, "rep", pairs)
    other_narrow = lax.ppermute(own_narrow, "rep", pairs)
    first_core = rep_index % 2 == 0
    query_update = jnp.where(first_core, own_wide, other_wide)
    out_update = jnp.where(first_core, other_wide, own_wide)
    key_update = jnp.where(first_core, own_narrow, other_narrow)
    value_update = jnp.where(first_core, other_narrow, own_narrow)
    gate_grad, gate_next, gate_update, up_grad, up_next, up_update = expert_update(
        expert_grads, (0, 1), (gate_moment, up_moment)
    )
    down_grad, down_next, down_update = expert_update(expert_grads, (2,), (down_moment,))
    return (
        mixed,
        grad_tokens,
        query_grad,
        query_next,
        query_update,
        key_grad,
        key_next,
        key_update,
        value_grad,
        value_next,
        value_update,
        out_grad,
        out_next,
        out_update,
        prenorm_grad,
        prenorm_next,
        prenorm_update,
        midnorm_grad,
        midnorm_next,
        midnorm_update,
        gate_grad,
        gate_next,
        gate_update,
        up_grad,
        up_next,
        up_update,
        down_grad,
        down_next,
        down_update,
    )


def solution(mesh):
    return jax.shard_map(
        local,
        mesh=mesh,
        in_specs=(
            P(("rep", "shard"), None),
            P(("rep", "shard")),
            P(("rep", "shard"), None),
            P(("rep", "shard"), None),
            P(("rep", "shard"), None),
            P("shard", None),
            P("shard", None),
            P("shard", None),
            P("shard", None),
            P("shard"),
            P("shard"),
            P("shard", None, None),
            P("shard", None, None),
            P("shard", None, None),
            P("shard", None),
            P("shard", None),
            P("shard", None),
            P("shard", None),
            P("shard"),
            P("shard"),
            P("shard", None, None),
            P("shard", None, None),
            P("shard", None, None),
        ),
        out_specs=(
            P(("rep", "shard"), None),
            P(("rep", "shard"), None),
            P("shard", None),
            P("shard", None),
            P("shard", None),
            P("shard", None),
            P("shard", None),
            P("shard", None),
            P("shard", None),
            P("shard", None),
            P("shard", None),
            P("shard", None),
            P("shard", None),
            P("shard", None),
            P("shard"),
            P("shard"),
            P("shard"),
            P("shard"),
            P("shard"),
            P("shard"),
            P("shard", None, None),
            P("shard", None, None),
            P("shard", None, None),
            P("shard", None, None),
            P("shard", None, None),
            P("shard", None, None),
            P("shard", None, None),
            P("shard", None, None),
            P("shard", None, None),
        ),
        check_vma=False,
    )
```

```python
import functools
import math

import jax
import jax.numpy as jnp
from jax import lax
from jax.experimental import pallas as pl
from jax.experimental.pallas import tpu as pltpu
from jax.sharding import PartitionSpec as P

NHEADS = 16
KVHEADS = 8
HEAD = 64
EXPERTS = 16
NS_ITERS = 2


norm_epsilon = 1e-06
rotary_base = 10000.0
momentum_keep = 0.9
rate_matrix = 0.5
rate_gain = 0.0002
newton_first = 3.4445
newton_second = -4.775
newton_third = 2.0315
masked_score = -1e30


def normalize(values):
    inverse = lax.rsqrt(jnp.mean(values * values, axis=-1, keepdims=True) + norm_epsilon)
    return (values * inverse, inverse)


def normalize_back(grad_normed, scaling, scaled, inverse):
    grad_scaled = grad_normed * scaling
    inner_mean = jnp.mean(grad_scaled * scaled, axis=-1, keepdims=True)
    return (
        inverse * (grad_scaled - scaled * inner_mean),
        jnp.sum(grad_normed * scaled, axis=0, keepdims=True),
    )


def dot_nn(left, right):
    return jnp.dot(left, right, preferred_element_type=jnp.float32)


def dot_nt(left, right):
    return lax.dot_general(
        left, right, (((1,), (1,)), ((), ())), preferred_element_type=jnp.float32
    )


def dot_tn(left, right):
    return lax.dot_general(
        left, right, (((0,), (0,)), ((), ())), preferred_element_type=jnp.float32
    )


def rotate(values, table_ref, sign):
    return (
        values * table_ref[0]
        + sign * pltpu.roll(values, 96, 1) * table_ref[1]
        + sign * pltpu.roll(values, 32, 1) * table_ref[2]
    )


def lane_low(shape):
    return lax.broadcasted_iota(jnp.int32, shape, 1) < HEAD


def twice(pair, upper):
    wide = pair.astype(jnp.float32)
    turned = pltpu.roll(wide, HEAD, 1)
    first = lane_low(pair.shape)
    return jnp.where(first != upper, wide, turned).astype(pair.dtype)


def stacked(pair):
    first = lane_low(pair.shape)
    zero = jnp.zeros_like(pair)
    return jnp.concatenate([jnp.where(first, pair, zero), jnp.where(first, zero, pair)], axis=0)


def unstacked(rows):
    half = rows.shape[0] // 2
    return jnp.where(lane_low((half, rows.shape[1])), rows[:half], rows[half:])


def allowed_pairs(start_column, start_row):
    shape = (start_column.shape[0], start_row.shape[1])
    query_places = lax.broadcasted_iota(jnp.int32, shape, 0)
    key_places = lax.broadcasted_iota(jnp.int32, shape, 1)
    one = (start_column == start_row) & (key_places <= query_places)
    return jnp.where(jnp.concatenate([one, one], axis=0), 0.0, masked_score)


def block_lanes(ref, block):
    return ref[:, block * 2 * HEAD : (block + 1) * 2 * HEAD]


def attend_pair(block, query_ref, pair_ref, bias):
    key = twice(block_lanes(pair_ref, block // 2), block % 2 == 1)
    value = twice(block_lanes(pair_ref, KVHEADS // 2 + block // 2), block % 2 == 1)
    queries = stacked(block_lanes(query_ref, block))
    scores = dot_nt(queries, key) * (1.0 / math.sqrt(HEAD)) + bias
    return (queries, key, value, scores)


def project_inputs(normed, weights, query_ref, pair_ref, table_ref):
    queries = dot_nn(normed, weights(0))
    for block in range(NHEADS // 2):
        lanes = slice(block * 2 * HEAD, (block + 1) * 2 * HEAD)
        query_ref[:, lanes] = rotate(queries[:, lanes], table_ref, 1.0).astype(jnp.bfloat16)
    pairs = dot_nn(normed, weights(1))
    for block in range(KVHEADS):
        lanes = slice(block * 2 * HEAD, (block + 1) * 2 * HEAD)
        value = pairs[:, lanes]
        if block < KVHEADS // 2:
            value = rotate(value, table_ref, 1.0)
        pair_ref[:, lanes] = value.astype(jnp.bfloat16)


def attend_forward(blocks, query_ref, pair_ref, bias, head_ref, total_ref):
    for block in blocks:
        _, _, value, scores = attend_pair(block, query_ref, pair_ref, bias)
        row_max = jnp.max(scores, axis=-1, keepdims=True)
        exponents = jnp.exp(scores - row_max)
        totals = jnp.sum(exponents, axis=-1, keepdims=True)
        softmax_low = (exponents * (1.0 / totals)).astype(jnp.bfloat16)
        head_ref[:, block * 2 * HEAD : (block + 1) * 2 * HEAD] = unstacked(
            dot_nn(softmax_low, value)
        ).astype(jnp.bfloat16)
        total_ref[:, block : block + 1] = row_max + jnp.log(totals)


def attend_backward(query_ref, pair_ref, bias, total_ref, grad_ref, table_ref, delta_ref):
    folded = []
    for block in range(KVHEADS):
        queries, key, value, scores = attend_pair(block, query_ref, pair_ref, bias)
        grads = stacked(block_lanes(grad_ref, block))
        softmax_full = jnp.exp(scores - total_ref[:, block : block + 1])
        grad_softmax = dot_nt(grads, value)
        inner = jnp.sum(softmax_full * grad_softmax, axis=-1, keepdims=True)
        grad_scores = (softmax_full * (grad_softmax - inner)).astype(jnp.bfloat16)
        scale = 1.0 / math.sqrt(HEAD)
        grad_query = unstacked(dot_nn(grad_scores, key)) * scale
        lanes = slice(block * 2 * HEAD, (block + 1) * 2 * HEAD)
        delta_ref[:, lanes] = rotate(grad_query, table_ref, -1.0).astype(jnp.bfloat16)
        grad_key = dot_tn(grad_scores, queries) * scale
        grad_value = dot_tn(softmax_full.astype(jnp.bfloat16), grads)
        folded.append(
            (
                grad_key + pltpu.roll(grad_key, HEAD, 1),
                grad_value + pltpu.roll(grad_value, HEAD, 1),
            )
        )
        if block % 2 == 1:
            first = lane_low(grad_key.shape)
            both = [jnp.where(first, low, high) for low, high in zip(*folded)]
            folded = []
            base = NHEADS * HEAD + (block // 2) * 2 * HEAD
            delta_ref[:, base : base + 2 * HEAD] = rotate(both[0], table_ref, -1.0).astype(
                jnp.bfloat16
            )
            base = base + KVHEADS * HEAD
            delta_ref[:, base : base + 2 * HEAD] = both[1].astype(jnp.bfloat16)


def rotary_tables(positions):
    half_size = HEAD // 2
    frequency = rotary_base ** (-(jnp.arange(half_size, dtype=jnp.float32) * 2.0) / HEAD)
    angles = positions.astype(jnp.float32)[:, None] * frequency[None, :]
    cosine, sine = (jnp.cos(angles), jnp.sin(angles))
    zero = jnp.zeros_like(sine)
    return jnp.stack(
        [
            jnp.concatenate([cosine] * 4, axis=1),
            jnp.concatenate([-sine, zero] * 2, axis=1),
            jnp.concatenate([zero, sine] * 2, axis=1),
        ]
    )


def newton_parts(grams):
    a, b, c = newton_first, newton_second, newton_third

    def times(left, right):
        return jnp.dot(left, right, preferred_element_type=jnp.float32)

    lows = [gram.astype(jnp.bfloat16) for gram in grams]
    firsts = [b * gram + c * times(low, low) for gram, low in zip(grams, lows)]
    first_lows = [first.astype(jnp.bfloat16) for first in firsts]
    mixes = [times(low, first) for low, first in zip(lows, first_lows)]
    nexts = [
        (a * a) * gram + (2.0 * a) * mix + times(mix.astype(jnp.bfloat16), first)
        for gram, mix, first in zip(grams, mixes, first_lows)
    ]
    next_lows = [gram.astype(jnp.bfloat16) for gram in nexts]
    seconds = [b * gram + c * times(low, low) for gram, low in zip(nexts, next_lows)]
    second_lows = [second.astype(jnp.bfloat16) for second in seconds]
    return list(zip(firsts, first_lows, seconds, second_lows))


def scaled_gram(gram):
    shape = gram.shape
    rows = lax.broadcasted_iota(jnp.int32, shape, 0)
    diagonal = rows == lax.broadcasted_iota(jnp.int32, shape, 1)
    inverse = 1.0 / (jnp.sqrt(jnp.sum(jnp.where(diagonal, gram, 0.0))) + 1e-07)
    return (gram * (inverse * inverse), inverse)


def expert_update_kernel(kinds, scale, *refs):
    a = newton_first
    grads_ref = refs[0]
    moments = refs[1 : 1 + len(kinds)]
    outs = refs[1 + len(kinds) :]
    half = grads_ref.shape[3]
    tall = kinds[0] < 2
    states = []
    for index in range(len(kinds)):
        for e in range(grads_ref.shape[0]):
            grad = grads_ref[e, index].astype(jnp.float32)
            if not tall:
                grad = jnp.concatenate([grad[:half], grad[half:]], axis=1)
            moment = momentum_keep * moments[index][e] + grad
            outs[3 * index][e] = grad
            outs[3 * index + 1][e] = moment
            low = moment.astype(jnp.bfloat16)
            sides = (((0,), (0,)), ((), ())) if tall else (((1,), (1,)), ((), ()))
            gram, inverse = scaled_gram(
                lax.dot_general(low, low, sides, preferred_element_type=jnp.float32)
            )
            states.append((index, e, inverse, low, gram))
    parts = newton_parts([state[-1] for state in states])
    for (index, e, inverse, low, _), (first, first_low, second, second_low) in zip(states, parts):
        rest = a * (first + second) + jnp.dot(
            first_low, second_low, preferred_element_type=jnp.float32
        )
        rest = ((-scale * inverse) * rest).astype(jnp.bfloat16)
        if tall:
            step = jnp.dot(low, rest, preferred_element_type=jnp.float32)
        else:
            step = jnp.dot(rest, low, preferred_element_type=jnp.float32)
        outs[3 * index + 2][e] = (-scale * a * a * inverse) * outs[3 * index + 1][e] + step


def expert_update(grads, kinds, moments):
    count, rows, columns = moments[0].shape
    group = 2 // len(kinds)
    scale = rate_matrix * math.sqrt(max(1.0, columns / rows))
    block = pl.BlockSpec((group, rows, columns), lambda i: (i, 0, 0))
    place = kinds[0] // len(kinds)
    taken = pl.BlockSpec((group, len(kinds)) + grads.shape[2:], lambda i: (i, place, 0, 0))
    shape = jax.ShapeDtypeStruct(moments[0].shape, jnp.float32)
    return pl.pallas_call(
        functools.partial(expert_update_kernel, kinds, scale),
        grid=(count // group,),
        in_specs=[taken] + [block] * len(kinds),
        out_specs=[block] * (3 * len(kinds)),
        out_shape=[shape] * (3 * len(kinds)),
        compiler_params=pltpu.CompilerParams(vmem_limit_bytes=60 * 1024 * 1024),
        name="expert_update",
        cost_estimate=pl.CostEstimate(
            flops=count * len(kinds) * 2500000000,
            bytes_accessed=moments[0].size * len(kinds) * 18,
            transcendentals=0,
        ),
    )(grads, *moments)


def dense_update_kernel(layout, place_ref, grads_ref, moments_ref, *refs):
    a = newton_first
    amount = len(layout)
    own_moments = refs[:amount]
    outs = refs[amount : 3 * amount]
    updates = refs[3 * amount : 3 * amount + 2]
    matrices = refs[3 * amount + 2 : 3 * amount + 4]
    own_grads = refs[3 * amount + 4]
    blocks, count, block_rows, width = grads_ref.shape
    part = width // 3
    me = place_ref[0]
    core = place_ref[1]
    start = pl.multiple_of(me * block_rows, block_rows)

    def momentum(moments, grads):
        return (
            (momentum_keep * moments.astype(jnp.float32) + grads.astype(jnp.float32))
            .astype(jnp.bfloat16)
            .reshape(count * block_rows, part)
        )

    for block in range(blocks):
        outer = slice(block * part, (block + 1) * part)
        lanes = pl.ds(pl.multiple_of(2 * core * part, part), part)
        matrices[0][:, outer] = momentum(
            moments_ref[2 * core, :, :, outer], grads_ref[block, :, :, lanes]
        )
        for index in range(3):
            columns = slice(8 * part * index + block * part, 8 * part * index + (block + 1) * part)
            inner = slice(index * part, (index + 1) * part)
            own_grads[:, columns] = grads_ref[block, me, :, inner].astype(jnp.float32)
    for block in range(blocks // 2):
        outer = slice(block * part, (block + 1) * part)
        lanes = pl.ds(pl.multiple_of((core * (blocks // 2) + block) * part, part), part)
        matrices[1][:, outer] = momentum(
            moments_ref[1, :, :, lanes],
            grads_ref[core * (blocks // 2) + block, :, :, part : 2 * part],
        )
    for index, (begin, size) in enumerate(layout):
        grad = own_grads[:, begin : begin + size]
        outs[2 * index][...] = grad
        outs[2 * index + 1][...] = momentum_keep * own_moments[index][...] + grad
    states = []
    for matrix in matrices:
        low = matrix[...]
        states.append(
            scaled_gram(
                lax.dot_general(
                    low, low, (((0,), (0,)), ((), ())), preferred_element_type=jnp.float32
                )
            )
        )
    parts = newton_parts([state[0] for state in states])
    for matrix, update, (_, inverse), (_, first_low, _, second_low) in zip(
        matrices, updates, states, parts
    ):
        rows, columns = matrix.shape
        scale = rate_matrix * math.sqrt(max(1.0, columns / rows))
        own = matrix[pl.ds(start, block_rows)]
        once = a * own.astype(jnp.float32) + jnp.dot(
            own, first_low, preferred_element_type=jnp.float32
        )
        update[...] = (-scale * inverse) * (
            a * once
            + jnp.dot(once.astype(jnp.bfloat16), second_low, preferred_element_type=jnp.float32)
        )


def dense_update(grads, moments, own_moments, layout, shard_index, rep_index):
    _, count, block_rows, width = moments.shape
    whole = lambda shape: pl.BlockSpec(shape, lambda i: (0,) * len(shape))
    shapes = []
    for _, size in layout:
        shapes += [jax.ShapeDtypeStruct((block_rows, size), jnp.float32)] * 2
    shapes += [
        jax.ShapeDtypeStruct((block_rows, width), jnp.float32),
        jax.ShapeDtypeStruct((block_rows, width // 2), jnp.float32),
    ]
    place = jnp.stack([shard_index, rep_index % 2]).astype(jnp.int32)
    return pl.pallas_call(
        functools.partial(dense_update_kernel, layout),
        grid=(1,),
        in_specs=[pl.BlockSpec(memory_space=pltpu.SMEM), whole(grads.shape), whole(moments.shape)]
        + [whole(moment.shape) for moment in own_moments],
        out_specs=[whole(shape.shape) for shape in shapes],
        out_shape=shapes,
        scratch_shapes=[
            pltpu.VMEM((count * block_rows, width), jnp.bfloat16),
            pltpu.VMEM((count * block_rows, width // 2), jnp.bfloat16),
            pltpu.VMEM((block_rows, 3 * width), jnp.float32),
        ],
        compiler_params=pltpu.CompilerParams(vmem_limit_bytes=63 * 1024 * 1024),
        name="dense_update",
        cost_estimate=pl.CostEstimate(
            flops=14000000000, bytes_accessed=24 * width * width, transcendentals=0
        ),
    )(place, grads, moments, *own_moments)


LAYOUT = ((0, 1024), (1024, 512), (1536, 512), (2048, 1024))


MESH = pl.DeviceIdType.MESH


def flip(index, bit):
    return index + bit - 2 * bit * ((index // bit) % 2)


def greet(peers):
    barrier = pltpu.get_barrier_semaphore()
    for peer in peers:
        pl.semaphore_signal(barrier, inc=1, device_id=peer, device_id_type=MESH)
    pl.semaphore_wait(barrier, len(peers))


def stream_plan(rep, bits, base, size):
    stages = []
    starts = [base, base + size]
    for step in range(len(bits)):
        size = size // 2
        stage = []
        for stream in range(2):
            bit = bits[(step + stream) % len(bits)]
            side = (rep // bit) % 2
            keep = starts[stream] + side * size
            send = starts[stream] + (1 - side) * size
            starts[stream] = keep
            stage.append((bit, stream, keep, send, size))
        stages.append(stage)
    return stages


def rows_of(start, size):
    return pl.ds(pl.multiple_of(start, 16), size)


def moe_kernel(
    count,
    bits,
    own_ref,
    cot_ref,
    weight_ref,
    gate_hbm,
    up_hbm,
    down_hbm,
    stage_out,
    back_ref,
    share_ref,
    tok,
    turned,
    mats,
    hid,
    gate_delta,
    up_delta,
    stage_back,
    got_back,
    *rest,
):
    landing = rest[: 1 + 2 * len(bits)]
    (
        load_sem,
        right_sem,
        left_sem,
        arrive_sem,
        back_send,
        back_recv,
        sum_send,
        sum_recv,
    ) = rest[1 + 2 * len(bits) :]
    rep = lax.axis_index("rep")
    me = lax.axis_index("shard")
    experts = mats.shape[0]
    tokens = own_ref.shape[0]
    half = mats.shape[2] // 2
    core = rep % 2

    loads = [
        pltpu.make_async_copy(gate_hbm, mats.at[:, 0], load_sem.at[0]),
        pltpu.make_async_copy(up_hbm, mats.at[:, 1], load_sem.at[1]),
        pltpu.make_async_copy(
            down_hbm.at[:, :, pl.ds(0, half)], mats.at[:, 2, pl.ds(0, half)], load_sem.at[2]
        ),
        pltpu.make_async_copy(
            down_hbm.at[:, :, pl.ds(half, half)], mats.at[:, 2, pl.ds(half, half)], load_sem.at[3]
        ),
    ]
    for load in loads:
        load.start()
    peers = [(rep, lax.rem(me + k, count)) for k in range(1, count)]
    peers += [(flip(rep, bit), me) for bit in (1,) + bits]
    greet(peers)

    right_peer = (rep, jnp.minimum(me + 1, count - 1))
    left_peer = (rep, jnp.maximum(me - 1, 0))

    def hand_on(block, to_right):
        return pltpu.make_async_remote_copy(
            src_ref=tok.at[block],
            dst_ref=tok.at[block],
            send_sem=(right_sem if to_right else left_sem).at[block],
            recv_sem=arrive_sem.at[block],
            device_id=right_peer if to_right else left_peer,
            device_id_type=MESH,
        )

    def returning(stage, got, send_sem, recv_sem, block):
        return pltpu.make_async_remote_copy(
            src_ref=stage.at[block],
            dst_ref=got.at[me],
            send_sem=send_sem.at[block],
            recv_sem=recv_sem.at[me],
            device_id=(rep, block),
            device_id_type=MESH,
        )

    tok[me] = own_ref[...]

    @pl.when(me < count - 1)
    def _():
        hand_on(me, True).start()

    @pl.when(me > 0)
    def _():
        hand_on(me, False).start()

    for load in loads:
        load.wait()

    margin = jnp.minimum(me, count - 1 - me)
    longer = jnp.where(me < count - 1 - me, 1, -1)
    inward = jnp.where(2 * me < count, 1, -1)
    nt = (((1,), (1,)), ((), ()))

    def dot(left, right):
        return jnp.dot(left, right, preferred_element_type=jnp.float32)

    def dot_nt(left, right):
        return lax.dot_general(left, right, nt, preferred_element_type=jnp.float32)

    def visit(j, carry):
        lower = me - j
        upper = me + j

        @pl.when((j > 0) & (lower >= 0))
        def _():
            hand_on(jnp.maximum(lower, 0), True).wait_recv()

            @pl.when(me < count - 1)
            def _():
                hand_on(jnp.maximum(lower, 0), True).start()

        @pl.when((j > 0) & (upper < count))
        def _():
            hand_on(jnp.minimum(upper, count - 1), False).wait_recv()

            @pl.when(me > 0)
            def _():
                hand_on(jnp.minimum(upper, count - 1), False).start()

        near = (j + 1) // 2
        alternating = me + near - 2 * near * (j % 2)
        block = jnp.where(j <= 2 * margin, alternating, me + longer * (j - margin))
        places = pl.ds(pl.multiple_of(block * tokens, tokens), tokens)
        rows = tok[block]
        grads = cot_ref[block]
        turned[:, places] = rows.T
        hiddens = []
        for e in range(experts):
            weight = weight_ref[block, :, e : e + 1]
            u = dot(rows, mats[e, 0])
            w = dot(rows, mats[e, 1])
            gate = 1.0 / (1.0 + jnp.exp(-u))
            act = u * gate
            hidden = (weight * (act * w)).astype(jnp.bfloat16)
            hid[e, :, places] = hidden.T
            hiddens.append(hidden)
            pulled = weight * (
                dot_nt(grads[:, :half], mats[e, 2, :half])
                + dot_nt(grads[:, half:], mats[e, 2, half:])
            )
            gate_delta[e, places] = (pulled * w * (gate + act * (1.0 - gate))).astype(jnp.bfloat16)
            up_delta[e, places] = (pulled * act).astype(jnp.bfloat16)
        for side in range(2):
            part = slice(side * half, (side + 1) * half)
            total_back = None
            total_out = None
            for e in range(experts):
                back = dot_nt(gate_delta[e, places], mats[e, 0, part]) + dot_nt(
                    up_delta[e, places], mats[e, 1, part]
                )
                out = dot(hiddens[e], mats[e, 2, part])
                total_back = back if e == 0 else total_back + back
                total_out = out if e == 0 else total_out + out
            stage_back[block, :, part] = total_back.astype(jnp.bfloat16)
            stage_out[block, :, part] = total_out.astype(jnp.bfloat16)

        @pl.when((j > 0) & ((block - me) * inward > 0))
        def _():
            returning(stage_back, got_back, back_send, back_recv, block).start()

        return carry

    lax.fori_loop(0, count, visit, 0)
    for block in range(count):

        @pl.when((block - me) * inward < 0)
        def _():
            returning(stage_back, got_back, back_send, back_recv, block).start()

    plan = stream_plan(rep, bits, core * half, half // 2)

    def sum_copy(stage, slot, e, start, size, bit):
        return pltpu.make_async_remote_copy(
            src_ref=mats.at[e, :, rows_of(start, size)],
            dst_ref=landing[slot].at[e],
            send_sem=sum_send.at[slot, e],
            recv_sem=sum_recv.at[slot, e],
            device_id=(flip(rep, bit), me),
            device_id_type=MESH,
        )

    def copies(stage, e):
        if stage == 0:
            return [(sum_copy(0, 0, e, (1 - core) * half, half, 1), 0, core * half, half)]
        return [
            (
                sum_copy(stage, 1 + 2 * (stage - 1) + stream, e, send, size, bit),
                1 + 2 * (stage - 1) + stream,
                keep,
                size,
            )
            for bit, stream, keep, send, size in plan[stage - 1]
        ]

    def finish(stage, e):
        for copy, slot, keep, size in copies(stage, e):
            copy.wait_recv()
            place = rows_of(keep, size)
            for kind in range(3):
                mats[e, kind, place] = (
                    mats[e, kind, place].astype(jnp.float32)
                    + landing[slot][e, kind].astype(jnp.float32)
                ).astype(jnp.bfloat16)

    stages = 1 + len(bits)
    for turn in range(experts + stages):
        if turn < experts:
            e = turn
            for side in range(2):
                part = slice(side * half, (side + 1) * half)
                mats[e, 0, part] = dot(turned[part], gate_delta[e]).astype(jnp.bfloat16)
                mats[e, 1, part] = dot(turned[part], up_delta[e]).astype(jnp.bfloat16)
                mats[e, 2, part] = dot(hid[e], cot_ref[:, :, part].reshape(count * tokens, half)).astype(jnp.bfloat16)
            copies(0, e)[0][0].start()
        for stage in range(stages):
            e = turn - 1 - stage
            if 0 <= e < experts:
                finish(stage, e)
                if stage + 1 < stages:
                    for copy, _, _, _ in copies(stage + 1, e):
                        copy.start()
                else:
                    for _, stream, keep, _, size in plan[-1]:
                        share_ref[e, :, stream] = mats[e, :, rows_of(keep, size)]

    total = stage_back[me].astype(jnp.float32)
    for k in range(1, count):
        source = lax.rem(me + k, count)
        pltpu.make_async_remote_copy(
            src_ref=stage_back.at[source],
            dst_ref=got_back.at[source],
            send_sem=back_send.at[source],
            recv_sem=back_recv.at[source],
            device_id=(rep, source),
            device_id_type=MESH,
        ).wait_recv()
        total = total + got_back[source].astype(jnp.float32)
    back_ref[...] = total
    for k in range(1, count):
        block = lax.rem(me + k, count)
        returning(stage_back, got_back, back_send, back_recv, block).wait_send()
    for e in range(experts):
        for stage in range(stages):
            for copy, _, _, _ in copies(stage, e):
                copy.wait_send()
    for block in range(count):

        @pl.when((block <= me) & (me < count - 1))
        def _():
            hand_on(block, True).wait_send()

        @pl.when((block >= me) & (me > 0))
        def _():
            hand_on(block, False).wait_send()


def moe(normed, cotangents, weights, gate_proj, up_proj, down_proj, bits, count):
    tokens, width = normed.shape
    experts, _, hidden = gate_proj.shape
    half = width // 2
    low = jnp.bfloat16
    final = (half // 2) >> len(bits)
    vmem = pl.BlockSpec(memory_space=pltpu.VMEM)
    anywhere = pl.BlockSpec(memory_space=pl.ANY)
    landings = [pltpu.VMEM((experts, 3, half, hidden), low)]
    for step in range(len(bits)):
        size = (half // 2) >> (step + 1)
        landings += [pltpu.VMEM((experts, 3, size, hidden), low)] * 2
    slots = len(landings)
    dma = pltpu.SemaphoreType.DMA
    return pl.pallas_call(
        functools.partial(moe_kernel, count, bits),
        in_specs=[vmem, vmem, vmem, anywhere, anywhere, anywhere],
        out_specs=[vmem, vmem, vmem],
        out_shape=[
            jax.ShapeDtypeStruct((count, tokens, width), low),
            jax.ShapeDtypeStruct((tokens, width), jnp.float32),
            jax.ShapeDtypeStruct((experts, 3, 2, final, hidden), low),
        ],
        scratch_shapes=[
            pltpu.VMEM((count, tokens, width), low),
            pltpu.VMEM((width, count * tokens), low),
            pltpu.VMEM((experts, 3, width, hidden), low),
            pltpu.VMEM((experts, hidden, count * tokens), low),
            pltpu.VMEM((experts, count * tokens, hidden), low),
            pltpu.VMEM((experts, count * tokens, hidden), low),
            pltpu.VMEM((count, tokens, width), low),
            pltpu.VMEM((count, tokens, width), low),
        ]
        + landings
        + [
            dma((4,)),
            dma((count,)),
            dma((count,)),
            dma((count,)),
            dma((count,)),
            dma((count,)),
            dma((slots, experts)),
            dma((slots, experts)),
        ],
        compiler_params=pltpu.CompilerParams(
            collective_id=1, has_side_effects=True, vmem_limit_bytes=63 * 1024 * 1024
        ),
        name="moe",
        cost_estimate=pl.CostEstimate(
            flops=39000000000, bytes_accessed=20000000, transcendentals=2000000
        ),
    )(normed, cotangents, weights, gate_proj, up_proj, down_proj)


def rep_bits(rep_count):
    bits = []
    bit = 2
    while bit < rep_count:
        bits.append(bit)
        bit = bit * 2
    return tuple(bits)


def spread_kernel(
    count,
    bits,
    share_ref,
    returned_ref,
    normed_ref,
    head_ref,
    weights_ref,
    small_ref,
    tokens_ref,
    cot_ref,
    second_ref,
    middle_ref,
    query_ref,
    pair_ref,
    total_ref,
    table_ref,
    column_ref,
    row_ref,
    experts_hbm,
    dense_out,
    gains_out,
    tokens_out,
    mixed_out,
    experts_out,
    got_ref,
    delta_ref,
    branch_ref,
    heads_ref,
    dense_ref,
    total,
    land_core,
    land_first,
    *rest,
):
    later = len(bits) - 1
    land_later = rest[:later]
    (
        piece_send,
        piece_land,
        piece,
        gains_send,
        gains_land,
        gains_all,
        local_sem,
        core_send,
        core_recv,
        half_send,
        half_recv,
        shard_send,
        shard_recv,
        grow_send,
        grow_recv,
        line_send,
        line_recv,
        join_send,
        join_recv,
        expert_send,
        expert_recv,
        gain_send,
        gain_recv,
        gain_line_send,
        gain_line_recv,
        back_send,
        back_recv,
    ) = rest[later:]
    rep = lax.axis_index("rep")
    me = lax.axis_index("shard")
    core = rep % 2
    rows = dense_ref.shape[2]
    expert_rows = experts_out.shape[2]
    steps = len(bits)
    streams = range(2)

    def remote(source, target, send_sem, recv_sem, peer):
        return pltpu.make_async_remote_copy(
            src_ref=source,
            dst_ref=target,
            send_sem=send_sem,
            recv_sem=recv_sem,
            device_id=peer,
            device_id_type=MESH,
        )

    def across(bit):
        return (flip(rep, bit), me)

    def order(stream):
        return [bits[(step + stream) % steps] for step in range(steps)]

    def side(bit):
        return (rep // bit) % 2

    plan = stream_plan(rep, bits, core * (expert_rows // 2), expert_rows // 4)
    base = [(core * (expert_rows // 2)) + stream * (expert_rows // 4) for stream in streams]

    def expert_copy(level, stream):
        if level == steps:
            place = rows_of(base[stream], expert_rows // 4)
            peer = across(1)
        else:
            bit, _, keep, _, size = plan[steps - 1 - level][stream]
            place = rows_of(keep, size)
            peer = across(bit)
        source = experts_out.at[:, :, place]
        if level == 0:
            source = share_ref.at[:, :, stream]
        return remote(
            source,
            experts_out.at[:, :, place],
            expert_send.at[level, stream],
            expert_recv.at[level, stream],
            peer,
        )

    def own_copy(stream):
        _, _, keep, _, size = plan[-1][stream]
        return pltpu.make_async_copy(
            share_ref.at[:, :, stream],
            experts_out.at[:, :, rows_of(keep, size)],
            local_sem.at[stream],
        )

    for stream in streams:
        own_copy(stream).start()
    peers = [(rep, lax.rem(me + k, count)) for k in range(1, count)]
    peers += [across(bit) for bit in (1,) + bits]
    greet(peers)

    def returning(peer, source):
        return remote(
            returned_ref.at[peer],
            got_ref.at[source],
            back_send.at[peer],
            back_recv.at[source],
            (rep, peer),
        )

    def core_copy(block):
        return remote(
            dense_ref.at[4 * (1 - core) + block],
            land_core.at[block],
            core_send.at[block],
            core_recv.at[block],
            across(1),
        )

    gain_bits = (1,) + bits

    def gain_copy(stage):
        return remote(
            gains_send.at[stage],
            gains_land.at[stage],
            gain_send.at[stage],
            gain_recv.at[stage],
            across(gain_bits[stage]),
        )

    for stream in streams:
        expert_copy(0, stream).start()

    for k in range(1, count):
        returning(lax.rem(me + k, count), me).start()

    def whole(index):
        return weights_ref[index].reshape(count * rows, -1)

    def gain(index):
        at = EXPERTS + index
        return jnp.concatenate([small_ref[z, at : at + 1, :rows] for z in range(count)], axis=1)

    scaled, inverse = normalize(middle_ref[...])
    middle_extra, midnorm_part = normalize_back(second_ref[...], gain(1), scaled, inverse)
    grad_middle = cot_ref[...].astype(jnp.float32) + middle_extra
    tokens_out[...] = grad_middle
    branch_ref[...] = grad_middle.astype(jnp.bfloat16)
    heads_ref[...] = dot_nt(branch_ref[...], whole(2)).astype(jnp.bfloat16)
    bias = allowed_pairs(column_ref[...], row_ref[...])
    attend_backward(query_ref, pair_ref, bias, total_ref, heads_ref, table_ref, delta_ref)

    part = dense_ref.shape[3] // 3
    normed_turned = normed_ref[...].T
    head_turned = head_ref[...].T

    def make_block(block):
        def columns(ref, offset):
            return ref[:, pl.ds(pl.multiple_of(offset + block * part, part), part)]

        pair = jnp.concatenate([columns(delta_ref, 0), columns(delta_ref, 8 * part)], axis=1)
        left = jnp.dot(normed_turned, pair, preferred_element_type=jnp.float32)
        right = jnp.dot(head_turned, columns(branch_ref, 0), preferred_element_type=jnp.float32)
        for line in range(count):
            place = slice(line * rows, (line + 1) * rows)
            dense_ref[block, line, :, : 2 * part] = left[place].astype(jnp.bfloat16)
            dense_ref[block, line, :, 2 * part :] = right[place].astype(jnp.bfloat16)

    for block in range(4):
        make_block(4 * (1 - core) + block)
        core_copy(block).start()
    for block in range(4):
        make_block(4 * core + block)

    def gain_step(stage):
        gain_copy(stage).wait_recv()
        gains_send[stage + 1] = gains_send[stage] + gains_land[stage]
        if stage + 1 < len(gain_bits):
            gain_copy(stage + 1).start()

    first = [side(order(stream)[0]) for stream in streams]
    held = [2 * stream + first[stream] for stream in streams]
    given = [2 * stream + 1 - first[stream] for stream in streams]

    def first_copy(stream):
        return remote(
            total.at[given[stream]],
            land_first.at[stream],
            half_send.at[0, stream],
            half_recv.at[0, stream],
            across(order(stream)[0]),
        )

    def add_core(block):
        for line in range(count):
            total[block, line] = (
                dense_ref[4 * core + block, line].astype(jnp.float32)
                + land_core[block, line].astype(jnp.float32)
            ).astype(jnp.bfloat16)

    for block in range(4):
        core_copy(block).wait_recv()
    for stream in streams:
        add_core(given[stream])
        first_copy(stream).start()
    for stream in streams:
        add_core(held[stream])
    grad_first = dot_nt(delta_ref[:, : NHEADS * HEAD], whole(0)) + dot_nt(
        delta_ref[:, NHEADS * HEAD :], whole(1)
    )
    scaled, inverse = normalize(tokens_ref[...].astype(jnp.float32))
    input_extra, prenorm_part = normalize_back(grad_first, gain(0), scaled, inverse)
    tokens_out[...] = tokens_out[...] + input_extra
    gains_send[0] = jnp.concatenate(
        [prenorm_part, midnorm_part, jnp.zeros((6, prenorm_part.shape[1]), jnp.float32)], axis=0
    )
    gain_copy(0).start()
    gain_step(0)

    starts = []
    for stream in streams:
        start, size, line = 0, rows, []
        for step in range(1, steps):
            size = size // 2
            near = side(order(stream)[step])
            line.append((start + near * size, start + (1 - near) * size, size))
            start = start + near * size
        starts.append((start, size, line))

    def later_copy(step, stream):
        keep, send, size = starts[stream][2][step - 1]
        return remote(
            total.at[held[stream], :, rows_of(send, size)],
            land_later[step - 1].at[stream],
            half_send.at[step, stream],
            half_recv.at[step, stream],
            across(order(stream)[step]),
        )

    for stream in streams:
        first_copy(stream).wait_recv()
        for line in range(count):
            total[held[stream], line] = (
                total[held[stream], line].astype(jnp.float32)
                + land_first[stream, line].astype(jnp.float32)
            ).astype(jnp.bfloat16)
        if steps > 1:
            later_copy(1, stream).start()
    gain_step(1)

    for step in range(1, steps):
        for stream in streams:
            later_copy(step, stream).wait_recv()
            keep, _, size = starts[stream][2][step - 1]
            for line in range(count):
                place = rows_of(keep, size)
                total[held[stream], line, place] = (
                    total[held[stream], line, place].astype(jnp.float32)
                    + land_later[step - 1][stream, line].astype(jnp.float32)
                ).astype(jnp.bfloat16)
            if step + 1 < steps:
                later_copy(step + 1, stream).start()
        gain_step(step + 1)

    for stream in streams:
        own_copy(stream).wait()
        expert_copy(0, stream).wait_recv()
        if steps > 1:
            expert_copy(1, stream).start()

    last = starts[0][1]
    places = [rows_of(starts[stream][0], last) for stream in streams]
    for stream in streams:
        for line in range(count):
            piece_send[line, stream] = total[held[stream], line, places[stream]]

    def shard_copy(k):
        target = lax.rem(me + k, count)
        return remote(
            piece_send.at[target],
            piece_land.at[me],
            shard_send.at[target],
            shard_recv.at[me],
            (rep, target),
        )

    def shard_arrival(source):
        return remote(
            piece_send.at[source],
            piece_land.at[source],
            shard_send.at[source],
            shard_recv.at[source],
            (rep, source),
        )

    def gain_line(k):
        target = lax.rem(me + k, count)
        return remote(
            gains_send.at[len(gain_bits)],
            gains_all.at[me],
            gain_line_send.at[target],
            gain_line_recv.at[me],
            (rep, target),
        )

    def gain_arrival(source):
        return remote(
            gains_send.at[len(gain_bits)],
            gains_all.at[source],
            gain_line_send.at[source],
            gain_line_recv.at[source],
            (rep, source),
        )

    for k in range(1, count):
        shard_copy(k).start()
        gain_line(k).start()
    summed = piece_send[me].astype(jnp.float32)
    for k in range(1, count):
        source = lax.rem(me + k, count)
        shard_arrival(source).wait_recv()
        summed = summed + piece_land[source].astype(jnp.float32)
    piece[...] = summed.astype(jnp.bfloat16)

    def line_copy(k, stream):
        target = lax.rem(me + k, count)
        return remote(
            piece.at[stream],
            dense_out.at[4 * core + held[stream], me, places[stream]],
            line_send.at[stream, target],
            line_recv.at[stream, me],
            (rep, target),
        )

    def line_arrival(source, stream):
        return remote(
            piece.at[stream],
            dense_out.at[4 * core + held[stream], source, places[stream]],
            line_send.at[stream, source],
            line_recv.at[stream, source],
            (rep, source),
        )

    def own_piece(stream):
        return pltpu.make_async_copy(
            piece.at[stream],
            dense_out.at[4 * core + held[stream], me, places[stream]],
            local_sem.at[2 + stream],
        )

    for stream in streams:
        own_piece(stream).start()
        for k in range(1, count):
            line_copy(k, stream).start()
    gained = gains_send[len(gain_bits)]
    for k in range(1, count):
        source = lax.rem(me + k, count)
        gain_arrival(source).wait_recv()
        gained = gained + gains_all[source]
    gains_out[...] = gained

    for level in range(1, steps):
        for stream in streams:
            expert_copy(level, stream).wait_recv()
            expert_copy(level + 1, stream).start()
    if steps == 1:
        for stream in streams:
            expert_copy(1, stream).start()

    def grow_copy(step, stream):
        if step == 0:
            place = dense_out.at[4 * core + held[stream]]
        else:
            keep, _, size = starts[stream][2][step - 1]
            place = dense_out.at[4 * core + held[stream], :, rows_of(keep, size)]
        return remote(
            place,
            place,
            grow_send.at[step, stream],
            grow_recv.at[step, stream],
            across(order(stream)[step]),
        )

    for stream in streams:
        own_piece(stream).wait()
        for k in range(1, count):
            line_arrival(lax.rem(me + k, count), stream).wait_recv()
        grow_copy(steps - 1, stream).start()
    mixed = middle_ref[...] + returned_ref[me].astype(jnp.float32)
    for k in range(1, count):
        source = lax.rem(me + k, count)
        returning(source, source).wait_recv()
        mixed = mixed + got_ref[source].astype(jnp.float32)
    mixed_out[...] = mixed.astype(mixed_out.dtype)
    for stream in streams:
        expert_copy(steps, stream).wait()
    leave = pltpu.make_async_copy(experts_out, experts_hbm, local_sem.at[0])
    leave.start()
    for step in reversed(range(steps)):
        for stream in streams:
            grow_copy(step, stream).wait_recv()
            if step > 0:
                grow_copy(step - 1, stream).start()

    def join_copy(stream):
        place = dense_out.at[pl.ds(4 * core + 2 * stream, 2)]
        return remote(place, place, join_send.at[stream], join_recv.at[stream], across(1))

    for stream in streams:
        join_copy(stream).start()
    for stream in streams:
        join_copy(stream).wait()
        for level in range(steps):
            expert_copy(level, stream).wait_send()
        first_copy(stream).wait_send()
        for step in range(1, steps):
            later_copy(step, stream).wait_send()
        for k in range(1, count):
            line_copy(k, stream).wait_send()
        for step in range(steps):
            grow_copy(step, stream).wait_send()
    for block in range(4):
        core_copy(block).wait_send()
    for stage in range(len(gain_bits)):
        gain_copy(stage).wait_send()
    for k in range(1, count):
        shard_copy(k).wait_send()
        gain_line(k).wait_send()
        returning(lax.rem(me + k, count), me).wait_send()
    leave.wait()


def spread(
    share, returned, normed, head_low, weights, small, tokens, cotangent, second, middle, *rest, bits, count
):
    query, pair, log_total, tables, starts = rest
    experts, _, _, final, hidden = share.shape
    token_count, features = normed.shape
    rows = features // count
    width = 3 * features // 8
    dense_shape = (8, count, rows, width)
    gains_shape = (8, features)
    steps = len(bits)
    last = rows >> (steps - 1)
    low = jnp.bfloat16
    vmem = pl.BlockSpec(memory_space=pltpu.VMEM)
    dma = pltpu.SemaphoreType.DMA
    return pl.pallas_call(
        functools.partial(spread_kernel, count, bits),
        in_specs=[vmem] * 16,
        out_specs=[pl.BlockSpec(memory_space=pl.ANY)] + [vmem] * 4,
        out_shape=[
            jax.ShapeDtypeStruct((experts, 3, 4 * (final << steps), hidden), low),
            jax.ShapeDtypeStruct(dense_shape, low),
            jax.ShapeDtypeStruct(gains_shape, jnp.float32),
            jax.ShapeDtypeStruct((token_count, features), jnp.float32),
            jax.ShapeDtypeStruct((token_count, features), low),
        ],
        scratch_shapes=[
            pltpu.VMEM((experts, 3, 4 * (final << steps), hidden), low),
            pltpu.VMEM((count, token_count, features), low),
            pltpu.VMEM((token_count, 2 * features), low),
            pltpu.VMEM((token_count, features), low),
            pltpu.VMEM((token_count, features), low),
            pltpu.VMEM(dense_shape, low),
            pltpu.VMEM((4, count, rows, width), low),
            pltpu.VMEM((4, count, rows, width), low),
            pltpu.VMEM((2, count, rows, width), low),
        ]
        + [pltpu.VMEM((2, count, rows >> step, width), low) for step in range(1, steps)]
        + [
            pltpu.VMEM((count, 2, last, width), low),
            pltpu.VMEM((count, 2, last, width), low),
            pltpu.VMEM((2, last, width), low),
            pltpu.VMEM((steps + 2,) + gains_shape, jnp.float32),
            pltpu.VMEM((steps + 1,) + gains_shape, jnp.float32),
            pltpu.VMEM((count,) + gains_shape, jnp.float32),
            dma((4,)),
            dma((4,)),
            dma((4,)),
            dma((steps, 2)),
            dma((steps, 2)),
            dma((count,)),
            dma((count,)),
            dma((steps, 2)),
            dma((steps, 2)),
            dma((2, count)),
            dma((2, count)),
            dma((2,)),
            dma((2,)),
            dma((steps + 1, 2)),
            dma((steps + 1, 2)),
            dma((steps + 1,)),
            dma((steps + 1,)),
            dma((count,)),
            dma((count,)),
            dma((count,)),
            dma((count,)),
        ],
        compiler_params=pltpu.CompilerParams(
            collective_id=2, has_side_effects=True, vmem_limit_bytes=63 * 1024 * 1024
        ),
        name="spread",
    )(
        share,
        returned,
        normed,
        head_low,
        weights,
        small,
        tokens,
        cotangent,
        second,
        middle,
        query,
        pair,
        log_total,
        tables,
        starts[:, None],
        starts[None, :],
    )


def gather_kernel(
    count,
    bits,
    query_weight,
    key_weight,
    value_weight,
    out_weight,
    query_moment,
    key_moment,
    value_moment,
    out_moment,
    small_ref,
    tokens_ref,
    cot_ref,
    table_ref,
    column_ref,
    row_ref,
    weights_hbm,
    moments_hbm,
    small_out,
    cot_out,
    middle_out,
    first_out,
    second_out,
    query_out,
    pair_out,
    head_out,
    total_out,
    weights_out,
    moments_out,
    weights_ref,
    moments_ref,
    local_sem,
    line_send,
    line_recv,
    grow_send,
    grow_recv,
    join_send,
    join_recv,
    small_send,
    small_recv,
    right_sem,
    left_sem,
    arrive_sem,
):
    rep = lax.axis_index("rep")
    me = lax.axis_index("shard")
    core = rep % 2
    steps = len(bits)
    streams = range(2)
    owns = (weights_ref, moments_ref)
    fulls = (weights_out, moments_out)
    rows, width = weights_ref.shape[1:]
    half = width // 2
    fine = half // 4
    groups = 2
    others = [lax.rem(me + k, count) for k in range(1, count)]

    def columns_of(start, size):
        return pl.ds(pl.multiple_of(start, 128), size)

    def order(stream):
        return [bits[(step + stream) % steps] for step in range(steps)]

    def side(bit):
        return (rep // bit) % 2

    narrow = width // 2
    for target, sources in (
        (weights_ref, (query_weight, key_weight, value_weight, out_weight)),
        (moments_ref, (query_moment, key_moment, value_moment, out_moment)),
    ):
        target[0] = sources[0][...].astype(target.dtype)
        target[1, :, :narrow] = sources[1][...].astype(target.dtype)
        target[1, :, narrow:] = sources[2][...].astype(target.dtype)
        target[2] = sources[3][...].astype(target.dtype)
    own_copies = [
        pltpu.make_async_copy(weights_ref, weights_out.at[:, me], local_sem.at[0]),
        pltpu.make_async_copy(moments_ref, moments_out.at[:, me], local_sem.at[1]),
    ]
    for own_copy in own_copies:
        own_copy.start()
    small_out[me] = small_ref[...]
    cot_out[me] = cot_ref[...]
    peers = [(rep, other) for other in others]
    peers += [(flip(rep, bit), me) for bit in (1,) + bits]
    greet(peers)

    regions = []
    for stream in streams:
        column = core * half + stream * 2 * fine
        narrow = columns_of(column + side(order(stream)[0]) * fine, fine)
        start, size = 0, rows
        held = [(pl.ds(0, rows), narrow)]
        for step in range(1, steps):
            size = size // 2
            start = start + side(order(stream)[step]) * size
            held.append((rows_of(start, size), narrow))
        regions.append((held, columns_of(column, 2 * fine)))

    def remote(source, target, send_sem, recv_sem, peer):
        return pltpu.make_async_remote_copy(
            src_ref=source,
            dst_ref=target,
            send_sem=send_sem,
            recv_sem=recv_sem,
            device_id=peer,
            device_id_type=MESH,
        )

    def line_copy(group, stream, source, peer):
        place, columns = regions[stream][0][-1]
        return remote(
            owns[group].at[:, place, columns],
            fulls[group].at[:, source, place, columns],
            line_send.at[group, stream, peer],
            line_recv.at[group, stream, source],
            (rep, peer),
        )

    def grow_copy(step, group, stream, source):
        place, columns = regions[stream][0][step]
        part = fulls[group].at[:, source, place, columns]
        return remote(
            part,
            part,
            grow_send.at[step, group, stream, source],
            grow_recv.at[step, group, stream, source],
            (flip(rep, order(stream)[step]), me),
        )

    def join_copy(group, stream, source):
        part = fulls[group].at[:, source, :, regions[stream][1]]
        return remote(
            part,
            part,
            join_send.at[group, stream, source],
            join_recv.at[group, stream, source],
            (flip(rep, 1), me),
        )

    def small_copy(source, peer):
        return remote(
            small_ref,
            small_out.at[source],
            small_send.at[peer],
            small_recv.at[source],
            (rep, peer),
        )

    def hand_on(block, to_right):
        peer = jnp.minimum(me + 1, count - 1) if to_right else jnp.maximum(me - 1, 0)
        return remote(
            cot_out.at[block],
            cot_out.at[block],
            (right_sem if to_right else left_sem).at[block],
            arrive_sem.at[block],
            (rep, peer),
        )

    def line_start():
        @pl.when(me < count - 1)
        def _():
            hand_on(me, True).start()

        @pl.when(me > 0)
        def _():
            hand_on(me, False).start()

    def line_step(step):
        lower = me - step
        upper = me + step

        @pl.when(lower >= 0)
        def _():
            hand_on(jnp.maximum(lower, 0), True).wait_recv()

            @pl.when(me < count - 1)
            def _():
                hand_on(jnp.maximum(lower, 0), True).start()

        @pl.when(upper < count)
        def _():
            hand_on(jnp.minimum(upper, count - 1), False).wait_recv()

            @pl.when(me > 0)
            def _():
                hand_on(jnp.minimum(upper, count - 1), False).start()

    def line_send_group(group):
        for other in others:
            for stream in streams:
                line_copy(group, stream, me, other).start()

    def advance(level, group):
        for other in others:
            for stream in streams:
                if level == 0:
                    line_copy(group, stream, other, other).wait_recv()
                else:
                    grow_copy(steps - level, group, stream, other).wait_recv()
                if level < steps:
                    grow_copy(steps - 1 - level, group, stream, other).start()
                else:
                    join_copy(group, stream, other).start()

    for other in others:
        small_copy(me, other).start()
    line_send_group(0)
    for other in others:
        small_copy(other, other).wait_recv()

    def gain(index):
        at = EXPERTS + index
        return jnp.concatenate([small_out[z, at : at + 1, :rows] for z in range(count)], axis=1)

    inputs = tokens_ref[...].astype(jnp.float32)
    first_out[...] = (normalize(inputs)[0] * gain(0)).astype(jnp.bfloat16)
    advance(0, 0)
    line_send_group(1)
    for level in range(1, steps + 1):
        advance(level, 0)
    advance(0, 1)
    line_start()
    for other in others:
        for stream in streams:
            join_copy(0, stream, other).wait_recv()
    own_copies[0].wait()
    leave = pltpu.make_async_copy(weights_out, weights_hbm, local_sem.at[2])
    leave.start()

    def whole(index):
        return weights_out[index].reshape(count * rows, width)

    project_inputs(first_out[...], whole, query_out, pair_out, table_ref)
    bias = allowed_pairs(column_ref[...], row_ref[...])
    quarter = KVHEADS // 4
    advance(1, 1)
    attend_forward(range(2 * quarter), query_out, pair_out, bias, head_out, total_out)
    line_step(1)
    attend_forward(range(2 * quarter, KVHEADS), query_out, pair_out, bias, head_out, total_out)
    for level in range(2, steps + 1):
        advance(level, 1)
    leaving = pltpu.make_async_copy(moments_out, moments_hbm, local_sem.at[3])

    def moments_leave():
        for other in others:
            for stream in streams:
                join_copy(1, stream, other).wait_recv()
        own_copies[1].wait()
        leaving.start()

    middle = inputs + dot_nn(head_out[...], whole(2))
    middle_out[...] = middle
    second_out[...] = (normalize(middle)[0] * gain(1)).astype(jnp.bfloat16)
    for step in range(2, count):
        line_step(step)
        if step == 2:
            moments_leave()
    if count < 3:
        moments_leave()
    for group in range(groups):
        for other in others:
            for stream in streams:
                join_copy(group, stream, other).wait_send()
                line_copy(group, stream, me, other).wait_send()
                for step in range(steps):
                    grow_copy(step, group, stream, other).wait_send()
    for other in others:
        small_copy(me, other).wait_send()
    for block in range(count):

        @pl.when((block <= me) & (me < count - 1))
        def _():
            hand_on(block, True).wait_send()

        @pl.when((block >= me) & (me > 0))
        def _():
            hand_on(block, False).wait_send()

    leave.wait()
    leaving.wait()


def gather(weights, moments, small, tokens, cotangent, tables, starts, bits, count):
    rows, width = weights[0].shape
    depth = 3
    token_count = tokens.shape[0]
    steps = len(bits)
    low = jnp.bfloat16
    vmem = pl.BlockSpec(memory_space=pltpu.VMEM)
    dma = pltpu.SemaphoreType.DMA
    whole = jax.ShapeDtypeStruct((depth, count, rows, width), low)
    features = jax.ShapeDtypeStruct((token_count, width), low)
    return pl.pallas_call(
        functools.partial(gather_kernel, count, bits),
        in_specs=[vmem] * 14,
        out_specs=[pl.BlockSpec(memory_space=pl.ANY)] * 2 + [vmem] * 9,
        out_shape=[
            whole,
            whole,
            jax.ShapeDtypeStruct((count,) + small.shape, small.dtype),
            jax.ShapeDtypeStruct((count, token_count, width), low),
            jax.ShapeDtypeStruct((token_count, width), jnp.float32),
            features,
            features,
            features,
            features,
            features,
            jax.ShapeDtypeStruct((2 * token_count, KVHEADS), jnp.float32),
        ],
        scratch_shapes=[
            pltpu.VMEM(whole.shape, low),
            pltpu.VMEM(whole.shape, low),
            pltpu.VMEM((depth, rows, width), low),
            pltpu.VMEM((depth, rows, width), low),
            dma((4,)),
            dma((2, 2, count)),
            dma((2, 2, count)),
            dma((steps, 2, 2, count)),
            dma((steps, 2, 2, count)),
            dma((2, 2, count)),
            dma((2, 2, count)),
            dma((count,)),
            dma((count,)),
            dma((count,)),
            dma((count,)),
            dma((count,)),
        ],
        compiler_params=pltpu.CompilerParams(
            collective_id=3, has_side_effects=True, vmem_limit_bytes=56 * 1024 * 1024
        ),
        name="gather",
    )(
        *weights,
        *moments,
        small,
        tokens,
        cotangent,
        tables,
        starts[:, None],
        starts[None, :],
    )


def local(
    tokens,
    sequence_start,
    routes,
    route_weights,
    cotangent,
    query_proj,
    key_proj,
    value_proj,
    out_proj,
    prenorm,
    midnorm,
    gate_proj,
    up_proj,
    down_proj,
    query_moment,
    key_moment,
    value_moment,
    out_moment,
    prenorm_moment,
    midnorm_moment,
    gate_moment,
    up_moment,
    down_moment,
):
    shard_index = lax.axis_index("shard")
    rep_count = lax.axis_size("rep")
    shard_count = lax.axis_size("shard")
    row_block = query_proj.shape[0]
    bits = rep_bits(rep_count)
    experts_here = gate_proj.shape[0]
    dense_weights = jnp.sum(
        jnp.where(
            routes.T[None, :, :] == jnp.arange(EXPERTS, dtype=jnp.int32)[:, None, None],
            route_weights.T[None, :, :],
            0.0,
        ),
        axis=1,
    )
    gain_rows = jnp.pad(
        jnp.stack([prenorm, midnorm]).astype(jnp.float32),
        ((0, 6), (0, tokens.shape[0] - row_block)),
    )
    tables = rotary_tables(jnp.arange(tokens.shape[0], dtype=jnp.int32) - sequence_start)
    (
        weights,
        moments,
        small,
        cotangent_all,
        middle,
        normed_first,
        normed_second,
        query,
        pair,
        head_low,
        log_total,
    ) = gather(
        (query_proj, key_proj, value_proj, out_proj),
        (query_moment, key_moment, value_moment, out_moment),
        jnp.concatenate([dense_weights, gain_rows], axis=0),
        tokens,
        cotangent,
        tables,
        sequence_start,
        bits,
        shard_count,
    )
    expert_weights = lax.dynamic_slice_in_dim(
        small, shard_index * experts_here, experts_here, 1
    ).transpose(0, 2, 1)
    returned, grad_second, expert_share = moe(
        normed_second,
        cotangent_all,
        expert_weights,
        gate_proj,
        up_proj,
        down_proj,
        bits,
        shard_count,
    )
    expert_grads, dense_grads, gains_grad, grad_tokens, mixed = spread(
        expert_share,
        returned,
        normed_first,
        head_low,
        weights,
        small,
        tokens,
        cotangent,
        grad_second,
        middle,
        query,
        pair,
        log_total,
        tables,
        sequence_start,
        bits=bits,
        count=shard_count,
    )
    gains_here = lax.dynamic_slice_in_dim(gains_grad, shard_index * row_block, row_block, 1)
    prenorm_grad = gains_here[0]
    midnorm_grad = gains_here[1]
    prenorm_next = momentum_keep * prenorm_moment + prenorm_grad
    midnorm_next = momentum_keep * midnorm_moment + midnorm_grad
    prenorm_update = -rate_gain * prenorm_next
    midnorm_update = -rate_gain * midnorm_next
    rep_index = lax.axis_index("rep")
    (
        query_grad,
        query_next,
        key_grad,
        key_next,
        value_grad,
        value_next,
        out_grad,
        out_next,
        own_wide,
        own_narrow,
    ) = dense_update(
        dense_grads,
        moments,
        (query_moment, key_moment, value_moment, out_moment),
        LAYOUT,
        shard_index,
        rep_index,
    )
    pairs = [(index, index + 1 - 2 * (index % 2)) for index in range(rep_count)]
    other_wide = lax.ppermute(own_wide, "rep", pairs)
    other_narrow = lax.ppermute(own_narrow, "rep", pairs)
    first_core = rep_index % 2 == 0
    query_update = jnp.where(first_core, own_wide, other_wide)
    out_update = jnp.where(first_core, other_wide, own_wide)
    key_update = jnp.where(first_core, own_narrow, other_narrow)
    value_update = jnp.where(first_core, other_narrow, own_narrow)
    gate_grad, gate_next, gate_update, up_grad, up_next, up_update = expert_update(
        expert_grads, (0, 1), (gate_moment, up_moment)
    )
    down_grad, down_next, down_update = expert_update(expert_grads, (2,), (down_moment,))
    return (
        mixed,
        grad_tokens,
        query_grad,
        query_next,
        query_update,
        key_grad,
        key_next,
        key_update,
        value_grad,
        value_next,
        value_update,
        out_grad,
        out_next,
        out_update,
        prenorm_grad,
        prenorm_next,
        prenorm_update,
        midnorm_grad,
        midnorm_next,
        midnorm_update,
        gate_grad,
        gate_next,
        gate_update,
        up_grad,
        up_next,
        up_update,
        down_grad,
        down_next,
        down_update,
    )


def solution(mesh):
    return jax.shard_map(
        local,
        mesh=mesh,
        in_specs=(
            P(("rep", "shard"), None),
            P(("rep", "shard")),
            P(("rep", "shard"), None),
            P(("rep", "shard"), None),
            P(("rep", "shard"), None),
            P("shard", None),
            P("shard", None),
            P("shard", None),
            P("shard", None),
            P("shard"),
            P("shard"),
            P("shard", None, None),
            P("shard", None, None),
            P("shard", None, None),
            P("shard", None),
            P("shard", None),
            P("shard", None),
            P("shard", None),
            P("shard"),
            P("shard"),
            P("shard", None, None),
            P("shard", None, None),
            P("shard", None, None),
        ),
        out_specs=(
            P(("rep", "shard"), None),
            P(("rep", "shard"), None),
            P("shard", None),
            P("shard", None),
            P("shard", None),
            P("shard", None),
            P("shard", None),
            P("shard", None),
            P("shard", None),
            P("shard", None),
            P("shard", None),
            P("shard", None),
            P("shard", None),
            P("shard", None),
            P("shard"),
            P("shard"),
            P("shard"),
            P("shard"),
            P("shard"),
            P("shard"),
            P("shard", None, None),
            P("shard", None, None),
            P("shard", None, None),
            P("shard", None, None),
            P("shard", None, None),
            P("shard", None, None),
            P("shard", None, None),
            P("shard", None, None),
            P("shard", None, None),
        ),
        check_vma=False,
    )
```

```python
import functools
import math

import jax
import jax.numpy as jnp
from jax import lax
from jax.experimental import pallas as pl
from jax.experimental.pallas import tpu as pltpu
from jax.sharding import PartitionSpec as P

NHEADS = 16
KVHEADS = 8
HEAD = 64
EXPERTS = 16
NS_ITERS = 2


norm_epsilon = 1e-06
rotary_base = 10000.0
momentum_keep = 0.9
rate_matrix = 0.5
rate_gain = 0.0002
newton_first = 3.4445
newton_second = -4.775
newton_third = 2.0315
masked_score = -1e30


def normalize(values):
    inverse = lax.rsqrt(jnp.mean(values * values, axis=-1, keepdims=True) + norm_epsilon)
    return (values * inverse, inverse)


def normalize_back(grad_normed, scaling, scaled, inverse):
    grad_scaled = grad_normed * scaling
    inner_mean = jnp.mean(grad_scaled * scaled, axis=-1, keepdims=True)
    return (
        inverse * (grad_scaled - scaled * inner_mean),
        jnp.sum(grad_normed * scaled, axis=0, keepdims=True),
    )


def dot_nn(left, right):
    return jnp.dot(left, right, preferred_element_type=jnp.float32)


def dot_nt(left, right):
    return lax.dot_general(
        left, right, (((1,), (1,)), ((), ())), preferred_element_type=jnp.float32
    )


def dot_tn(left, right):
    return lax.dot_general(
        left, right, (((0,), (0,)), ((), ())), preferred_element_type=jnp.float32
    )


def rotate(values, table_ref, sign):
    return (
        values * table_ref[0]
        + sign * pltpu.roll(values, 96, 1) * table_ref[1]
        + sign * pltpu.roll(values, 32, 1) * table_ref[2]
    )


def lane_low(shape):
    return lax.broadcasted_iota(jnp.int32, shape, 1) < HEAD


def twice(pair, upper):
    wide = pair.astype(jnp.float32)
    turned = pltpu.roll(wide, HEAD, 1)
    first = lane_low(pair.shape)
    return jnp.where(first != upper, wide, turned).astype(pair.dtype)


def stacked(pair):
    first = lane_low(pair.shape)
    zero = jnp.zeros_like(pair)
    return jnp.concatenate([jnp.where(first, pair, zero), jnp.where(first, zero, pair)], axis=0)


def unstacked(rows):
    half = rows.shape[0] // 2
    return jnp.where(lane_low((half, rows.shape[1])), rows[:half], rows[half:])


def allowed_pairs(start_column, start_row):
    shape = (start_column.shape[0], start_row.shape[1])
    query_places = lax.broadcasted_iota(jnp.int32, shape, 0)
    key_places = lax.broadcasted_iota(jnp.int32, shape, 1)
    one = (start_column == start_row) & (key_places <= query_places)
    return jnp.where(jnp.concatenate([one, one], axis=0), 0.0, masked_score)


def block_lanes(ref, block):
    return ref[:, block * 2 * HEAD : (block + 1) * 2 * HEAD]


def attend_pair(block, query_ref, pair_ref, bias):
    key = twice(block_lanes(pair_ref, block // 2), block % 2 == 1)
    value = twice(block_lanes(pair_ref, KVHEADS // 2 + block // 2), block % 2 == 1)
    queries = stacked(block_lanes(query_ref, block))
    scores = dot_nt(queries, key) * (1.0 / math.sqrt(HEAD)) + bias
    return (queries, key, value, scores)


def project_inputs(normed, weights, query_ref, pair_ref, table_ref):
    queries = dot_nn(normed, weights(0))
    for block in range(NHEADS // 2):
        lanes = slice(block * 2 * HEAD, (block + 1) * 2 * HEAD)
        query_ref[:, lanes] = rotate(queries[:, lanes], table_ref, 1.0).astype(jnp.bfloat16)
    pairs = dot_nn(normed, weights(1))
    for block in range(KVHEADS):
        lanes = slice(block * 2 * HEAD, (block + 1) * 2 * HEAD)
        value = pairs[:, lanes]
        if block < KVHEADS // 2:
            value = rotate(value, table_ref, 1.0)
        pair_ref[:, lanes] = value.astype(jnp.bfloat16)


def attend_forward(blocks, query_ref, pair_ref, bias, head_ref, total_ref):
    for block in blocks:
        _, _, value, scores = attend_pair(block, query_ref, pair_ref, bias)
        row_max = jnp.max(scores, axis=-1, keepdims=True)
        exponents = jnp.exp(scores - row_max)
        totals = jnp.sum(exponents, axis=-1, keepdims=True)
        softmax_low = (exponents * (1.0 / totals)).astype(jnp.bfloat16)
        head_ref[:, block * 2 * HEAD : (block + 1) * 2 * HEAD] = unstacked(
            dot_nn(softmax_low, value)
        ).astype(jnp.bfloat16)
        total_ref[:, block : block + 1] = row_max + jnp.log(totals)


def attend_backward(query_ref, pair_ref, bias, total_ref, grad_ref, table_ref, delta_ref):
    folded = []
    for block in range(KVHEADS):
        queries, key, value, scores = attend_pair(block, query_ref, pair_ref, bias)
        grads = stacked(block_lanes(grad_ref, block))
        softmax_full = jnp.exp(scores - total_ref[:, block : block + 1])
        grad_softmax = dot_nt(grads, value)
        inner = jnp.sum(softmax_full * grad_softmax, axis=-1, keepdims=True)
        grad_scores = (softmax_full * (grad_softmax - inner)).astype(jnp.bfloat16)
        scale = 1.0 / math.sqrt(HEAD)
        grad_query = unstacked(dot_nn(grad_scores, key)) * scale
        lanes = slice(block * 2 * HEAD, (block + 1) * 2 * HEAD)
        delta_ref[:, lanes] = rotate(grad_query, table_ref, -1.0).astype(jnp.bfloat16)
        grad_key = dot_tn(grad_scores, queries) * scale
        grad_value = dot_tn(softmax_full.astype(jnp.bfloat16), grads)
        folded.append(
            (
                grad_key + pltpu.roll(grad_key, HEAD, 1),
                grad_value + pltpu.roll(grad_value, HEAD, 1),
            )
        )
        if block % 2 == 1:
            first = lane_low(grad_key.shape)
            both = [jnp.where(first, low, high) for low, high in zip(*folded)]
            folded = []
            base = NHEADS * HEAD + (block // 2) * 2 * HEAD
            delta_ref[:, base : base + 2 * HEAD] = rotate(both[0], table_ref, -1.0).astype(
                jnp.bfloat16
            )
            base = base + KVHEADS * HEAD
            delta_ref[:, base : base + 2 * HEAD] = both[1].astype(jnp.bfloat16)


def rotary_tables(positions):
    half_size = HEAD // 2
    frequency = rotary_base ** (-(jnp.arange(half_size, dtype=jnp.float32) * 2.0) / HEAD)
    angles = positions.astype(jnp.float32)[:, None] * frequency[None, :]
    cosine, sine = (jnp.cos(angles), jnp.sin(angles))
    zero = jnp.zeros_like(sine)
    return jnp.stack(
        [
            jnp.concatenate([cosine] * 4, axis=1),
            jnp.concatenate([-sine, zero] * 2, axis=1),
            jnp.concatenate([zero, sine] * 2, axis=1),
        ]
    )


def newton_parts(grams):
    a, b, c = newton_first, newton_second, newton_third

    def times(left, right):
        return jnp.dot(left, right, preferred_element_type=jnp.float32)

    lows = [gram.astype(jnp.bfloat16) for gram in grams]
    firsts = [b * gram + c * times(low, low) for gram, low in zip(grams, lows)]
    first_lows = [first.astype(jnp.bfloat16) for first in firsts]
    mixes = [times(low, first) for low, first in zip(lows, first_lows)]
    nexts = [
        (a * a) * gram + (2.0 * a) * mix + times(mix.astype(jnp.bfloat16), first)
        for gram, mix, first in zip(grams, mixes, first_lows)
    ]
    next_lows = [gram.astype(jnp.bfloat16) for gram in nexts]
    seconds = [b * gram + c * times(low, low) for gram, low in zip(nexts, next_lows)]
    second_lows = [second.astype(jnp.bfloat16) for second in seconds]
    return list(zip(firsts, first_lows, seconds, second_lows))


def scaled_gram(gram):
    shape = gram.shape
    rows = lax.broadcasted_iota(jnp.int32, shape, 0)
    diagonal = rows == lax.broadcasted_iota(jnp.int32, shape, 1)
    inverse = 1.0 / (jnp.sqrt(jnp.sum(jnp.where(diagonal, gram, 0.0))) + 1e-07)
    return (gram * (inverse * inverse), inverse)


def expert_update_kernel(kinds, scale, *refs):
    a = newton_first
    grads_ref = refs[0]
    moments = refs[1 : 1 + len(kinds)]
    outs = refs[1 + len(kinds) :]
    half = grads_ref.shape[3]
    tall = kinds[0] < 2
    states = []
    for index in range(len(kinds)):
        for e in range(grads_ref.shape[0]):
            grad = grads_ref[e, index].astype(jnp.float32)
            if not tall:
                grad = jnp.concatenate([grad[:half], grad[half:]], axis=1)
            moment = momentum_keep * moments[index][e] + grad
            outs[3 * index][e] = grad
            outs[3 * index + 1][e] = moment
            low = moment.astype(jnp.bfloat16)
            sides = (((0,), (0,)), ((), ())) if tall else (((1,), (1,)), ((), ()))
            gram, inverse = scaled_gram(
                lax.dot_general(low, low, sides, preferred_element_type=jnp.float32)
            )
            states.append((index, e, inverse, low, gram))
    parts = newton_parts([state[-1] for state in states])
    for (index, e, inverse, low, _), (first, first_low, second, second_low) in zip(states, parts):
        rest = a * (first + second) + jnp.dot(
            first_low, second_low, preferred_element_type=jnp.float32
        )
        rest = ((-scale * inverse) * rest).astype(jnp.bfloat16)
        if tall:
            step = jnp.dot(low, rest, preferred_element_type=jnp.float32)
        else:
            step = jnp.dot(rest, low, preferred_element_type=jnp.float32)
        outs[3 * index + 2][e] = (-scale * a * a * inverse) * outs[3 * index + 1][e] + step


def expert_update(grads, kinds, moments):
    count, rows, columns = moments[0].shape
    group = 2 // len(kinds)
    scale = rate_matrix * math.sqrt(max(1.0, columns / rows))
    block = pl.BlockSpec((group, rows, columns), lambda i: (i, 0, 0))
    place = kinds[0] // len(kinds)
    taken = pl.BlockSpec((group, len(kinds)) + grads.shape[2:], lambda i: (i, place, 0, 0))
    shape = jax.ShapeDtypeStruct(moments[0].shape, jnp.float32)
    return pl.pallas_call(
        functools.partial(expert_update_kernel, kinds, scale),
        grid=(count // group,),
        in_specs=[taken] + [block] * len(kinds),
        out_specs=[block] * (3 * len(kinds)),
        out_shape=[shape] * (3 * len(kinds)),
        compiler_params=pltpu.CompilerParams(vmem_limit_bytes=60 * 1024 * 1024),
        name="expert_update",
        cost_estimate=pl.CostEstimate(
            flops=count * len(kinds) * 2500000000,
            bytes_accessed=moments[0].size * len(kinds) * 18,
            transcendentals=0,
        ),
    )(grads, *moments)


def dense_update_kernel(layout, place_ref, next_ref, grads_ref, *refs):
    a = newton_first
    amount = len(layout)
    own_moments = refs[:amount]
    outs = refs[amount : 3 * amount]
    updates = refs[3 * amount : 3 * amount + 2]
    matrices = refs[3 * amount + 2 : 3 * amount + 4]
    own_grads = refs[3 * amount + 4]
    blocks, count, block_rows, width = next_ref.shape
    part = width // 3
    me = place_ref[0]
    core = place_ref[1]
    start = pl.multiple_of(me * block_rows, block_rows)

    for block in range(blocks):
        outer = slice(block * part, (block + 1) * part)
        lanes = pl.ds(pl.multiple_of(2 * core * part, part), part)
        matrices[0][:, outer] = next_ref[block, :, :, lanes].reshape(count * block_rows, part)
        for index in range(3):
            columns = slice(8 * part * index + block * part, 8 * part * index + (block + 1) * part)
            inner = slice(index * part, (index + 1) * part)
            own_grads[:, columns] = grads_ref[block, :, inner].astype(jnp.float32)
    for block in range(blocks // 2):
        outer = slice(block * part, (block + 1) * part)
        matrices[1][:, outer] = next_ref[
            core * (blocks // 2) + block, :, :, part : 2 * part
        ].reshape(count * block_rows, part)
    for index, (begin, size) in enumerate(layout):
        grad = own_grads[:, begin : begin + size]
        outs[2 * index][...] = grad
        outs[2 * index + 1][...] = momentum_keep * own_moments[index][...] + grad
    states = []
    for matrix in matrices:
        low = matrix[...]
        states.append(
            scaled_gram(
                lax.dot_general(
                    low, low, (((0,), (0,)), ((), ())), preferred_element_type=jnp.float32
                )
            )
        )
    parts = newton_parts([state[0] for state in states])
    for matrix, update, (_, inverse), (_, first_low, _, second_low) in zip(
        matrices, updates, states, parts
    ):
        rows, columns = matrix.shape
        scale = rate_matrix * math.sqrt(max(1.0, columns / rows))
        own = matrix[pl.ds(start, block_rows)]
        once = a * own.astype(jnp.float32) + jnp.dot(
            own, first_low, preferred_element_type=jnp.float32
        )
        update[...] = (-scale * inverse) * (
            a * once
            + jnp.dot(once.astype(jnp.bfloat16), second_low, preferred_element_type=jnp.float32)
        )


def dense_update(nexts, grads, own_moments, layout, shard_index, rep_index):
    _, count, block_rows, _ = nexts.shape
    width = own_moments[0].shape[1]
    whole = lambda shape: pl.BlockSpec(shape, lambda i: (0,) * len(shape))
    shapes = []
    for _, size in layout:
        shapes += [jax.ShapeDtypeStruct((block_rows, size), jnp.float32)] * 2
    shapes += [
        jax.ShapeDtypeStruct((block_rows, width), jnp.float32),
        jax.ShapeDtypeStruct((block_rows, width // 2), jnp.float32),
    ]
    place = jnp.stack([shard_index, rep_index % 2]).astype(jnp.int32)
    return pl.pallas_call(
        functools.partial(dense_update_kernel, layout),
        grid=(1,),
        in_specs=[pl.BlockSpec(memory_space=pltpu.SMEM), whole(nexts.shape), whole(grads.shape)]
        + [whole(moment.shape) for moment in own_moments],
        out_specs=[whole(shape.shape) for shape in shapes],
        out_shape=shapes,
        scratch_shapes=[
            pltpu.VMEM((count * block_rows, width), jnp.bfloat16),
            pltpu.VMEM((count * block_rows, width // 2), jnp.bfloat16),
            pltpu.VMEM((block_rows, 3 * width), jnp.float32),
        ],
        compiler_params=pltpu.CompilerParams(vmem_limit_bytes=63 * 1024 * 1024),
        name="dense_update",
        cost_estimate=pl.CostEstimate(
            flops=14000000000, bytes_accessed=24 * width * width, transcendentals=0
        ),
    )(place, nexts, grads, *own_moments)


LAYOUT = ((0, 1024), (1024, 512), (1536, 512), (2048, 1024))


MESH = pl.DeviceIdType.MESH


def flip(index, bit):
    return index + bit - 2 * bit * ((index // bit) % 2)


def greet(peers):
    barrier = pltpu.get_barrier_semaphore()
    for peer in peers:
        pl.semaphore_signal(barrier, inc=1, device_id=peer, device_id_type=MESH)
    pl.semaphore_wait(barrier, len(peers))


def stream_plan(rep, bits, base, size):
    stages = []
    starts = [base, base + size]
    for step in range(len(bits)):
        size = size // 2
        stage = []
        for stream in range(2):
            bit = bits[(step + stream) % len(bits)]
            side = (rep // bit) % 2
            keep = starts[stream] + side * size
            send = starts[stream] + (1 - side) * size
            starts[stream] = keep
            stage.append((bit, stream, keep, send, size))
        stages.append(stage)
    return stages


def rows_of(start, size):
    return pl.ds(pl.multiple_of(start, 16), size)


def moe_kernel(
    count,
    bits,
    own_ref,
    cot_ref,
    weight_ref,
    gate_hbm,
    up_hbm,
    down_hbm,
    stage_out,
    back_ref,
    share_ref,
    tok,
    turned,
    mats,
    hid,
    gate_delta,
    up_delta,
    stage_back,
    got_back,
    sum_back,
    sum_out,
    *rest,
):
    landing = rest[: 1 + 2 * len(bits)]
    (
        load_sem,
        right_sem,
        left_sem,
        arrive_sem,
        back_send,
        back_recv,
        sum_send,
        sum_recv,
    ) = rest[1 + 2 * len(bits) :]
    rep = lax.axis_index("rep")
    me = lax.axis_index("shard")
    experts = mats.shape[0]
    tokens = own_ref.shape[0]
    half = mats.shape[2] // 2
    core = rep % 2

    loads = [
        pltpu.make_async_copy(gate_hbm, mats.at[:, 0], load_sem.at[0]),
        pltpu.make_async_copy(up_hbm, mats.at[:, 1], load_sem.at[1]),
        pltpu.make_async_copy(
            down_hbm.at[:, :, pl.ds(0, half)], mats.at[:, 2, pl.ds(0, half)], load_sem.at[2]
        ),
        pltpu.make_async_copy(
            down_hbm.at[:, :, pl.ds(half, half)], mats.at[:, 2, pl.ds(half, half)], load_sem.at[3]
        ),
    ]
    for load in loads:
        load.start()
    peers = [(rep, lax.rem(me + k, count)) for k in range(1, count)]
    peers += [(flip(rep, bit), me) for bit in (1,) + bits]
    greet(peers)

    right_peer = (rep, jnp.minimum(me + 1, count - 1))
    left_peer = (rep, jnp.maximum(me - 1, 0))

    def hand_on(block, to_right):
        return pltpu.make_async_remote_copy(
            src_ref=tok.at[block],
            dst_ref=tok.at[block],
            send_sem=(right_sem if to_right else left_sem).at[block],
            recv_sem=arrive_sem.at[block],
            device_id=right_peer if to_right else left_peer,
            device_id_type=MESH,
        )

    def returning(stage, got, send_sem, recv_sem, block):
        return pltpu.make_async_remote_copy(
            src_ref=stage.at[block],
            dst_ref=got.at[me],
            send_sem=send_sem.at[block],
            recv_sem=recv_sem.at[me],
            device_id=(rep, block),
            device_id_type=MESH,
        )

    tok[me] = own_ref[...]

    @pl.when(me < count - 1)
    def _():
        hand_on(me, True).start()

    @pl.when(me > 0)
    def _():
        hand_on(me, False).start()

    for load in loads:
        load.wait()

    margin = jnp.minimum(me, count - 1 - me)
    longer = jnp.where(me < count - 1 - me, 1, -1)
    inward = jnp.where(2 * me < count, 1, -1)
    nt = (((1,), (1,)), ((), ()))

    def dot(left, right):
        return jnp.dot(left, right, preferred_element_type=jnp.float32)

    def dot_nt(left, right):
        return lax.dot_general(left, right, nt, preferred_element_type=jnp.float32)

    def arrivals(j):
        lower = me - j
        upper = me + j

        @pl.when((j > 0) & (lower >= 0))
        def _():
            hand_on(jnp.maximum(lower, 0), True).wait_recv()

            @pl.when(me < count - 1)
            def _():
                hand_on(jnp.maximum(lower, 0), True).start()

        @pl.when((j > 0) & (upper < count))
        def _():
            hand_on(jnp.minimum(upper, count - 1), False).wait_recv()

            @pl.when(me > 0)
            def _():
                hand_on(jnp.minimum(upper, count - 1), False).start()

    def block_at(j):
        near = (j + 1) // 2
        alternating = me + near - 2 * near * (j % 2)
        return jnp.where(j <= 2 * margin, alternating, me + longer * (j - margin))

    def places_of(block):
        return pl.ds(pl.multiple_of(block * tokens, tokens), tokens)

    def factors(e, block):
        places = places_of(block)
        rows = tok[block]
        grads = cot_ref[block]
        weight = weight_ref[block, :, e : e + 1]
        u = dot(rows, mats[e, 0])
        w = dot(rows, mats[e, 1])
        gate = 1.0 / (1.0 + jnp.exp(-u))
        act = u * gate
        hidden = (weight * (act * w)).astype(jnp.bfloat16)
        hid[e, :, places] = hidden.T
        pulled = weight * (
            dot_nt(grads[:, :half], mats[e, 2, :half])
            + dot_nt(grads[:, half:], mats[e, 2, half:])
        )
        gate_delta[e, places] = (pulled * w * (gate + act * (1.0 - gate))).astype(jnp.bfloat16)
        up_delta[e, places] = (pulled * act).astype(jnp.bfloat16)
        return hidden

    def sums(block, e, hidden, place):
        places = places_of(block)
        for side in range(2):
            part = slice(side * half, (side + 1) * half)
            back = dot_nt(gate_delta[e, places], mats[e, 0, part]) + dot_nt(
                up_delta[e, places], mats[e, 1, part]
            )
            out = dot(hidden, mats[e, 2, part])
            if e > 0:
                back = place[0][:, part] + back
                out = place[1][:, part] + out
            place[0][:, part] = back
            place[1][:, part] = out

    def visit(j, carry):
        arrivals(j)
        block = block_at(j)
        places = places_of(block)
        turned[:, places] = tok[block].T
        hiddens = [factors(e, block) for e in range(experts)]
        for side in range(2):
            part = slice(side * half, (side + 1) * half)
            total_back = None
            total_out = None
            for e in range(experts):
                back = dot_nt(gate_delta[e, places], mats[e, 0, part]) + dot_nt(
                    up_delta[e, places], mats[e, 1, part]
                )
                out = dot(hiddens[e], mats[e, 2, part])
                total_back = back if e == 0 else total_back + back
                total_out = out if e == 0 else total_out + out
            stage_back[block, :, part] = total_back.astype(jnp.bfloat16)
            stage_out[block, :, part] = total_out.astype(jnp.bfloat16)

        @pl.when((j > 0) & ((block - me) * inward > 0))
        def _():
            returning(stage_back, got_back, back_send, back_recv, block).start()

        return carry

    lax.fori_loop(0, count - 1, visit, 0)
    arrivals(count - 1)
    last = block_at(count - 1)
    for k in range(1, count):
        block = block_at(k - 1)

        @pl.when((block - me) * inward < 0)
        def _():
            returning(stage_back, got_back, back_send, back_recv, block).start()

    turned[:, places_of(last)] = tok[last].T
    plan = stream_plan(rep, bits, core * half, half // 2)

    def sum_copy(stage, slot, e, start, size, bit):
        return pltpu.make_async_remote_copy(
            src_ref=mats.at[e, :, rows_of(start, size)],
            dst_ref=landing[slot].at[e],
            send_sem=sum_send.at[slot, e],
            recv_sem=sum_recv.at[slot, e],
            device_id=(flip(rep, bit), me),
            device_id_type=MESH,
        )

    def copies(stage, e):
        if stage == 0:
            return [(sum_copy(0, 0, e, (1 - core) * half, half, 1), 0, core * half, half)]
        return [
            (
                sum_copy(stage, 1 + 2 * (stage - 1) + stream, e, send, size, bit),
                1 + 2 * (stage - 1) + stream,
                keep,
                size,
            )
            for bit, stream, keep, send, size in plan[stage - 1]
        ]

    def finish(stage, e):
        for copy, slot, keep, size in copies(stage, e):
            copy.wait_recv()
            place = rows_of(keep, size)
            for kind in range(3):
                mats[e, kind, place] = (
                    mats[e, kind, place].astype(jnp.float32)
                    + landing[slot][e, kind].astype(jnp.float32)
                ).astype(jnp.bfloat16)

    stages = 1 + len(bits)
    for turn in range(experts + stages):
        if turn < experts:
            e = turn
            sums(last, e, factors(e, last), (sum_back, sum_out))
            for side in range(2):
                part = slice(side * half, (side + 1) * half)
                mats[e, 0, part] = dot(turned[part], gate_delta[e]).astype(jnp.bfloat16)
                mats[e, 1, part] = dot(turned[part], up_delta[e]).astype(jnp.bfloat16)
                mats[e, 2, part] = dot(hid[e], cot_ref[:, :, part].reshape(count * tokens, half)).astype(jnp.bfloat16)
            copies(0, e)[0][0].start()
            if e == experts - 1:
                stage_back[last] = sum_back[...].astype(jnp.bfloat16)
                stage_out[last] = sum_out[...].astype(jnp.bfloat16)
                returning(stage_back, got_back, back_send, back_recv, last).start()
        for stage in range(stages):
            e = turn - 1 - stage
            if 0 <= e < experts:
                finish(stage, e)
                if stage + 1 < stages:
                    for copy, _, _, _ in copies(stage + 1, e):
                        copy.start()
                else:
                    for _, stream, keep, _, size in plan[-1]:
                        share_ref[e, :, stream] = mats[e, :, rows_of(keep, size)]

    total = stage_back[me].astype(jnp.float32)
    for k in range(1, count):
        source = lax.rem(me + k, count)
        pltpu.make_async_remote_copy(
            src_ref=stage_back.at[source],
            dst_ref=got_back.at[source],
            send_sem=back_send.at[source],
            recv_sem=back_recv.at[source],
            device_id=(rep, source),
            device_id_type=MESH,
        ).wait_recv()
        total = total + got_back[source].astype(jnp.float32)
    back_ref[...] = total
    for k in range(1, count):
        block = lax.rem(me + k, count)
        returning(stage_back, got_back, back_send, back_recv, block).wait_send()
    for e in range(experts):
        for stage in range(stages):
            for copy, _, _, _ in copies(stage, e):
                copy.wait_send()
    for block in range(count):

        @pl.when((block <= me) & (me < count - 1))
        def _():
            hand_on(block, True).wait_send()

        @pl.when((block >= me) & (me > 0))
        def _():
            hand_on(block, False).wait_send()


def moe(normed, cotangents, weights, gate_proj, up_proj, down_proj, bits, count):
    tokens, width = normed.shape
    experts, _, hidden = gate_proj.shape
    half = width // 2
    low = jnp.bfloat16
    final = (half // 2) >> len(bits)
    vmem = pl.BlockSpec(memory_space=pltpu.VMEM)
    anywhere = pl.BlockSpec(memory_space=pl.ANY)
    landings = [pltpu.VMEM((experts, 3, half, hidden), low)]
    for step in range(len(bits)):
        size = (half // 2) >> (step + 1)
        landings += [pltpu.VMEM((experts, 3, size, hidden), low)] * 2
    slots = len(landings)
    dma = pltpu.SemaphoreType.DMA
    return pl.pallas_call(
        functools.partial(moe_kernel, count, bits),
        in_specs=[vmem, vmem, vmem, anywhere, anywhere, anywhere],
        out_specs=[vmem, vmem, vmem],
        out_shape=[
            jax.ShapeDtypeStruct((count, tokens, width), low),
            jax.ShapeDtypeStruct((tokens, width), jnp.float32),
            jax.ShapeDtypeStruct((experts, 3, 2, final, hidden), low),
        ],
        scratch_shapes=[
            pltpu.VMEM((count, tokens, width), low),
            pltpu.VMEM((width, count * tokens), low),
            pltpu.VMEM((experts, 3, width, hidden), low),
            pltpu.VMEM((experts, hidden, count * tokens), low),
            pltpu.VMEM((experts, count * tokens, hidden), low),
            pltpu.VMEM((experts, count * tokens, hidden), low),
            pltpu.VMEM((count, tokens, width), low),
            pltpu.VMEM((count, tokens, width), low),
            pltpu.VMEM((tokens, width), jnp.float32),
            pltpu.VMEM((tokens, width), jnp.float32),
        ]
        + landings
        + [
            dma((4,)),
            dma((count,)),
            dma((count,)),
            dma((count,)),
            dma((count,)),
            dma((count,)),
            dma((slots, experts)),
            dma((slots, experts)),
        ],
        compiler_params=pltpu.CompilerParams(
            collective_id=1, has_side_effects=True, vmem_limit_bytes=63 * 1024 * 1024
        ),
        name="moe",
        cost_estimate=pl.CostEstimate(
            flops=39000000000, bytes_accessed=20000000, transcendentals=2000000
        ),
    )(normed, cotangents, weights, gate_proj, up_proj, down_proj)


def rep_bits(rep_count):
    bits = []
    bit = 2
    while bit < rep_count:
        bits.append(bit)
        bit = bit * 2
    return tuple(bits)


def spread_kernel(
    count,
    bits,
    share_ref,
    returned_ref,
    normed_ref,
    head_ref,
    weights_ref,
    small_ref,
    tokens_ref,
    cot_ref,
    second_ref,
    middle_ref,
    query_ref,
    pair_ref,
    total_ref,
    table_ref,
    column_ref,
    row_ref,
    query_moment,
    key_moment,
    value_moment,
    out_moment,
    experts_hbm,
    dense_out,
    grads_out,
    gains_out,
    tokens_out,
    mixed_out,
    experts_out,
    got_ref,
    moment_piece,
    delta_ref,
    branch_ref,
    heads_ref,
    dense_ref,
    total,
    land_core,
    land_first,
    *rest,
):
    later = len(bits) - 1
    land_later = rest[:later]
    (
        piece_send,
        piece_land,
        piece,
        gains_send,
        gains_land,
        gains_all,
        local_sem,
        core_send,
        core_recv,
        half_send,
        half_recv,
        shard_send,
        shard_recv,
        grow_send,
        grow_recv,
        line_send,
        line_recv,
        join_send,
        join_recv,
        expert_send,
        expert_recv,
        gain_send,
        gain_recv,
        gain_line_send,
        gain_line_recv,
        back_send,
        back_recv,
        moment_sem,
        own_send,
        own_recv,
        own_join_send,
        own_join_recv,
    ) = rest[later:]
    rep = lax.axis_index("rep")
    me = lax.axis_index("shard")
    core = rep % 2
    rows = dense_ref.shape[2]
    expert_rows = experts_out.shape[2]
    steps = len(bits)
    streams = range(2)

    def remote(source, target, send_sem, recv_sem, peer):
        return pltpu.make_async_remote_copy(
            src_ref=source,
            dst_ref=target,
            send_sem=send_sem,
            recv_sem=recv_sem,
            device_id=peer,
            device_id_type=MESH,
        )

    def across(bit):
        return (flip(rep, bit), me)

    def order(stream):
        return [bits[(step + stream) % steps] for step in range(steps)]

    def side(bit):
        return (rep // bit) % 2

    plan = stream_plan(rep, bits, core * (expert_rows // 2), expert_rows // 4)
    base = [(core * (expert_rows // 2)) + stream * (expert_rows // 4) for stream in streams]

    def expert_copy(level, stream):
        if level == steps:
            place = rows_of(base[stream], expert_rows // 4)
            peer = across(1)
        else:
            bit, _, keep, _, size = plan[steps - 1 - level][stream]
            place = rows_of(keep, size)
            peer = across(bit)
        source = experts_out.at[:, :, place]
        if level == 0:
            source = share_ref.at[:, :, stream]
        return remote(
            source,
            experts_out.at[:, :, place],
            expert_send.at[level, stream],
            expert_recv.at[level, stream],
            peer,
        )

    def own_copy(stream):
        _, _, keep, _, size = plan[-1][stream]
        return pltpu.make_async_copy(
            share_ref.at[:, :, stream],
            experts_out.at[:, :, rows_of(keep, size)],
            local_sem.at[stream],
        )

    for stream in streams:
        own_copy(stream).start()
    peers = [(rep, lax.rem(me + k, count)) for k in range(1, count)]
    peers += [across(bit) for bit in (1,) + bits]
    greet(peers)

    def returning(peer, source):
        return remote(
            returned_ref.at[peer],
            got_ref.at[source],
            back_send.at[peer],
            back_recv.at[source],
            (rep, peer),
        )

    def core_copy(block):
        return remote(
            dense_ref.at[4 * (1 - core) + block],
            land_core.at[block],
            core_send.at[block],
            core_recv.at[block],
            across(1),
        )

    gain_bits = (1,) + bits

    def gain_copy(stage):
        return remote(
            gains_send.at[stage],
            gains_land.at[stage],
            gain_send.at[stage],
            gain_recv.at[stage],
            across(gain_bits[stage]),
        )

    for stream in streams:
        expert_copy(0, stream).start()

    for k in range(1, count):
        returning(lax.rem(me + k, count), me).start()

    def whole(index):
        return weights_ref[index].reshape(count * rows, -1)

    def gain(index):
        at = EXPERTS + index
        return jnp.concatenate([small_ref[z, at : at + 1, :rows] for z in range(count)], axis=1)

    scaled, inverse = normalize(middle_ref[...])
    middle_extra, midnorm_part = normalize_back(second_ref[...], gain(1), scaled, inverse)
    grad_middle = cot_ref[...].astype(jnp.float32) + middle_extra
    tokens_out[...] = grad_middle
    branch_ref[...] = grad_middle.astype(jnp.bfloat16)
    heads_ref[...] = dot_nt(branch_ref[...], whole(2)).astype(jnp.bfloat16)
    bias = allowed_pairs(column_ref[...], row_ref[...])
    attend_backward(query_ref, pair_ref, bias, total_ref, heads_ref, table_ref, delta_ref)

    part = dense_ref.shape[3] // 3
    normed_turned = normed_ref[...].T
    head_turned = head_ref[...].T

    def make_block(block):
        def columns(ref, offset):
            return ref[:, pl.ds(pl.multiple_of(offset + block * part, part), part)]

        pair = jnp.concatenate([columns(delta_ref, 0), columns(delta_ref, 8 * part)], axis=1)
        left = jnp.dot(normed_turned, pair, preferred_element_type=jnp.float32)
        right = jnp.dot(head_turned, columns(branch_ref, 0), preferred_element_type=jnp.float32)
        for line in range(count):
            place = slice(line * rows, (line + 1) * rows)
            dense_ref[block, line, :, : 2 * part] = left[place].astype(jnp.bfloat16)
            dense_ref[block, line, :, 2 * part :] = right[place].astype(jnp.bfloat16)

    for block in range(4):
        make_block(4 * (1 - core) + block)
        core_copy(block).start()
    for block in range(4):
        make_block(4 * core + block)

    def gain_step(stage):
        gain_copy(stage).wait_recv()
        gains_send[stage + 1] = gains_send[stage] + gains_land[stage]
        if stage + 1 < len(gain_bits):
            gain_copy(stage + 1).start()

    first = [side(order(stream)[0]) for stream in streams]
    held = [2 * stream + first[stream] for stream in streams]
    given = [2 * stream + 1 - first[stream] for stream in streams]

    def first_copy(stream):
        return remote(
            total.at[given[stream]],
            land_first.at[stream],
            half_send.at[0, stream],
            half_recv.at[0, stream],
            across(order(stream)[0]),
        )

    def add_core(block):
        for line in range(count):
            total[block, line] = (
                dense_ref[4 * core + block, line].astype(jnp.float32)
                + land_core[block, line].astype(jnp.float32)
            ).astype(jnp.bfloat16)

    for block in range(4):
        core_copy(block).wait_recv()
    for stream in streams:
        add_core(given[stream])
        first_copy(stream).start()
    for stream in streams:
        add_core(held[stream])
    grad_first = dot_nt(delta_ref[:, : NHEADS * HEAD], whole(0)) + dot_nt(
        delta_ref[:, NHEADS * HEAD :], whole(1)
    )
    scaled, inverse = normalize(tokens_ref[...].astype(jnp.float32))
    input_extra, prenorm_part = normalize_back(grad_first, gain(0), scaled, inverse)
    tokens_out[...] = tokens_out[...] + input_extra
    gains_send[0] = jnp.concatenate(
        [prenorm_part, midnorm_part, jnp.zeros((6, prenorm_part.shape[1]), jnp.float32)], axis=0
    )
    gain_copy(0).start()
    gain_step(0)

    starts = []
    for stream in streams:
        start, size, line = 0, rows, []
        for step in range(1, steps):
            size = size // 2
            near = side(order(stream)[step])
            line.append((start + near * size, start + (1 - near) * size, size))
            start = start + near * size
        starts.append((start, size, line))

    last = starts[0][1]
    places = [rows_of(starts[stream][0], last) for stream in streams]
    inner = [slice(index * part, (index + 1) * part) for index in range(3)]

    def moment_copy(stream, index):
        block = 4 * core + held[stream]
        lanes = pl.ds(pl.multiple_of((held[stream] if index == 1 else block) * part, part), part)
        source = (query_moment, key_moment, out_moment)[index]
        return pltpu.make_async_copy(
            source.at[places[stream], lanes],
            moment_piece.at[stream, :, inner[index]],
            moment_sem.at[stream, index],
        )

    def moment_other(stream):
        lanes = pl.ds(pl.multiple_of(held[stream] * part, part), part)
        return pltpu.make_async_copy(
            value_moment.at[places[stream], lanes],
            moment_piece.at[stream, :, inner[1]],
            moment_sem.at[stream, 1],
        )

    for stream in streams:
        moment_copy(stream, 0).start()
        moment_copy(stream, 2).start()

        @pl.when(core == 0)
        def _():
            moment_copy(stream, 1).start()

        @pl.when(core == 1)
        def _():
            moment_other(stream).start()

    def later_copy(step, stream):
        keep, send, size = starts[stream][2][step - 1]
        return remote(
            total.at[held[stream], :, rows_of(send, size)],
            land_later[step - 1].at[stream],
            half_send.at[step, stream],
            half_recv.at[step, stream],
            across(order(stream)[step]),
        )

    for stream in streams:
        first_copy(stream).wait_recv()
        for line in range(count):
            total[held[stream], line] = (
                total[held[stream], line].astype(jnp.float32)
                + land_first[stream, line].astype(jnp.float32)
            ).astype(jnp.bfloat16)
        if steps > 1:
            later_copy(1, stream).start()
    gain_step(1)

    for step in range(1, steps):
        for stream in streams:
            later_copy(step, stream).wait_recv()
            keep, _, size = starts[stream][2][step - 1]
            for line in range(count):
                place = rows_of(keep, size)
                total[held[stream], line, place] = (
                    total[held[stream], line, place].astype(jnp.float32)
                    + land_later[step - 1][stream, line].astype(jnp.float32)
                ).astype(jnp.bfloat16)
            if step + 1 < steps:
                later_copy(step + 1, stream).start()
        gain_step(step + 1)

    for stream in streams:
        own_copy(stream).wait()
        expert_copy(0, stream).wait_recv()
        if steps > 1:
            expert_copy(1, stream).start()

    for stream in streams:
        for line in range(count):
            piece_send[line, stream] = total[held[stream], line, places[stream]]

    def shard_copy(k):
        target = lax.rem(me + k, count)
        return remote(
            piece_send.at[target],
            piece_land.at[me],
            shard_send.at[target],
            shard_recv.at[me],
            (rep, target),
        )

    def shard_arrival(source):
        return remote(
            piece_send.at[source],
            piece_land.at[source],
            shard_send.at[source],
            shard_recv.at[source],
            (rep, source),
        )

    def gain_line(k):
        target = lax.rem(me + k, count)
        return remote(
            gains_send.at[len(gain_bits)],
            gains_all.at[me],
            gain_line_send.at[target],
            gain_line_recv.at[me],
            (rep, target),
        )

    def gain_arrival(source):
        return remote(
            gains_send.at[len(gain_bits)],
            gains_all.at[source],
            gain_line_send.at[source],
            gain_line_recv.at[source],
            (rep, source),
        )

    def own_grow(step, stream):
        block = 4 * core + held[stream]
        if step == 0:
            part_ref = grads_out.at[block]
        else:
            keep, _, size = starts[stream][2][step - 1]
            part_ref = grads_out.at[block, rows_of(keep, size)]
        return remote(
            part_ref,
            part_ref,
            own_send.at[step, stream],
            own_recv.at[step, stream],
            across(order(stream)[step]),
        )

    def own_join(stream):
        part_ref = grads_out.at[pl.ds(4 * core + 2 * stream, 2)]
        return remote(
            part_ref, part_ref, own_join_send.at[stream], own_join_recv.at[stream], across(1)
        )

    for k in range(1, count):
        shard_copy(k).start()
        gain_line(k).start()
    summed = piece_send[me].astype(jnp.float32)
    for k in range(1, count):
        source = lax.rem(me + k, count)
        shard_arrival(source).wait_recv()
        summed = summed + piece_land[source].astype(jnp.float32)
    for stream in streams:
        for index in range(3):
            moment_copy(stream, index).wait()
        grads_out[4 * core + held[stream], places[stream]] = summed[stream].astype(jnp.bfloat16)
        own_grow(steps - 1, stream).start()
    piece[...] = (momentum_keep * moment_piece[...] + summed).astype(jnp.bfloat16)

    def line_copy(k, stream):
        target = lax.rem(me + k, count)
        return remote(
            piece.at[stream],
            dense_out.at[4 * core + held[stream], me, places[stream]],
            line_send.at[stream, target],
            line_recv.at[stream, me],
            (rep, target),
        )

    def line_arrival(source, stream):
        return remote(
            piece.at[stream],
            dense_out.at[4 * core + held[stream], source, places[stream]],
            line_send.at[stream, source],
            line_recv.at[stream, source],
            (rep, source),
        )

    def own_piece(stream):
        return pltpu.make_async_copy(
            piece.at[stream],
            dense_out.at[4 * core + held[stream], me, places[stream]],
            local_sem.at[2 + stream],
        )

    for stream in streams:
        own_piece(stream).start()
        for k in range(1, count):
            line_copy(k, stream).start()
    gained = gains_send[len(gain_bits)]
    for k in range(1, count):
        source = lax.rem(me + k, count)
        gain_arrival(source).wait_recv()
        gained = gained + gains_all[source]
    gains_out[...] = gained

    for level in range(1, steps):
        for stream in streams:
            expert_copy(level, stream).wait_recv()
            expert_copy(level + 1, stream).start()
    if steps == 1:
        for stream in streams:
            expert_copy(1, stream).start()

    def grow_copy(step, stream):
        if step == 0:
            place = dense_out.at[4 * core + held[stream]]
        else:
            keep, _, size = starts[stream][2][step - 1]
            place = dense_out.at[4 * core + held[stream], :, rows_of(keep, size)]
        return remote(
            place,
            place,
            grow_send.at[step, stream],
            grow_recv.at[step, stream],
            across(order(stream)[step]),
        )

    for stream in streams:
        own_piece(stream).wait()
        for k in range(1, count):
            line_arrival(lax.rem(me + k, count), stream).wait_recv()
        grow_copy(steps - 1, stream).start()
    for step in reversed(range(steps)):
        for stream in streams:
            own_grow(step, stream).wait_recv()
            if step > 0:
                own_grow(step - 1, stream).start()
            else:
                own_join(stream).start()
    mixed = middle_ref[...] + returned_ref[me].astype(jnp.float32)
    for k in range(1, count):
        source = lax.rem(me + k, count)
        returning(source, source).wait_recv()
        mixed = mixed + got_ref[source].astype(jnp.float32)
    mixed_out[...] = mixed.astype(mixed_out.dtype)
    for stream in streams:
        expert_copy(steps, stream).wait()
    leave = pltpu.make_async_copy(experts_out, experts_hbm, local_sem.at[0])
    leave.start()
    for step in reversed(range(steps)):
        for stream in streams:
            grow_copy(step, stream).wait_recv()
            if step > 0:
                grow_copy(step - 1, stream).start()

    def join_copy(stream):
        place = dense_out.at[pl.ds(4 * core + 2 * stream, 2)]
        return remote(place, place, join_send.at[stream], join_recv.at[stream], across(1))

    for stream in streams:
        join_copy(stream).start()
    for stream in streams:
        join_copy(stream).wait()
        own_join(stream).wait()
        for step in range(steps):
            own_grow(step, stream).wait_send()
        for level in range(steps):
            expert_copy(level, stream).wait_send()
        first_copy(stream).wait_send()
        for step in range(1, steps):
            later_copy(step, stream).wait_send()
        for k in range(1, count):
            line_copy(k, stream).wait_send()
        for step in range(steps):
            grow_copy(step, stream).wait_send()
    for block in range(4):
        core_copy(block).wait_send()
    for stage in range(len(gain_bits)):
        gain_copy(stage).wait_send()
    for k in range(1, count):
        shard_copy(k).wait_send()
        gain_line(k).wait_send()
        returning(lax.rem(me + k, count), me).wait_send()
    leave.wait()


def spread(
    share, returned, normed, head_low, weights, small, tokens, cotangent, second, middle, *rest, bits, count
):
    query, pair, log_total, tables, starts, moments = rest
    experts, _, _, final, hidden = share.shape
    token_count, features = normed.shape
    rows = features // count
    width = 3 * features // 8
    dense_shape = (8, count, rows, width)
    gains_shape = (8, features)
    steps = len(bits)
    last = rows >> (steps - 1)
    low = jnp.bfloat16
    vmem = pl.BlockSpec(memory_space=pltpu.VMEM)
    dma = pltpu.SemaphoreType.DMA
    return pl.pallas_call(
        functools.partial(spread_kernel, count, bits),
        in_specs=[vmem] * 16 + [pl.BlockSpec(memory_space=pl.ANY)] * 4,
        out_specs=[pl.BlockSpec(memory_space=pl.ANY)] + [vmem] * 5,
        out_shape=[
            jax.ShapeDtypeStruct((experts, 3, 4 * (final << steps), hidden), low),
            jax.ShapeDtypeStruct(dense_shape, low),
            jax.ShapeDtypeStruct((8, rows, width), low),
            jax.ShapeDtypeStruct(gains_shape, jnp.float32),
            jax.ShapeDtypeStruct((token_count, features), jnp.float32),
            jax.ShapeDtypeStruct((token_count, features), low),
        ],
        scratch_shapes=[
            pltpu.VMEM((experts, 3, 4 * (final << steps), hidden), low),
            pltpu.VMEM((count, token_count, features), low),
            pltpu.VMEM((2, last, width), jnp.float32),
            pltpu.VMEM((token_count, 2 * features), low),
            pltpu.VMEM((token_count, features), low),
            pltpu.VMEM((token_count, features), low),
            pltpu.VMEM(dense_shape, low),
            pltpu.VMEM((4, count, rows, width), low),
            pltpu.VMEM((4, count, rows, width), low),
            pltpu.VMEM((2, count, rows, width), low),
        ]
        + [pltpu.VMEM((2, count, rows >> step, width), low) for step in range(1, steps)]
        + [
            pltpu.VMEM((count, 2, last, width), low),
            pltpu.VMEM((count, 2, last, width), low),
            pltpu.VMEM((2, last, width), low),
            pltpu.VMEM((steps + 2,) + gains_shape, jnp.float32),
            pltpu.VMEM((steps + 1,) + gains_shape, jnp.float32),
            pltpu.VMEM((count,) + gains_shape, jnp.float32),
            dma((4,)),
            dma((4,)),
            dma((4,)),
            dma((steps, 2)),
            dma((steps, 2)),
            dma((count,)),
            dma((count,)),
            dma((steps, 2)),
            dma((steps, 2)),
            dma((2, count)),
            dma((2, count)),
            dma((2,)),
            dma((2,)),
            dma((steps + 1, 2)),
            dma((steps + 1, 2)),
            dma((steps + 1,)),
            dma((steps + 1,)),
            dma((count,)),
            dma((count,)),
            dma((count,)),
            dma((count,)),
            dma((2, 3)),
            dma((steps, 2)),
            dma((steps, 2)),
            dma((2,)),
            dma((2,)),
        ],
        compiler_params=pltpu.CompilerParams(
            collective_id=2, has_side_effects=True, vmem_limit_bytes=63 * 1024 * 1024
        ),
        name="spread",
    )(
        share,
        returned,
        normed,
        head_low,
        weights,
        small,
        tokens,
        cotangent,
        second,
        middle,
        query,
        pair,
        log_total,
        tables,
        starts[:, None],
        starts[None, :],
        *moments,
    )


def gather_kernel(
    count,
    bits,
    query_weight,
    key_weight,
    value_weight,
    out_weight,
    small_ref,
    tokens_ref,
    cot_ref,
    table_ref,
    column_ref,
    row_ref,
    weights_hbm,
    small_out,
    cot_out,
    middle_out,
    first_out,
    second_out,
    query_out,
    pair_out,
    head_out,
    total_out,
    weights_out,
    weights_ref,
    local_sem,
    line_send,
    line_recv,
    grow_send,
    grow_recv,
    join_send,
    join_recv,
    small_send,
    small_recv,
    right_sem,
    left_sem,
    arrive_sem,
):
    rep = lax.axis_index("rep")
    me = lax.axis_index("shard")
    core = rep % 2
    steps = len(bits)
    streams = range(2)
    rows, width = weights_ref.shape[1:]
    half = width // 2
    fine = half // 4
    others = [lax.rem(me + k, count) for k in range(1, count)]

    def columns_of(start, size):
        return pl.ds(pl.multiple_of(start, 128), size)

    def order(stream):
        return [bits[(step + stream) % steps] for step in range(steps)]

    def side(bit):
        return (rep // bit) % 2

    narrow = width // 2
    weights_ref[0] = query_weight[...]
    weights_ref[1, :, :narrow] = key_weight[...]
    weights_ref[1, :, narrow:] = value_weight[...]
    weights_ref[2] = out_weight[...]
    own_copy = pltpu.make_async_copy(weights_ref, weights_out.at[:, me], local_sem.at[0])
    own_copy.start()
    small_out[me] = small_ref[...]
    cot_out[me] = cot_ref[...]
    peers = [(rep, other) for other in others]
    peers += [(flip(rep, bit), me) for bit in (1,) + bits]
    greet(peers)

    regions = []
    for stream in streams:
        column = core * half + stream * 2 * fine
        narrow = columns_of(column + side(order(stream)[0]) * fine, fine)
        start, size = 0, rows
        held = [(pl.ds(0, rows), narrow)]
        for step in range(1, steps):
            size = size // 2
            start = start + side(order(stream)[step]) * size
            held.append((rows_of(start, size), narrow))
        regions.append((held, columns_of(column, 2 * fine)))

    def remote(source, target, send_sem, recv_sem, peer):
        return pltpu.make_async_remote_copy(
            src_ref=source,
            dst_ref=target,
            send_sem=send_sem,
            recv_sem=recv_sem,
            device_id=peer,
            device_id_type=MESH,
        )

    def line_copy(stream, source, peer):
        place, columns = regions[stream][0][-1]
        return remote(
            weights_ref.at[:, place, columns],
            weights_out.at[:, source, place, columns],
            line_send.at[stream, peer],
            line_recv.at[stream, source],
            (rep, peer),
        )

    def grow_copy(step, stream, source):
        place, columns = regions[stream][0][step]
        part = weights_out.at[:, source, place, columns]
        return remote(
            part,
            part,
            grow_send.at[step, stream, source],
            grow_recv.at[step, stream, source],
            (flip(rep, order(stream)[step]), me),
        )

    def join_copy(stream, source):
        part = weights_out.at[:, source, :, regions[stream][1]]
        return remote(
            part,
            part,
            join_send.at[stream, source],
            join_recv.at[stream, source],
            (flip(rep, 1), me),
        )

    def small_copy(source, peer):
        return remote(
            small_ref,
            small_out.at[source],
            small_send.at[peer],
            small_recv.at[source],
            (rep, peer),
        )

    def hand_on(block, to_right):
        peer = jnp.minimum(me + 1, count - 1) if to_right else jnp.maximum(me - 1, 0)
        return remote(
            cot_out.at[block],
            cot_out.at[block],
            (right_sem if to_right else left_sem).at[block],
            arrive_sem.at[block],
            (rep, peer),
        )

    def line_start():
        @pl.when(me < count - 1)
        def _():
            hand_on(me, True).start()

        @pl.when(me > 0)
        def _():
            hand_on(me, False).start()

    def line_step(step):
        lower = me - step
        upper = me + step

        @pl.when(lower >= 0)
        def _():
            hand_on(jnp.maximum(lower, 0), True).wait_recv()

            @pl.when(me < count - 1)
            def _():
                hand_on(jnp.maximum(lower, 0), True).start()

        @pl.when(upper < count)
        def _():
            hand_on(jnp.minimum(upper, count - 1), False).wait_recv()

            @pl.when(me > 0)
            def _():
                hand_on(jnp.minimum(upper, count - 1), False).start()

    def line_send_all():
        for other in others:
            for stream in streams:
                line_copy(stream, me, other).start()

    def advance(level):
        for other in others:
            for stream in streams:
                if level == 0:
                    line_copy(stream, other, other).wait_recv()
                else:
                    grow_copy(steps - level, stream, other).wait_recv()
                if level < steps:
                    grow_copy(steps - 1 - level, stream, other).start()
                else:
                    join_copy(stream, other).start()

    for other in others:
        small_copy(me, other).start()
    line_send_all()
    for other in others:
        small_copy(other, other).wait_recv()

    def gain(index):
        at = EXPERTS + index
        return jnp.concatenate([small_out[z, at : at + 1, :rows] for z in range(count)], axis=1)

    inputs = tokens_ref[...].astype(jnp.float32)
    first_out[...] = (normalize(inputs)[0] * gain(0)).astype(jnp.bfloat16)
    advance(0)
    line_start()
    for level in range(1, steps + 1):
        advance(level)
        if level == 1:
            line_step(1)
    for other in others:
        for stream in streams:
            join_copy(stream, other).wait_recv()
    own_copy.wait()
    leave = pltpu.make_async_copy(weights_out, weights_hbm, local_sem.at[2])
    leave.start()

    def whole(index):
        return weights_out[index].reshape(count * rows, width)

    project_inputs(first_out[...], whole, query_out, pair_out, table_ref)
    bias = allowed_pairs(column_ref[...], row_ref[...])
    if count > 2:
        line_step(2)
    attend_forward(range(KVHEADS // 2), query_out, pair_out, bias, head_out, total_out)
    for step in range(3, count - 1):
        line_step(step)
    attend_forward(range(KVHEADS // 2, KVHEADS), query_out, pair_out, bias, head_out, total_out)
    middle = inputs + dot_nn(head_out[...], whole(2))
    middle_out[...] = middle
    second_out[...] = (normalize(middle)[0] * gain(1)).astype(jnp.bfloat16)
    if count > 3:
        line_step(count - 1)
    for other in others:
        for stream in streams:
            join_copy(stream, other).wait_send()
            line_copy(stream, me, other).wait_send()
            for step in range(steps):
                grow_copy(step, stream, other).wait_send()
    for other in others:
        small_copy(me, other).wait_send()
    for block in range(count):

        @pl.when((block <= me) & (me < count - 1))
        def _():
            hand_on(block, True).wait_send()

        @pl.when((block >= me) & (me > 0))
        def _():
            hand_on(block, False).wait_send()

    leave.wait()


def gather(weights, small, tokens, cotangent, tables, starts, bits, count):
    rows, width = weights[0].shape
    depth = 3
    token_count = tokens.shape[0]
    steps = len(bits)
    low = jnp.bfloat16
    vmem = pl.BlockSpec(memory_space=pltpu.VMEM)
    dma = pltpu.SemaphoreType.DMA
    whole = jax.ShapeDtypeStruct((depth, count, rows, width), low)
    features = jax.ShapeDtypeStruct((token_count, width), low)
    return pl.pallas_call(
        functools.partial(gather_kernel, count, bits),
        in_specs=[vmem] * 10,
        out_specs=[pl.BlockSpec(memory_space=pl.ANY)] + [vmem] * 9,
        out_shape=[
            whole,
            jax.ShapeDtypeStruct((count,) + small.shape, small.dtype),
            jax.ShapeDtypeStruct((count, token_count, width), low),
            jax.ShapeDtypeStruct((token_count, width), jnp.float32),
            features,
            features,
            features,
            features,
            features,
            jax.ShapeDtypeStruct((2 * token_count, KVHEADS), jnp.float32),
        ],
        scratch_shapes=[
            pltpu.VMEM(whole.shape, low),
            pltpu.VMEM((depth, rows, width), low),
            dma((3,)),
            dma((2, count)),
            dma((2, count)),
            dma((steps, 2, count)),
            dma((steps, 2, count)),
            dma((2, count)),
            dma((2, count)),
            dma((count,)),
            dma((count,)),
            dma((count,)),
            dma((count,)),
            dma((count,)),
        ],
        compiler_params=pltpu.CompilerParams(
            collective_id=3, has_side_effects=True, vmem_limit_bytes=56 * 1024 * 1024
        ),
        name="gather",
    )(
        *weights,
        small,
        tokens,
        cotangent,
        tables,
        starts[:, None],
        starts[None, :],
    )


def local(
    tokens,
    sequence_start,
    routes,
    route_weights,
    cotangent,
    query_proj,
    key_proj,
    value_proj,
    out_proj,
    prenorm,
    midnorm,
    gate_proj,
    up_proj,
    down_proj,
    query_moment,
    key_moment,
    value_moment,
    out_moment,
    prenorm_moment,
    midnorm_moment,
    gate_moment,
    up_moment,
    down_moment,
):
    shard_index = lax.axis_index("shard")
    rep_count = lax.axis_size("rep")
    shard_count = lax.axis_size("shard")
    row_block = query_proj.shape[0]
    bits = rep_bits(rep_count)
    experts_here = gate_proj.shape[0]
    dense_weights = jnp.sum(
        jnp.where(
            routes.T[None, :, :] == jnp.arange(EXPERTS, dtype=jnp.int32)[:, None, None],
            route_weights.T[None, :, :],
            0.0,
        ),
        axis=1,
    )
    gain_rows = jnp.pad(
        jnp.stack([prenorm, midnorm]).astype(jnp.float32),
        ((0, 6), (0, tokens.shape[0] - row_block)),
    )
    tables = rotary_tables(jnp.arange(tokens.shape[0], dtype=jnp.int32) - sequence_start)
    (
        weights,
        small,
        cotangent_all,
        middle,
        normed_first,
        normed_second,
        query,
        pair,
        head_low,
        log_total,
    ) = gather(
        (query_proj, key_proj, value_proj, out_proj),
        jnp.concatenate([dense_weights, gain_rows], axis=0),
        tokens,
        cotangent,
        tables,
        sequence_start,
        bits,
        shard_count,
    )
    expert_weights = lax.dynamic_slice_in_dim(
        small, shard_index * experts_here, experts_here, 1
    ).transpose(0, 2, 1)
    returned, grad_second, expert_share = moe(
        normed_second,
        cotangent_all,
        expert_weights,
        gate_proj,
        up_proj,
        down_proj,
        bits,
        shard_count,
    )
    own_moments = (query_moment, key_moment, value_moment, out_moment)
    expert_grads, dense_next, dense_grads, gains_grad, grad_tokens, mixed = spread(
        expert_share,
        returned,
        normed_first,
        head_low,
        weights,
        small,
        tokens,
        cotangent,
        grad_second,
        middle,
        query,
        pair,
        log_total,
        tables,
        sequence_start,
        own_moments,
        bits=bits,
        count=shard_count,
    )
    gains_here = lax.dynamic_slice_in_dim(gains_grad, shard_index * row_block, row_block, 1)
    prenorm_grad = gains_here[0]
    midnorm_grad = gains_here[1]
    prenorm_next = momentum_keep * prenorm_moment + prenorm_grad
    midnorm_next = momentum_keep * midnorm_moment + midnorm_grad
    prenorm_update = -rate_gain * prenorm_next
    midnorm_update = -rate_gain * midnorm_next
    rep_index = lax.axis_index("rep")
    (
        query_grad,
        query_next,
        key_grad,
        key_next,
        value_grad,
        value_next,
        out_grad,
        out_next,
        own_wide,
        own_narrow,
    ) = dense_update(
        dense_next,
        dense_grads,
        own_moments,
        LAYOUT,
        shard_index,
        rep_index,
    )
    pairs = [(index, index + 1 - 2 * (index % 2)) for index in range(rep_count)]
    other_wide = lax.ppermute(own_wide, "rep", pairs)
    other_narrow = lax.ppermute(own_narrow, "rep", pairs)
    first_core = rep_index % 2 == 0
    query_update = jnp.where(first_core, own_wide, other_wide)
    out_update = jnp.where(first_core, other_wide, own_wide)
    key_update = jnp.where(first_core, own_narrow, other_narrow)
    value_update = jnp.where(first_core, other_narrow, own_narrow)
    gate_grad, gate_next, gate_update, up_grad, up_next, up_update = expert_update(
        expert_grads, (0, 1), (gate_moment, up_moment)
    )
    down_grad, down_next, down_update = expert_update(expert_grads, (2,), (down_moment,))
    return (
        mixed,
        grad_tokens,
        query_grad,
        query_next,
        query_update,
        key_grad,
        key_next,
        key_update,
        value_grad,
        value_next,
        value_update,
        out_grad,
        out_next,
        out_update,
        prenorm_grad,
        prenorm_next,
        prenorm_update,
        midnorm_grad,
        midnorm_next,
        midnorm_update,
        gate_grad,
        gate_next,
        gate_update,
        up_grad,
        up_next,
        up_update,
        down_grad,
        down_next,
        down_update,
    )


def solution(mesh):
    return jax.shard_map(
        local,
        mesh=mesh,
        in_specs=(
            P(("rep", "shard"), None),
            P(("rep", "shard")),
            P(("rep", "shard"), None),
            P(("rep", "shard"), None),
            P(("rep", "shard"), None),
            P("shard", None),
            P("shard", None),
            P("shard", None),
            P("shard", None),
            P("shard"),
            P("shard"),
            P("shard", None, None),
            P("shard", None, None),
            P("shard", None, None),
            P("shard", None),
            P("shard", None),
            P("shard", None),
            P("shard", None),
            P("shard"),
            P("shard"),
            P("shard", None, None),
            P("shard", None, None),
            P("shard", None, None),
        ),
        out_specs=(
            P(("rep", "shard"), None),
            P(("rep", "shard"), None),
            P("shard", None),
            P("shard", None),
            P("shard", None),
            P("shard", None),
            P("shard", None),
            P("shard", None),
            P("shard", None),
            P("shard", None),
            P("shard", None),
            P("shard", None),
            P("shard", None),
            P("shard", None),
            P("shard"),
            P("shard"),
            P("shard"),
            P("shard"),
            P("shard"),
            P("shard"),
            P("shard", None, None),
            P("shard", None, None),
            P("shard", None, None),
            P("shard", None, None),
            P("shard", None, None),
            P("shard", None, None),
            P("shard", None, None),
            P("shard", None, None),
            P("shard", None, None),
        ),
        check_vma=False,
    )
```

```python
import functools
import math

import jax
import jax.numpy as jnp
from jax import lax
from jax.experimental import pallas as pl
from jax.experimental.pallas import tpu as pltpu
from jax.sharding import PartitionSpec as P

NHEADS = 16
KVHEADS = 8
HEAD = 64
EXPERTS = 16
NS_ITERS = 2


norm_epsilon = 1e-06
rotary_base = 10000.0
momentum_keep = 0.9
rate_matrix = 0.5
rate_gain = 0.0002
newton_first = 3.4445
newton_second = -4.775
newton_third = 2.0315
masked_score = -1e30


def normalize(values):
    inverse = lax.rsqrt(jnp.mean(values * values, axis=-1, keepdims=True) + norm_epsilon)
    return (values * inverse, inverse)


def normalize_back(grad_normed, scaling, scaled, inverse):
    grad_scaled = grad_normed * scaling
    inner_mean = jnp.mean(grad_scaled * scaled, axis=-1, keepdims=True)
    return (
        inverse * (grad_scaled - scaled * inner_mean),
        jnp.sum(grad_normed * scaled, axis=0, keepdims=True),
    )


def dot_nn(left, right):
    return jnp.dot(left, right, preferred_element_type=jnp.float32)


def dot_nt(left, right):
    return lax.dot_general(
        left, right, (((1,), (1,)), ((), ())), preferred_element_type=jnp.float32
    )


def dot_tn(left, right):
    return lax.dot_general(
        left, right, (((0,), (0,)), ((), ())), preferred_element_type=jnp.float32
    )


def rotate(values, table_ref, sign):
    return (
        values * table_ref[0]
        + sign * pltpu.roll(values, 96, 1) * table_ref[1]
        + sign * pltpu.roll(values, 32, 1) * table_ref[2]
    )


def lane_low(shape):
    return lax.broadcasted_iota(jnp.int32, shape, 1) < HEAD


def twice(pair, upper):
    wide = pair.astype(jnp.float32)
    turned = pltpu.roll(wide, HEAD, 1)
    first = lane_low(pair.shape)
    return jnp.where(first != upper, wide, turned).astype(pair.dtype)


def stacked(pair):
    first = lane_low(pair.shape)
    zero = jnp.zeros_like(pair)
    return jnp.concatenate([jnp.where(first, pair, zero), jnp.where(first, zero, pair)], axis=0)


def unstacked(rows):
    half = rows.shape[0] // 2
    return jnp.where(lane_low((half, rows.shape[1])), rows[:half], rows[half:])


def allowed_pairs(start_column, start_row):
    shape = (start_column.shape[0], start_row.shape[1])
    query_places = lax.broadcasted_iota(jnp.int32, shape, 0)
    key_places = lax.broadcasted_iota(jnp.int32, shape, 1)
    one = (start_column == start_row) & (key_places <= query_places)
    return jnp.where(jnp.concatenate([one, one], axis=0), 0.0, masked_score)


def block_lanes(ref, block):
    return ref[:, block * 2 * HEAD : (block + 1) * 2 * HEAD]


def attend_pair(block, query_ref, pair_ref, bias):
    key = twice(block_lanes(pair_ref, block // 2), block % 2 == 1)
    value = twice(block_lanes(pair_ref, KVHEADS // 2 + block // 2), block % 2 == 1)
    queries = stacked(block_lanes(query_ref, block))
    scores = dot_nt(queries, key) * (1.0 / math.sqrt(HEAD)) + bias
    return (queries, key, value, scores)


def project_inputs(normed, weights, query_ref, pair_ref, table_ref):
    queries = dot_nn(normed, weights(0))
    for block in range(NHEADS // 2):
        lanes = slice(block * 2 * HEAD, (block + 1) * 2 * HEAD)
        query_ref[:, lanes] = rotate(queries[:, lanes], table_ref, 1.0).astype(jnp.bfloat16)
    pairs = dot_nn(normed, weights(1))
    for block in range(KVHEADS):
        lanes = slice(block * 2 * HEAD, (block + 1) * 2 * HEAD)
        value = pairs[:, lanes]
        if block < KVHEADS // 2:
            value = rotate(value, table_ref, 1.0)
        pair_ref[:, lanes] = value.astype(jnp.bfloat16)


def attend_forward(blocks, query_ref, pair_ref, bias, head_ref, total_ref):
    for block in blocks:
        _, _, value, scores = attend_pair(block, query_ref, pair_ref, bias)
        row_max = jnp.max(scores, axis=-1, keepdims=True)
        exponents = jnp.exp(scores - row_max)
        totals = jnp.sum(exponents, axis=-1, keepdims=True)
        softmax_low = (exponents * (1.0 / totals)).astype(jnp.bfloat16)
        head_ref[:, block * 2 * HEAD : (block + 1) * 2 * HEAD] = unstacked(
            dot_nn(softmax_low, value)
        ).astype(jnp.bfloat16)
        total_ref[:, block : block + 1] = row_max + jnp.log(totals)


def attend_backward(
    blocks, query_ref, pair_ref, bias, total_ref, grad_ref, table_ref, delta_ref
):
    folded = []
    for block in blocks:
        queries, key, value, scores = attend_pair(block, query_ref, pair_ref, bias)
        grads = stacked(block_lanes(grad_ref, block))
        softmax_full = jnp.exp(scores - total_ref[:, block : block + 1])
        grad_softmax = dot_nt(grads, value)
        inner = jnp.sum(softmax_full * grad_softmax, axis=-1, keepdims=True)
        grad_scores = (softmax_full * (grad_softmax - inner)).astype(jnp.bfloat16)
        scale = 1.0 / math.sqrt(HEAD)
        grad_query = unstacked(dot_nn(grad_scores, key)) * scale
        lanes = slice(block * 2 * HEAD, (block + 1) * 2 * HEAD)
        delta_ref[:, lanes] = rotate(grad_query, table_ref, -1.0).astype(jnp.bfloat16)
        grad_key = dot_tn(grad_scores, queries) * scale
        grad_value = dot_tn(softmax_full.astype(jnp.bfloat16), grads)
        folded.append(
            (
                grad_key + pltpu.roll(grad_key, HEAD, 1),
                grad_value + pltpu.roll(grad_value, HEAD, 1),
            )
        )
        if block % 2 == 1:
            first = lane_low(grad_key.shape)
            both = [jnp.where(first, low, high) for low, high in zip(*folded)]
            folded = []
            base = NHEADS * HEAD + (block // 2) * 2 * HEAD
            delta_ref[:, base : base + 2 * HEAD] = rotate(both[0], table_ref, -1.0).astype(
                jnp.bfloat16
            )
            base = base + KVHEADS * HEAD
            delta_ref[:, base : base + 2 * HEAD] = both[1].astype(jnp.bfloat16)


def rotary_tables(positions):
    half_size = HEAD // 2
    frequency = rotary_base ** (-(jnp.arange(half_size, dtype=jnp.float32) * 2.0) / HEAD)
    angles = positions.astype(jnp.float32)[:, None] * frequency[None, :]
    cosine, sine = (jnp.cos(angles), jnp.sin(angles))
    zero = jnp.zeros_like(sine)
    return jnp.stack(
        [
            jnp.concatenate([cosine] * 4, axis=1),
            jnp.concatenate([-sine, zero] * 2, axis=1),
            jnp.concatenate([zero, sine] * 2, axis=1),
        ]
    )


def newton_parts(grams):
    a, b, c = newton_first, newton_second, newton_third

    def times(left, right):
        return jnp.dot(left, right, preferred_element_type=jnp.float32)

    lows = [gram.astype(jnp.bfloat16) for gram in grams]
    firsts = [b * gram + c * times(low, low) for gram, low in zip(grams, lows)]
    first_lows = [first.astype(jnp.bfloat16) for first in firsts]
    mixes = [times(low, first) for low, first in zip(lows, first_lows)]
    nexts = [
        (a * a) * gram + (2.0 * a) * mix + times(mix.astype(jnp.bfloat16), first)
        for gram, mix, first in zip(grams, mixes, first_lows)
    ]
    next_lows = [gram.astype(jnp.bfloat16) for gram in nexts]
    seconds = [b * gram + c * times(low, low) for gram, low in zip(nexts, next_lows)]
    second_lows = [second.astype(jnp.bfloat16) for second in seconds]
    return list(zip(firsts, first_lows, seconds, second_lows))


def scaled_gram(gram):
    shape = gram.shape
    rows = lax.broadcasted_iota(jnp.int32, shape, 0)
    diagonal = rows == lax.broadcasted_iota(jnp.int32, shape, 1)
    inverse = 1.0 / (jnp.sqrt(jnp.sum(jnp.where(diagonal, gram, 0.0))) + 1e-07)
    return (gram * (inverse * inverse), inverse)


def expert_update_kernel(kinds, scale, *refs):
    a = newton_first
    grads_ref = refs[0]
    moments = refs[1 : 1 + len(kinds)]
    outs = refs[1 + len(kinds) :]
    half = grads_ref.shape[3]
    tall = kinds[0] < 2
    states = []
    for index in range(len(kinds)):
        for e in range(grads_ref.shape[0]):
            grad = grads_ref[e, index].astype(jnp.float32)
            if not tall:
                grad = jnp.concatenate([grad[:half], grad[half:]], axis=1)
            moment = momentum_keep * moments[index][e] + grad
            outs[3 * index][e] = grad
            outs[3 * index + 1][e] = moment
            low = moment.astype(jnp.bfloat16)
            sides = (((0,), (0,)), ((), ())) if tall else (((1,), (1,)), ((), ()))
            gram, inverse = scaled_gram(
                lax.dot_general(low, low, sides, preferred_element_type=jnp.float32)
            )
            states.append((index, e, inverse, low, gram))
    parts = newton_parts([state[-1] for state in states])
    for (index, e, inverse, low, _), (first, first_low, second, second_low) in zip(states, parts):
        rest = a * (first + second) + jnp.dot(
            first_low, second_low, preferred_element_type=jnp.float32
        )
        rest = ((-scale * inverse) * rest).astype(jnp.bfloat16)
        if tall:
            step = jnp.dot(low, rest, preferred_element_type=jnp.float32)
        else:
            step = jnp.dot(rest, low, preferred_element_type=jnp.float32)
        outs[3 * index + 2][e] = (-scale * a * a * inverse) * outs[3 * index + 1][e] + step


def expert_update(grads, kinds, moments):
    count, rows, columns = moments[0].shape
    group = 2 // len(kinds)
    scale = rate_matrix * math.sqrt(max(1.0, columns / rows))
    block = pl.BlockSpec((group, rows, columns), lambda i: (i, 0, 0))
    place = kinds[0] // len(kinds)
    taken = pl.BlockSpec((group, len(kinds)) + grads.shape[2:], lambda i: (i, place, 0, 0))
    shape = jax.ShapeDtypeStruct(moments[0].shape, jnp.float32)
    return pl.pallas_call(
        functools.partial(expert_update_kernel, kinds, scale),
        grid=(count // group,),
        in_specs=[taken] + [block] * len(kinds),
        out_specs=[block] * (3 * len(kinds)),
        out_shape=[shape] * (3 * len(kinds)),
        compiler_params=pltpu.CompilerParams(vmem_limit_bytes=60 * 1024 * 1024),
        name="expert_update",
        cost_estimate=pl.CostEstimate(
            flops=count * len(kinds) * 2500000000,
            bytes_accessed=moments[0].size * len(kinds) * 18,
            transcendentals=0,
        ),
    )(grads, *moments)


def dense_update_kernel(layout, place_ref, next_ref, grads_ref, *refs):
    a = newton_first
    amount = len(layout)
    own_moments = refs[:amount]
    outs = refs[amount : 3 * amount]
    updates = refs[3 * amount : 3 * amount + 2]
    matrices = refs[3 * amount + 2 : 3 * amount + 4]
    own_grads = refs[3 * amount + 4]
    blocks, count, block_rows, width = next_ref.shape
    part = width // 3
    me = place_ref[0]
    core = place_ref[1]
    start = pl.multiple_of(me * block_rows, block_rows)

    for block in range(blocks):
        outer = slice(block * part, (block + 1) * part)
        lanes = pl.ds(pl.multiple_of(2 * core * part, part), part)
        matrices[0][:, outer] = next_ref[block, :, :, lanes].reshape(count * block_rows, part)
        for index in range(3):
            columns = slice(8 * part * index + block * part, 8 * part * index + (block + 1) * part)
            inner = slice(index * part, (index + 1) * part)
            own_grads[:, columns] = grads_ref[block, :, inner].astype(jnp.float32)
    for block in range(blocks // 2):
        outer = slice(block * part, (block + 1) * part)
        matrices[1][:, outer] = next_ref[
            core * (blocks // 2) + block, :, :, part : 2 * part
        ].reshape(count * block_rows, part)
    for index, (begin, size) in enumerate(layout):
        grad = own_grads[:, begin : begin + size]
        outs[2 * index][...] = grad
        outs[2 * index + 1][...] = momentum_keep * own_moments[index][...] + grad
    states = []
    for matrix in matrices:
        low = matrix[...]
        states.append(
            scaled_gram(
                lax.dot_general(
                    low, low, (((0,), (0,)), ((), ())), preferred_element_type=jnp.float32
                )
            )
        )
    parts = newton_parts([state[0] for state in states])
    for matrix, update, (_, inverse), (_, first_low, _, second_low) in zip(
        matrices, updates, states, parts
    ):
        rows, columns = matrix.shape
        scale = rate_matrix * math.sqrt(max(1.0, columns / rows))
        own = matrix[pl.ds(start, block_rows)]
        once = a * own.astype(jnp.float32) + jnp.dot(
            own, first_low, preferred_element_type=jnp.float32
        )
        update[...] = (-scale * inverse) * (
            a * once
            + jnp.dot(once.astype(jnp.bfloat16), second_low, preferred_element_type=jnp.float32)
        )


def dense_update(nexts, grads, own_moments, layout, shard_index, rep_index):
    _, count, block_rows, _ = nexts.shape
    width = own_moments[0].shape[1]
    whole = lambda shape: pl.BlockSpec(shape, lambda i: (0,) * len(shape))
    shapes = []
    for _, size in layout:
        shapes += [jax.ShapeDtypeStruct((block_rows, size), jnp.float32)] * 2
    shapes += [
        jax.ShapeDtypeStruct((block_rows, width), jnp.float32),
        jax.ShapeDtypeStruct((block_rows, width // 2), jnp.float32),
    ]
    place = jnp.stack([shard_index, rep_index % 2]).astype(jnp.int32)
    return pl.pallas_call(
        functools.partial(dense_update_kernel, layout),
        grid=(1,),
        in_specs=[pl.BlockSpec(memory_space=pltpu.SMEM), whole(nexts.shape), whole(grads.shape)]
        + [whole(moment.shape) for moment in own_moments],
        out_specs=[whole(shape.shape) for shape in shapes],
        out_shape=shapes,
        scratch_shapes=[
            pltpu.VMEM((count * block_rows, width), jnp.bfloat16),
            pltpu.VMEM((count * block_rows, width // 2), jnp.bfloat16),
            pltpu.VMEM((block_rows, 3 * width), jnp.float32),
        ],
        compiler_params=pltpu.CompilerParams(vmem_limit_bytes=63 * 1024 * 1024),
        name="dense_update",
        cost_estimate=pl.CostEstimate(
            flops=14000000000, bytes_accessed=24 * width * width, transcendentals=0
        ),
    )(place, nexts, grads, *own_moments)


LAYOUT = ((0, 1024), (1024, 512), (1536, 512), (2048, 1024))


MESH = pl.DeviceIdType.MESH


def flip(index, bit):
    return index + bit - 2 * bit * ((index // bit) % 2)


def greet(peers):
    barrier = pltpu.get_barrier_semaphore()
    for peer in peers:
        pl.semaphore_signal(barrier, inc=1, device_id=peer, device_id_type=MESH)
    pl.semaphore_wait(barrier, len(peers))


def stream_plan(rep, bits, base, size):
    stages = []
    starts = [base, base + size]
    for step in range(len(bits)):
        size = size // 2
        stage = []
        for stream in range(2):
            bit = bits[(step + stream) % len(bits)]
            side = (rep // bit) % 2
            keep = starts[stream] + side * size
            send = starts[stream] + (1 - side) * size
            starts[stream] = keep
            stage.append((bit, stream, keep, send, size))
        stages.append(stage)
    return stages


def rows_of(start, size):
    return pl.ds(pl.multiple_of(start, 16), size)


def moe_kernel(
    count,
    bits,
    own_ref,
    cot_ref,
    weight_ref,
    gate_hbm,
    up_hbm,
    down_hbm,
    stage_out,
    back_ref,
    share_ref,
    tok,
    turned,
    mats,
    hid,
    gate_delta,
    up_delta,
    stage_back,
    got_back,
    sum_back,
    sum_out,
    *rest,
):
    landing = rest[: 1 + 2 * len(bits)]
    (
        load_sem,
        right_sem,
        left_sem,
        arrive_sem,
        back_send,
        back_recv,
        sum_send,
        sum_recv,
    ) = rest[1 + 2 * len(bits) :]
    rep = lax.axis_index("rep")
    me = lax.axis_index("shard")
    experts = mats.shape[0]
    tokens = own_ref.shape[0]
    half = mats.shape[2] // 2
    core = rep % 2

    loads = [
        pltpu.make_async_copy(gate_hbm, mats.at[:, 0], load_sem.at[0]),
        pltpu.make_async_copy(up_hbm, mats.at[:, 1], load_sem.at[1]),
        pltpu.make_async_copy(
            down_hbm.at[:, :, pl.ds(0, half)], mats.at[:, 2, pl.ds(0, half)], load_sem.at[2]
        ),
        pltpu.make_async_copy(
            down_hbm.at[:, :, pl.ds(half, half)], mats.at[:, 2, pl.ds(half, half)], load_sem.at[3]
        ),
    ]
    for load in loads:
        load.start()
    peers = [(rep, lax.rem(me + k, count)) for k in range(1, count)]
    peers += [(flip(rep, bit), me) for bit in (1,) + bits]
    greet(peers)

    right_peer = (rep, jnp.minimum(me + 1, count - 1))
    left_peer = (rep, jnp.maximum(me - 1, 0))

    def hand_on(block, to_right):
        return pltpu.make_async_remote_copy(
            src_ref=tok.at[block],
            dst_ref=tok.at[block],
            send_sem=(right_sem if to_right else left_sem).at[block],
            recv_sem=arrive_sem.at[block],
            device_id=right_peer if to_right else left_peer,
            device_id_type=MESH,
        )

    def returning(stage, got, send_sem, recv_sem, block):
        return pltpu.make_async_remote_copy(
            src_ref=stage.at[block],
            dst_ref=got.at[me],
            send_sem=send_sem.at[block],
            recv_sem=recv_sem.at[me],
            device_id=(rep, block),
            device_id_type=MESH,
        )

    tok[me] = own_ref[...]

    @pl.when(me < count - 1)
    def _():
        hand_on(me, True).start()

    @pl.when(me > 0)
    def _():
        hand_on(me, False).start()

    for load in loads:
        load.wait()

    margin = jnp.minimum(me, count - 1 - me)
    longer = jnp.where(me < count - 1 - me, 1, -1)
    inward = jnp.where(2 * me < count, 1, -1)
    nt = (((1,), (1,)), ((), ()))

    def dot(left, right):
        return jnp.dot(left, right, preferred_element_type=jnp.float32)

    def dot_nt(left, right):
        return lax.dot_general(left, right, nt, preferred_element_type=jnp.float32)

    def arrivals(j):
        lower = me - j
        upper = me + j

        @pl.when((j > 0) & (lower >= 0))
        def _():
            hand_on(jnp.maximum(lower, 0), True).wait_recv()

            @pl.when(me < count - 1)
            def _():
                hand_on(jnp.maximum(lower, 0), True).start()

        @pl.when((j > 0) & (upper < count))
        def _():
            hand_on(jnp.minimum(upper, count - 1), False).wait_recv()

            @pl.when(me > 0)
            def _():
                hand_on(jnp.minimum(upper, count - 1), False).start()

    def block_at(j):
        near = (j + 1) // 2
        alternating = me + near - 2 * near * (j % 2)
        return jnp.where(j <= 2 * margin, alternating, me + longer * (j - margin))

    def places_of(block):
        return pl.ds(pl.multiple_of(block * tokens, tokens), tokens)

    def factors(e, block):
        places = places_of(block)
        rows = tok[block]
        grads = cot_ref[block]
        weight = weight_ref[block, :, e : e + 1]
        u = dot(rows, mats[e, 0])
        w = dot(rows, mats[e, 1])
        gate = 1.0 / (1.0 + jnp.exp(-u))
        act = u * gate
        hidden = (weight * (act * w)).astype(jnp.bfloat16)
        hid[e, :, places] = hidden.T
        pulled = weight * (
            dot_nt(grads[:, :half], mats[e, 2, :half])
            + dot_nt(grads[:, half:], mats[e, 2, half:])
        )
        gate_delta[e, places] = (pulled * w * (gate + act * (1.0 - gate))).astype(jnp.bfloat16)
        up_delta[e, places] = (pulled * act).astype(jnp.bfloat16)
        return hidden

    def sums(block, e, hidden, place):
        places = places_of(block)
        for side in range(2):
            part = slice(side * half, (side + 1) * half)
            back = dot_nt(gate_delta[e, places], mats[e, 0, part]) + dot_nt(
                up_delta[e, places], mats[e, 1, part]
            )
            out = dot(hidden, mats[e, 2, part])
            if e > 0:
                back = place[0][:, part] + back
                out = place[1][:, part] + out
            place[0][:, part] = back
            place[1][:, part] = out

    def visit(j, carry):
        arrivals(j)
        block = block_at(j)
        places = places_of(block)
        turned[:, places] = tok[block].T
        hiddens = [factors(e, block) for e in range(experts)]
        for side in range(2):
            part = slice(side * half, (side + 1) * half)
            total_back = None
            total_out = None
            for e in range(experts):
                back = dot_nt(gate_delta[e, places], mats[e, 0, part]) + dot_nt(
                    up_delta[e, places], mats[e, 1, part]
                )
                out = dot(hiddens[e], mats[e, 2, part])
                total_back = back if e == 0 else total_back + back
                total_out = out if e == 0 else total_out + out
            stage_back[block, :, part] = total_back.astype(jnp.bfloat16)
            stage_out[block, :, part] = total_out.astype(jnp.bfloat16)

        @pl.when((j > 0) & ((block - me) * inward > 0))
        def _():
            returning(stage_back, got_back, back_send, back_recv, block).start()

        return carry

    lax.fori_loop(0, count - 1, visit, 0)
    arrivals(count - 1)
    last = block_at(count - 1)
    for k in range(1, count):
        block = block_at(k - 1)

        @pl.when((block - me) * inward < 0)
        def _():
            returning(stage_back, got_back, back_send, back_recv, block).start()

    turned[:, places_of(last)] = tok[last].T
    plan = stream_plan(rep, bits, core * half, half // 2)

    def sum_copy(stage, slot, e, start, size, bit):
        return pltpu.make_async_remote_copy(
            src_ref=mats.at[e, :, rows_of(start, size)],
            dst_ref=landing[slot].at[e],
            send_sem=sum_send.at[slot, e],
            recv_sem=sum_recv.at[slot, e],
            device_id=(flip(rep, bit), me),
            device_id_type=MESH,
        )

    def copies(stage, e):
        if stage == 0:
            return [(sum_copy(0, 0, e, (1 - core) * half, half, 1), 0, core * half, half)]
        return [
            (
                sum_copy(stage, 1 + 2 * (stage - 1) + stream, e, send, size, bit),
                1 + 2 * (stage - 1) + stream,
                keep,
                size,
            )
            for bit, stream, keep, send, size in plan[stage - 1]
        ]

    def finish(stage, e):
        for copy, slot, keep, size in copies(stage, e):
            copy.wait_recv()
            place = rows_of(keep, size)
            for kind in range(3):
                mats[e, kind, place] = (
                    mats[e, kind, place].astype(jnp.float32)
                    + landing[slot][e, kind].astype(jnp.float32)
                ).astype(jnp.bfloat16)

    stages = 1 + len(bits)
    for turn in range(experts + stages):
        if turn < experts:
            e = turn
            sums(last, e, factors(e, last), (sum_back, sum_out))
            for side in range(2):
                part = slice(side * half, (side + 1) * half)
                mats[e, 0, part] = dot(turned[part], gate_delta[e]).astype(jnp.bfloat16)
                mats[e, 1, part] = dot(turned[part], up_delta[e]).astype(jnp.bfloat16)
                mats[e, 2, part] = dot(hid[e], cot_ref[:, :, part].reshape(count * tokens, half)).astype(jnp.bfloat16)
            copies(0, e)[0][0].start()
            if e == experts - 1:
                stage_back[last] = sum_back[...].astype(jnp.bfloat16)
                stage_out[last] = sum_out[...].astype(jnp.bfloat16)
                returning(stage_back, got_back, back_send, back_recv, last).start()
        for stage in range(stages):
            e = turn - 1 - stage
            if 0 <= e < experts:
                finish(stage, e)
                if stage + 1 < stages:
                    for copy, _, _, _ in copies(stage + 1, e):
                        copy.start()
                else:
                    for _, stream, keep, _, size in plan[-1]:
                        share_ref[e, :, stream] = mats[e, :, rows_of(keep, size)]

    total = stage_back[me].astype(jnp.float32)
    for k in range(1, count):
        source = lax.rem(me + k, count)
        pltpu.make_async_remote_copy(
            src_ref=stage_back.at[source],
            dst_ref=got_back.at[source],
            send_sem=back_send.at[source],
            recv_sem=back_recv.at[source],
            device_id=(rep, source),
            device_id_type=MESH,
        ).wait_recv()
        total = total + got_back[source].astype(jnp.float32)
    back_ref[...] = total
    for k in range(1, count):
        block = lax.rem(me + k, count)
        returning(stage_back, got_back, back_send, back_recv, block).wait_send()
    for e in range(experts):
        for stage in range(stages):
            for copy, _, _, _ in copies(stage, e):
                copy.wait_send()
    for block in range(count):

        @pl.when((block <= me) & (me < count - 1))
        def _():
            hand_on(block, True).wait_send()

        @pl.when((block >= me) & (me > 0))
        def _():
            hand_on(block, False).wait_send()


def moe(normed, cotangents, weights, gate_proj, up_proj, down_proj, bits, count):
    tokens, width = normed.shape
    experts, _, hidden = gate_proj.shape
    half = width // 2
    low = jnp.bfloat16
    final = (half // 2) >> len(bits)
    vmem = pl.BlockSpec(memory_space=pltpu.VMEM)
    anywhere = pl.BlockSpec(memory_space=pl.ANY)
    landings = [pltpu.VMEM((experts, 3, half, hidden), low)]
    for step in range(len(bits)):
        size = (half // 2) >> (step + 1)
        landings += [pltpu.VMEM((experts, 3, size, hidden), low)] * 2
    slots = len(landings)
    dma = pltpu.SemaphoreType.DMA
    return pl.pallas_call(
        functools.partial(moe_kernel, count, bits),
        in_specs=[vmem, vmem, vmem, anywhere, anywhere, anywhere],
        out_specs=[vmem, vmem, vmem],
        out_shape=[
            jax.ShapeDtypeStruct((count, tokens, width), low),
            jax.ShapeDtypeStruct((tokens, width), jnp.float32),
            jax.ShapeDtypeStruct((experts, 3, 2, final, hidden), low),
        ],
        scratch_shapes=[
            pltpu.VMEM((count, tokens, width), low),
            pltpu.VMEM((width, count * tokens), low),
            pltpu.VMEM((experts, 3, width, hidden), low),
            pltpu.VMEM((experts, hidden, count * tokens), low),
            pltpu.VMEM((experts, count * tokens, hidden), low),
            pltpu.VMEM((experts, count * tokens, hidden), low),
            pltpu.VMEM((count, tokens, width), low),
            pltpu.VMEM((count, tokens, width), low),
            pltpu.VMEM((tokens, width), jnp.float32),
            pltpu.VMEM((tokens, width), jnp.float32),
        ]
        + landings
        + [
            dma((4,)),
            dma((count,)),
            dma((count,)),
            dma((count,)),
            dma((count,)),
            dma((count,)),
            dma((slots, experts)),
            dma((slots, experts)),
        ],
        compiler_params=pltpu.CompilerParams(
            collective_id=1, has_side_effects=True, vmem_limit_bytes=63 * 1024 * 1024
        ),
        name="moe",
        cost_estimate=pl.CostEstimate(
            flops=39000000000, bytes_accessed=20000000, transcendentals=2000000
        ),
    )(normed, cotangents, weights, gate_proj, up_proj, down_proj)


def rep_bits(rep_count):
    bits = []
    bit = 2
    while bit < rep_count:
        bits.append(bit)
        bit = bit * 2
    return tuple(bits)


def spread_kernel(
    count,
    bits,
    share_ref,
    returned_ref,
    normed_ref,
    head_ref,
    weights_ref,
    small_ref,
    tokens_ref,
    cot_ref,
    second_ref,
    middle_ref,
    query_ref,
    pair_ref,
    total_ref,
    table_ref,
    column_ref,
    row_ref,
    query_moment,
    key_moment,
    value_moment,
    out_moment,
    experts_hbm,
    dense_out,
    grads_out,
    gains_out,
    tokens_out,
    mixed_out,
    experts_out,
    got_ref,
    moment_piece,
    delta_ref,
    branch_ref,
    heads_ref,
    dense_ref,
    total,
    land_core,
    land_first,
    *rest,
):
    later = len(bits) - 1
    land_later = rest[:later]
    (
        piece_send,
        piece_land,
        piece,
        gains_send,
        gains_land,
        gains_all,
        local_sem,
        core_send,
        core_recv,
        half_send,
        half_recv,
        shard_send,
        shard_recv,
        grow_send,
        grow_recv,
        line_send,
        line_recv,
        join_send,
        join_recv,
        expert_send,
        expert_recv,
        gain_send,
        gain_recv,
        gain_line_send,
        gain_line_recv,
        back_send,
        back_recv,
        moment_sem,
        own_send,
        own_recv,
        own_join_send,
        own_join_recv,
    ) = rest[later:]
    rep = lax.axis_index("rep")
    me = lax.axis_index("shard")
    core = rep % 2
    rows = dense_ref.shape[2]
    expert_rows = experts_out.shape[2]
    steps = len(bits)
    streams = range(2)

    def remote(source, target, send_sem, recv_sem, peer):
        return pltpu.make_async_remote_copy(
            src_ref=source,
            dst_ref=target,
            send_sem=send_sem,
            recv_sem=recv_sem,
            device_id=peer,
            device_id_type=MESH,
        )

    def across(bit):
        return (flip(rep, bit), me)

    def order(stream):
        return [bits[(step + stream) % steps] for step in range(steps)]

    def side(bit):
        return (rep // bit) % 2

    plan = stream_plan(rep, bits, core * (expert_rows // 2), expert_rows // 4)
    base = [(core * (expert_rows // 2)) + stream * (expert_rows // 4) for stream in streams]

    def expert_copy(level, stream):
        if level == steps:
            place = rows_of(base[stream], expert_rows // 4)
            peer = across(1)
        else:
            bit, _, keep, _, size = plan[steps - 1 - level][stream]
            place = rows_of(keep, size)
            peer = across(bit)
        source = experts_out.at[:, :, place]
        if level == 0:
            source = share_ref.at[:, :, stream]
        return remote(
            source,
            experts_out.at[:, :, place],
            expert_send.at[level, stream],
            expert_recv.at[level, stream],
            peer,
        )

    def own_copy(stream):
        _, _, keep, _, size = plan[-1][stream]
        return pltpu.make_async_copy(
            share_ref.at[:, :, stream],
            experts_out.at[:, :, rows_of(keep, size)],
            local_sem.at[stream],
        )

    for stream in streams:
        own_copy(stream).start()
    peers = [(rep, lax.rem(me + k, count)) for k in range(1, count)]
    peers += [across(bit) for bit in (1,) + bits]
    greet(peers)

    def returning(peer, source):
        return remote(
            returned_ref.at[peer],
            got_ref.at[source],
            back_send.at[peer],
            back_recv.at[source],
            (rep, peer),
        )

    gain_bits = (1,) + bits

    def gain_copy(stage):
        return remote(
            gains_send.at[stage],
            gains_land.at[stage],
            gain_send.at[stage],
            gain_recv.at[stage],
            across(gain_bits[stage]),
        )

    def gain_step(stage):
        gain_copy(stage).wait_recv()
        gains_send[stage + 1] = gains_send[stage] + gains_land[stage]
        if stage + 1 < len(gain_bits):
            gain_copy(stage + 1).start()

    def whole(index):
        return weights_ref[index].reshape(count * rows, -1)

    def gain(index):
        at = EXPERTS + index
        return jnp.concatenate([small_ref[z, at : at + 1, :rows] for z in range(count)], axis=1)

    part = dense_ref.shape[3] // 3
    chunks = (pl.ds(2 * part, part), pl.ds(0, 2 * part))
    chunk_parts = ((2,), (0, 1))
    inner = [slice(index * part, (index + 1) * part) for index in range(3)]
    first = [side(order(stream)[0]) for stream in streams]
    held = [2 * stream + first[stream] for stream in streams]
    given = [2 * stream + 1 - first[stream] for stream in streams]

    starts = []
    for stream in streams:
        start, size, line = 0, rows, []
        for step in range(1, steps):
            size = size // 2
            near = side(order(stream)[step])
            line.append((start + near * size, start + (1 - near) * size, size))
            start = start + near * size
        starts.append((start, size, line))
    last = starts[0][1]
    places = [rows_of(starts[stream][0], last) for stream in streams]
    others = [lax.rem(me + k, count) for k in range(1, count)]

    def moment_copy(stream, index):
        block = 4 * core + held[stream]
        lanes = pl.ds(pl.multiple_of((held[stream] if index == 1 else block) * part, part), part)
        source = (query_moment, key_moment, out_moment)[index]
        return pltpu.make_async_copy(
            source.at[places[stream], lanes],
            moment_piece.at[stream, :, inner[index]],
            moment_sem.at[stream, index],
        )

    def moment_other(stream):
        lanes = pl.ds(pl.multiple_of(held[stream] * part, part), part)
        return pltpu.make_async_copy(
            value_moment.at[places[stream], lanes],
            moment_piece.at[stream, :, inner[1]],
            moment_sem.at[stream, 1],
        )

    def columns(ref, offset, block):
        return ref[:, pl.ds(pl.multiple_of(offset + block * part, part), part)]

    def make_block(chunk, block, turned):
        if chunk == 0:
            values = dot_nn(turned, columns(branch_ref, 0, block))
        else:
            values = dot_nn(
                turned,
                jnp.concatenate(
                    [columns(delta_ref, 0, block), columns(delta_ref, 8 * part, block)], axis=1
                ),
            )
        for line in range(count):
            dense_ref[block, line, :, chunks[chunk]] = values[
                line * rows : (line + 1) * rows
            ].astype(jnp.bfloat16)

    def core_copy(chunk, block):
        return remote(
            dense_ref.at[4 * (1 - core) + block, :, :, chunks[chunk]],
            land_core.at[block, :, :, chunks[chunk]],
            core_send.at[chunk, block],
            core_recv.at[chunk, block],
            across(1),
        )

    def first_copy(chunk, stream):
        return remote(
            total.at[given[stream], :, :, chunks[chunk]],
            land_first.at[stream, :, :, chunks[chunk]],
            half_send.at[chunk, 0, stream],
            half_recv.at[chunk, 0, stream],
            across(order(stream)[0]),
        )

    def later_copy(chunk, step, stream):
        _, send, size = starts[stream][2][step - 1]
        return remote(
            total.at[held[stream], :, rows_of(send, size), chunks[chunk]],
            land_later[step - 1].at[stream, :, :, chunks[chunk]],
            half_send.at[chunk, step, stream],
            half_recv.at[chunk, step, stream],
            across(order(stream)[step]),
        )

    def shard_copy(chunk, source, peer):
        return remote(
            piece_send.at[peer, :, :, chunks[chunk]],
            piece_land.at[source, :, :, chunks[chunk]],
            shard_send.at[chunk, peer],
            shard_recv.at[chunk, source],
            (rep, peer),
        )

    def line_copy(chunk, stream, source, peer):
        return remote(
            piece.at[stream, :, chunks[chunk]],
            dense_out.at[4 * core + held[stream], source, places[stream], chunks[chunk]],
            line_send.at[chunk, stream, peer],
            line_recv.at[chunk, stream, source],
            (rep, peer),
        )

    def own_piece(chunk, stream):
        return pltpu.make_async_copy(
            piece.at[stream, :, chunks[chunk]],
            dense_out.at[4 * core + held[stream], me, places[stream], chunks[chunk]],
            local_sem.at[2 + 2 * chunk + stream],
        )

    def region(step, stream):
        if step == 0:
            return pl.ds(0, rows)
        keep, _, size = starts[stream][2][step - 1]
        return rows_of(keep, size)

    def grow_copy(chunk, step, stream):
        place = dense_out.at[
            4 * core + held[stream], :, region(step, stream), chunks[chunk]
        ]
        return remote(
            place,
            place,
            grow_send.at[chunk, step, stream],
            grow_recv.at[chunk, step, stream],
            across(order(stream)[step]),
        )

    def own_grow(chunk, step, stream):
        place = grads_out.at[4 * core + held[stream], region(step, stream), chunks[chunk]]
        return remote(
            place,
            place,
            own_send.at[chunk, step, stream],
            own_recv.at[chunk, step, stream],
            across(order(stream)[step]),
        )

    def join_copy(chunk, stream):
        place = dense_out.at[pl.ds(4 * core + 2 * stream, 2), :, :, chunks[chunk]]
        return remote(
            place, place, join_send.at[chunk, stream], join_recv.at[chunk, stream], across(1)
        )

    def own_join(chunk, stream):
        place = grads_out.at[pl.ds(4 * core + 2 * stream, 2), :, chunks[chunk]]
        return remote(
            place,
            place,
            own_join_send.at[chunk, stream],
            own_join_recv.at[chunk, stream],
            across(1),
        )

    def add_into(block, line, place, lanes, one, two):
        total[block, line, place, lanes] = (
            one.astype(jnp.float32) + two.astype(jnp.float32)
        ).astype(jnp.bfloat16)

    def chain(chunk):
        lanes = chunks[chunk]
        turned = (head_ref if chunk == 0 else normed_ref)[...].T
        every = pl.ds(0, rows)
        for block in range(4):
            make_block(chunk, 4 * (1 - core) + block, turned)
            core_copy(chunk, block).start()
        for block in range(4):
            make_block(chunk, 4 * core + block, turned)
        yield

        def add_core(block):
            for line in range(count):
                add_into(
                    block,
                    line,
                    every,
                    lanes,
                    dense_ref[4 * core + block, line, :, lanes],
                    land_core[block, line, :, lanes],
                )

        for block in range(4):
            core_copy(chunk, block).wait_recv()
        for stream in streams:
            add_core(given[stream])
            first_copy(chunk, stream).start()
        for stream in streams:
            add_core(held[stream])
        yield
        for stream in streams:
            first_copy(chunk, stream).wait_recv()
            for line in range(count):
                add_into(
                    held[stream],
                    line,
                    every,
                    lanes,
                    total[held[stream], line, :, lanes],
                    land_first[stream, line, :, lanes],
                )
            if steps > 1:
                later_copy(chunk, 1, stream).start()
        yield
        for step in range(1, steps):
            for stream in streams:
                later_copy(chunk, step, stream).wait_recv()
                place = region(step, stream)
                for line in range(count):
                    add_into(
                        held[stream],
                        line,
                        place,
                        lanes,
                        total[held[stream], line, place, lanes],
                        land_later[step - 1][stream, line, :, lanes],
                    )
                if step + 1 < steps:
                    later_copy(chunk, step + 1, stream).start()
            if step + 1 < steps:
                yield
        for stream in streams:
            for line in range(count):
                piece_send[line, stream, :, lanes] = total[
                    held[stream], line, places[stream], lanes
                ]
        for other in others:
            shard_copy(chunk, me, other).start()
        yield
        summed = piece_send[me, :, :, lanes].astype(jnp.float32)
        for other in others:
            shard_copy(chunk, other, other).wait_recv()
            summed = summed + piece_land[other, :, :, lanes].astype(jnp.float32)
        for stream in streams:
            for index in chunk_parts[chunk]:
                moment_copy(stream, index).wait()
            grads_out[4 * core + held[stream], places[stream], lanes] = summed[stream].astype(
                jnp.bfloat16
            )
            own_grow(chunk, steps - 1, stream).start()
        piece[:, :, lanes] = (momentum_keep * moment_piece[:, :, lanes] + summed).astype(
            jnp.bfloat16
        )
        for stream in streams:
            own_piece(chunk, stream).start()
            for other in others:
                line_copy(chunk, stream, me, other).start()
        yield
        for stream in streams:
            own_piece(chunk, stream).wait()
            for other in others:
                line_copy(chunk, stream, other, other).wait_recv()
            grow_copy(chunk, steps - 1, stream).start()
        yield
        for step in reversed(range(steps)):
            for stream in streams:
                grow_copy(chunk, step, stream).wait_recv()
                own_grow(chunk, step, stream).wait_recv()
                if step > 0:
                    grow_copy(chunk, step - 1, stream).start()
                    own_grow(chunk, step - 1, stream).start()
                else:
                    join_copy(chunk, stream).start()
                    own_join(chunk, stream).start()
            yield
        for stream in streams:
            join_copy(chunk, stream).wait()
            own_join(chunk, stream).wait()

    early, late = chain(0), chain(1)

    def go(steps_of):
        next(steps_of, None)

    for stream in streams:
        moment_copy(stream, 0).start()
        moment_copy(stream, 2).start()

        @pl.when(core == 0)
        def _():
            moment_copy(stream, 1).start()

        @pl.when(core == 1)
        def _():
            moment_other(stream).start()

    scaled, inverse = normalize(middle_ref[...])
    middle_extra, midnorm_part = normalize_back(second_ref[...], gain(1), scaled, inverse)
    grad_middle = cot_ref[...].astype(jnp.float32) + middle_extra
    tokens_out[...] = grad_middle
    branch_ref[...] = grad_middle.astype(jnp.bfloat16)
    go(early)
    for stream in streams:
        expert_copy(0, stream).start()
    for other in others:
        returning(other, me).start()
    heads_ref[...] = dot_nt(branch_ref[...], whole(2)).astype(jnp.bfloat16)
    bias = allowed_pairs(column_ref[...], row_ref[...])

    def backward(begin, end):
        attend_backward(
            range(begin, end),
            query_ref,
            pair_ref,
            bias,
            total_ref,
            heads_ref,
            table_ref,
            delta_ref,
        )

    quarter = KVHEADS // 4
    backward(0, quarter)
    go(early)
    backward(quarter, 3 * quarter)
    go(early)
    backward(3 * quarter, KVHEADS)
    go(late)
    go(early)
    go(late)
    grad_first = dot_nt(delta_ref[:, : NHEADS * HEAD], whole(0)) + dot_nt(
        delta_ref[:, NHEADS * HEAD :], whole(1)
    )
    scaled, inverse = normalize(tokens_ref[...].astype(jnp.float32))
    input_extra, prenorm_part = normalize_back(grad_first, gain(0), scaled, inverse)
    tokens_out[...] = tokens_out[...] + input_extra
    gains_send[0] = jnp.concatenate(
        [prenorm_part, midnorm_part, jnp.zeros((6, prenorm_part.shape[1]), jnp.float32)], axis=0
    )
    gain_copy(0).start()
    go(early)
    gain_step(0)
    go(late)
    go(early)
    for stream in streams:
        own_copy(stream).wait()
        expert_copy(0, stream).wait_recv()
        expert_copy(1, stream).start()
    gain_step(1)
    go(late)
    for stage in range(2, len(gain_bits)):
        gain_step(stage)

    def gain_line(source, peer):
        return remote(
            gains_send.at[len(gain_bits)],
            gains_all.at[source],
            gain_line_send.at[peer],
            gain_line_recv.at[source],
            (rep, peer),
        )

    for other in others:
        gain_line(me, other).start()
    go(early)
    go(late)
    go(early)
    gained = gains_send[len(gain_bits)]
    for other in others:
        gain_line(other, other).wait_recv()
        gained = gained + gains_all[other]
    gains_out[...] = gained
    mixed = middle_ref[...] + returned_ref[me].astype(jnp.float32)
    for other in others:
        returning(other, other).wait_recv()
        mixed = mixed + got_ref[other].astype(jnp.float32)
    mixed_out[...] = mixed.astype(mixed_out.dtype)
    go(late)
    for level in range(1, steps):
        for stream in streams:
            expert_copy(level, stream).wait_recv()
            expert_copy(level + 1, stream).start()
    go(late)
    for stream in streams:
        expert_copy(steps, stream).wait()
    leave = pltpu.make_async_copy(experts_out, experts_hbm, local_sem.at[0])
    leave.start()
    for _ in late:
        pass
    for _ in early:
        pass

    for stream in streams:
        for level in range(steps):
            expert_copy(level, stream).wait_send()
        for chunk in range(2):
            first_copy(chunk, stream).wait_send()
            for step in range(1, steps):
                later_copy(chunk, step, stream).wait_send()
            for other in others:
                line_copy(chunk, stream, me, other).wait_send()
            for step in range(steps):
                grow_copy(chunk, step, stream).wait_send()
                own_grow(chunk, step, stream).wait_send()
    for chunk in range(2):
        for block in range(4):
            core_copy(chunk, block).wait_send()
        for other in others:
            shard_copy(chunk, me, other).wait_send()
    for stage in range(len(gain_bits)):
        gain_copy(stage).wait_send()
    for other in others:
        gain_line(me, other).wait_send()
        returning(other, me).wait_send()
    leave.wait()


def spread(
    share, returned, normed, head_low, weights, small, tokens, cotangent, second, middle, *rest, bits, count
):
    query, pair, log_total, tables, starts, moments = rest
    experts, _, _, final, hidden = share.shape
    token_count, features = normed.shape
    rows = features // count
    width = 3 * features // 8
    dense_shape = (8, count, rows, width)
    gains_shape = (8, features)
    steps = len(bits)
    last = rows >> (steps - 1)
    low = jnp.bfloat16
    vmem = pl.BlockSpec(memory_space=pltpu.VMEM)
    dma = pltpu.SemaphoreType.DMA
    return pl.pallas_call(
        functools.partial(spread_kernel, count, bits),
        in_specs=[vmem] * 16 + [pl.BlockSpec(memory_space=pl.ANY)] * 4,
        out_specs=[pl.BlockSpec(memory_space=pl.ANY)] + [vmem] * 5,
        out_shape=[
            jax.ShapeDtypeStruct((experts, 3, 4 * (final << steps), hidden), low),
            jax.ShapeDtypeStruct(dense_shape, low),
            jax.ShapeDtypeStruct((8, rows, width), low),
            jax.ShapeDtypeStruct(gains_shape, jnp.float32),
            jax.ShapeDtypeStruct((token_count, features), jnp.float32),
            jax.ShapeDtypeStruct((token_count, features), low),
        ],
        scratch_shapes=[
            pltpu.VMEM((experts, 3, 4 * (final << steps), hidden), low),
            pltpu.VMEM((count, token_count, features), low),
            pltpu.VMEM((2, last, width), jnp.float32),
            pltpu.VMEM((token_count, 2 * features), low),
            pltpu.VMEM((token_count, features), low),
            pltpu.VMEM((token_count, features), low),
            pltpu.VMEM(dense_shape, low),
            pltpu.VMEM((4, count, rows, width), low),
            pltpu.VMEM((4, count, rows, width), low),
            pltpu.VMEM((2, count, rows, width), low),
        ]
        + [pltpu.VMEM((2, count, rows >> step, width), low) for step in range(1, steps)]
        + [
            pltpu.VMEM((count, 2, last, width), low),
            pltpu.VMEM((count, 2, last, width), low),
            pltpu.VMEM((2, last, width), low),
            pltpu.VMEM((steps + 2,) + gains_shape, jnp.float32),
            pltpu.VMEM((steps + 1,) + gains_shape, jnp.float32),
            pltpu.VMEM((count,) + gains_shape, jnp.float32),
            dma((6,)),
            dma((2, 4)),
            dma((2, 4)),
            dma((2, steps, 2)),
            dma((2, steps, 2)),
            dma((2, count)),
            dma((2, count)),
            dma((2, steps, 2)),
            dma((2, steps, 2)),
            dma((2, 2, count)),
            dma((2, 2, count)),
            dma((2, 2)),
            dma((2, 2)),
            dma((steps + 1, 2)),
            dma((steps + 1, 2)),
            dma((steps + 1,)),
            dma((steps + 1,)),
            dma((count,)),
            dma((count,)),
            dma((count,)),
            dma((count,)),
            dma((2, 3)),
            dma((2, steps, 2)),
            dma((2, steps, 2)),
            dma((2, 2)),
            dma((2, 2)),
        ],
        compiler_params=pltpu.CompilerParams(
            collective_id=2, has_side_effects=True, vmem_limit_bytes=63 * 1024 * 1024
        ),
        name="spread",
    )(
        share,
        returned,
        normed,
        head_low,
        weights,
        small,
        tokens,
        cotangent,
        second,
        middle,
        query,
        pair,
        log_total,
        tables,
        starts[:, None],
        starts[None, :],
        *moments,
    )


def gather_kernel(
    count,
    bits,
    query_weight,
    key_weight,
    value_weight,
    out_weight,
    small_ref,
    tokens_ref,
    cot_ref,
    table_ref,
    column_ref,
    row_ref,
    weights_hbm,
    small_out,
    cot_out,
    middle_out,
    first_out,
    second_out,
    query_out,
    pair_out,
    head_out,
    total_out,
    weights_out,
    weights_ref,
    local_sem,
    line_send,
    line_recv,
    grow_send,
    grow_recv,
    join_send,
    join_recv,
    small_send,
    small_recv,
    right_sem,
    left_sem,
    arrive_sem,
):
    rep = lax.axis_index("rep")
    me = lax.axis_index("shard")
    core = rep % 2
    steps = len(bits)
    streams = range(2)
    rows, width = weights_ref.shape[1:]
    half = width // 2
    fine = half // 4
    others = [lax.rem(me + k, count) for k in range(1, count)]

    def columns_of(start, size):
        return pl.ds(pl.multiple_of(start, 128), size)

    def order(stream):
        return [bits[(step + stream) % steps] for step in range(steps)]

    def side(bit):
        return (rep // bit) % 2

    narrow = width // 2
    weights_ref[0] = query_weight[...]
    weights_ref[1, :, :narrow] = key_weight[...]
    weights_ref[1, :, narrow:] = value_weight[...]
    weights_ref[2] = out_weight[...]
    own_copy = pltpu.make_async_copy(weights_ref, weights_out.at[:, me], local_sem.at[0])
    own_copy.start()
    small_out[me] = small_ref[...]
    cot_out[me] = cot_ref[...]
    peers = [(rep, other) for other in others]
    peers += [(flip(rep, bit), me) for bit in (1,) + bits]
    greet(peers)

    regions = []
    for stream in streams:
        column = core * half + stream * 2 * fine
        narrow = columns_of(column + side(order(stream)[0]) * fine, fine)
        start, size = 0, rows
        held = [(pl.ds(0, rows), narrow)]
        for step in range(1, steps):
            size = size // 2
            start = start + side(order(stream)[step]) * size
            held.append((rows_of(start, size), narrow))
        regions.append((held, columns_of(column, 2 * fine)))

    def remote(source, target, send_sem, recv_sem, peer):
        return pltpu.make_async_remote_copy(
            src_ref=source,
            dst_ref=target,
            send_sem=send_sem,
            recv_sem=recv_sem,
            device_id=peer,
            device_id_type=MESH,
        )

    def line_copy(stream, source, peer):
        place, columns = regions[stream][0][-1]
        return remote(
            weights_ref.at[:, place, columns],
            weights_out.at[:, source, place, columns],
            line_send.at[stream, peer],
            line_recv.at[stream, source],
            (rep, peer),
        )

    def grow_copy(step, stream, source):
        place, columns = regions[stream][0][step]
        part = weights_out.at[:, source, place, columns]
        return remote(
            part,
            part,
            grow_send.at[step, stream, source],
            grow_recv.at[step, stream, source],
            (flip(rep, order(stream)[step]), me),
        )

    def join_copy(stream, source):
        part = weights_out.at[:, source, :, regions[stream][1]]
        return remote(
            part,
            part,
            join_send.at[stream, source],
            join_recv.at[stream, source],
            (flip(rep, 1), me),
        )

    def small_copy(source, peer):
        return remote(
            small_ref,
            small_out.at[source],
            small_send.at[peer],
            small_recv.at[source],
            (rep, peer),
        )

    def hand_on(block, to_right):
        peer = jnp.minimum(me + 1, count - 1) if to_right else jnp.maximum(me - 1, 0)
        return remote(
            cot_out.at[block],
            cot_out.at[block],
            (right_sem if to_right else left_sem).at[block],
            arrive_sem.at[block],
            (rep, peer),
        )

    def line_start():
        @pl.when(me < count - 1)
        def _():
            hand_on(me, True).start()

        @pl.when(me > 0)
        def _():
            hand_on(me, False).start()

    def line_step(step):
        lower = me - step
        upper = me + step

        @pl.when(lower >= 0)
        def _():
            hand_on(jnp.maximum(lower, 0), True).wait_recv()

            @pl.when(me < count - 1)
            def _():
                hand_on(jnp.maximum(lower, 0), True).start()

        @pl.when(upper < count)
        def _():
            hand_on(jnp.minimum(upper, count - 1), False).wait_recv()

            @pl.when(me > 0)
            def _():
                hand_on(jnp.minimum(upper, count - 1), False).start()

    def line_send_all():
        for other in others:
            for stream in streams:
                line_copy(stream, me, other).start()

    def advance(level):
        for other in others:
            for stream in streams:
                if level == 0:
                    line_copy(stream, other, other).wait_recv()
                else:
                    grow_copy(steps - level, stream, other).wait_recv()
                if level < steps:
                    grow_copy(steps - 1 - level, stream, other).start()
                else:
                    join_copy(stream, other).start()

    for other in others:
        small_copy(me, other).start()
    line_send_all()
    for other in others:
        small_copy(other, other).wait_recv()

    def gain(index):
        at = EXPERTS + index
        return jnp.concatenate([small_out[z, at : at + 1, :rows] for z in range(count)], axis=1)

    inputs = tokens_ref[...].astype(jnp.float32)
    first_out[...] = (normalize(inputs)[0] * gain(0)).astype(jnp.bfloat16)
    advance(0)
    line_start()
    for level in range(1, steps + 1):
        advance(level)
        if level == 1:
            line_step(1)
    for other in others:
        for stream in streams:
            join_copy(stream, other).wait_recv()
    own_copy.wait()
    leave = pltpu.make_async_copy(weights_out, weights_hbm, local_sem.at[2])
    leave.start()

    def whole(index):
        return weights_out[index].reshape(count * rows, width)

    project_inputs(first_out[...], whole, query_out, pair_out, table_ref)
    bias = allowed_pairs(column_ref[...], row_ref[...])
    if count > 2:
        line_step(2)
    attend_forward(range(KVHEADS // 2), query_out, pair_out, bias, head_out, total_out)
    for step in range(3, count - 1):
        line_step(step)
    attend_forward(range(KVHEADS // 2, KVHEADS), query_out, pair_out, bias, head_out, total_out)
    middle = inputs + dot_nn(head_out[...], whole(2))
    middle_out[...] = middle
    second_out[...] = (normalize(middle)[0] * gain(1)).astype(jnp.bfloat16)
    if count > 3:
        line_step(count - 1)
    for other in others:
        for stream in streams:
            join_copy(stream, other).wait_send()
            line_copy(stream, me, other).wait_send()
            for step in range(steps):
                grow_copy(step, stream, other).wait_send()
    for other in others:
        small_copy(me, other).wait_send()
    for block in range(count):

        @pl.when((block <= me) & (me < count - 1))
        def _():
            hand_on(block, True).wait_send()

        @pl.when((block >= me) & (me > 0))
        def _():
            hand_on(block, False).wait_send()

    leave.wait()


def gather(weights, small, tokens, cotangent, tables, starts, bits, count):
    rows, width = weights[0].shape
    depth = 3
    token_count = tokens.shape[0]
    steps = len(bits)
    low = jnp.bfloat16
    vmem = pl.BlockSpec(memory_space=pltpu.VMEM)
    dma = pltpu.SemaphoreType.DMA
    whole = jax.ShapeDtypeStruct((depth, count, rows, width), low)
    features = jax.ShapeDtypeStruct((token_count, width), low)
    return pl.pallas_call(
        functools.partial(gather_kernel, count, bits),
        in_specs=[vmem] * 10,
        out_specs=[pl.BlockSpec(memory_space=pl.ANY)] + [vmem] * 9,
        out_shape=[
            whole,
            jax.ShapeDtypeStruct((count,) + small.shape, small.dtype),
            jax.ShapeDtypeStruct((count, token_count, width), low),
            jax.ShapeDtypeStruct((token_count, width), jnp.float32),
            features,
            features,
            features,
            features,
            features,
            jax.ShapeDtypeStruct((2 * token_count, KVHEADS), jnp.float32),
        ],
        scratch_shapes=[
            pltpu.VMEM(whole.shape, low),
            pltpu.VMEM((depth, rows, width), low),
            dma((3,)),
            dma((2, count)),
            dma((2, count)),
            dma((steps, 2, count)),
            dma((steps, 2, count)),
            dma((2, count)),
            dma((2, count)),
            dma((count,)),
            dma((count,)),
            dma((count,)),
            dma((count,)),
            dma((count,)),
        ],
        compiler_params=pltpu.CompilerParams(
            collective_id=3, has_side_effects=True, vmem_limit_bytes=56 * 1024 * 1024
        ),
        name="gather",
    )(
        *weights,
        small,
        tokens,
        cotangent,
        tables,
        starts[:, None],
        starts[None, :],
    )


def local(
    tokens,
    sequence_start,
    routes,
    route_weights,
    cotangent,
    query_proj,
    key_proj,
    value_proj,
    out_proj,
    prenorm,
    midnorm,
    gate_proj,
    up_proj,
    down_proj,
    query_moment,
    key_moment,
    value_moment,
    out_moment,
    prenorm_moment,
    midnorm_moment,
    gate_moment,
    up_moment,
    down_moment,
):
    shard_index = lax.axis_index("shard")
    rep_count = lax.axis_size("rep")
    shard_count = lax.axis_size("shard")
    row_block = query_proj.shape[0]
    bits = rep_bits(rep_count)
    experts_here = gate_proj.shape[0]
    dense_weights = jnp.sum(
        jnp.where(
            routes.T[None, :, :] == jnp.arange(EXPERTS, dtype=jnp.int32)[:, None, None],
            route_weights.T[None, :, :],
            0.0,
        ),
        axis=1,
    )
    gain_rows = jnp.pad(
        jnp.stack([prenorm, midnorm]).astype(jnp.float32),
        ((0, 6), (0, tokens.shape[0] - row_block)),
    )
    tables = rotary_tables(jnp.arange(tokens.shape[0], dtype=jnp.int32) - sequence_start)
    (
        weights,
        small,
        cotangent_all,
        middle,
        normed_first,
        normed_second,
        query,
        pair,
        head_low,
        log_total,
    ) = gather(
        (query_proj, key_proj, value_proj, out_proj),
        jnp.concatenate([dense_weights, gain_rows], axis=0),
        tokens,
        cotangent,
        tables,
        sequence_start,
        bits,
        shard_count,
    )
    expert_weights = lax.dynamic_slice_in_dim(
        small, shard_index * experts_here, experts_here, 1
    ).transpose(0, 2, 1)
    returned, grad_second, expert_share = moe(
        normed_second,
        cotangent_all,
        expert_weights,
        gate_proj,
        up_proj,
        down_proj,
        bits,
        shard_count,
    )
    own_moments = (query_moment, key_moment, value_moment, out_moment)
    expert_grads, dense_next, dense_grads, gains_grad, grad_tokens, mixed = spread(
        expert_share,
        returned,
        normed_first,
        head_low,
        weights,
        small,
        tokens,
        cotangent,
        grad_second,
        middle,
        query,
        pair,
        log_total,
        tables,
        sequence_start,
        own_moments,
        bits=bits,
        count=shard_count,
    )
    gains_here = lax.dynamic_slice_in_dim(gains_grad, shard_index * row_block, row_block, 1)
    prenorm_grad = gains_here[0]
    midnorm_grad = gains_here[1]
    prenorm_next = momentum_keep * prenorm_moment + prenorm_grad
    midnorm_next = momentum_keep * midnorm_moment + midnorm_grad
    prenorm_update = -rate_gain * prenorm_next
    midnorm_update = -rate_gain * midnorm_next
    rep_index = lax.axis_index("rep")
    (
        query_grad,
        query_next,
        key_grad,
        key_next,
        value_grad,
        value_next,
        out_grad,
        out_next,
        own_wide,
        own_narrow,
    ) = dense_update(
        dense_next,
        dense_grads,
        own_moments,
        LAYOUT,
        shard_index,
        rep_index,
    )
    pairs = [(index, index + 1 - 2 * (index % 2)) for index in range(rep_count)]
    other_wide = lax.ppermute(own_wide, "rep", pairs)
    other_narrow = lax.ppermute(own_narrow, "rep", pairs)
    first_core = rep_index % 2 == 0
    query_update = jnp.where(first_core, own_wide, other_wide)
    out_update = jnp.where(first_core, other_wide, own_wide)
    key_update = jnp.where(first_core, own_narrow, other_narrow)
    value_update = jnp.where(first_core, other_narrow, own_narrow)
    gate_grad, gate_next, gate_update, up_grad, up_next, up_update = expert_update(
        expert_grads, (0, 1), (gate_moment, up_moment)
    )
    down_grad, down_next, down_update = expert_update(expert_grads, (2,), (down_moment,))
    return (
        mixed,
        grad_tokens,
        query_grad,
        query_next,
        query_update,
        key_grad,
        key_next,
        key_update,
        value_grad,
        value_next,
        value_update,
        out_grad,
        out_next,
        out_update,
        prenorm_grad,
        prenorm_next,
        prenorm_update,
        midnorm_grad,
        midnorm_next,
        midnorm_update,
        gate_grad,
        gate_next,
        gate_update,
        up_grad,
        up_next,
        up_update,
        down_grad,
        down_next,
        down_update,
    )


def solution(mesh):
    return jax.shard_map(
        local,
        mesh=mesh,
        in_specs=(
            P(("rep", "shard"), None),
            P(("rep", "shard")),
            P(("rep", "shard"), None),
            P(("rep", "shard"), None),
            P(("rep", "shard"), None),
            P("shard", None),
            P("shard", None),
            P("shard", None),
            P("shard", None),
            P("shard"),
            P("shard"),
            P("shard", None, None),
            P("shard", None, None),
            P("shard", None, None),
            P("shard", None),
            P("shard", None),
            P("shard", None),
            P("shard", None),
            P("shard"),
            P("shard"),
            P("shard", None, None),
            P("shard", None, None),
            P("shard", None, None),
        ),
        out_specs=(
            P(("rep", "shard"), None),
            P(("rep", "shard"), None),
            P("shard", None),
            P("shard", None),
            P("shard", None),
            P("shard", None),
            P("shard", None),
            P("shard", None),
            P("shard", None),
            P("shard", None),
            P("shard", None),
            P("shard", None),
            P("shard", None),
            P("shard", None),
            P("shard"),
            P("shard"),
            P("shard"),
            P("shard"),
            P("shard"),
            P("shard"),
            P("shard", None, None),
            P("shard", None, None),
            P("shard", None, None),
            P("shard", None, None),
            P("shard", None, None),
            P("shard", None, None),
            P("shard", None, None),
            P("shard", None, None),
            P("shard", None, None),
        ),
        check_vma=False,
    )
```

```python
import functools
import math

import jax
import jax.numpy as jnp
from jax import lax
from jax.experimental import pallas as pl
from jax.experimental.pallas import tpu as pltpu
from jax.sharding import PartitionSpec as P

NHEADS = 16
KVHEADS = 8
HEAD = 64
EXPERTS = 16
NS_ITERS = 2


norm_epsilon = 1e-06
rotary_base = 10000.0
momentum_keep = 0.9
rate_matrix = 0.5
rate_gain = 0.0002
newton_first = 3.4445
newton_second = -4.775
newton_third = 2.0315
masked_score = -1e30


def normalize(values):
    inverse = lax.rsqrt(jnp.mean(values * values, axis=-1, keepdims=True) + norm_epsilon)
    return (values * inverse, inverse)


def normalize_back(grad_normed, scaling, scaled, inverse):
    grad_scaled = grad_normed * scaling
    inner_mean = jnp.mean(grad_scaled * scaled, axis=-1, keepdims=True)
    return (
        inverse * (grad_scaled - scaled * inner_mean),
        jnp.sum(grad_normed * scaled, axis=0, keepdims=True),
    )


def dot_nn(left, right):
    return jnp.dot(left, right, preferred_element_type=jnp.float32)


def dot_nt(left, right):
    return lax.dot_general(
        left, right, (((1,), (1,)), ((), ())), preferred_element_type=jnp.float32
    )


def dot_tn(left, right):
    return lax.dot_general(
        left, right, (((0,), (0,)), ((), ())), preferred_element_type=jnp.float32
    )


def rotate(values, table_ref, sign):
    return (
        values * table_ref[0]
        + sign * pltpu.roll(values, 96, 1) * table_ref[1]
        + sign * pltpu.roll(values, 32, 1) * table_ref[2]
    )


def lane_low(shape):
    return lax.broadcasted_iota(jnp.int32, shape, 1) < HEAD


def twice(pair, upper):
    wide = pair.astype(jnp.float32)
    turned = pltpu.roll(wide, HEAD, 1)
    first = lane_low(pair.shape)
    return jnp.where(first != upper, wide, turned).astype(pair.dtype)


def stacked(pair):
    first = lane_low(pair.shape)
    zero = jnp.zeros_like(pair)
    return jnp.concatenate([jnp.where(first, pair, zero), jnp.where(first, zero, pair)], axis=0)


def unstacked(rows):
    half = rows.shape[0] // 2
    return jnp.where(lane_low((half, rows.shape[1])), rows[:half], rows[half:])


def allowed_pairs(start_column, start_row):
    shape = (start_column.shape[0], start_row.shape[1])
    query_places = lax.broadcasted_iota(jnp.int32, shape, 0)
    key_places = lax.broadcasted_iota(jnp.int32, shape, 1)
    one = (start_column == start_row) & (key_places <= query_places)
    return jnp.where(jnp.concatenate([one, one], axis=0), 0.0, masked_score)


def block_lanes(ref, block):
    return ref[:, block * 2 * HEAD : (block + 1) * 2 * HEAD]


def attend_pair(block, query_ref, pair_ref, bias):
    key = twice(block_lanes(pair_ref, block // 2), block % 2 == 1)
    value = twice(block_lanes(pair_ref, KVHEADS // 2 + block // 2), block % 2 == 1)
    queries = stacked(block_lanes(query_ref, block))
    scores = dot_nt(queries, key) * (1.0 / math.sqrt(HEAD)) + bias
    return (queries, key, value, scores)


def project_inputs(normed, weights, query_ref, pair_ref, table_ref):
    queries = dot_nn(normed, weights(0))
    for block in range(NHEADS // 2):
        lanes = slice(block * 2 * HEAD, (block + 1) * 2 * HEAD)
        query_ref[:, lanes] = rotate(queries[:, lanes], table_ref, 1.0).astype(jnp.bfloat16)
    pairs = dot_nn(normed, weights(1))
    for block in range(KVHEADS):
        lanes = slice(block * 2 * HEAD, (block + 1) * 2 * HEAD)
        value = pairs[:, lanes]
        if block < KVHEADS // 2:
            value = rotate(value, table_ref, 1.0)
        pair_ref[:, lanes] = value.astype(jnp.bfloat16)


def attend_forward(blocks, query_ref, pair_ref, bias, head_ref, total_ref):
    for block in blocks:
        _, _, value, scores = attend_pair(block, query_ref, pair_ref, bias)
        row_max = jnp.max(scores, axis=-1, keepdims=True)
        exponents = jnp.exp(scores - row_max)
        totals = jnp.sum(exponents, axis=-1, keepdims=True)
        softmax_low = (exponents * (1.0 / totals)).astype(jnp.bfloat16)
        head_ref[:, block * 2 * HEAD : (block + 1) * 2 * HEAD] = unstacked(
            dot_nn(softmax_low, value)
        ).astype(jnp.bfloat16)
        total_ref[:, block : block + 1] = row_max + jnp.log(totals)


def attend_backward(query_ref, pair_ref, bias, total_ref, grad_ref, table_ref, delta_ref):
    folded = []
    for block in range(KVHEADS):
        queries, key, value, scores = attend_pair(block, query_ref, pair_ref, bias)
        grads = stacked(block_lanes(grad_ref, block))
        softmax_full = jnp.exp(scores - total_ref[:, block : block + 1])
        grad_softmax = dot_nt(grads, value)
        inner = jnp.sum(softmax_full * grad_softmax, axis=-1, keepdims=True)
        grad_scores = (softmax_full * (grad_softmax - inner)).astype(jnp.bfloat16)
        scale = 1.0 / math.sqrt(HEAD)
        grad_query = unstacked(dot_nn(grad_scores, key)) * scale
        lanes = slice(block * 2 * HEAD, (block + 1) * 2 * HEAD)
        delta_ref[:, lanes] = rotate(grad_query, table_ref, -1.0).astype(jnp.bfloat16)
        grad_key = dot_tn(grad_scores, queries) * scale
        grad_value = dot_tn(softmax_full.astype(jnp.bfloat16), grads)
        folded.append(
            (
                grad_key + pltpu.roll(grad_key, HEAD, 1),
                grad_value + pltpu.roll(grad_value, HEAD, 1),
            )
        )
        if block % 2 == 1:
            first = lane_low(grad_key.shape)
            both = [jnp.where(first, low, high) for low, high in zip(*folded)]
            folded = []
            base = NHEADS * HEAD + (block // 2) * 2 * HEAD
            delta_ref[:, base : base + 2 * HEAD] = rotate(both[0], table_ref, -1.0).astype(
                jnp.bfloat16
            )
            base = base + KVHEADS * HEAD
            delta_ref[:, base : base + 2 * HEAD] = both[1].astype(jnp.bfloat16)


def rotary_tables(positions):
    half_size = HEAD // 2
    frequency = rotary_base ** (-(jnp.arange(half_size, dtype=jnp.float32) * 2.0) / HEAD)
    angles = positions.astype(jnp.float32)[:, None] * frequency[None, :]
    cosine, sine = (jnp.cos(angles), jnp.sin(angles))
    zero = jnp.zeros_like(sine)
    return jnp.stack(
        [
            jnp.concatenate([cosine] * 4, axis=1),
            jnp.concatenate([-sine, zero] * 2, axis=1),
            jnp.concatenate([zero, sine] * 2, axis=1),
        ]
    )


def newton_parts(grams):
    a, b, c = newton_first, newton_second, newton_third

    def times(left, right):
        return jnp.dot(left, right, preferred_element_type=jnp.float32)

    lows = [gram.astype(jnp.bfloat16) for gram in grams]
    firsts = [b * gram + c * times(low, low) for gram, low in zip(grams, lows)]
    first_lows = [first.astype(jnp.bfloat16) for first in firsts]
    mixes = [times(low, first) for low, first in zip(lows, first_lows)]
    nexts = [
        (a * a) * gram + (2.0 * a) * mix + times(mix.astype(jnp.bfloat16), first)
        for gram, mix, first in zip(grams, mixes, first_lows)
    ]
    next_lows = [gram.astype(jnp.bfloat16) for gram in nexts]
    seconds = [b * gram + c * times(low, low) for gram, low in zip(nexts, next_lows)]
    second_lows = [second.astype(jnp.bfloat16) for second in seconds]
    return list(zip(firsts, first_lows, seconds, second_lows))


def scaled_gram(gram):
    shape = gram.shape
    rows = lax.broadcasted_iota(jnp.int32, shape, 0)
    diagonal = rows == lax.broadcasted_iota(jnp.int32, shape, 1)
    inverse = 1.0 / (jnp.sqrt(jnp.sum(jnp.where(diagonal, gram, 0.0))) + 1e-07)
    return (gram * (inverse * inverse), inverse)


def expert_update_kernel(kinds, scale, carried, *refs):
    a = newton_first
    grads_ref = refs[0]
    moments = refs[1 : 1 + len(kinds)]
    given = refs[1 + len(kinds) : 1 + len(kinds) + carried]
    outs = refs[1 + len(kinds) + carried :]
    if carried:
        taken = outs[3 * len(kinds) : 3 * len(kinds) + carried]
        sem = outs[-1]
        core = lax.axis_index("rep") % 2

        def move(source, target):
            return pltpu.make_async_copy(given[source], taken[target], sem.at[target])

        @pl.when(pl.program_id(0) == 0)
        def _():
            for pair in (0, 2):

                @pl.when(core == 0)
                def _():
                    move(pair, pair).start()
                    move(pair + 1, pair + 1).start()

                @pl.when(core == 1)
                def _():
                    move(pair + 1, pair).start()
                    move(pair, pair + 1).start()

            for index in range(4, carried):
                move(index, index).start()

    half = grads_ref.shape[3]
    tall = kinds[0] < 2
    states = []
    for index in range(len(kinds)):
        for e in range(grads_ref.shape[0]):
            grad = grads_ref[e, index].astype(jnp.float32)
            if not tall:
                grad = jnp.concatenate([grad[:half], grad[half:]], axis=1)
            moment = momentum_keep * moments[index][e] + grad
            outs[3 * index][e] = grad
            outs[3 * index + 1][e] = moment
            low = moment.astype(jnp.bfloat16)
            sides = (((0,), (0,)), ((), ())) if tall else (((1,), (1,)), ((), ()))
            gram, inverse = scaled_gram(
                lax.dot_general(low, low, sides, preferred_element_type=jnp.float32)
            )
            states.append((index, e, inverse, low, gram))
    parts = newton_parts([state[-1] for state in states])
    for (index, e, inverse, low, _), (first, first_low, second, second_low) in zip(states, parts):
        rest = a * (first + second) + jnp.dot(
            first_low, second_low, preferred_element_type=jnp.float32
        )
        rest = ((-scale * inverse) * rest).astype(jnp.bfloat16)
        if tall:
            step = jnp.dot(low, rest, preferred_element_type=jnp.float32)
        else:
            step = jnp.dot(rest, low, preferred_element_type=jnp.float32)
        outs[3 * index + 2][e] = (-scale * a * a * inverse) * outs[3 * index + 1][e] + step
    if carried:

        @pl.when(pl.program_id(0) == pl.num_programs(0) - 1)
        def _():
            for index in range(carried):
                move(index, index).wait()


def expert_update(grads, kinds, moments, carried=()):
    count, rows, columns = moments[0].shape
    group = 2 // len(kinds)
    scale = rate_matrix * math.sqrt(max(1.0, columns / rows))
    block = pl.BlockSpec((group, rows, columns), lambda i: (i, 0, 0))
    place = kinds[0] // len(kinds)
    taken = pl.BlockSpec((group, len(kinds)) + grads.shape[2:], lambda i: (i, place, 0, 0))
    shape = jax.ShapeDtypeStruct(moments[0].shape, jnp.float32)
    hand_on = [pl.BlockSpec(memory_space=pl.ANY)] * len(carried)
    return pl.pallas_call(
        functools.partial(expert_update_kernel, kinds, scale, len(carried)),
        grid=(count // group,),
        in_specs=[taken] + [block] * len(kinds) + hand_on,
        out_specs=[block] * (3 * len(kinds)) + hand_on,
        out_shape=[shape] * (3 * len(kinds))
        + [jax.ShapeDtypeStruct(array.shape, array.dtype) for array in carried],
        scratch_shapes=[pltpu.SemaphoreType.DMA((len(carried),))] if carried else [],
        compiler_params=pltpu.CompilerParams(vmem_limit_bytes=60 * 1024 * 1024),
        name="expert_update",
        cost_estimate=pl.CostEstimate(
            flops=count * len(kinds) * 2500000000,
            bytes_accessed=moments[0].size * len(kinds) * 18,
            transcendentals=0,
        ),
    )(grads, *moments, *carried)


def dense_update_kernel(layout, place_ref, next_ref, grads_ref, *refs):
    a = newton_first
    amount = len(layout)
    own_moments = refs[:amount]
    outs = refs[amount : 3 * amount]
    updates = refs[3 * amount : 3 * amount + 2]
    matrices = refs[3 * amount + 2 : 3 * amount + 4]
    own_grads, own_next, sem = refs[3 * amount + 4 :]
    blocks, count, block_rows, width = next_ref.shape
    part = width // 3
    me = place_ref[0]
    core = place_ref[1]
    start = pl.multiple_of(me * block_rows, block_rows)
    loads = [
        pltpu.make_async_copy(
            own_moments[index], own_next.at[:, begin : begin + size], sem.at[2 * index]
        )
        for index, (begin, size) in enumerate(layout)
    ]
    for load in loads:
        load.start()

    for block in range(blocks):
        outer = slice(block * part, (block + 1) * part)
        lanes = pl.ds(pl.multiple_of(2 * core * part, part), part)
        matrices[0][:, outer] = next_ref[block, :, :, lanes].reshape(count * block_rows, part)
        for index in range(3):
            columns = slice(8 * part * index + block * part, 8 * part * index + (block + 1) * part)
            inner = slice(index * part, (index + 1) * part)
            own_grads[:, columns] = grads_ref[block, :, inner].astype(jnp.float32)
    for block in range(blocks // 2):
        outer = slice(block * part, (block + 1) * part)
        matrices[1][:, outer] = next_ref[
            core * (blocks // 2) + block, :, :, part : 2 * part
        ].reshape(count * block_rows, part)
    leaving = []
    for index, (begin, size) in enumerate(layout):
        loads[index].wait()
        lanes = slice(begin, begin + size)
        own_next[:, lanes] = momentum_keep * own_next[:, lanes] + own_grads[:, lanes]
        leaving += [
            pltpu.make_async_copy(own_grads.at[:, lanes], outs[2 * index], sem.at[2 * index]),
            pltpu.make_async_copy(own_next.at[:, lanes], outs[2 * index + 1], sem.at[2 * index + 1]),
        ]
        leaving[-2].start()
        leaving[-1].start()
    states = []
    for matrix in matrices:
        low = matrix[...]
        states.append(
            scaled_gram(
                lax.dot_general(
                    low, low, (((0,), (0,)), ((), ())), preferred_element_type=jnp.float32
                )
            )
        )
    parts = newton_parts([state[0] for state in states])
    for matrix, update, (_, inverse), (_, first_low, _, second_low) in zip(
        matrices, updates, states, parts
    ):
        rows, columns = matrix.shape
        scale = rate_matrix * math.sqrt(max(1.0, columns / rows))
        own = matrix[pl.ds(start, block_rows)]
        once = a * own.astype(jnp.float32) + jnp.dot(
            own, first_low, preferred_element_type=jnp.float32
        )
        update[...] = (-scale * inverse) * (
            a * once
            + jnp.dot(once.astype(jnp.bfloat16), second_low, preferred_element_type=jnp.float32)
        )
    for copy in leaving:
        copy.wait()


def dense_update(nexts, grads, own_moments, layout, shard_index, rep_index):
    _, count, block_rows, _ = nexts.shape
    width = own_moments[0].shape[1]
    whole = lambda shape: pl.BlockSpec(shape, lambda i: (0,) * len(shape))
    anywhere = pl.BlockSpec(memory_space=pl.ANY)
    shapes = []
    for _, size in layout:
        shapes += [jax.ShapeDtypeStruct((block_rows, size), jnp.float32)] * 2
    shapes += [
        jax.ShapeDtypeStruct((block_rows, width), jnp.float32),
        jax.ShapeDtypeStruct((block_rows, width // 2), jnp.float32),
    ]
    place = jnp.stack([shard_index, rep_index % 2]).astype(jnp.int32)
    return pl.pallas_call(
        functools.partial(dense_update_kernel, layout),
        grid=(1,),
        in_specs=[pl.BlockSpec(memory_space=pltpu.SMEM), whole(nexts.shape), whole(grads.shape)]
        + [anywhere] * len(own_moments),
        out_specs=[anywhere] * (2 * len(layout)) + [whole(shape.shape) for shape in shapes[-2:]],
        out_shape=shapes,
        scratch_shapes=[
            pltpu.VMEM((count * block_rows, width), jnp.bfloat16),
            pltpu.VMEM((count * block_rows, width // 2), jnp.bfloat16),
            pltpu.VMEM((block_rows, 3 * width), jnp.float32),
            pltpu.VMEM((block_rows, 3 * width), jnp.float32),
            pltpu.SemaphoreType.DMA((2 * len(layout),)),
        ],
        compiler_params=pltpu.CompilerParams(vmem_limit_bytes=63 * 1024 * 1024),
        name="dense_update",
        cost_estimate=pl.CostEstimate(
            flops=14000000000, bytes_accessed=24 * width * width, transcendentals=0
        ),
    )(place, nexts, grads, *own_moments)


LAYOUT = ((0, 1024), (1024, 512), (1536, 512), (2048, 1024))


MESH = pl.DeviceIdType.MESH


def flip(index, bit):
    return index + bit - 2 * bit * ((index // bit) % 2)


def greet(peers):
    barrier = pltpu.get_barrier_semaphore()
    for peer in peers:
        pl.semaphore_signal(barrier, inc=1, device_id=peer, device_id_type=MESH)
    pl.semaphore_wait(barrier, len(peers))


def stream_plan(rep, bits, base, size):
    stages = []
    starts = [base, base + size]
    for step in range(len(bits)):
        size = size // 2
        stage = []
        for stream in range(2):
            bit = bits[(step + stream) % len(bits)]
            side = (rep // bit) % 2
            keep = starts[stream] + side * size
            send = starts[stream] + (1 - side) * size
            starts[stream] = keep
            stage.append((bit, stream, keep, send, size))
        stages.append(stage)
    return stages


def rows_of(start, size):
    return pl.ds(pl.multiple_of(start, 16), size)


def moe_kernel(
    count,
    bits,
    own_ref,
    cot_ref,
    weight_ref,
    gate_hbm,
    up_hbm,
    down_hbm,
    stage_out,
    back_ref,
    share_ref,
    tok,
    turned,
    mats,
    hid,
    gate_delta,
    up_delta,
    stage_back,
    got_back,
    sum_back,
    sum_out,
    *rest,
):
    landing = rest[: 1 + 2 * len(bits)]
    (
        load_sem,
        right_sem,
        left_sem,
        arrive_sem,
        back_send,
        back_recv,
        sum_send,
        sum_recv,
    ) = rest[1 + 2 * len(bits) :]
    rep = lax.axis_index("rep")
    me = lax.axis_index("shard")
    experts = mats.shape[0]
    tokens = own_ref.shape[0]
    half = mats.shape[2] // 2
    core = rep % 2

    loads = [
        pltpu.make_async_copy(gate_hbm, mats.at[:, 0], load_sem.at[0]),
        pltpu.make_async_copy(up_hbm, mats.at[:, 1], load_sem.at[1]),
        pltpu.make_async_copy(
            down_hbm.at[:, :, pl.ds(0, half)], mats.at[:, 2, pl.ds(0, half)], load_sem.at[2]
        ),
        pltpu.make_async_copy(
            down_hbm.at[:, :, pl.ds(half, half)], mats.at[:, 2, pl.ds(half, half)], load_sem.at[3]
        ),
    ]
    for load in loads:
        load.start()
    peers = [(rep, lax.rem(me + k, count)) for k in range(1, count)]
    peers += [(flip(rep, bit), me) for bit in (1,) + bits]
    greet(peers)

    right_peer = (rep, jnp.minimum(me + 1, count - 1))
    left_peer = (rep, jnp.maximum(me - 1, 0))

    def hand_on(block, to_right):
        return pltpu.make_async_remote_copy(
            src_ref=tok.at[block],
            dst_ref=tok.at[block],
            send_sem=(right_sem if to_right else left_sem).at[block],
            recv_sem=arrive_sem.at[block],
            device_id=right_peer if to_right else left_peer,
            device_id_type=MESH,
        )

    def returning(stage, got, send_sem, recv_sem, block):
        return pltpu.make_async_remote_copy(
            src_ref=stage.at[block],
            dst_ref=got.at[me],
            send_sem=send_sem.at[block],
            recv_sem=recv_sem.at[me],
            device_id=(rep, block),
            device_id_type=MESH,
        )

    tok[me] = own_ref[...]

    @pl.when(me < count - 1)
    def _():
        hand_on(me, True).start()

    @pl.when(me > 0)
    def _():
        hand_on(me, False).start()

    for load in loads:
        load.wait()

    margin = jnp.minimum(me, count - 1 - me)
    longer = jnp.where(me < count - 1 - me, 1, -1)
    inward = jnp.where(2 * me < count, 1, -1)
    nt = (((1,), (1,)), ((), ()))

    def dot(left, right):
        return jnp.dot(left, right, preferred_element_type=jnp.float32)

    def dot_nt(left, right):
        return lax.dot_general(left, right, nt, preferred_element_type=jnp.float32)

    def arrivals(j):
        lower = me - j
        upper = me + j

        @pl.when((j > 0) & (lower >= 0))
        def _():
            hand_on(jnp.maximum(lower, 0), True).wait_recv()

            @pl.when(me < count - 1)
            def _():
                hand_on(jnp.maximum(lower, 0), True).start()

        @pl.when((j > 0) & (upper < count))
        def _():
            hand_on(jnp.minimum(upper, count - 1), False).wait_recv()

            @pl.when(me > 0)
            def _():
                hand_on(jnp.minimum(upper, count - 1), False).start()

    def block_at(j):
        near = (j + 1) // 2
        alternating = me + near - 2 * near * (j % 2)
        return jnp.where(j <= 2 * margin, alternating, me + longer * (j - margin))

    def places_of(block):
        return pl.ds(pl.multiple_of(block * tokens, tokens), tokens)

    def factors(e, block):
        places = places_of(block)
        rows = tok[block]
        grads = cot_ref[block]
        weight = weight_ref[block, :, e : e + 1]
        u = dot(rows, mats[e, 0])
        w = dot(rows, mats[e, 1])
        gate = 1.0 / (1.0 + jnp.exp(-u))
        act = u * gate
        hidden = (weight * (act * w)).astype(jnp.bfloat16)
        hid[e, :, places] = hidden.T
        pulled = weight * (
            dot_nt(grads[:, :half], mats[e, 2, :half])
            + dot_nt(grads[:, half:], mats[e, 2, half:])
        )
        gate_delta[e, places] = (pulled * w * (gate + act * (1.0 - gate))).astype(jnp.bfloat16)
        up_delta[e, places] = (pulled * act).astype(jnp.bfloat16)
        return hidden

    def sums(block, e, hidden, place):
        places = places_of(block)
        for side in range(2):
            part = slice(side * half, (side + 1) * half)
            back = dot_nt(gate_delta[e, places], mats[e, 0, part]) + dot_nt(
                up_delta[e, places], mats[e, 1, part]
            )
            out = dot(hidden, mats[e, 2, part])
            if e > 0:
                back = place[0][:, part] + back
                out = place[1][:, part] + out
            place[0][:, part] = back
            place[1][:, part] = out

    def visit(j, carry):
        arrivals(j)
        block = block_at(j)
        places = places_of(block)
        turned[:, places] = tok[block].T
        hiddens = [factors(e, block) for e in range(experts)]
        for side in range(2):
            part = slice(side * half, (side + 1) * half)
            total_back = None
            total_out = None
            for e in range(experts):
                back = dot_nt(gate_delta[e, places], mats[e, 0, part]) + dot_nt(
                    up_delta[e, places], mats[e, 1, part]
                )
                out = dot(hiddens[e], mats[e, 2, part])
                total_back = back if e == 0 else total_back + back
                total_out = out if e == 0 else total_out + out
            stage_back[block, :, part] = total_back.astype(jnp.bfloat16)
            stage_out[block, :, part] = total_out.astype(jnp.bfloat16)

        @pl.when((j > 0) & ((block - me) * inward > 0))
        def _():
            returning(stage_back, got_back, back_send, back_recv, block).start()

        return carry

    lax.fori_loop(0, count - 1, visit, 0)
    arrivals(count - 1)
    last = block_at(count - 1)
    for k in range(1, count):
        block = block_at(k - 1)

        @pl.when((block - me) * inward < 0)
        def _():
            returning(stage_back, got_back, back_send, back_recv, block).start()

    turned[:, places_of(last)] = tok[last].T
    plan = stream_plan(rep, bits, core * half, half // 2)

    def sum_copy(stage, slot, e, start, size, bit):
        return pltpu.make_async_remote_copy(
            src_ref=mats.at[e, :, rows_of(start, size)],
            dst_ref=landing[slot].at[e],
            send_sem=sum_send.at[slot, e],
            recv_sem=sum_recv.at[slot, e],
            device_id=(flip(rep, bit), me),
            device_id_type=MESH,
        )

    def copies(stage, e):
        if stage == 0:
            return [(sum_copy(0, 0, e, (1 - core) * half, half, 1), 0, core * half, half)]
        return [
            (
                sum_copy(stage, 1 + 2 * (stage - 1) + stream, e, send, size, bit),
                1 + 2 * (stage - 1) + stream,
                keep,
                size,
            )
            for bit, stream, keep, send, size in plan[stage - 1]
        ]

    def finish(stage, e):
        for copy, slot, keep, size in copies(stage, e):
            copy.wait_recv()
            place = rows_of(keep, size)
            for kind in range(3):
                mats[e, kind, place] = (
                    mats[e, kind, place].astype(jnp.float32)
                    + landing[slot][e, kind].astype(jnp.float32)
                ).astype(jnp.bfloat16)

    stages = 1 + len(bits)
    for turn in range(experts + stages):
        if turn < experts:
            e = turn
            sums(last, e, factors(e, last), (sum_back, sum_out))
            for side in range(2):
                part = slice(side * half, (side + 1) * half)
                mats[e, 0, part] = dot(turned[part], gate_delta[e]).astype(jnp.bfloat16)
                mats[e, 1, part] = dot(turned[part], up_delta[e]).astype(jnp.bfloat16)
                mats[e, 2, part] = dot(hid[e], cot_ref[:, :, part].reshape(count * tokens, half)).astype(jnp.bfloat16)
            copies(0, e)[0][0].start()
            if e == experts - 1:
                stage_back[last] = sum_back[...].astype(jnp.bfloat16)
                stage_out[last] = sum_out[...].astype(jnp.bfloat16)
                returning(stage_back, got_back, back_send, back_recv, last).start()
        for stage in range(stages):
            e = turn - 1 - stage
            if 0 <= e < experts:
                finish(stage, e)
                if stage + 1 < stages:
                    for copy, _, _, _ in copies(stage + 1, e):
                        copy.start()
                else:
                    for _, stream, keep, _, size in plan[-1]:
                        share_ref[e, :, stream] = mats[e, :, rows_of(keep, size)]

    total = stage_back[me].astype(jnp.float32)
    for k in range(1, count):
        source = lax.rem(me + k, count)
        pltpu.make_async_remote_copy(
            src_ref=stage_back.at[source],
            dst_ref=got_back.at[source],
            send_sem=back_send.at[source],
            recv_sem=back_recv.at[source],
            device_id=(rep, source),
            device_id_type=MESH,
        ).wait_recv()
        total = total + got_back[source].astype(jnp.float32)
    back_ref[...] = total
    for k in range(1, count):
        block = lax.rem(me + k, count)
        returning(stage_back, got_back, back_send, back_recv, block).wait_send()
    for e in range(experts):
        for stage in range(stages):
            for copy, _, _, _ in copies(stage, e):
                copy.wait_send()
    for block in range(count):

        @pl.when((block <= me) & (me < count - 1))
        def _():
            hand_on(block, True).wait_send()

        @pl.when((block >= me) & (me > 0))
        def _():
            hand_on(block, False).wait_send()


def moe(normed, cotangents, weights, gate_proj, up_proj, down_proj, bits, count):
    tokens, width = normed.shape
    experts, _, hidden = gate_proj.shape
    half = width // 2
    low = jnp.bfloat16
    final = (half // 2) >> len(bits)
    vmem = pl.BlockSpec(memory_space=pltpu.VMEM)
    anywhere = pl.BlockSpec(memory_space=pl.ANY)
    landings = [pltpu.VMEM((experts, 3, half, hidden), low)]
    for step in range(len(bits)):
        size = (half // 2) >> (step + 1)
        landings += [pltpu.VMEM((experts, 3, size, hidden), low)] * 2
    slots = len(landings)
    dma = pltpu.SemaphoreType.DMA
    return pl.pallas_call(
        functools.partial(moe_kernel, count, bits),
        in_specs=[vmem, vmem, vmem, anywhere, anywhere, anywhere],
        out_specs=[vmem, vmem, vmem],
        out_shape=[
            jax.ShapeDtypeStruct((count, tokens, width), low),
            jax.ShapeDtypeStruct((tokens, width), jnp.float32),
            jax.ShapeDtypeStruct((experts, 3, 2, final, hidden), low),
        ],
        scratch_shapes=[
            pltpu.VMEM((count, tokens, width), low),
            pltpu.VMEM((width, count * tokens), low),
            pltpu.VMEM((experts, 3, width, hidden), low),
            pltpu.VMEM((experts, hidden, count * tokens), low),
            pltpu.VMEM((experts, count * tokens, hidden), low),
            pltpu.VMEM((experts, count * tokens, hidden), low),
            pltpu.VMEM((count, tokens, width), low),
            pltpu.VMEM((count, tokens, width), low),
            pltpu.VMEM((tokens, width), jnp.float32),
            pltpu.VMEM((tokens, width), jnp.float32),
        ]
        + landings
        + [
            dma((4,)),
            dma((count,)),
            dma((count,)),
            dma((count,)),
            dma((count,)),
            dma((count,)),
            dma((slots, experts)),
            dma((slots, experts)),
        ],
        compiler_params=pltpu.CompilerParams(
            collective_id=1, has_side_effects=True, vmem_limit_bytes=63 * 1024 * 1024
        ),
        name="moe",
        cost_estimate=pl.CostEstimate(
            flops=39000000000, bytes_accessed=20000000, transcendentals=2000000
        ),
    )(normed, cotangents, weights, gate_proj, up_proj, down_proj)


def rep_bits(rep_count):
    bits = []
    bit = 2
    while bit < rep_count:
        bits.append(bit)
        bit = bit * 2
    return tuple(bits)


def spread_kernel(
    count,
    bits,
    share_ref,
    returned_ref,
    normed_ref,
    head_ref,
    weights_ref,
    small_ref,
    tokens_ref,
    cot_ref,
    second_ref,
    middle_ref,
    query_ref,
    pair_ref,
    total_ref,
    table_ref,
    column_ref,
    row_ref,
    query_moment,
    key_moment,
    value_moment,
    out_moment,
    experts_hbm,
    dense_out,
    grads_out,
    gains_out,
    tokens_out,
    mixed_out,
    experts_out,
    got_ref,
    moment_piece,
    delta_ref,
    branch_ref,
    heads_ref,
    dense_ref,
    total,
    land_core,
    land_first,
    *rest,
):
    later = len(bits) - 1
    land_later = rest[:later]
    (
        piece_send,
        piece_land,
        piece,
        gains_send,
        gains_land,
        gains_all,
        local_sem,
        core_send,
        core_recv,
        half_send,
        half_recv,
        shard_send,
        shard_recv,
        grow_send,
        grow_recv,
        line_send,
        line_recv,
        join_send,
        join_recv,
        expert_send,
        expert_recv,
        gain_send,
        gain_recv,
        gain_line_send,
        gain_line_recv,
        back_send,
        back_recv,
        moment_sem,
        own_send,
        own_recv,
        own_join_send,
        own_join_recv,
    ) = rest[later:]
    rep = lax.axis_index("rep")
    me = lax.axis_index("shard")
    core = rep % 2
    rows = dense_ref.shape[2]
    expert_rows = experts_out.shape[2]
    steps = len(bits)
    streams = range(2)

    def remote(source, target, send_sem, recv_sem, peer):
        return pltpu.make_async_remote_copy(
            src_ref=source,
            dst_ref=target,
            send_sem=send_sem,
            recv_sem=recv_sem,
            device_id=peer,
            device_id_type=MESH,
        )

    def across(bit):
        return (flip(rep, bit), me)

    def order(stream):
        return [bits[(step + stream) % steps] for step in range(steps)]

    def side(bit):
        return (rep // bit) % 2

    plan = stream_plan(rep, bits, core * (expert_rows // 2), expert_rows // 4)
    base = [(core * (expert_rows // 2)) + stream * (expert_rows // 4) for stream in streams]

    def expert_copy(level, stream):
        if level == steps:
            place = rows_of(base[stream], expert_rows // 4)
            peer = across(1)
        else:
            bit, _, keep, _, size = plan[steps - 1 - level][stream]
            place = rows_of(keep, size)
            peer = across(bit)
        source = experts_out.at[:, :, place]
        if level == 0:
            source = share_ref.at[:, :, stream]
        return remote(
            source,
            experts_out.at[:, :, place],
            expert_send.at[level, stream],
            expert_recv.at[level, stream],
            peer,
        )

    def own_copy(stream):
        _, _, keep, _, size = plan[-1][stream]
        return pltpu.make_async_copy(
            share_ref.at[:, :, stream],
            experts_out.at[:, :, rows_of(keep, size)],
            local_sem.at[stream],
        )

    for stream in streams:
        own_copy(stream).start()
    peers = [(rep, lax.rem(me + k, count)) for k in range(1, count)]
    peers += [across(bit) for bit in (1,) + bits]
    greet(peers)

    def returning(peer, source):
        return remote(
            returned_ref.at[peer],
            got_ref.at[source],
            back_send.at[peer],
            back_recv.at[source],
            (rep, peer),
        )

    def core_copy(block):
        return remote(
            dense_ref.at[4 * (1 - core) + block],
            land_core.at[block],
            core_send.at[block],
            core_recv.at[block],
            across(1),
        )

    gain_bits = (1,) + bits

    def gain_copy(stage):
        return remote(
            gains_send.at[stage],
            gains_land.at[stage],
            gain_send.at[stage],
            gain_recv.at[stage],
            across(gain_bits[stage]),
        )

    for stream in streams:
        expert_copy(0, stream).start()

    for k in range(1, count):
        returning(lax.rem(me + k, count), me).start()

    def whole(index):
        return weights_ref[index].reshape(count * rows, -1)

    def gain(index):
        at = EXPERTS + index
        return jnp.concatenate([small_ref[z, at : at + 1, :rows] for z in range(count)], axis=1)

    scaled, inverse = normalize(middle_ref[...])
    middle_extra, midnorm_part = normalize_back(second_ref[...], gain(1), scaled, inverse)
    grad_middle = cot_ref[...].astype(jnp.float32) + middle_extra
    tokens_out[...] = grad_middle
    branch_ref[...] = grad_middle.astype(jnp.bfloat16)
    heads_ref[...] = dot_nt(branch_ref[...], whole(2)).astype(jnp.bfloat16)
    bias = allowed_pairs(column_ref[...], row_ref[...])
    attend_backward(query_ref, pair_ref, bias, total_ref, heads_ref, table_ref, delta_ref)

    part = dense_ref.shape[3] // 3
    normed_turned = normed_ref[...].T
    head_turned = head_ref[...].T

    def make_block(block):
        def columns(ref, offset):
            return ref[:, pl.ds(pl.multiple_of(offset + block * part, part), part)]

        pair = jnp.concatenate([columns(delta_ref, 0), columns(delta_ref, 8 * part)], axis=1)
        left = jnp.dot(normed_turned, pair, preferred_element_type=jnp.float32)
        right = jnp.dot(head_turned, columns(branch_ref, 0), preferred_element_type=jnp.float32)
        for line in range(count):
            place = slice(line * rows, (line + 1) * rows)
            dense_ref[block, line, :, : 2 * part] = left[place].astype(jnp.bfloat16)
            dense_ref[block, line, :, 2 * part :] = right[place].astype(jnp.bfloat16)

    for block in range(4):
        make_block(4 * (1 - core) + block)
        core_copy(block).start()
    for block in range(4):
        make_block(4 * core + block)

    def gain_step(stage):
        gain_copy(stage).wait_recv()
        gains_send[stage + 1] = gains_send[stage] + gains_land[stage]
        if stage + 1 < len(gain_bits):
            gain_copy(stage + 1).start()

    first = [side(order(stream)[0]) for stream in streams]
    held = [2 * stream + first[stream] for stream in streams]
    given = [2 * stream + 1 - first[stream] for stream in streams]

    def first_copy(stream):
        return remote(
            total.at[given[stream]],
            land_first.at[stream],
            half_send.at[0, stream],
            half_recv.at[0, stream],
            across(order(stream)[0]),
        )

    def add_core(block):
        for line in range(count):
            total[block, line] = (
                dense_ref[4 * core + block, line].astype(jnp.float32)
                + land_core[block, line].astype(jnp.float32)
            ).astype(jnp.bfloat16)

    for block in range(4):
        core_copy(block).wait_recv()
    for stream in streams:
        add_core(given[stream])
        first_copy(stream).start()
    for stream in streams:
        add_core(held[stream])
    grad_first = dot_nt(delta_ref[:, : NHEADS * HEAD], whole(0)) + dot_nt(
        delta_ref[:, NHEADS * HEAD :], whole(1)
    )
    scaled, inverse = normalize(tokens_ref[...].astype(jnp.float32))
    input_extra, prenorm_part = normalize_back(grad_first, gain(0), scaled, inverse)
    tokens_out[...] = tokens_out[...] + input_extra
    gains_send[0] = jnp.concatenate(
        [prenorm_part, midnorm_part, jnp.zeros((6, prenorm_part.shape[1]), jnp.float32)], axis=0
    )
    gain_copy(0).start()
    gain_step(0)

    starts = []
    for stream in streams:
        start, size, line = 0, rows, []
        for step in range(1, steps):
            size = size // 2
            near = side(order(stream)[step])
            line.append((start + near * size, start + (1 - near) * size, size))
            start = start + near * size
        starts.append((start, size, line))

    last = starts[0][1]
    places = [rows_of(starts[stream][0], last) for stream in streams]
    inner = [slice(index * part, (index + 1) * part) for index in range(3)]

    def moment_copy(stream, index):
        block = 4 * core + held[stream]
        lanes = pl.ds(pl.multiple_of((held[stream] if index == 1 else block) * part, part), part)
        source = (query_moment, key_moment, out_moment)[index]
        return pltpu.make_async_copy(
            source.at[places[stream], lanes],
            moment_piece.at[stream, :, inner[index]],
            moment_sem.at[stream, index],
        )

    def moment_other(stream):
        lanes = pl.ds(pl.multiple_of(held[stream] * part, part), part)
        return pltpu.make_async_copy(
            value_moment.at[places[stream], lanes],
            moment_piece.at[stream, :, inner[1]],
            moment_sem.at[stream, 1],
        )

    for stream in streams:
        moment_copy(stream, 0).start()
        moment_copy(stream, 2).start()

        @pl.when(core == 0)
        def _():
            moment_copy(stream, 1).start()

        @pl.when(core == 1)
        def _():
            moment_other(stream).start()

    def later_copy(step, stream):
        keep, send, size = starts[stream][2][step - 1]
        return remote(
            total.at[held[stream], :, rows_of(send, size)],
            land_later[step - 1].at[stream],
            half_send.at[step, stream],
            half_recv.at[step, stream],
            across(order(stream)[step]),
        )

    for stream in streams:
        first_copy(stream).wait_recv()
        for line in range(count):
            total[held[stream], line] = (
                total[held[stream], line].astype(jnp.float32)
                + land_first[stream, line].astype(jnp.float32)
            ).astype(jnp.bfloat16)
        if steps > 1:
            later_copy(1, stream).start()
    gain_step(1)

    for step in range(1, steps):
        for stream in streams:
            later_copy(step, stream).wait_recv()
            keep, _, size = starts[stream][2][step - 1]
            for line in range(count):
                place = rows_of(keep, size)
                total[held[stream], line, place] = (
                    total[held[stream], line, place].astype(jnp.float32)
                    + land_later[step - 1][stream, line].astype(jnp.float32)
                ).astype(jnp.bfloat16)
            if step + 1 < steps:
                later_copy(step + 1, stream).start()
        gain_step(step + 1)

    for stream in streams:
        own_copy(stream).wait()
        expert_copy(0, stream).wait_recv()
        if steps > 1:
            expert_copy(1, stream).start()

    for stream in streams:
        for line in range(count):
            piece_send[line, stream] = total[held[stream], line, places[stream]]

    def shard_copy(k):
        target = lax.rem(me + k, count)
        return remote(
            piece_send.at[target],
            piece_land.at[me],
            shard_send.at[target],
            shard_recv.at[me],
            (rep, target),
        )

    def shard_arrival(source):
        return remote(
            piece_send.at[source],
            piece_land.at[source],
            shard_send.at[source],
            shard_recv.at[source],
            (rep, source),
        )

    def gain_line(k):
        target = lax.rem(me + k, count)
        return remote(
            gains_send.at[len(gain_bits)],
            gains_all.at[me],
            gain_line_send.at[target],
            gain_line_recv.at[me],
            (rep, target),
        )

    def gain_arrival(source):
        return remote(
            gains_send.at[len(gain_bits)],
            gains_all.at[source],
            gain_line_send.at[source],
            gain_line_recv.at[source],
            (rep, source),
        )

    def own_grow(step, stream):
        block = 4 * core + held[stream]
        if step == 0:
            part_ref = grads_out.at[block]
        else:
            keep, _, size = starts[stream][2][step - 1]
            part_ref = grads_out.at[block, rows_of(keep, size)]
        return remote(
            part_ref,
            part_ref,
            own_send.at[step, stream],
            own_recv.at[step, stream],
            across(order(stream)[step]),
        )

    def own_join(stream):
        part_ref = grads_out.at[pl.ds(4 * core + 2 * stream, 2)]
        return remote(
            part_ref, part_ref, own_join_send.at[stream], own_join_recv.at[stream], across(1)
        )

    for k in range(1, count):
        shard_copy(k).start()
        gain_line(k).start()
    summed = piece_send[me].astype(jnp.float32)
    for k in range(1, count):
        source = lax.rem(me + k, count)
        shard_arrival(source).wait_recv()
        summed = summed + piece_land[source].astype(jnp.float32)
    for stream in streams:
        for index in range(3):
            moment_copy(stream, index).wait()
        grads_out[4 * core + held[stream], places[stream]] = summed[stream].astype(jnp.bfloat16)
        own_grow(steps - 1, stream).start()
    piece[...] = (momentum_keep * moment_piece[...] + summed).astype(jnp.bfloat16)

    def line_copy(k, stream):
        target = lax.rem(me + k, count)
        return remote(
            piece.at[stream],
            dense_out.at[4 * core + held[stream], me, places[stream]],
            line_send.at[stream, target],
            line_recv.at[stream, me],
            (rep, target),
        )

    def line_arrival(source, stream):
        return remote(
            piece.at[stream],
            dense_out.at[4 * core + held[stream], source, places[stream]],
            line_send.at[stream, source],
            line_recv.at[stream, source],
            (rep, source),
        )

    def own_piece(stream):
        return pltpu.make_async_copy(
            piece.at[stream],
            dense_out.at[4 * core + held[stream], me, places[stream]],
            local_sem.at[2 + stream],
        )

    for stream in streams:
        own_piece(stream).start()
        for k in range(1, count):
            line_copy(k, stream).start()
    gained = gains_send[len(gain_bits)]
    for k in range(1, count):
        source = lax.rem(me + k, count)
        gain_arrival(source).wait_recv()
        gained = gained + gains_all[source]
    gains_out[...] = gained

    for level in range(1, steps):
        for stream in streams:
            expert_copy(level, stream).wait_recv()
            expert_copy(level + 1, stream).start()
    if steps == 1:
        for stream in streams:
            expert_copy(1, stream).start()

    def grow_copy(step, stream):
        if step == 0:
            place = dense_out.at[4 * core + held[stream]]
        else:
            keep, _, size = starts[stream][2][step - 1]
            place = dense_out.at[4 * core + held[stream], :, rows_of(keep, size)]
        return remote(
            place,
            place,
            grow_send.at[step, stream],
            grow_recv.at[step, stream],
            across(order(stream)[step]),
        )

    for stream in streams:
        own_piece(stream).wait()
        for k in range(1, count):
            line_arrival(lax.rem(me + k, count), stream).wait_recv()
        grow_copy(steps - 1, stream).start()
    for step in reversed(range(steps)):
        for stream in streams:
            own_grow(step, stream).wait_recv()
            if step > 0:
                own_grow(step - 1, stream).start()
            else:
                own_join(stream).start()
    mixed = middle_ref[...] + returned_ref[me].astype(jnp.float32)
    for k in range(1, count):
        source = lax.rem(me + k, count)
        returning(source, source).wait_recv()
        mixed = mixed + got_ref[source].astype(jnp.float32)
    mixed_out[...] = mixed.astype(mixed_out.dtype)
    for stream in streams:
        expert_copy(steps, stream).wait()
    leave = pltpu.make_async_copy(experts_out, experts_hbm, local_sem.at[0])
    leave.start()
    for step in reversed(range(steps)):
        for stream in streams:
            grow_copy(step, stream).wait_recv()
            if step > 0:
                grow_copy(step - 1, stream).start()

    def join_copy(stream):
        place = dense_out.at[pl.ds(4 * core + 2 * stream, 2)]
        return remote(place, place, join_send.at[stream], join_recv.at[stream], across(1))

    for stream in streams:
        join_copy(stream).start()
    for stream in streams:
        join_copy(stream).wait()
        own_join(stream).wait()
        for step in range(steps):
            own_grow(step, stream).wait_send()
        for level in range(steps):
            expert_copy(level, stream).wait_send()
        first_copy(stream).wait_send()
        for step in range(1, steps):
            later_copy(step, stream).wait_send()
        for k in range(1, count):
            line_copy(k, stream).wait_send()
        for step in range(steps):
            grow_copy(step, stream).wait_send()
    for block in range(4):
        core_copy(block).wait_send()
    for stage in range(len(gain_bits)):
        gain_copy(stage).wait_send()
    for k in range(1, count):
        shard_copy(k).wait_send()
        gain_line(k).wait_send()
        returning(lax.rem(me + k, count), me).wait_send()
    leave.wait()


def spread(
    share, returned, normed, head_low, weights, small, tokens, cotangent, second, middle, *rest, bits, count
):
    query, pair, log_total, tables, starts, moments = rest
    experts, _, _, final, hidden = share.shape
    token_count, features = normed.shape
    rows = features // count
    width = 3 * features // 8
    dense_shape = (8, count, rows, width)
    gains_shape = (8, features)
    steps = len(bits)
    last = rows >> (steps - 1)
    low = jnp.bfloat16
    vmem = pl.BlockSpec(memory_space=pltpu.VMEM)
    dma = pltpu.SemaphoreType.DMA
    return pl.pallas_call(
        functools.partial(spread_kernel, count, bits),
        in_specs=[vmem] * 16 + [pl.BlockSpec(memory_space=pl.ANY)] * 4,
        out_specs=[pl.BlockSpec(memory_space=pl.ANY)] + [vmem] * 5,
        out_shape=[
            jax.ShapeDtypeStruct((experts, 3, 4 * (final << steps), hidden), low),
            jax.ShapeDtypeStruct(dense_shape, low),
            jax.ShapeDtypeStruct((8, rows, width), low),
            jax.ShapeDtypeStruct(gains_shape, jnp.float32),
            jax.ShapeDtypeStruct((token_count, features), jnp.float32),
            jax.ShapeDtypeStruct((token_count, features), low),
        ],
        scratch_shapes=[
            pltpu.VMEM((experts, 3, 4 * (final << steps), hidden), low),
            pltpu.VMEM((count, token_count, features), low),
            pltpu.VMEM((2, last, width), jnp.float32),
            pltpu.VMEM((token_count, 2 * features), low),
            pltpu.VMEM((token_count, features), low),
            pltpu.VMEM((token_count, features), low),
            pltpu.VMEM(dense_shape, low),
            pltpu.VMEM((4, count, rows, width), low),
            pltpu.VMEM((4, count, rows, width), low),
            pltpu.VMEM((2, count, rows, width), low),
        ]
        + [pltpu.VMEM((2, count, rows >> step, width), low) for step in range(1, steps)]
        + [
            pltpu.VMEM((count, 2, last, width), low),
            pltpu.VMEM((count, 2, last, width), low),
            pltpu.VMEM((2, last, width), low),
            pltpu.VMEM((steps + 2,) + gains_shape, jnp.float32),
            pltpu.VMEM((steps + 1,) + gains_shape, jnp.float32),
            pltpu.VMEM((count,) + gains_shape, jnp.float32),
            dma((4,)),
            dma((4,)),
            dma((4,)),
            dma((steps, 2)),
            dma((steps, 2)),
            dma((count,)),
            dma((count,)),
            dma((steps, 2)),
            dma((steps, 2)),
            dma((2, count)),
            dma((2, count)),
            dma((2,)),
            dma((2,)),
            dma((steps + 1, 2)),
            dma((steps + 1, 2)),
            dma((steps + 1,)),
            dma((steps + 1,)),
            dma((count,)),
            dma((count,)),
            dma((count,)),
            dma((count,)),
            dma((2, 3)),
            dma((steps, 2)),
            dma((steps, 2)),
            dma((2,)),
            dma((2,)),
        ],
        compiler_params=pltpu.CompilerParams(
            collective_id=2, has_side_effects=True, vmem_limit_bytes=63 * 1024 * 1024
        ),
        name="spread",
    )(
        share,
        returned,
        normed,
        head_low,
        weights,
        small,
        tokens,
        cotangent,
        second,
        middle,
        query,
        pair,
        log_total,
        tables,
        starts[:, None],
        starts[None, :],
        *moments,
    )


def gather_kernel(
    count,
    bits,
    query_weight,
    key_weight,
    value_weight,
    out_weight,
    small_ref,
    tokens_ref,
    cot_ref,
    table_ref,
    column_ref,
    row_ref,
    weights_hbm,
    small_out,
    cot_out,
    middle_out,
    first_out,
    second_out,
    query_out,
    pair_out,
    head_out,
    total_out,
    weights_out,
    weights_ref,
    local_sem,
    line_send,
    line_recv,
    grow_send,
    grow_recv,
    join_send,
    join_recv,
    small_send,
    small_recv,
    right_sem,
    left_sem,
    arrive_sem,
):
    rep = lax.axis_index("rep")
    me = lax.axis_index("shard")
    core = rep % 2
    steps = len(bits)
    streams = range(2)
    rows, width = weights_ref.shape[1:]
    half = width // 2
    fine = half // 4
    others = [lax.rem(me + k, count) for k in range(1, count)]

    def columns_of(start, size):
        return pl.ds(pl.multiple_of(start, 128), size)

    def order(stream):
        return [bits[(step + stream) % steps] for step in range(steps)]

    def side(bit):
        return (rep // bit) % 2

    narrow = width // 2
    weights_ref[0] = query_weight[...]
    weights_ref[1, :, :narrow] = key_weight[...]
    weights_ref[1, :, narrow:] = value_weight[...]
    weights_ref[2] = out_weight[...]
    own_copy = pltpu.make_async_copy(weights_ref, weights_out.at[:, me], local_sem.at[0])
    own_copy.start()
    small_out[me] = small_ref[...]
    cot_out[me] = cot_ref[...]
    peers = [(rep, other) for other in others]
    peers += [(flip(rep, bit), me) for bit in (1,) + bits]
    greet(peers)

    regions = []
    for stream in streams:
        column = core * half + stream * 2 * fine
        narrow = columns_of(column + side(order(stream)[0]) * fine, fine)
        start, size = 0, rows
        held = [(pl.ds(0, rows), narrow)]
        for step in range(1, steps):
            size = size // 2
            start = start + side(order(stream)[step]) * size
            held.append((rows_of(start, size), narrow))
        regions.append((held, columns_of(column, 2 * fine)))

    def remote(source, target, send_sem, recv_sem, peer):
        return pltpu.make_async_remote_copy(
            src_ref=source,
            dst_ref=target,
            send_sem=send_sem,
            recv_sem=recv_sem,
            device_id=peer,
            device_id_type=MESH,
        )

    def line_copy(stream, source, peer):
        place, columns = regions[stream][0][-1]
        return remote(
            weights_ref.at[:, place, columns],
            weights_out.at[:, source, place, columns],
            line_send.at[stream, peer],
            line_recv.at[stream, source],
            (rep, peer),
        )

    def grow_copy(step, stream, source):
        place, columns = regions[stream][0][step]
        part = weights_out.at[:, source, place, columns]
        return remote(
            part,
            part,
            grow_send.at[step, stream, source],
            grow_recv.at[step, stream, source],
            (flip(rep, order(stream)[step]), me),
        )

    def join_copy(stream, source):
        part = weights_out.at[:, source, :, regions[stream][1]]
        return remote(
            part,
            part,
            join_send.at[stream, source],
            join_recv.at[stream, source],
            (flip(rep, 1), me),
        )

    def small_copy(source, peer):
        return remote(
            small_ref,
            small_out.at[source],
            small_send.at[peer],
            small_recv.at[source],
            (rep, peer),
        )

    def hand_on(block, to_right):
        peer = jnp.minimum(me + 1, count - 1) if to_right else jnp.maximum(me - 1, 0)
        return remote(
            cot_out.at[block],
            cot_out.at[block],
            (right_sem if to_right else left_sem).at[block],
            arrive_sem.at[block],
            (rep, peer),
        )

    def line_start():
        @pl.when(me < count - 1)
        def _():
            hand_on(me, True).start()

        @pl.when(me > 0)
        def _():
            hand_on(me, False).start()

    def line_step(step):
        lower = me - step
        upper = me + step

        @pl.when(lower >= 0)
        def _():
            hand_on(jnp.maximum(lower, 0), True).wait_recv()

            @pl.when(me < count - 1)
            def _():
                hand_on(jnp.maximum(lower, 0), True).start()

        @pl.when(upper < count)
        def _():
            hand_on(jnp.minimum(upper, count - 1), False).wait_recv()

            @pl.when(me > 0)
            def _():
                hand_on(jnp.minimum(upper, count - 1), False).start()

    def line_send_all():
        for other in others:
            for stream in streams:
                line_copy(stream, me, other).start()

    def advance(level):
        for other in others:
            for stream in streams:
                if level == 0:
                    line_copy(stream, other, other).wait_recv()
                else:
                    grow_copy(steps - level, stream, other).wait_recv()
                if level < steps:
                    grow_copy(steps - 1 - level, stream, other).start()
                else:
                    join_copy(stream, other).start()

    for other in others:
        small_copy(me, other).start()
    line_send_all()
    for other in others:
        small_copy(other, other).wait_recv()

    def gain(index):
        at = EXPERTS + index
        return jnp.concatenate([small_out[z, at : at + 1, :rows] for z in range(count)], axis=1)

    inputs = tokens_ref[...].astype(jnp.float32)
    first_out[...] = (normalize(inputs)[0] * gain(0)).astype(jnp.bfloat16)
    advance(0)
    line_start()
    for level in range(1, steps + 1):
        advance(level)
        if level == 1:
            line_step(1)
    for other in others:
        for stream in streams:
            join_copy(stream, other).wait_recv()
    own_copy.wait()
    leave = pltpu.make_async_copy(weights_out, weights_hbm, local_sem.at[2])
    leave.start()

    def whole(index):
        return weights_out[index].reshape(count * rows, width)

    project_inputs(first_out[...], whole, query_out, pair_out, table_ref)
    bias = allowed_pairs(column_ref[...], row_ref[...])
    if count > 2:
        line_step(2)
    attend_forward(range(KVHEADS // 2), query_out, pair_out, bias, head_out, total_out)
    for step in range(3, count - 1):
        line_step(step)
    attend_forward(range(KVHEADS // 2, KVHEADS), query_out, pair_out, bias, head_out, total_out)
    middle = inputs + dot_nn(head_out[...], whole(2))
    middle_out[...] = middle
    second_out[...] = (normalize(middle)[0] * gain(1)).astype(jnp.bfloat16)
    if count > 3:
        line_step(count - 1)
    for other in others:
        for stream in streams:
            join_copy(stream, other).wait_send()
            line_copy(stream, me, other).wait_send()
            for step in range(steps):
                grow_copy(step, stream, other).wait_send()
    for other in others:
        small_copy(me, other).wait_send()
    for block in range(count):

        @pl.when((block <= me) & (me < count - 1))
        def _():
            hand_on(block, True).wait_send()

        @pl.when((block >= me) & (me > 0))
        def _():
            hand_on(block, False).wait_send()

    leave.wait()


def gather(weights, small, tokens, cotangent, tables, starts, bits, count):
    rows, width = weights[0].shape
    depth = 3
    token_count = tokens.shape[0]
    steps = len(bits)
    low = jnp.bfloat16
    vmem = pl.BlockSpec(memory_space=pltpu.VMEM)
    dma = pltpu.SemaphoreType.DMA
    whole = jax.ShapeDtypeStruct((depth, count, rows, width), low)
    features = jax.ShapeDtypeStruct((token_count, width), low)
    return pl.pallas_call(
        functools.partial(gather_kernel, count, bits),
        in_specs=[vmem] * 10,
        out_specs=[pl.BlockSpec(memory_space=pl.ANY)] + [vmem] * 9,
        out_shape=[
            whole,
            jax.ShapeDtypeStruct((count,) + small.shape, small.dtype),
            jax.ShapeDtypeStruct((count, token_count, width), low),
            jax.ShapeDtypeStruct((token_count, width), jnp.float32),
            features,
            features,
            features,
            features,
            features,
            jax.ShapeDtypeStruct((2 * token_count, KVHEADS), jnp.float32),
        ],
        scratch_shapes=[
            pltpu.VMEM(whole.shape, low),
            pltpu.VMEM((depth, rows, width), low),
            dma((3,)),
            dma((2, count)),
            dma((2, count)),
            dma((steps, 2, count)),
            dma((steps, 2, count)),
            dma((2, count)),
            dma((2, count)),
            dma((count,)),
            dma((count,)),
            dma((count,)),
            dma((count,)),
            dma((count,)),
        ],
        compiler_params=pltpu.CompilerParams(
            collective_id=3, has_side_effects=True, vmem_limit_bytes=56 * 1024 * 1024
        ),
        name="gather",
    )(
        *weights,
        small,
        tokens,
        cotangent,
        tables,
        starts[:, None],
        starts[None, :],
    )


def local(
    tokens,
    sequence_start,
    routes,
    route_weights,
    cotangent,
    query_proj,
    key_proj,
    value_proj,
    out_proj,
    prenorm,
    midnorm,
    gate_proj,
    up_proj,
    down_proj,
    query_moment,
    key_moment,
    value_moment,
    out_moment,
    prenorm_moment,
    midnorm_moment,
    gate_moment,
    up_moment,
    down_moment,
):
    shard_index = lax.axis_index("shard")
    rep_count = lax.axis_size("rep")
    shard_count = lax.axis_size("shard")
    row_block = query_proj.shape[0]
    bits = rep_bits(rep_count)
    experts_here = gate_proj.shape[0]
    dense_weights = jnp.sum(
        jnp.where(
            routes.T[None, :, :] == jnp.arange(EXPERTS, dtype=jnp.int32)[:, None, None],
            route_weights.T[None, :, :],
            0.0,
        ),
        axis=1,
    )
    gain_rows = jnp.pad(
        jnp.stack([prenorm, midnorm]).astype(jnp.float32),
        ((0, 6), (0, tokens.shape[0] - row_block)),
    )
    tables = rotary_tables(jnp.arange(tokens.shape[0], dtype=jnp.int32) - sequence_start)
    (
        weights,
        small,
        cotangent_all,
        middle,
        normed_first,
        normed_second,
        query,
        pair,
        head_low,
        log_total,
    ) = gather(
        (query_proj, key_proj, value_proj, out_proj),
        jnp.concatenate([dense_weights, gain_rows], axis=0),
        tokens,
        cotangent,
        tables,
        sequence_start,
        bits,
        shard_count,
    )
    expert_weights = lax.dynamic_slice_in_dim(
        small, shard_index * experts_here, experts_here, 1
    ).transpose(0, 2, 1)
    returned, grad_second, expert_share = moe(
        normed_second,
        cotangent_all,
        expert_weights,
        gate_proj,
        up_proj,
        down_proj,
        bits,
        shard_count,
    )
    own_moments = (query_moment, key_moment, value_moment, out_moment)
    expert_grads, dense_next, dense_grads, gains_grad, grad_tokens, mixed = spread(
        expert_share,
        returned,
        normed_first,
        head_low,
        weights,
        small,
        tokens,
        cotangent,
        grad_second,
        middle,
        query,
        pair,
        log_total,
        tables,
        sequence_start,
        own_moments,
        bits=bits,
        count=shard_count,
    )
    gains_here = lax.dynamic_slice_in_dim(gains_grad, shard_index * row_block, row_block, 1)
    prenorm_grad = gains_here[0]
    midnorm_grad = gains_here[1]
    prenorm_next = momentum_keep * prenorm_moment + prenorm_grad
    midnorm_next = momentum_keep * midnorm_moment + midnorm_grad
    prenorm_update = -rate_gain * prenorm_next
    midnorm_update = -rate_gain * midnorm_next
    rep_index = lax.axis_index("rep")
    (
        query_grad,
        query_next,
        key_grad,
        key_next,
        value_grad,
        value_next,
        out_grad,
        out_next,
        own_wide,
        own_narrow,
    ) = dense_update(
        dense_next,
        dense_grads,
        own_moments,
        LAYOUT,
        shard_index,
        rep_index,
    )
    pairs = [(index, index + 1 - 2 * (index % 2)) for index in range(rep_count)]
    other_wide = lax.ppermute(own_wide, "rep", pairs)
    other_narrow = lax.ppermute(own_narrow, "rep", pairs)
    gate_grad, gate_next, gate_update, up_grad, up_next, up_update = expert_update(
        expert_grads, (0, 1), (gate_moment, up_moment)
    )
    (
        down_grad,
        down_next,
        down_update,
        query_update,
        out_update,
        key_update,
        value_update,
        grad_tokens,
        mixed,
    ) = expert_update(
        expert_grads,
        (2,),
        (down_moment,),
        (own_wide, other_wide, own_narrow, other_narrow, grad_tokens, mixed),
    )
    return (
        mixed,
        grad_tokens,
        query_grad,
        query_next,
        query_update,
        key_grad,
        key_next,
        key_update,
        value_grad,
        value_next,
        value_update,
        out_grad,
        out_next,
        out_update,
        prenorm_grad,
        prenorm_next,
        prenorm_update,
        midnorm_grad,
        midnorm_next,
        midnorm_update,
        gate_grad,
        gate_next,
        gate_update,
        up_grad,
        up_next,
        up_update,
        down_grad,
        down_next,
        down_update,
    )


def solution(mesh):
    return jax.shard_map(
        local,
        mesh=mesh,
        in_specs=(
            P(("rep", "shard"), None),
            P(("rep", "shard")),
            P(("rep", "shard"), None),
            P(("rep", "shard"), None),
            P(("rep", "shard"), None),
            P("shard", None),
            P("shard", None),
            P("shard", None),
            P("shard", None),
            P("shard"),
            P("shard"),
            P("shard", None, None),
            P("shard", None, None),
            P("shard", None, None),
            P("shard", None),
            P("shard", None),
            P("shard", None),
            P("shard", None),
            P("shard"),
            P("shard"),
            P("shard", None, None),
            P("shard", None, None),
            P("shard", None, None),
        ),
        out_specs=(
            P(("rep", "shard"), None),
            P(("rep", "shard"), None),
            P("shard", None),
            P("shard", None),
            P("shard", None),
            P("shard", None),
            P("shard", None),
            P("shard", None),
            P("shard", None),
            P("shard", None),
            P("shard", None),
            P("shard", None),
            P("shard", None),
            P("shard", None),
            P("shard"),
            P("shard"),
            P("shard"),
            P("shard"),
            P("shard"),
            P("shard"),
            P("shard", None, None),
            P("shard", None, None),
            P("shard", None, None),
            P("shard", None, None),
            P("shard", None, None),
            P("shard", None, None),
            P("shard", None, None),
            P("shard", None, None),
            P("shard", None, None),
        ),
        check_vma=False,
    )
```

```python
import functools
import math

import jax
import jax.numpy as jnp
from jax import lax
from jax.experimental import pallas as pl
from jax.experimental.pallas import tpu as pltpu
from jax.sharding import PartitionSpec as P

NHEADS = 16
KVHEADS = 8
HEAD = 64
EXPERTS = 16
NS_ITERS = 2


norm_epsilon = 1e-06
rotary_base = 10000.0
momentum_keep = 0.9
rate_matrix = 0.5
rate_gain = 0.0002
newton_first = 3.4445
newton_second = -4.775
newton_third = 2.0315
masked_score = -1e30


def normalize(values):
    inverse = lax.rsqrt(jnp.mean(values * values, axis=-1, keepdims=True) + norm_epsilon)
    return (values * inverse, inverse)


def normalize_back(grad_normed, scaling, scaled, inverse):
    grad_scaled = grad_normed * scaling
    inner_mean = jnp.mean(grad_scaled * scaled, axis=-1, keepdims=True)
    return (
        inverse * (grad_scaled - scaled * inner_mean),
        jnp.sum(grad_normed * scaled, axis=0, keepdims=True),
    )


def dot_nn(left, right):
    return jnp.dot(left, right, preferred_element_type=jnp.float32)


def dot_nt(left, right):
    return lax.dot_general(
        left, right, (((1,), (1,)), ((), ())), preferred_element_type=jnp.float32
    )


def dot_tn(left, right):
    return lax.dot_general(
        left, right, (((0,), (0,)), ((), ())), preferred_element_type=jnp.float32
    )


def rotate(values, table_ref, sign):
    return (
        values * table_ref[0]
        + sign * pltpu.roll(values, 96, 1) * table_ref[1]
        + sign * pltpu.roll(values, 32, 1) * table_ref[2]
    )


def lane_low(shape):
    return lax.broadcasted_iota(jnp.int32, shape, 1) < HEAD


def twice(pair, upper):
    wide = pair.astype(jnp.float32)
    turned = pltpu.roll(wide, HEAD, 1)
    first = lane_low(pair.shape)
    return jnp.where(first != upper, wide, turned).astype(pair.dtype)


def stacked(pair):
    first = lane_low(pair.shape)
    zero = jnp.zeros_like(pair)
    return jnp.concatenate([jnp.where(first, pair, zero), jnp.where(first, zero, pair)], axis=0)


def unstacked(rows):
    half = rows.shape[0] // 2
    return jnp.where(lane_low((half, rows.shape[1])), rows[:half], rows[half:])


def allowed_pairs(start_column, start_row):
    shape = (start_column.shape[0], start_row.shape[1])
    query_places = lax.broadcasted_iota(jnp.int32, shape, 0)
    key_places = lax.broadcasted_iota(jnp.int32, shape, 1)
    one = (start_column == start_row) & (key_places <= query_places)
    return jnp.where(jnp.concatenate([one, one], axis=0), 0.0, masked_score)


def block_lanes(ref, block):
    return ref[:, block * 2 * HEAD : (block + 1) * 2 * HEAD]


def attend_pair(block, query_ref, pair_ref, bias):
    key = twice(block_lanes(pair_ref, block // 2), block % 2 == 1)
    value = twice(block_lanes(pair_ref, KVHEADS // 2 + block // 2), block % 2 == 1)
    queries = stacked(block_lanes(query_ref, block))
    scores = dot_nt(queries, key) * (1.0 / math.sqrt(HEAD)) + bias
    return (queries, key, value, scores)


def project_inputs(normed, weights, query_ref, pair_ref, table_ref):
    queries = dot_nn(normed, weights(0))
    for block in range(NHEADS // 2):
        lanes = slice(block * 2 * HEAD, (block + 1) * 2 * HEAD)
        query_ref[:, lanes] = rotate(queries[:, lanes], table_ref, 1.0).astype(jnp.bfloat16)
    pairs = dot_nn(normed, weights(1))
    for block in range(KVHEADS):
        lanes = slice(block * 2 * HEAD, (block + 1) * 2 * HEAD)
        value = pairs[:, lanes]
        if block < KVHEADS // 2:
            value = rotate(value, table_ref, 1.0)
        pair_ref[:, lanes] = value.astype(jnp.bfloat16)


def attend_forward(blocks, query_ref, pair_ref, bias, head_ref, total_ref):
    for block in blocks:
        _, _, value, scores = attend_pair(block, query_ref, pair_ref, bias)
        row_max = jnp.max(scores, axis=-1, keepdims=True)
        exponents = jnp.exp(scores - row_max)
        totals = jnp.sum(exponents, axis=-1, keepdims=True)
        softmax_low = (exponents * (1.0 / totals)).astype(jnp.bfloat16)
        head_ref[:, block * 2 * HEAD : (block + 1) * 2 * HEAD] = unstacked(
            dot_nn(softmax_low, value)
        ).astype(jnp.bfloat16)
        total_ref[:, block : block + 1] = row_max + jnp.log(totals)


def attend_backward(query_ref, pair_ref, bias, total_ref, grad_ref, table_ref, delta_ref):
    folded = []
    for block in range(KVHEADS):
        queries, key, value, scores = attend_pair(block, query_ref, pair_ref, bias)
        grads = stacked(block_lanes(grad_ref, block))
        softmax_full = jnp.exp(scores - total_ref[:, block : block + 1])
        grad_softmax = dot_nt(grads, value)
        inner = jnp.sum(softmax_full * grad_softmax, axis=-1, keepdims=True)
        grad_scores = (softmax_full * (grad_softmax - inner)).astype(jnp.bfloat16)
        scale = 1.0 / math.sqrt(HEAD)
        grad_query = unstacked(dot_nn(grad_scores, key)) * scale
        lanes = slice(block * 2 * HEAD, (block + 1) * 2 * HEAD)
        delta_ref[:, lanes] = rotate(grad_query, table_ref, -1.0).astype(jnp.bfloat16)
        grad_key = dot_tn(grad_scores, queries) * scale
        grad_value = dot_tn(softmax_full.astype(jnp.bfloat16), grads)
        folded.append(
            (
                grad_key + pltpu.roll(grad_key, HEAD, 1),
                grad_value + pltpu.roll(grad_value, HEAD, 1),
            )
        )
        if block % 2 == 1:
            first = lane_low(grad_key.shape)
            both = [jnp.where(first, low, high) for low, high in zip(*folded)]
            folded = []
            base = NHEADS * HEAD + (block // 2) * 2 * HEAD
            delta_ref[:, base : base + 2 * HEAD] = rotate(both[0], table_ref, -1.0).astype(
                jnp.bfloat16
            )
            base = base + KVHEADS * HEAD
            delta_ref[:, base : base + 2 * HEAD] = both[1].astype(jnp.bfloat16)


def rotary_tables(positions):
    half_size = HEAD // 2
    frequency = rotary_base ** (-(jnp.arange(half_size, dtype=jnp.float32) * 2.0) / HEAD)
    angles = positions.astype(jnp.float32)[:, None] * frequency[None, :]
    cosine, sine = (jnp.cos(angles), jnp.sin(angles))
    zero = jnp.zeros_like(sine)
    return jnp.stack(
        [
            jnp.concatenate([cosine] * 4, axis=1),
            jnp.concatenate([-sine, zero] * 2, axis=1),
            jnp.concatenate([zero, sine] * 2, axis=1),
        ]
    )


def newton_parts(grams):
    a, b, c = newton_first, newton_second, newton_third

    def times(left, right):
        return jnp.dot(left, right, preferred_element_type=jnp.float32)

    lows = [gram.astype(jnp.bfloat16) for gram in grams]
    firsts = [b * gram + c * times(low, low) for gram, low in zip(grams, lows)]
    first_lows = [first.astype(jnp.bfloat16) for first in firsts]
    mixes = [times(low, first) for low, first in zip(lows, first_lows)]
    nexts = [
        (a * a) * gram + (2.0 * a) * mix + times(mix.astype(jnp.bfloat16), first)
        for gram, mix, first in zip(grams, mixes, first_lows)
    ]
    next_lows = [gram.astype(jnp.bfloat16) for gram in nexts]
    seconds = [b * gram + c * times(low, low) for gram, low in zip(nexts, next_lows)]
    second_lows = [second.astype(jnp.bfloat16) for second in seconds]
    return list(zip(firsts, first_lows, seconds, second_lows))


def scaled_gram(gram):
    shape = gram.shape
    rows = lax.broadcasted_iota(jnp.int32, shape, 0)
    diagonal = rows == lax.broadcasted_iota(jnp.int32, shape, 1)
    inverse = 1.0 / (jnp.sqrt(jnp.sum(jnp.where(diagonal, gram, 0.0))) + 1e-07)
    return (gram * (inverse * inverse), inverse)


def expert_update_kernel(kinds, scale, carried, *refs):
    a = newton_first
    grads_ref = refs[0]
    moments = refs[1 : 1 + len(kinds)]
    given = refs[1 + len(kinds) : 1 + len(kinds) + carried]
    outs = refs[1 + len(kinds) + carried :]
    if carried:
        taken = outs[3 * len(kinds) : 3 * len(kinds) + carried]
        held = outs[3 * len(kinds) + carried : -2]
        load_sem, store_sem = outs[-2:]
        core = lax.axis_index("rep") % 2

        def load(index):
            return pltpu.make_async_copy(given[index], held[index], load_sem.at[index])

        def store(source, target):
            return pltpu.make_async_copy(held[source], taken[target], store_sem.at[target])

        @pl.when(pl.program_id(0) == 0)
        def _():
            for index in range(carried):
                load(index).start()

    half = grads_ref.shape[3]
    tall = kinds[0] < 2
    states = []
    for index in range(len(kinds)):
        for e in range(grads_ref.shape[0]):
            grad = grads_ref[e, index].astype(jnp.float32)
            if not tall:
                grad = jnp.concatenate([grad[:half], grad[half:]], axis=1)
            moment = momentum_keep * moments[index][e] + grad
            outs[3 * index][e] = grad
            outs[3 * index + 1][e] = moment
            low = moment.astype(jnp.bfloat16)
            sides = (((0,), (0,)), ((), ())) if tall else (((1,), (1,)), ((), ()))
            gram, inverse = scaled_gram(
                lax.dot_general(low, low, sides, preferred_element_type=jnp.float32)
            )
            states.append((index, e, inverse, low, gram))
    parts = newton_parts([state[-1] for state in states])
    for (index, e, inverse, low, _), (first, first_low, second, second_low) in zip(states, parts):
        rest = a * (first + second) + jnp.dot(
            first_low, second_low, preferred_element_type=jnp.float32
        )
        rest = ((-scale * inverse) * rest).astype(jnp.bfloat16)
        if tall:
            step = jnp.dot(low, rest, preferred_element_type=jnp.float32)
        else:
            step = jnp.dot(rest, low, preferred_element_type=jnp.float32)
        outs[3 * index + 2][e] = (-scale * a * a * inverse) * outs[3 * index + 1][e] + step
    if carried:

        @pl.when(pl.program_id(0) == 0)
        def _():
            for index in range(carried):
                load(index).wait()
            for pair in (0, 2):

                @pl.when(core == 0)
                def _():
                    store(pair, pair).start()
                    store(pair + 1, pair + 1).start()

                @pl.when(core == 1)
                def _():
                    store(pair + 1, pair).start()
                    store(pair, pair + 1).start()

            for index in range(4, carried):
                store(index, index).start()

        @pl.when(pl.program_id(0) == pl.num_programs(0) - 1)
        def _():
            for index in range(carried):
                store(index, index).wait()


def expert_update(grads, kinds, moments, carried=()):
    count, rows, columns = moments[0].shape
    group = 2 // len(kinds)
    scale = rate_matrix * math.sqrt(max(1.0, columns / rows))
    block = pl.BlockSpec((group, rows, columns), lambda i: (i, 0, 0))
    place = kinds[0] // len(kinds)
    taken = pl.BlockSpec((group, len(kinds)) + grads.shape[2:], lambda i: (i, place, 0, 0))
    shape = jax.ShapeDtypeStruct(moments[0].shape, jnp.float32)
    hand_on = [pl.BlockSpec(memory_space=pl.ANY)] * len(carried)
    return pl.pallas_call(
        functools.partial(expert_update_kernel, kinds, scale, len(carried)),
        grid=(count // group,),
        in_specs=[taken] + [block] * len(kinds) + hand_on,
        out_specs=[block] * (3 * len(kinds)) + hand_on,
        out_shape=[shape] * (3 * len(kinds))
        + [jax.ShapeDtypeStruct(array.shape, array.dtype) for array in carried],
        scratch_shapes=[pltpu.VMEM(array.shape, array.dtype) for array in carried]
        + [pltpu.SemaphoreType.DMA((len(carried),))] * (2 if carried else 0),
        compiler_params=pltpu.CompilerParams(vmem_limit_bytes=60 * 1024 * 1024),
        name="expert_update",
        cost_estimate=pl.CostEstimate(
            flops=count * len(kinds) * 2500000000,
            bytes_accessed=moments[0].size * len(kinds) * 18,
            transcendentals=0,
        ),
    )(grads, *moments, *carried)


def dense_update_kernel(layout, place_ref, next_ref, grads_ref, *refs):
    a = newton_first
    amount = len(layout)
    own_moments = refs[:amount]
    outs = refs[amount : 3 * amount]
    updates = refs[3 * amount : 3 * amount + 2]
    matrices = refs[3 * amount + 2 : 3 * amount + 4]
    own_grads, own_next, sem = refs[3 * amount + 4 :]
    blocks, count, block_rows, width = next_ref.shape
    part = width // 3
    me = place_ref[0]
    core = place_ref[1]
    start = pl.multiple_of(me * block_rows, block_rows)
    loads = [
        pltpu.make_async_copy(
            own_moments[index], own_next.at[:, begin : begin + size], sem.at[2 * index]
        )
        for index, (begin, size) in enumerate(layout)
    ]
    for load in loads:
        load.start()

    for block in range(blocks):
        outer = slice(block * part, (block + 1) * part)
        lanes = pl.ds(pl.multiple_of(2 * core * part, part), part)
        matrices[0][:, outer] = next_ref[block, :, :, lanes].reshape(count * block_rows, part)
        for index in range(3):
            columns = slice(8 * part * index + block * part, 8 * part * index + (block + 1) * part)
            inner = slice(index * part, (index + 1) * part)
            own_grads[:, columns] = grads_ref[block, :, inner].astype(jnp.float32)
    for block in range(blocks // 2):
        outer = slice(block * part, (block + 1) * part)
        matrices[1][:, outer] = next_ref[
            core * (blocks // 2) + block, :, :, part : 2 * part
        ].reshape(count * block_rows, part)
    leaving = []
    for index, (begin, size) in enumerate(layout):
        loads[index].wait()
        lanes = slice(begin, begin + size)
        own_next[:, lanes] = momentum_keep * own_next[:, lanes] + own_grads[:, lanes]
        leaving += [
            pltpu.make_async_copy(own_grads.at[:, lanes], outs[2 * index], sem.at[2 * index]),
            pltpu.make_async_copy(own_next.at[:, lanes], outs[2 * index + 1], sem.at[2 * index + 1]),
        ]
        leaving[-2].start()
        leaving[-1].start()
    states = []
    for matrix in matrices:
        low = matrix[...]
        states.append(
            scaled_gram(
                lax.dot_general(
                    low, low, (((0,), (0,)), ((), ())), preferred_element_type=jnp.float32
                )
            )
        )
    parts = newton_parts([state[0] for state in states])
    for matrix, update, (_, inverse), (_, first_low, _, second_low) in zip(
        matrices, updates, states, parts
    ):
        rows, columns = matrix.shape
        scale = rate_matrix * math.sqrt(max(1.0, columns / rows))
        own = matrix[pl.ds(start, block_rows)]
        once = a * own.astype(jnp.float32) + jnp.dot(
            own, first_low, preferred_element_type=jnp.float32
        )
        update[...] = (-scale * inverse) * (
            a * once
            + jnp.dot(once.astype(jnp.bfloat16), second_low, preferred_element_type=jnp.float32)
        )
    for copy in leaving:
        copy.wait()


def dense_update(nexts, grads, own_moments, layout, shard_index, rep_index):
    _, count, block_rows, _ = nexts.shape
    width = own_moments[0].shape[1]
    whole = lambda shape: pl.BlockSpec(shape, lambda i: (0,) * len(shape))
    anywhere = pl.BlockSpec(memory_space=pl.ANY)
    shapes = []
    for _, size in layout:
        shapes += [jax.ShapeDtypeStruct((block_rows, size), jnp.float32)] * 2
    shapes += [
        jax.ShapeDtypeStruct((block_rows, width), jnp.float32),
        jax.ShapeDtypeStruct((block_rows, width // 2), jnp.float32),
    ]
    place = jnp.stack([shard_index, rep_index % 2]).astype(jnp.int32)
    return pl.pallas_call(
        functools.partial(dense_update_kernel, layout),
        grid=(1,),
        in_specs=[pl.BlockSpec(memory_space=pltpu.SMEM), whole(nexts.shape), whole(grads.shape)]
        + [anywhere] * len(own_moments),
        out_specs=[anywhere] * (2 * len(layout)) + [whole(shape.shape) for shape in shapes[-2:]],
        out_shape=shapes,
        scratch_shapes=[
            pltpu.VMEM((count * block_rows, width), jnp.bfloat16),
            pltpu.VMEM((count * block_rows, width // 2), jnp.bfloat16),
            pltpu.VMEM((block_rows, 3 * width), jnp.float32),
            pltpu.VMEM((block_rows, 3 * width), jnp.float32),
            pltpu.SemaphoreType.DMA((2 * len(layout),)),
        ],
        compiler_params=pltpu.CompilerParams(vmem_limit_bytes=63 * 1024 * 1024),
        name="dense_update",
        cost_estimate=pl.CostEstimate(
            flops=14000000000, bytes_accessed=24 * width * width, transcendentals=0
        ),
    )(place, nexts, grads, *own_moments)


LAYOUT = ((0, 1024), (1024, 512), (1536, 512), (2048, 1024))


MESH = pl.DeviceIdType.MESH


def flip(index, bit):
    return index + bit - 2 * bit * ((index // bit) % 2)


def greet(peers):
    barrier = pltpu.get_barrier_semaphore()
    for peer in peers:
        pl.semaphore_signal(barrier, inc=1, device_id=peer, device_id_type=MESH)
    pl.semaphore_wait(barrier, len(peers))


def stream_plan(rep, bits, base, size):
    stages = []
    starts = [base, base + size]
    for step in range(len(bits)):
        size = size // 2
        stage = []
        for stream in range(2):
            bit = bits[(step + stream) % len(bits)]
            side = (rep // bit) % 2
            keep = starts[stream] + side * size
            send = starts[stream] + (1 - side) * size
            starts[stream] = keep
            stage.append((bit, stream, keep, send, size))
        stages.append(stage)
    return stages


def rows_of(start, size):
    return pl.ds(pl.multiple_of(start, 16), size)


def moe_kernel(
    count,
    bits,
    own_ref,
    cot_ref,
    weight_ref,
    gate_hbm,
    up_hbm,
    down_hbm,
    stage_out,
    back_ref,
    share_ref,
    tok,
    turned,
    mats,
    hid,
    gate_delta,
    up_delta,
    stage_back,
    got_back,
    sum_back,
    sum_out,
    *rest,
):
    landing = rest[: 1 + 2 * len(bits)]
    (
        load_sem,
        right_sem,
        left_sem,
        arrive_sem,
        back_send,
        back_recv,
        sum_send,
        sum_recv,
    ) = rest[1 + 2 * len(bits) :]
    rep = lax.axis_index("rep")
    me = lax.axis_index("shard")
    experts = mats.shape[0]
    tokens = own_ref.shape[0]
    half = mats.shape[2] // 2
    core = rep % 2

    loads = [
        pltpu.make_async_copy(gate_hbm, mats.at[:, 0], load_sem.at[0]),
        pltpu.make_async_copy(up_hbm, mats.at[:, 1], load_sem.at[1]),
        pltpu.make_async_copy(
            down_hbm.at[:, :, pl.ds(0, half)], mats.at[:, 2, pl.ds(0, half)], load_sem.at[2]
        ),
        pltpu.make_async_copy(
            down_hbm.at[:, :, pl.ds(half, half)], mats.at[:, 2, pl.ds(half, half)], load_sem.at[3]
        ),
    ]
    for load in loads:
        load.start()
    peers = [(rep, lax.rem(me + k, count)) for k in range(1, count)]
    peers += [(flip(rep, bit), me) for bit in (1,) + bits]
    greet(peers)

    right_peer = (rep, jnp.minimum(me + 1, count - 1))
    left_peer = (rep, jnp.maximum(me - 1, 0))

    def hand_on(block, to_right):
        return pltpu.make_async_remote_copy(
            src_ref=tok.at[block],
            dst_ref=tok.at[block],
            send_sem=(right_sem if to_right else left_sem).at[block],
            recv_sem=arrive_sem.at[block],
            device_id=right_peer if to_right else left_peer,
            device_id_type=MESH,
        )

    def returning(stage, got, send_sem, recv_sem, block):
        return pltpu.make_async_remote_copy(
            src_ref=stage.at[block],
            dst_ref=got.at[me],
            send_sem=send_sem.at[block],
            recv_sem=recv_sem.at[me],
            device_id=(rep, block),
            device_id_type=MESH,
        )

    tok[me] = own_ref[...]

    @pl.when(me < count - 1)
    def _():
        hand_on(me, True).start()

    @pl.when(me > 0)
    def _():
        hand_on(me, False).start()

    for load in loads:
        load.wait()

    margin = jnp.minimum(me, count - 1 - me)
    longer = jnp.where(me < count - 1 - me, 1, -1)
    inward = jnp.where(2 * me < count, 1, -1)
    nt = (((1,), (1,)), ((), ()))

    def dot(left, right):
        return jnp.dot(left, right, preferred_element_type=jnp.float32)

    def dot_nt(left, right):
        return lax.dot_general(left, right, nt, preferred_element_type=jnp.float32)

    def arrivals(j):
        lower = me - j
        upper = me + j

        @pl.when((j > 0) & (lower >= 0))
        def _():
            hand_on(jnp.maximum(lower, 0), True).wait_recv()

            @pl.when(me < count - 1)
            def _():
                hand_on(jnp.maximum(lower, 0), True).start()

        @pl.when((j > 0) & (upper < count))
        def _():
            hand_on(jnp.minimum(upper, count - 1), False).wait_recv()

            @pl.when(me > 0)
            def _():
                hand_on(jnp.minimum(upper, count - 1), False).start()

    def block_at(j):
        near = (j + 1) // 2
        alternating = me + near - 2 * near * (j % 2)
        return jnp.where(j <= 2 * margin, alternating, me + longer * (j - margin))

    def places_of(block):
        return pl.ds(pl.multiple_of(block * tokens, tokens), tokens)

    def factors(e, block):
        places = places_of(block)
        rows = tok[block]
        grads = cot_ref[block]
        weight = weight_ref[block, :, e : e + 1]
        u = dot(rows, mats[e, 0])
        w = dot(rows, mats[e, 1])
        gate = 1.0 / (1.0 + jnp.exp(-u))
        act = u * gate
        hidden = (weight * (act * w)).astype(jnp.bfloat16)
        hid[e, :, places] = hidden.T
        pulled = weight * (
            dot_nt(grads[:, :half], mats[e, 2, :half])
            + dot_nt(grads[:, half:], mats[e, 2, half:])
        )
        gate_delta[e, places] = (pulled * w * (gate + act * (1.0 - gate))).astype(jnp.bfloat16)
        up_delta[e, places] = (pulled * act).astype(jnp.bfloat16)
        return hidden

    def sums(block, e, hidden, place):
        places = places_of(block)
        for side in range(2):
            part = slice(side * half, (side + 1) * half)
            back = dot_nt(gate_delta[e, places], mats[e, 0, part]) + dot_nt(
                up_delta[e, places], mats[e, 1, part]
            )
            out = dot(hidden, mats[e, 2, part])
            if e > 0:
                back = place[0][:, part] + back
                out = place[1][:, part] + out
            place[0][:, part] = back
            place[1][:, part] = out

    def visit(j, carry):
        arrivals(j)
        block = block_at(j)
        places = places_of(block)
        turned[:, places] = tok[block].T
        hiddens = [factors(e, block) for e in range(experts)]
        for side in range(2):
            part = slice(side * half, (side + 1) * half)
            total_back = None
            total_out = None
            for e in range(experts):
                back = dot_nt(gate_delta[e, places], mats[e, 0, part]) + dot_nt(
                    up_delta[e, places], mats[e, 1, part]
                )
                out = dot(hiddens[e], mats[e, 2, part])
                total_back = back if e == 0 else total_back + back
                total_out = out if e == 0 else total_out + out
            stage_back[block, :, part] = total_back.astype(jnp.bfloat16)
            stage_out[block, :, part] = total_out.astype(jnp.bfloat16)

        @pl.when((j > 0) & ((block - me) * inward > 0))
        def _():
            returning(stage_back, got_back, back_send, back_recv, block).start()

        return carry

    lax.fori_loop(0, count - 1, visit, 0)
    arrivals(count - 1)
    last = block_at(count - 1)
    for k in range(1, count):
        block = block_at(k - 1)

        @pl.when((block - me) * inward < 0)
        def _():
            returning(stage_back, got_back, back_send, back_recv, block).start()

    turned[:, places_of(last)] = tok[last].T
    plan = stream_plan(rep, bits, core * half, half // 2)

    def sum_copy(stage, slot, e, start, size, bit):
        return pltpu.make_async_remote_copy(
            src_ref=mats.at[e, :, rows_of(start, size)],
            dst_ref=landing[slot].at[e],
            send_sem=sum_send.at[slot, e],
            recv_sem=sum_recv.at[slot, e],
            device_id=(flip(rep, bit), me),
            device_id_type=MESH,
        )

    def copies(stage, e):
        if stage == 0:
            return [(sum_copy(0, 0, e, (1 - core) * half, half, 1), 0, core * half, half)]
        return [
            (
                sum_copy(stage, 1 + 2 * (stage - 1) + stream, e, send, size, bit),
                1 + 2 * (stage - 1) + stream,
                keep,
                size,
            )
            for bit, stream, keep, send, size in plan[stage - 1]
        ]

    def finish(stage, e):
        for copy, slot, keep, size in copies(stage, e):
            copy.wait_recv()
            place = rows_of(keep, size)
            for kind in range(3):
                mats[e, kind, place] = (
                    mats[e, kind, place].astype(jnp.float32)
                    + landing[slot][e, kind].astype(jnp.float32)
                ).astype(jnp.bfloat16)

    stages = 1 + len(bits)
    for turn in range(experts + stages):
        if turn < experts:
            e = turn
            sums(last, e, factors(e, last), (sum_back, sum_out))
            for side in range(2):
                part = slice(side * half, (side + 1) * half)
                mats[e, 0, part] = dot(turned[part], gate_delta[e]).astype(jnp.bfloat16)
                mats[e, 1, part] = dot(turned[part], up_delta[e]).astype(jnp.bfloat16)
                mats[e, 2, part] = dot(hid[e], cot_ref[:, :, part].reshape(count * tokens, half)).astype(jnp.bfloat16)
            copies(0, e)[0][0].start()
            if e == experts - 1:
                stage_back[last] = sum_back[...].astype(jnp.bfloat16)
                stage_out[last] = sum_out[...].astype(jnp.bfloat16)
                returning(stage_back, got_back, back_send, back_recv, last).start()
        for stage in range(stages):
            e = turn - 1 - stage
            if 0 <= e < experts:
                finish(stage, e)
                if stage + 1 < stages:
                    for copy, _, _, _ in copies(stage + 1, e):
                        copy.start()
                else:
                    for _, stream, keep, _, size in plan[-1]:
                        share_ref[e, :, stream] = mats[e, :, rows_of(keep, size)]

    total = stage_back[me].astype(jnp.float32)
    for k in range(1, count):
        source = lax.rem(me + k, count)
        pltpu.make_async_remote_copy(
            src_ref=stage_back.at[source],
            dst_ref=got_back.at[source],
            send_sem=back_send.at[source],
            recv_sem=back_recv.at[source],
            device_id=(rep, source),
            device_id_type=MESH,
        ).wait_recv()
        total = total + got_back[source].astype(jnp.float32)
    back_ref[...] = total
    for k in range(1, count):
        block = lax.rem(me + k, count)
        returning(stage_back, got_back, back_send, back_recv, block).wait_send()
    for e in range(experts):
        for stage in range(stages):
            for copy, _, _, _ in copies(stage, e):
                copy.wait_send()
    for block in range(count):

        @pl.when((block <= me) & (me < count - 1))
        def _():
            hand_on(block, True).wait_send()

        @pl.when((block >= me) & (me > 0))
        def _():
            hand_on(block, False).wait_send()


def moe(normed, cotangents, weights, gate_proj, up_proj, down_proj, bits, count):
    tokens, width = normed.shape
    experts, _, hidden = gate_proj.shape
    half = width // 2
    low = jnp.bfloat16
    final = (half // 2) >> len(bits)
    vmem = pl.BlockSpec(memory_space=pltpu.VMEM)
    anywhere = pl.BlockSpec(memory_space=pl.ANY)
    landings = [pltpu.VMEM((experts, 3, half, hidden), low)]
    for step in range(len(bits)):
        size = (half // 2) >> (step + 1)
        landings += [pltpu.VMEM((experts, 3, size, hidden), low)] * 2
    slots = len(landings)
    dma = pltpu.SemaphoreType.DMA
    return pl.pallas_call(
        functools.partial(moe_kernel, count, bits),
        in_specs=[vmem, vmem, vmem, anywhere, anywhere, anywhere],
        out_specs=[vmem, vmem, vmem],
        out_shape=[
            jax.ShapeDtypeStruct((count, tokens, width), low),
            jax.ShapeDtypeStruct((tokens, width), jnp.float32),
            jax.ShapeDtypeStruct((experts, 3, 2, final, hidden), low),
        ],
        scratch_shapes=[
            pltpu.VMEM((count, tokens, width), low),
            pltpu.VMEM((width, count * tokens), low),
            pltpu.VMEM((experts, 3, width, hidden), low),
            pltpu.VMEM((experts, hidden, count * tokens), low),
            pltpu.VMEM((experts, count * tokens, hidden), low),
            pltpu.VMEM((experts, count * tokens, hidden), low),
            pltpu.VMEM((count, tokens, width), low),
            pltpu.VMEM((count, tokens, width), low),
            pltpu.VMEM((tokens, width), jnp.float32),
            pltpu.VMEM((tokens, width), jnp.float32),
        ]
        + landings
        + [
            dma((4,)),
            dma((count,)),
            dma((count,)),
            dma((count,)),
            dma((count,)),
            dma((count,)),
            dma((slots, experts)),
            dma((slots, experts)),
        ],
        compiler_params=pltpu.CompilerParams(
            collective_id=1, has_side_effects=True, vmem_limit_bytes=63 * 1024 * 1024
        ),
        name="moe",
        cost_estimate=pl.CostEstimate(
            flops=39000000000, bytes_accessed=20000000, transcendentals=2000000
        ),
    )(normed, cotangents, weights, gate_proj, up_proj, down_proj)


def rep_bits(rep_count):
    bits = []
    bit = 2
    while bit < rep_count:
        bits.append(bit)
        bit = bit * 2
    return tuple(bits)


def spread_kernel(
    count,
    bits,
    share_ref,
    returned_ref,
    normed_ref,
    head_ref,
    weights_ref,
    small_ref,
    tokens_ref,
    cot_ref,
    second_ref,
    middle_ref,
    query_ref,
    pair_ref,
    total_ref,
    table_ref,
    column_ref,
    row_ref,
    query_moment,
    key_moment,
    value_moment,
    out_moment,
    experts_hbm,
    dense_out,
    grads_out,
    gains_out,
    tokens_out,
    mixed_out,
    experts_out,
    got_ref,
    moment_piece,
    delta_ref,
    branch_ref,
    heads_ref,
    dense_ref,
    total,
    land_core,
    land_first,
    *rest,
):
    later = len(bits) - 1
    land_later = rest[:later]
    (
        piece_send,
        piece_land,
        piece,
        gains_send,
        gains_land,
        gains_all,
        local_sem,
        core_send,
        core_recv,
        half_send,
        half_recv,
        shard_send,
        shard_recv,
        grow_send,
        grow_recv,
        line_send,
        line_recv,
        join_send,
        join_recv,
        expert_send,
        expert_recv,
        gain_send,
        gain_recv,
        gain_line_send,
        gain_line_recv,
        back_send,
        back_recv,
        moment_sem,
        own_send,
        own_recv,
        own_join_send,
        own_join_recv,
    ) = rest[later:]
    rep = lax.axis_index("rep")
    me = lax.axis_index("shard")
    core = rep % 2
    rows = dense_ref.shape[2]
    expert_rows = experts_out.shape[2]
    steps = len(bits)
    streams = range(2)

    def remote(source, target, send_sem, recv_sem, peer):
        return pltpu.make_async_remote_copy(
            src_ref=source,
            dst_ref=target,
            send_sem=send_sem,
            recv_sem=recv_sem,
            device_id=peer,
            device_id_type=MESH,
        )

    def across(bit):
        return (flip(rep, bit), me)

    def order(stream):
        return [bits[(step + stream) % steps] for step in range(steps)]

    def side(bit):
        return (rep // bit) % 2

    plan = stream_plan(rep, bits, core * (expert_rows // 2), expert_rows // 4)
    base = [(core * (expert_rows // 2)) + stream * (expert_rows // 4) for stream in streams]

    def expert_copy(level, stream):
        if level == steps:
            place = rows_of(base[stream], expert_rows // 4)
            peer = across(1)
        else:
            bit, _, keep, _, size = plan[steps - 1 - level][stream]
            place = rows_of(keep, size)
            peer = across(bit)
        source = experts_out.at[:, :, place]
        if level == 0:
            source = share_ref.at[:, :, stream]
        return remote(
            source,
            experts_out.at[:, :, place],
            expert_send.at[level, stream],
            expert_recv.at[level, stream],
            peer,
        )

    def own_copy(stream):
        _, _, keep, _, size = plan[-1][stream]
        return pltpu.make_async_copy(
            share_ref.at[:, :, stream],
            experts_out.at[:, :, rows_of(keep, size)],
            local_sem.at[stream],
        )

    for stream in streams:
        own_copy(stream).start()
    peers = [(rep, lax.rem(me + k, count)) for k in range(1, count)]
    peers += [across(bit) for bit in (1,) + bits]
    greet(peers)

    def returning(peer, source):
        return remote(
            returned_ref.at[peer],
            got_ref.at[source],
            back_send.at[peer],
            back_recv.at[source],
            (rep, peer),
        )

    def core_copy(block):
        return remote(
            dense_ref.at[4 * (1 - core) + block],
            land_core.at[block],
            core_send.at[block],
            core_recv.at[block],
            across(1),
        )

    gain_bits = (1,) + bits

    def gain_copy(stage):
        return remote(
            gains_send.at[stage],
            gains_land.at[stage],
            gain_send.at[stage],
            gain_recv.at[stage],
            across(gain_bits[stage]),
        )

    for stream in streams:
        expert_copy(0, stream).start()

    for k in range(1, count):
        returning(lax.rem(me + k, count), me).start()

    def whole(index):
        return weights_ref[index].reshape(count * rows, -1)

    def gain(index):
        at = EXPERTS + index
        return jnp.concatenate([small_ref[z, at : at + 1, :rows] for z in range(count)], axis=1)

    scaled, inverse = normalize(middle_ref[...])
    middle_extra, midnorm_part = normalize_back(second_ref[...], gain(1), scaled, inverse)
    grad_middle = cot_ref[...].astype(jnp.float32) + middle_extra
    tokens_out[...] = grad_middle
    branch_ref[...] = grad_middle.astype(jnp.bfloat16)
    heads_ref[...] = dot_nt(branch_ref[...], whole(2)).astype(jnp.bfloat16)
    bias = allowed_pairs(column_ref[...], row_ref[...])
    attend_backward(query_ref, pair_ref, bias, total_ref, heads_ref, table_ref, delta_ref)

    part = dense_ref.shape[3] // 3
    normed_turned = normed_ref[...].T
    head_turned = head_ref[...].T

    def make_block(block):
        def columns(ref, offset):
            return ref[:, pl.ds(pl.multiple_of(offset + block * part, part), part)]

        pair = jnp.concatenate([columns(delta_ref, 0), columns(delta_ref, 8 * part)], axis=1)
        left = jnp.dot(normed_turned, pair, preferred_element_type=jnp.float32)
        right = jnp.dot(head_turned, columns(branch_ref, 0), preferred_element_type=jnp.float32)
        for line in range(count):
            place = slice(line * rows, (line + 1) * rows)
            dense_ref[block, line, :, : 2 * part] = left[place].astype(jnp.bfloat16)
            dense_ref[block, line, :, 2 * part :] = right[place].astype(jnp.bfloat16)

    for block in range(4):
        make_block(4 * (1 - core) + block)
        core_copy(block).start()
    for block in range(4):
        make_block(4 * core + block)

    def gain_step(stage):
        gain_copy(stage).wait_recv()
        gains_send[stage + 1] = gains_send[stage] + gains_land[stage]
        if stage + 1 < len(gain_bits):
            gain_copy(stage + 1).start()

    first = [side(order(stream)[0]) for stream in streams]
    held = [2 * stream + first[stream] for stream in streams]
    given = [2 * stream + 1 - first[stream] for stream in streams]

    def first_copy(stream):
        return remote(
            total.at[given[stream]],
            land_first.at[stream],
            half_send.at[0, stream],
            half_recv.at[0, stream],
            across(order(stream)[0]),
        )

    def add_core(block):
        for line in range(count):
            total[block, line] = (
                dense_ref[4 * core + block, line].astype(jnp.float32)
                + land_core[block, line].astype(jnp.float32)
            ).astype(jnp.bfloat16)

    for block in range(4):
        core_copy(block).wait_recv()
    for stream in streams:
        add_core(given[stream])
        first_copy(stream).start()
    for stream in streams:
        add_core(held[stream])
    grad_first = dot_nt(delta_ref[:, : NHEADS * HEAD], whole(0)) + dot_nt(
        delta_ref[:, NHEADS * HEAD :], whole(1)
    )
    scaled, inverse = normalize(tokens_ref[...].astype(jnp.float32))
    input_extra, prenorm_part = normalize_back(grad_first, gain(0), scaled, inverse)
    tokens_out[...] = tokens_out[...] + input_extra
    gains_send[0] = jnp.concatenate(
        [prenorm_part, midnorm_part, jnp.zeros((6, prenorm_part.shape[1]), jnp.float32)], axis=0
    )
    gain_copy(0).start()
    gain_step(0)

    starts = []
    for stream in streams:
        start, size, line = 0, rows, []
        for step in range(1, steps):
            size = size // 2
            near = side(order(stream)[step])
            line.append((start + near * size, start + (1 - near) * size, size))
            start = start + near * size
        starts.append((start, size, line))

    last = starts[0][1]
    places = [rows_of(starts[stream][0], last) for stream in streams]
    inner = [slice(index * part, (index + 1) * part) for index in range(3)]

    def moment_copy(stream, index):
        block = 4 * core + held[stream]
        lanes = pl.ds(pl.multiple_of((held[stream] if index == 1 else block) * part, part), part)
        source = (query_moment, key_moment, out_moment)[index]
        return pltpu.make_async_copy(
            source.at[places[stream], lanes],
            moment_piece.at[stream, :, inner[index]],
            moment_sem.at[stream, index],
        )

    def moment_other(stream):
        lanes = pl.ds(pl.multiple_of(held[stream] * part, part), part)
        return pltpu.make_async_copy(
            value_moment.at[places[stream], lanes],
            moment_piece.at[stream, :, inner[1]],
            moment_sem.at[stream, 1],
        )

    for stream in streams:
        moment_copy(stream, 0).start()
        moment_copy(stream, 2).start()

        @pl.when(core == 0)
        def _():
            moment_copy(stream, 1).start()

        @pl.when(core == 1)
        def _():
            moment_other(stream).start()

    def later_copy(step, stream):
        keep, send, size = starts[stream][2][step - 1]
        return remote(
            total.at[held[stream], :, rows_of(send, size)],
            land_later[step - 1].at[stream],
            half_send.at[step, stream],
            half_recv.at[step, stream],
            across(order(stream)[step]),
        )

    for stream in streams:
        first_copy(stream).wait_recv()
        for line in range(count):
            total[held[stream], line] = (
                total[held[stream], line].astype(jnp.float32)
                + land_first[stream, line].astype(jnp.float32)
            ).astype(jnp.bfloat16)
        if steps > 1:
            later_copy(1, stream).start()
    gain_step(1)

    for step in range(1, steps):
        for stream in streams:
            later_copy(step, stream).wait_recv()
            keep, _, size = starts[stream][2][step - 1]
            for line in range(count):
                place = rows_of(keep, size)
                total[held[stream], line, place] = (
                    total[held[stream], line, place].astype(jnp.float32)
                    + land_later[step - 1][stream, line].astype(jnp.float32)
                ).astype(jnp.bfloat16)
            if step + 1 < steps:
                later_copy(step + 1, stream).start()
        gain_step(step + 1)

    for stream in streams:
        own_copy(stream).wait()
        expert_copy(0, stream).wait_recv()
        if steps > 1:
            expert_copy(1, stream).start()

    for stream in streams:
        for line in range(count):
            piece_send[line, stream] = total[held[stream], line, places[stream]]

    def shard_copy(k):
        target = lax.rem(me + k, count)
        return remote(
            piece_send.at[target],
            piece_land.at[me],
            shard_send.at[target],
            shard_recv.at[me],
            (rep, target),
        )

    def shard_arrival(source):
        return remote(
            piece_send.at[source],
            piece_land.at[source],
            shard_send.at[source],
            shard_recv.at[source],
            (rep, source),
        )

    def gain_line(k):
        target = lax.rem(me + k, count)
        return remote(
            gains_send.at[len(gain_bits)],
            gains_all.at[me],
            gain_line_send.at[target],
            gain_line_recv.at[me],
            (rep, target),
        )

    def gain_arrival(source):
        return remote(
            gains_send.at[len(gain_bits)],
            gains_all.at[source],
            gain_line_send.at[source],
            gain_line_recv.at[source],
            (rep, source),
        )

    def own_grow(step, stream):
        block = 4 * core + held[stream]
        if step == 0:
            part_ref = grads_out.at[block]
        else:
            keep, _, size = starts[stream][2][step - 1]
            part_ref = grads_out.at[block, rows_of(keep, size)]
        return remote(
            part_ref,
            part_ref,
            own_send.at[step, stream],
            own_recv.at[step, stream],
            across(order(stream)[step]),
        )

    def own_join(stream):
        part_ref = grads_out.at[pl.ds(4 * core + 2 * stream, 2)]
        return remote(
            part_ref, part_ref, own_join_send.at[stream], own_join_recv.at[stream], across(1)
        )

    for k in range(1, count):
        shard_copy(k).start()
        gain_line(k).start()
    summed = piece_send[me].astype(jnp.float32)
    for k in range(1, count):
        source = lax.rem(me + k, count)
        shard_arrival(source).wait_recv()
        summed = summed + piece_land[source].astype(jnp.float32)
    for stream in streams:
        for index in range(3):
            moment_copy(stream, index).wait()
        grads_out[4 * core + held[stream], places[stream]] = summed[stream].astype(jnp.bfloat16)
        own_grow(steps - 1, stream).start()
    piece[...] = (momentum_keep * moment_piece[...] + summed).astype(jnp.bfloat16)

    def line_copy(k, stream):
        target = lax.rem(me + k, count)
        return remote(
            piece.at[stream],
            dense_out.at[4 * core + held[stream], me, places[stream]],
            line_send.at[stream, target],
            line_recv.at[stream, me],
            (rep, target),
        )

    def line_arrival(source, stream):
        return remote(
            piece.at[stream],
            dense_out.at[4 * core + held[stream], source, places[stream]],
            line_send.at[stream, source],
            line_recv.at[stream, source],
            (rep, source),
        )

    def own_piece(stream):
        return pltpu.make_async_copy(
            piece.at[stream],
            dense_out.at[4 * core + held[stream], me, places[stream]],
            local_sem.at[2 + stream],
        )

    for stream in streams:
        own_piece(stream).start()
        for k in range(1, count):
            line_copy(k, stream).start()
    gained = gains_send[len(gain_bits)]
    for k in range(1, count):
        source = lax.rem(me + k, count)
        gain_arrival(source).wait_recv()
        gained = gained + gains_all[source]
    gains_out[...] = gained

    for level in range(1, steps):
        for stream in streams:
            expert_copy(level, stream).wait_recv()
            expert_copy(level + 1, stream).start()
    if steps == 1:
        for stream in streams:
            expert_copy(1, stream).start()

    def grow_copy(step, stream):
        if step == 0:
            place = dense_out.at[4 * core + held[stream]]
        else:
            keep, _, size = starts[stream][2][step - 1]
            place = dense_out.at[4 * core + held[stream], :, rows_of(keep, size)]
        return remote(
            place,
            place,
            grow_send.at[step, stream],
            grow_recv.at[step, stream],
            across(order(stream)[step]),
        )

    for stream in streams:
        own_piece(stream).wait()
        for k in range(1, count):
            line_arrival(lax.rem(me + k, count), stream).wait_recv()
        grow_copy(steps - 1, stream).start()
    for step in reversed(range(steps)):
        for stream in streams:
            own_grow(step, stream).wait_recv()
            if step > 0:
                own_grow(step - 1, stream).start()
            else:
                own_join(stream).start()
    mixed = middle_ref[...] + returned_ref[me].astype(jnp.float32)
    for k in range(1, count):
        source = lax.rem(me + k, count)
        returning(source, source).wait_recv()
        mixed = mixed + got_ref[source].astype(jnp.float32)
    mixed_out[...] = mixed.astype(mixed_out.dtype)
    for stream in streams:
        expert_copy(steps, stream).wait()
    leave = pltpu.make_async_copy(experts_out, experts_hbm, local_sem.at[0])
    leave.start()
    for step in reversed(range(steps)):
        for stream in streams:
            grow_copy(step, stream).wait_recv()
            if step > 0:
                grow_copy(step - 1, stream).start()

    def join_copy(stream):
        place = dense_out.at[pl.ds(4 * core + 2 * stream, 2)]
        return remote(place, place, join_send.at[stream], join_recv.at[stream], across(1))

    for stream in streams:
        join_copy(stream).start()
    for stream in streams:
        join_copy(stream).wait()
        own_join(stream).wait()
        for step in range(steps):
            own_grow(step, stream).wait_send()
        for level in range(steps):
            expert_copy(level, stream).wait_send()
        first_copy(stream).wait_send()
        for step in range(1, steps):
            later_copy(step, stream).wait_send()
        for k in range(1, count):
            line_copy(k, stream).wait_send()
        for step in range(steps):
            grow_copy(step, stream).wait_send()
    for block in range(4):
        core_copy(block).wait_send()
    for stage in range(len(gain_bits)):
        gain_copy(stage).wait_send()
    for k in range(1, count):
        shard_copy(k).wait_send()
        gain_line(k).wait_send()
        returning(lax.rem(me + k, count), me).wait_send()
    leave.wait()


def spread(
    share, returned, normed, head_low, weights, small, tokens, cotangent, second, middle, *rest, bits, count
):
    query, pair, log_total, tables, starts, moments = rest
    experts, _, _, final, hidden = share.shape
    token_count, features = normed.shape
    rows = features // count
    width = 3 * features // 8
    dense_shape = (8, count, rows, width)
    gains_shape = (8, features)
    steps = len(bits)
    last = rows >> (steps - 1)
    low = jnp.bfloat16
    vmem = pl.BlockSpec(memory_space=pltpu.VMEM)
    dma = pltpu.SemaphoreType.DMA
    return pl.pallas_call(
        functools.partial(spread_kernel, count, bits),
        in_specs=[vmem] * 16 + [pl.BlockSpec(memory_space=pl.ANY)] * 4,
        out_specs=[pl.BlockSpec(memory_space=pl.ANY)] + [vmem] * 5,
        out_shape=[
            jax.ShapeDtypeStruct((experts, 3, 4 * (final << steps), hidden), low),
            jax.ShapeDtypeStruct(dense_shape, low),
            jax.ShapeDtypeStruct((8, rows, width), low),
            jax.ShapeDtypeStruct(gains_shape, jnp.float32),
            jax.ShapeDtypeStruct((token_count, features), jnp.float32),
            jax.ShapeDtypeStruct((token_count, features), low),
        ],
        scratch_shapes=[
            pltpu.VMEM((experts, 3, 4 * (final << steps), hidden), low),
            pltpu.VMEM((count, token_count, features), low),
            pltpu.VMEM((2, last, width), jnp.float32),
            pltpu.VMEM((token_count, 2 * features), low),
            pltpu.VMEM((token_count, features), low),
            pltpu.VMEM((token_count, features), low),
            pltpu.VMEM(dense_shape, low),
            pltpu.VMEM((4, count, rows, width), low),
            pltpu.VMEM((4, count, rows, width), low),
            pltpu.VMEM((2, count, rows, width), low),
        ]
        + [pltpu.VMEM((2, count, rows >> step, width), low) for step in range(1, steps)]
        + [
            pltpu.VMEM((count, 2, last, width), low),
            pltpu.VMEM((count, 2, last, width), low),
            pltpu.VMEM((2, last, width), low),
            pltpu.VMEM((steps + 2,) + gains_shape, jnp.float32),
            pltpu.VMEM((steps + 1,) + gains_shape, jnp.float32),
            pltpu.VMEM((count,) + gains_shape, jnp.float32),
            dma((4,)),
            dma((4,)),
            dma((4,)),
            dma((steps, 2)),
            dma((steps, 2)),
            dma((count,)),
            dma((count,)),
            dma((steps, 2)),
            dma((steps, 2)),
            dma((2, count)),
            dma((2, count)),
            dma((2,)),
            dma((2,)),
            dma((steps + 1, 2)),
            dma((steps + 1, 2)),
            dma((steps + 1,)),
            dma((steps + 1,)),
            dma((count,)),
            dma((count,)),
            dma((count,)),
            dma((count,)),
            dma((2, 3)),
            dma((steps, 2)),
            dma((steps, 2)),
            dma((2,)),
            dma((2,)),
        ],
        compiler_params=pltpu.CompilerParams(
            collective_id=2, has_side_effects=True, vmem_limit_bytes=63 * 1024 * 1024
        ),
        name="spread",
    )(
        share,
        returned,
        normed,
        head_low,
        weights,
        small,
        tokens,
        cotangent,
        second,
        middle,
        query,
        pair,
        log_total,
        tables,
        starts[:, None],
        starts[None, :],
        *moments,
    )


def gather_kernel(
    count,
    bits,
    query_weight,
    key_weight,
    value_weight,
    out_weight,
    small_ref,
    tokens_ref,
    cot_ref,
    table_ref,
    column_ref,
    row_ref,
    weights_hbm,
    small_out,
    cot_out,
    middle_out,
    first_out,
    second_out,
    query_out,
    pair_out,
    head_out,
    total_out,
    weights_out,
    weights_ref,
    local_sem,
    line_send,
    line_recv,
    grow_send,
    grow_recv,
    join_send,
    join_recv,
    small_send,
    small_recv,
    right_sem,
    left_sem,
    arrive_sem,
):
    rep = lax.axis_index("rep")
    me = lax.axis_index("shard")
    core = rep % 2
    steps = len(bits)
    streams = range(2)
    rows, width = weights_ref.shape[1:]
    half = width // 2
    fine = half // 4
    others = [lax.rem(me + k, count) for k in range(1, count)]

    def columns_of(start, size):
        return pl.ds(pl.multiple_of(start, 128), size)

    def order(stream):
        return [bits[(step + stream) % steps] for step in range(steps)]

    def side(bit):
        return (rep // bit) % 2

    narrow = width // 2
    weights_ref[0] = query_weight[...]
    weights_ref[1, :, :narrow] = key_weight[...]
    weights_ref[1, :, narrow:] = value_weight[...]
    weights_ref[2] = out_weight[...]
    own_copy = pltpu.make_async_copy(weights_ref, weights_out.at[:, me], local_sem.at[0])
    own_copy.start()
    small_out[me] = small_ref[...]
    cot_out[me] = cot_ref[...]
    peers = [(rep, other) for other in others]
    peers += [(flip(rep, bit), me) for bit in (1,) + bits]
    greet(peers)

    regions = []
    for stream in streams:
        column = core * half + stream * 2 * fine
        narrow = columns_of(column + side(order(stream)[0]) * fine, fine)
        start, size = 0, rows
        held = [(pl.ds(0, rows), narrow)]
        for step in range(1, steps):
            size = size // 2
            start = start + side(order(stream)[step]) * size
            held.append((rows_of(start, size), narrow))
        regions.append((held, columns_of(column, 2 * fine)))

    def remote(source, target, send_sem, recv_sem, peer):
        return pltpu.make_async_remote_copy(
            src_ref=source,
            dst_ref=target,
            send_sem=send_sem,
            recv_sem=recv_sem,
            device_id=peer,
            device_id_type=MESH,
        )

    def line_copy(stream, source, peer):
        place, columns = regions[stream][0][-1]
        return remote(
            weights_ref.at[:, place, columns],
            weights_out.at[:, source, place, columns],
            line_send.at[stream, peer],
            line_recv.at[stream, source],
            (rep, peer),
        )

    def grow_copy(step, stream, source):
        place, columns = regions[stream][0][step]
        part = weights_out.at[:, source, place, columns]
        return remote(
            part,
            part,
            grow_send.at[step, stream, source],
            grow_recv.at[step, stream, source],
            (flip(rep, order(stream)[step]), me),
        )

    def join_copy(stream, source):
        part = weights_out.at[:, source, :, regions[stream][1]]
        return remote(
            part,
            part,
            join_send.at[stream, source],
            join_recv.at[stream, source],
            (flip(rep, 1), me),
        )

    def small_copy(source, peer):
        return remote(
            small_ref,
            small_out.at[source],
            small_send.at[peer],
            small_recv.at[source],
            (rep, peer),
        )

    def hand_on(block, to_right):
        peer = jnp.minimum(me + 1, count - 1) if to_right else jnp.maximum(me - 1, 0)
        return remote(
            cot_out.at[block],
            cot_out.at[block],
            (right_sem if to_right else left_sem).at[block],
            arrive_sem.at[block],
            (rep, peer),
        )

    def line_start():
        @pl.when(me < count - 1)
        def _():
            hand_on(me, True).start()

        @pl.when(me > 0)
        def _():
            hand_on(me, False).start()

    def line_step(step):
        lower = me - step
        upper = me + step

        @pl.when(lower >= 0)
        def _():
            hand_on(jnp.maximum(lower, 0), True).wait_recv()

            @pl.when(me < count - 1)
            def _():
                hand_on(jnp.maximum(lower, 0), True).start()

        @pl.when(upper < count)
        def _():
            hand_on(jnp.minimum(upper, count - 1), False).wait_recv()

            @pl.when(me > 0)
            def _():
                hand_on(jnp.minimum(upper, count - 1), False).start()

    def line_send_all():
        for other in others:
            for stream in streams:
                line_copy(stream, me, other).start()

    def advance(level):
        for other in others:
            for stream in streams:
                if level == 0:
                    line_copy(stream, other, other).wait_recv()
                else:
                    grow_copy(steps - level, stream, other).wait_recv()
                if level < steps:
                    grow_copy(steps - 1 - level, stream, other).start()
                else:
                    join_copy(stream, other).start()

    for other in others:
        small_copy(me, other).start()
    line_send_all()
    for other in others:
        small_copy(other, other).wait_recv()

    def gain(index):
        at = EXPERTS + index
        return jnp.concatenate([small_out[z, at : at + 1, :rows] for z in range(count)], axis=1)

    inputs = tokens_ref[...].astype(jnp.float32)
    first_out[...] = (normalize(inputs)[0] * gain(0)).astype(jnp.bfloat16)
    advance(0)
    line_start()
    for level in range(1, steps + 1):
        advance(level)
        if level == 1:
            line_step(1)
    for other in others:
        for stream in streams:
            join_copy(stream, other).wait_recv()
    own_copy.wait()
    leave = pltpu.make_async_copy(weights_out, weights_hbm, local_sem.at[2])
    leave.start()

    def whole(index):
        return weights_out[index].reshape(count * rows, width)

    project_inputs(first_out[...], whole, query_out, pair_out, table_ref)
    bias = allowed_pairs(column_ref[...], row_ref[...])
    if count > 2:
        line_step(2)
    attend_forward(range(KVHEADS // 2), query_out, pair_out, bias, head_out, total_out)
    for step in range(3, count - 1):
        line_step(step)
    attend_forward(range(KVHEADS // 2, KVHEADS), query_out, pair_out, bias, head_out, total_out)
    middle = inputs + dot_nn(head_out[...], whole(2))
    middle_out[...] = middle
    second_out[...] = (normalize(middle)[0] * gain(1)).astype(jnp.bfloat16)
    if count > 3:
        line_step(count - 1)
    for other in others:
        for stream in streams:
            join_copy(stream, other).wait_send()
            line_copy(stream, me, other).wait_send()
            for step in range(steps):
                grow_copy(step, stream, other).wait_send()
    for other in others:
        small_copy(me, other).wait_send()
    for block in range(count):

        @pl.when((block <= me) & (me < count - 1))
        def _():
            hand_on(block, True).wait_send()

        @pl.when((block >= me) & (me > 0))
        def _():
            hand_on(block, False).wait_send()

    leave.wait()


def gather(weights, small, tokens, cotangent, tables, starts, bits, count):
    rows, width = weights[0].shape
    depth = 3
    token_count = tokens.shape[0]
    steps = len(bits)
    low = jnp.bfloat16
    vmem = pl.BlockSpec(memory_space=pltpu.VMEM)
    dma = pltpu.SemaphoreType.DMA
    whole = jax.ShapeDtypeStruct((depth, count, rows, width), low)
    features = jax.ShapeDtypeStruct((token_count, width), low)
    return pl.pallas_call(
        functools.partial(gather_kernel, count, bits),
        in_specs=[vmem] * 10,
        out_specs=[pl.BlockSpec(memory_space=pl.ANY)] + [vmem] * 9,
        out_shape=[
            whole,
            jax.ShapeDtypeStruct((count,) + small.shape, small.dtype),
            jax.ShapeDtypeStruct((count, token_count, width), low),
            jax.ShapeDtypeStruct((token_count, width), jnp.float32),
            features,
            features,
            features,
            features,
            features,
            jax.ShapeDtypeStruct((2 * token_count, KVHEADS), jnp.float32),
        ],
        scratch_shapes=[
            pltpu.VMEM(whole.shape, low),
            pltpu.VMEM((depth, rows, width), low),
            dma((3,)),
            dma((2, count)),
            dma((2, count)),
            dma((steps, 2, count)),
            dma((steps, 2, count)),
            dma((2, count)),
            dma((2, count)),
            dma((count,)),
            dma((count,)),
            dma((count,)),
            dma((count,)),
            dma((count,)),
        ],
        compiler_params=pltpu.CompilerParams(
            collective_id=3, has_side_effects=True, vmem_limit_bytes=56 * 1024 * 1024
        ),
        name="gather",
    )(
        *weights,
        small,
        tokens,
        cotangent,
        tables,
        starts[:, None],
        starts[None, :],
    )


def local(
    tokens,
    sequence_start,
    routes,
    route_weights,
    cotangent,
    query_proj,
    key_proj,
    value_proj,
    out_proj,
    prenorm,
    midnorm,
    gate_proj,
    up_proj,
    down_proj,
    query_moment,
    key_moment,
    value_moment,
    out_moment,
    prenorm_moment,
    midnorm_moment,
    gate_moment,
    up_moment,
    down_moment,
):
    shard_index = lax.axis_index("shard")
    rep_count = lax.axis_size("rep")
    shard_count = lax.axis_size("shard")
    row_block = query_proj.shape[0]
    bits = rep_bits(rep_count)
    experts_here = gate_proj.shape[0]
    dense_weights = jnp.sum(
        jnp.where(
            routes.T[None, :, :] == jnp.arange(EXPERTS, dtype=jnp.int32)[:, None, None],
            route_weights.T[None, :, :],
            0.0,
        ),
        axis=1,
    )
    gain_rows = jnp.pad(
        jnp.stack([prenorm, midnorm]).astype(jnp.float32),
        ((0, 6), (0, tokens.shape[0] - row_block)),
    )
    tables = rotary_tables(jnp.arange(tokens.shape[0], dtype=jnp.int32) - sequence_start)
    (
        weights,
        small,
        cotangent_all,
        middle,
        normed_first,
        normed_second,
        query,
        pair,
        head_low,
        log_total,
    ) = gather(
        (query_proj, key_proj, value_proj, out_proj),
        jnp.concatenate([dense_weights, gain_rows], axis=0),
        tokens,
        cotangent,
        tables,
        sequence_start,
        bits,
        shard_count,
    )
    expert_weights = lax.dynamic_slice_in_dim(
        small, shard_index * experts_here, experts_here, 1
    ).transpose(0, 2, 1)
    returned, grad_second, expert_share = moe(
        normed_second,
        cotangent_all,
        expert_weights,
        gate_proj,
        up_proj,
        down_proj,
        bits,
        shard_count,
    )
    own_moments = (query_moment, key_moment, value_moment, out_moment)
    expert_grads, dense_next, dense_grads, gains_grad, grad_tokens, mixed = spread(
        expert_share,
        returned,
        normed_first,
        head_low,
        weights,
        small,
        tokens,
        cotangent,
        grad_second,
        middle,
        query,
        pair,
        log_total,
        tables,
        sequence_start,
        own_moments,
        bits=bits,
        count=shard_count,
    )
    gains_here = lax.dynamic_slice_in_dim(gains_grad, shard_index * row_block, row_block, 1)
    prenorm_grad = gains_here[0]
    midnorm_grad = gains_here[1]
    prenorm_next = momentum_keep * prenorm_moment + prenorm_grad
    midnorm_next = momentum_keep * midnorm_moment + midnorm_grad
    prenorm_update = -rate_gain * prenorm_next
    midnorm_update = -rate_gain * midnorm_next
    rep_index = lax.axis_index("rep")
    (
        query_grad,
        query_next,
        key_grad,
        key_next,
        value_grad,
        value_next,
        out_grad,
        out_next,
        own_wide,
        own_narrow,
    ) = dense_update(
        dense_next,
        dense_grads,
        own_moments,
        LAYOUT,
        shard_index,
        rep_index,
    )
    pairs = [(index, index + 1 - 2 * (index % 2)) for index in range(rep_count)]
    other_wide = lax.ppermute(own_wide, "rep", pairs)
    other_narrow = lax.ppermute(own_narrow, "rep", pairs)
    gate_grad, gate_next, gate_update, up_grad, up_next, up_update = expert_update(
        expert_grads, (0, 1), (gate_moment, up_moment)
    )
    (
        down_grad,
        down_next,
        down_update,
        query_update,
        out_update,
        key_update,
        value_update,
        grad_tokens,
        mixed,
    ) = expert_update(
        expert_grads,
        (2,),
        (down_moment,),
        (own_wide, other_wide, own_narrow, other_narrow, grad_tokens, mixed),
    )
    return (
        mixed,
        grad_tokens,
        query_grad,
        query_next,
        query_update,
        key_grad,
        key_next,
        key_update,
        value_grad,
        value_next,
        value_update,
        out_grad,
        out_next,
        out_update,
        prenorm_grad,
        prenorm_next,
        prenorm_update,
        midnorm_grad,
        midnorm_next,
        midnorm_update,
        gate_grad,
        gate_next,
        gate_update,
        up_grad,
        up_next,
        up_update,
        down_grad,
        down_next,
        down_update,
    )


def solution(mesh):
    return jax.shard_map(
        local,
        mesh=mesh,
        in_specs=(
            P(("rep", "shard"), None),
            P(("rep", "shard")),
            P(("rep", "shard"), None),
            P(("rep", "shard"), None),
            P(("rep", "shard"), None),
            P("shard", None),
            P("shard", None),
            P("shard", None),
            P("shard", None),
            P("shard"),
            P("shard"),
            P("shard", None, None),
            P("shard", None, None),
            P("shard", None, None),
            P("shard", None),
            P("shard", None),
            P("shard", None),
            P("shard", None),
            P("shard"),
            P("shard"),
            P("shard", None, None),
            P("shard", None, None),
            P("shard", None, None),
        ),
        out_specs=(
            P(("rep", "shard"), None),
            P(("rep", "shard"), None),
            P("shard", None),
            P("shard", None),
            P("shard", None),
            P("shard", None),
            P("shard", None),
            P("shard", None),
            P("shard", None),
            P("shard", None),
            P("shard", None),
            P("shard", None),
            P("shard", None),
            P("shard", None),
            P("shard"),
            P("shard"),
            P("shard"),
            P("shard"),
            P("shard"),
            P("shard"),
            P("shard", None, None),
            P("shard", None, None),
            P("shard", None, None),
            P("shard", None, None),
            P("shard", None, None),
            P("shard", None, None),
            P("shard", None, None),
            P("shard", None, None),
            P("shard", None, None),
        ),
        check_vma=False,
    )
```

```python
import functools
import math

import jax
import jax.numpy as jnp
from jax import lax
from jax.experimental import pallas as pl
from jax.experimental.pallas import tpu as pltpu
from jax.sharding import PartitionSpec as P

NHEADS = 16
KVHEADS = 8
HEAD = 64
EXPERTS = 16
NS_ITERS = 2


norm_epsilon = 1e-06
rotary_base = 10000.0
momentum_keep = 0.9
rate_matrix = 0.5
rate_gain = 0.0002
newton_first = 3.4445
newton_second = -4.775
newton_third = 2.0315
masked_score = -1e30


def normalize(values):
    inverse = lax.rsqrt(jnp.mean(values * values, axis=-1, keepdims=True) + norm_epsilon)
    return (values * inverse, inverse)


def normalize_back(grad_normed, scaling, scaled, inverse):
    grad_scaled = grad_normed * scaling
    inner_mean = jnp.mean(grad_scaled * scaled, axis=-1, keepdims=True)
    return (
        inverse * (grad_scaled - scaled * inner_mean),
        jnp.sum(grad_normed * scaled, axis=0, keepdims=True),
    )


def dot_nn(left, right):
    return jnp.dot(left, right, preferred_element_type=jnp.float32)


def dot_nt(left, right):
    return lax.dot_general(
        left, right, (((1,), (1,)), ((), ())), preferred_element_type=jnp.float32
    )


def dot_tn(left, right):
    return lax.dot_general(
        left, right, (((0,), (0,)), ((), ())), preferred_element_type=jnp.float32
    )


def rotate(values, table_ref, sign):
    return (
        values * table_ref[0]
        + sign * pltpu.roll(values, 96, 1) * table_ref[1]
        + sign * pltpu.roll(values, 32, 1) * table_ref[2]
    )


def lane_low(shape):
    return lax.broadcasted_iota(jnp.int32, shape, 1) < HEAD


def twice(pair, upper):
    wide = pair.astype(jnp.float32)
    turned = pltpu.roll(wide, HEAD, 1)
    first = lane_low(pair.shape)
    return jnp.where(first != upper, wide, turned).astype(pair.dtype)


def stacked(pair):
    first = lane_low(pair.shape)
    zero = jnp.zeros_like(pair)
    return jnp.concatenate([jnp.where(first, pair, zero), jnp.where(first, zero, pair)], axis=0)


def unstacked(rows):
    half = rows.shape[0] // 2
    return jnp.where(lane_low((half, rows.shape[1])), rows[:half], rows[half:])


def allowed_pairs(start_row):
    shape = (start_row.shape[1], start_row.shape[1])
    keys = jnp.broadcast_to(start_row.astype(jnp.float32), shape)
    query_places = lax.broadcasted_iota(jnp.int32, shape, 0)
    key_places = lax.broadcasted_iota(jnp.int32, shape, 1)
    one = (keys.T == keys) & (key_places <= query_places)
    return jnp.where(jnp.concatenate([one, one], axis=0), 0.0, masked_score)


def block_lanes(ref, block):
    return ref[:, block * 2 * HEAD : (block + 1) * 2 * HEAD]


def attend_pair(block, query_ref, pair_ref, bias):
    key = twice(block_lanes(pair_ref, block // 2), block % 2 == 1)
    value = twice(block_lanes(pair_ref, KVHEADS // 2 + block // 2), block % 2 == 1)
    queries = stacked(block_lanes(query_ref, block))
    scores = dot_nt(queries, key) * (1.0 / math.sqrt(HEAD)) + bias
    return (queries, key, value, scores)


def project_inputs(normed, weights, query_ref, pair_ref, table_ref):
    queries = dot_nn(normed, weights(0))
    for block in range(NHEADS // 2):
        lanes = slice(block * 2 * HEAD, (block + 1) * 2 * HEAD)
        query_ref[:, lanes] = rotate(queries[:, lanes], table_ref, 1.0).astype(jnp.bfloat16)
    pairs = dot_nn(normed, weights(1))
    for block in range(KVHEADS):
        lanes = slice(block * 2 * HEAD, (block + 1) * 2 * HEAD)
        value = pairs[:, lanes]
        if block < KVHEADS // 2:
            value = rotate(value, table_ref, 1.0)
        pair_ref[:, lanes] = value.astype(jnp.bfloat16)


def attend_forward(blocks, query_ref, pair_ref, bias, head_ref, total_ref):
    for block in blocks:
        _, _, value, scores = attend_pair(block, query_ref, pair_ref, bias)
        row_max = jnp.max(scores, axis=-1, keepdims=True)
        exponents = jnp.exp(scores - row_max)
        totals = jnp.sum(exponents, axis=-1, keepdims=True)
        softmax_low = (exponents * (1.0 / totals)).astype(jnp.bfloat16)
        head_ref[:, block * 2 * HEAD : (block + 1) * 2 * HEAD] = unstacked(
            dot_nn(softmax_low, value)
        ).astype(jnp.bfloat16)
        total_ref[:, block : block + 1] = row_max + jnp.log(totals)


def attend_backward(query_ref, pair_ref, bias, total_ref, grad_ref, table_ref, delta_ref):
    folded = []
    for block in range(KVHEADS):
        queries, key, value, scores = attend_pair(block, query_ref, pair_ref, bias)
        grads = stacked(block_lanes(grad_ref, block))
        softmax_full = jnp.exp(scores - total_ref[:, block : block + 1])
        grad_softmax = dot_nt(grads, value)
        inner = jnp.sum(softmax_full * grad_softmax, axis=-1, keepdims=True)
        grad_scores = (softmax_full * (grad_softmax - inner)).astype(jnp.bfloat16)
        scale = 1.0 / math.sqrt(HEAD)
        grad_query = unstacked(dot_nn(grad_scores, key)) * scale
        lanes = slice(block * 2 * HEAD, (block + 1) * 2 * HEAD)
        delta_ref[:, lanes] = rotate(grad_query, table_ref, -1.0).astype(jnp.bfloat16)
        grad_key = dot_tn(grad_scores, queries) * scale
        grad_value = dot_tn(softmax_full.astype(jnp.bfloat16), grads)
        folded.append(
            (
                grad_key + pltpu.roll(grad_key, HEAD, 1),
                grad_value + pltpu.roll(grad_value, HEAD, 1),
            )
        )
        if block % 2 == 1:
            first = lane_low(grad_key.shape)
            both = [jnp.where(first, low, high) for low, high in zip(*folded)]
            folded = []
            base = NHEADS * HEAD + (block // 2) * 2 * HEAD
            delta_ref[:, base : base + 2 * HEAD] = rotate(both[0], table_ref, -1.0).astype(
                jnp.bfloat16
            )
            base = base + KVHEADS * HEAD
            delta_ref[:, base : base + 2 * HEAD] = both[1].astype(jnp.bfloat16)


def rotary_tables(positions):
    half_size = HEAD // 2
    frequency = rotary_base ** (-(jnp.arange(half_size, dtype=jnp.float32) * 2.0) / HEAD)
    angles = positions.astype(jnp.float32)[:, None] * frequency[None, :]
    cosine, sine = (jnp.cos(angles), jnp.sin(angles))
    zero = jnp.zeros_like(sine)
    return jnp.stack(
        [
            jnp.concatenate([cosine] * 4, axis=1),
            jnp.concatenate([-sine, zero] * 2, axis=1),
            jnp.concatenate([zero, sine] * 2, axis=1),
        ]
    )


def newton_parts(grams):
    a, b, c = newton_first, newton_second, newton_third

    def times(left, right):
        return jnp.dot(left, right, preferred_element_type=jnp.float32)

    lows = [gram.astype(jnp.bfloat16) for gram in grams]
    firsts = [b * gram + c * times(low, low) for gram, low in zip(grams, lows)]
    first_lows = [first.astype(jnp.bfloat16) for first in firsts]
    mixes = [times(low, first) for low, first in zip(lows, first_lows)]
    nexts = [
        (a * a) * gram + (2.0 * a) * mix + times(mix.astype(jnp.bfloat16), first)
        for gram, mix, first in zip(grams, mixes, first_lows)
    ]
    next_lows = [gram.astype(jnp.bfloat16) for gram in nexts]
    seconds = [b * gram + c * times(low, low) for gram, low in zip(nexts, next_lows)]
    second_lows = [second.astype(jnp.bfloat16) for second in seconds]
    return list(zip(firsts, first_lows, seconds, second_lows))


def scaled_gram(gram):
    shape = gram.shape
    rows = lax.broadcasted_iota(jnp.int32, shape, 0)
    diagonal = rows == lax.broadcasted_iota(jnp.int32, shape, 1)
    inverse = 1.0 / (jnp.sqrt(jnp.sum(jnp.where(diagonal, gram, 0.0))) + 1e-07)
    return (gram * (inverse * inverse), inverse)


def expert_update_kernel(kinds, scale, carried, *refs):
    a = newton_first
    grads_ref = refs[0]
    moments = refs[1 : 1 + len(kinds)]
    given = refs[1 + len(kinds) : 1 + len(kinds) + carried]
    outs = refs[1 + len(kinds) + carried :]
    if carried:
        taken = outs[3 * len(kinds) : 3 * len(kinds) + carried]
        held = outs[3 * len(kinds) + carried : -2]
        load_sem, store_sem = outs[-2:]
        core = lax.axis_index("rep") % 2

        def load(index):
            return pltpu.make_async_copy(given[index], held[index], load_sem.at[index])

        def store(source, target):
            return pltpu.make_async_copy(held[source], taken[target], store_sem.at[target])

        @pl.when(pl.program_id(0) == 0)
        def _():
            for index in range(carried):
                load(index).start()

    half = grads_ref.shape[3]
    tall = kinds[0] < 2
    states = []
    for index in range(len(kinds)):
        for e in range(grads_ref.shape[0]):
            grad = grads_ref[e, index].astype(jnp.float32)
            if not tall:
                grad = jnp.concatenate([grad[:half], grad[half:]], axis=1)
            moment = momentum_keep * moments[index][e] + grad
            outs[3 * index][e] = grad
            outs[3 * index + 1][e] = moment
            low = moment.astype(jnp.bfloat16)
            sides = (((0,), (0,)), ((), ())) if tall else (((1,), (1,)), ((), ()))
            gram, inverse = scaled_gram(
                lax.dot_general(low, low, sides, preferred_element_type=jnp.float32)
            )
            states.append((index, e, inverse, low, gram))
    parts = newton_parts([state[-1] for state in states])
    for (index, e, inverse, low, _), (first, first_low, second, second_low) in zip(states, parts):
        rest = a * (first + second) + jnp.dot(
            first_low, second_low, preferred_element_type=jnp.float32
        )
        rest = ((-scale * inverse) * rest).astype(jnp.bfloat16)
        if tall:
            step = jnp.dot(low, rest, preferred_element_type=jnp.float32)
        else:
            step = jnp.dot(rest, low, preferred_element_type=jnp.float32)
        outs[3 * index + 2][e] = (-scale * a * a * inverse) * outs[3 * index + 1][e] + step
    if carried:

        @pl.when(pl.program_id(0) == 0)
        def _():
            for index in range(carried):
                load(index).wait()
            for pair in (0, 2):

                @pl.when(core == 0)
                def _():
                    store(pair, pair).start()
                    store(pair + 1, pair + 1).start()

                @pl.when(core == 1)
                def _():
                    store(pair + 1, pair).start()
                    store(pair, pair + 1).start()

            for index in range(4, carried):
                store(index, index).start()

        @pl.when(pl.program_id(0) == pl.num_programs(0) - 1)
        def _():
            for index in range(carried):
                store(index, index).wait()


def expert_update(grads, kinds, moments, carried=()):
    count, rows, columns = moments[0].shape
    group = 2 // len(kinds)
    scale = rate_matrix * math.sqrt(max(1.0, columns / rows))
    block = pl.BlockSpec((group, rows, columns), lambda i: (i, 0, 0))
    place = kinds[0] // len(kinds)
    taken = pl.BlockSpec((group, len(kinds)) + grads.shape[2:], lambda i: (i, place, 0, 0))
    shape = jax.ShapeDtypeStruct(moments[0].shape, jnp.float32)
    hand_on = [pl.BlockSpec(memory_space=pl.ANY)] * len(carried)
    return pl.pallas_call(
        functools.partial(expert_update_kernel, kinds, scale, len(carried)),
        grid=(count // group,),
        in_specs=[taken] + [block] * len(kinds) + hand_on,
        out_specs=[block] * (3 * len(kinds)) + hand_on,
        out_shape=[shape] * (3 * len(kinds))
        + [jax.ShapeDtypeStruct(array.shape, array.dtype) for array in carried],
        scratch_shapes=[pltpu.VMEM(array.shape, array.dtype) for array in carried]
        + [pltpu.SemaphoreType.DMA((len(carried),))] * (2 if carried else 0),
        compiler_params=pltpu.CompilerParams(vmem_limit_bytes=60 * 1024 * 1024),
        name="expert_update",
        cost_estimate=pl.CostEstimate(
            flops=count * len(kinds) * 2500000000,
            bytes_accessed=moments[0].size * len(kinds) * 18,
            transcendentals=0,
        ),
    )(grads, *moments, *carried)


def dense_update_kernel(layout, place_ref, next_ref, grads_ref, *refs):
    a = newton_first
    amount = len(layout)
    own_moments = refs[:amount]
    outs = refs[amount : 3 * amount]
    updates = refs[3 * amount : 3 * amount + 2]
    matrices = refs[3 * amount + 2 : 3 * amount + 4]
    own_grads, own_next, sem = refs[3 * amount + 4 :]
    blocks, count, block_rows, width = next_ref.shape
    part = width // 3
    me = place_ref[0]
    core = place_ref[1]
    start = pl.multiple_of(me * block_rows, block_rows)
    loads = [
        pltpu.make_async_copy(
            own_moments[index], own_next.at[:, begin : begin + size], sem.at[2 * index]
        )
        for index, (begin, size) in enumerate(layout)
    ]
    for load in loads:
        load.start()

    for block in range(blocks):
        outer = slice(block * part, (block + 1) * part)
        lanes = pl.ds(pl.multiple_of(2 * core * part, part), part)
        matrices[0][:, outer] = next_ref[block, :, :, lanes].reshape(count * block_rows, part)
        for index in range(3):
            columns = slice(8 * part * index + block * part, 8 * part * index + (block + 1) * part)
            inner = slice(index * part, (index + 1) * part)
            own_grads[:, columns] = grads_ref[block, :, inner].astype(jnp.float32)
    for block in range(blocks // 2):
        outer = slice(block * part, (block + 1) * part)
        matrices[1][:, outer] = next_ref[
            core * (blocks // 2) + block, :, :, part : 2 * part
        ].reshape(count * block_rows, part)
    leaving = []
    for index, (begin, size) in enumerate(layout):
        loads[index].wait()
        lanes = slice(begin, begin + size)
        own_next[:, lanes] = momentum_keep * own_next[:, lanes] + own_grads[:, lanes]
        leaving += [
            pltpu.make_async_copy(own_grads.at[:, lanes], outs[2 * index], sem.at[2 * index]),
            pltpu.make_async_copy(own_next.at[:, lanes], outs[2 * index + 1], sem.at[2 * index + 1]),
        ]
        leaving[-2].start()
        leaving[-1].start()
    states = []
    for matrix in matrices:
        low = matrix[...]
        states.append(
            scaled_gram(
                lax.dot_general(
                    low, low, (((0,), (0,)), ((), ())), preferred_element_type=jnp.float32
                )
            )
        )
    parts = newton_parts([state[0] for state in states])
    for matrix, update, (_, inverse), (_, first_low, _, second_low) in zip(
        matrices, updates, states, parts
    ):
        rows, columns = matrix.shape
        scale = rate_matrix * math.sqrt(max(1.0, columns / rows))
        own = matrix[pl.ds(start, block_rows)]
        once = a * own.astype(jnp.float32) + jnp.dot(
            own, first_low, preferred_element_type=jnp.float32
        )
        update[...] = (-scale * inverse) * (
            a * once
            + jnp.dot(once.astype(jnp.bfloat16), second_low, preferred_element_type=jnp.float32)
        )
    for copy in leaving:
        copy.wait()


def dense_update(nexts, grads, own_moments, layout, shard_index, rep_index):
    _, count, block_rows, _ = nexts.shape
    width = own_moments[0].shape[1]
    whole = lambda shape: pl.BlockSpec(shape, lambda i: (0,) * len(shape))
    anywhere = pl.BlockSpec(memory_space=pl.ANY)
    shapes = []
    for _, size in layout:
        shapes += [jax.ShapeDtypeStruct((block_rows, size), jnp.float32)] * 2
    shapes += [
        jax.ShapeDtypeStruct((block_rows, width), jnp.float32),
        jax.ShapeDtypeStruct((block_rows, width // 2), jnp.float32),
    ]
    place = jnp.stack([shard_index, rep_index % 2]).astype(jnp.int32)
    return pl.pallas_call(
        functools.partial(dense_update_kernel, layout),
        grid=(1,),
        in_specs=[pl.BlockSpec(memory_space=pltpu.SMEM), whole(nexts.shape), whole(grads.shape)]
        + [anywhere] * len(own_moments),
        out_specs=[anywhere] * (2 * len(layout)) + [whole(shape.shape) for shape in shapes[-2:]],
        out_shape=shapes,
        scratch_shapes=[
            pltpu.VMEM((count * block_rows, width), jnp.bfloat16),
            pltpu.VMEM((count * block_rows, width // 2), jnp.bfloat16),
            pltpu.VMEM((block_rows, 3 * width), jnp.float32),
            pltpu.VMEM((block_rows, 3 * width), jnp.float32),
            pltpu.SemaphoreType.DMA((2 * len(layout),)),
        ],
        compiler_params=pltpu.CompilerParams(vmem_limit_bytes=63 * 1024 * 1024),
        name="dense_update",
        cost_estimate=pl.CostEstimate(
            flops=14000000000, bytes_accessed=24 * width * width, transcendentals=0
        ),
    )(place, nexts, grads, *own_moments)


LAYOUT = ((0, 1024), (1024, 512), (1536, 512), (2048, 1024))


MESH = pl.DeviceIdType.MESH


def flip(index, bit):
    return index + bit - 2 * bit * ((index // bit) % 2)


def greet(peers):
    barrier = pltpu.get_barrier_semaphore()
    for peer in peers:
        pl.semaphore_signal(barrier, inc=1, device_id=peer, device_id_type=MESH)
    pl.semaphore_wait(barrier, len(peers))


def stream_plan(rep, bits, base, size):
    stages = []
    starts = [base, base + size]
    for step in range(len(bits)):
        size = size // 2
        stage = []
        for stream in range(2):
            bit = bits[(step + stream) % len(bits)]
            side = (rep // bit) % 2
            keep = starts[stream] + side * size
            send = starts[stream] + (1 - side) * size
            starts[stream] = keep
            stage.append((bit, stream, keep, send, size))
        stages.append(stage)
    return stages


def rows_of(start, size):
    return pl.ds(pl.multiple_of(start, 16), size)


def moe_kernel(
    count,
    bits,
    own_ref,
    cot_ref,
    weight_ref,
    gate_hbm,
    up_hbm,
    down_hbm,
    stage_out,
    back_ref,
    share_ref,
    tok,
    turned,
    mats,
    hid,
    gate_delta,
    up_delta,
    stage_back,
    got_back,
    sum_back,
    sum_out,
    *rest,
):
    landing = rest[: 1 + 2 * len(bits)]
    (
        load_sem,
        right_sem,
        left_sem,
        arrive_sem,
        back_send,
        back_recv,
        sum_send,
        sum_recv,
        core_send,
        core_recv,
    ) = rest[1 + 2 * len(bits) :]
    rep = lax.axis_index("rep")
    me = lax.axis_index("shard")
    experts = mats.shape[0]
    tokens = own_ref.shape[0]
    half = mats.shape[2] // 2
    core = rep % 2

    loads = [
        pltpu.make_async_copy(gate_hbm, mats.at[:, 0], load_sem.at[0]),
        pltpu.make_async_copy(up_hbm, mats.at[:, 1], load_sem.at[1]),
        pltpu.make_async_copy(
            down_hbm.at[:, :, pl.ds(0, half)], mats.at[:, 2, pl.ds(0, half)], load_sem.at[2]
        ),
        pltpu.make_async_copy(
            down_hbm.at[:, :, pl.ds(half, half)], mats.at[:, 2, pl.ds(half, half)], load_sem.at[3]
        ),
    ]
    for load in loads:
        load.start()
    peers = [(rep, lax.rem(me + k, count)) for k in range(1, count)]
    peers += [(flip(rep, bit), me) for bit in (1,) + bits]
    greet(peers)

    right_peer = (rep, jnp.minimum(me + 1, count - 1))
    left_peer = (rep, jnp.maximum(me - 1, 0))

    def hand_on(block, to_right):
        return pltpu.make_async_remote_copy(
            src_ref=tok.at[block],
            dst_ref=tok.at[block],
            send_sem=(right_sem if to_right else left_sem).at[block],
            recv_sem=arrive_sem.at[block],
            device_id=right_peer if to_right else left_peer,
            device_id_type=MESH,
        )

    def returning(stage, got, send_sem, recv_sem, block):
        return pltpu.make_async_remote_copy(
            src_ref=stage.at[block],
            dst_ref=got.at[me],
            send_sem=send_sem.at[block],
            recv_sem=recv_sem.at[me],
            device_id=(rep, block),
            device_id_type=MESH,
        )

    tok[me] = own_ref[...]

    @pl.when(me < count - 1)
    def _():
        hand_on(me, True).start()

    @pl.when(me > 0)
    def _():
        hand_on(me, False).start()

    for load in loads:
        load.wait()

    margin = jnp.minimum(me, count - 1 - me)
    longer = jnp.where(me < count - 1 - me, 1, -1)
    inward = jnp.where(2 * me < count, 1, -1)
    nt = (((1,), (1,)), ((), ()))

    def dot(left, right):
        return jnp.dot(left, right, preferred_element_type=jnp.float32)

    def dot_nt(left, right):
        return lax.dot_general(left, right, nt, preferred_element_type=jnp.float32)

    def arrivals(j):
        lower = me - j
        upper = me + j

        @pl.when((j > 0) & (lower >= 0))
        def _():
            hand_on(jnp.maximum(lower, 0), True).wait_recv()

            @pl.when(me < count - 1)
            def _():
                hand_on(jnp.maximum(lower, 0), True).start()

        @pl.when((j > 0) & (upper < count))
        def _():
            hand_on(jnp.minimum(upper, count - 1), False).wait_recv()

            @pl.when(me > 0)
            def _():
                hand_on(jnp.minimum(upper, count - 1), False).start()

    def block_at(j):
        near = (j + 1) // 2
        alternating = me + near - 2 * near * (j % 2)
        return jnp.where(j <= 2 * margin, alternating, me + longer * (j - margin))

    def places_of(block):
        return pl.ds(pl.multiple_of(block * tokens, tokens), tokens)

    def factors(e, block):
        places = places_of(block)
        rows = tok[block]
        grads = cot_ref[block]
        weight = weight_ref[block, :, e : e + 1]
        u = dot(rows, mats[e, 0])
        w = dot(rows, mats[e, 1])
        gate = 1.0 / (1.0 + jnp.exp(-u))
        act = u * gate
        hidden = (weight * (act * w)).astype(jnp.bfloat16)
        hid[e, :, places] = hidden.T
        pulled = weight * (
            dot_nt(grads[:, :half], mats[e, 2, :half])
            + dot_nt(grads[:, half:], mats[e, 2, half:])
        )
        gate_delta[e, places] = (pulled * w * (gate + act * (1.0 - gate))).astype(jnp.bfloat16)
        up_delta[e, places] = (pulled * act).astype(jnp.bfloat16)
        return hidden

    def sums(block, e, hidden, place):
        places = places_of(block)
        for side in range(2):
            part = slice(side * half, (side + 1) * half)
            back = dot_nt(gate_delta[e, places], mats[e, 0, part]) + dot_nt(
                up_delta[e, places], mats[e, 1, part]
            )
            out = dot(hidden, mats[e, 2, part])
            if e > 0:
                back = place[0][:, part] + back
                out = place[1][:, part] + out
            place[0][:, part] = back
            place[1][:, part] = out

    def visit(j, carry):
        arrivals(j)
        block = block_at(j)
        places = places_of(block)
        turned[:, places] = tok[block].T
        hiddens = [factors(e, block) for e in range(experts)]
        for side in range(2):
            part = slice(side * half, (side + 1) * half)
            total_back = None
            total_out = None
            for e in range(experts):
                back = dot_nt(gate_delta[e, places], mats[e, 0, part]) + dot_nt(
                    up_delta[e, places], mats[e, 1, part]
                )
                out = dot(hiddens[e], mats[e, 2, part])
                total_back = back if e == 0 else total_back + back
                total_out = out if e == 0 else total_out + out
            stage_back[block, :, part] = total_back.astype(jnp.bfloat16)
            stage_out[block, :, part] = total_out.astype(jnp.bfloat16)

        @pl.when((j > 0) & ((block - me) * inward > 0))
        def _():
            returning(stage_back, got_back, back_send, back_recv, block).start()

        return carry

    lax.fori_loop(0, count - 1, visit, 0)
    arrivals(count - 1)
    last = block_at(count - 1)
    for k in range(1, count):
        block = block_at(k - 1)

        @pl.when((block - me) * inward < 0)
        def _():
            returning(stage_back, got_back, back_send, back_recv, block).start()

    turned[:, places_of(last)] = tok[last].T
    plan = stream_plan(rep, bits, core * half, half // 2)

    def sum_copy(stage, slot, e, start, size, bit):
        return pltpu.make_async_remote_copy(
            src_ref=mats.at[e, :, rows_of(start, size)],
            dst_ref=landing[slot].at[e],
            send_sem=sum_send.at[slot, e],
            recv_sem=sum_recv.at[slot, e],
            device_id=(flip(rep, bit), me),
            device_id_type=MESH,
        )

    def core_copy(e, kind):
        return pltpu.make_async_remote_copy(
            src_ref=mats.at[e, kind, rows_of((1 - core) * half, half)],
            dst_ref=landing[0].at[e, kind],
            send_sem=core_send.at[e, kind],
            recv_sem=core_recv.at[e, kind],
            device_id=(flip(rep, 1), me),
            device_id_type=MESH,
        )

    def copies(stage, e):
        return [
            (
                sum_copy(stage, 1 + 2 * (stage - 1) + stream, e, send, size, bit),
                1 + 2 * (stage - 1) + stream,
                keep,
                size,
            )
            for bit, stream, keep, send, size in plan[stage - 1]
        ]

    def finish(stage, e):
        if stage == 0:
            place = rows_of(core * half, half)
            for kind in range(3):
                core_copy(e, kind).wait_recv()
                mats[e, kind, place] = (
                    mats[e, kind, place].astype(jnp.float32)
                    + landing[0][e, kind].astype(jnp.float32)
                ).astype(jnp.bfloat16)
            return
        for copy, slot, keep, size in copies(stage, e):
            copy.wait_recv()
            place = rows_of(keep, size)
            for kind in range(3):
                mats[e, kind, place] = (
                    mats[e, kind, place].astype(jnp.float32)
                    + landing[slot][e, kind].astype(jnp.float32)
                ).astype(jnp.bfloat16)

    stages = 1 + len(bits)
    for turn in range(experts + stages):
        if turn < experts:
            e = turn
            sums(last, e, factors(e, last), (sum_back, sum_out))
            for kind in range(3):
                for side in range(2):
                    part = slice(side * half, (side + 1) * half)
                    if kind == 2:
                        values = dot(hid[e], cot_ref[:, :, part].reshape(count * tokens, half))
                    else:
                        values = dot(turned[part], (gate_delta, up_delta)[kind][e])
                    mats[e, kind, part] = values.astype(jnp.bfloat16)
                core_copy(e, kind).start()
            if e == experts - 1:
                stage_back[last] = sum_back[...].astype(jnp.bfloat16)
                stage_out[last] = sum_out[...].astype(jnp.bfloat16)
                returning(stage_back, got_back, back_send, back_recv, last).start()
        for stage in range(stages):
            e = turn - 1 - stage
            if 0 <= e < experts:
                finish(stage, e)
                if stage + 1 < stages:
                    for copy, _, _, _ in copies(stage + 1, e):
                        copy.start()
                else:
                    for _, stream, keep, _, size in plan[-1]:
                        share_ref[e, :, stream] = mats[e, :, rows_of(keep, size)]

    total = stage_back[me].astype(jnp.float32)
    for k in range(1, count):
        source = lax.rem(me + k, count)
        pltpu.make_async_remote_copy(
            src_ref=stage_back.at[source],
            dst_ref=got_back.at[source],
            send_sem=back_send.at[source],
            recv_sem=back_recv.at[source],
            device_id=(rep, source),
            device_id_type=MESH,
        ).wait_recv()
        total = total + got_back[source].astype(jnp.float32)
    back_ref[...] = total
    for k in range(1, count):
        block = lax.rem(me + k, count)
        returning(stage_back, got_back, back_send, back_recv, block).wait_send()
    for e in range(experts):
        for kind in range(3):
            core_copy(e, kind).wait_send()
        for stage in range(1, stages):
            for copy, _, _, _ in copies(stage, e):
                copy.wait_send()
    for block in range(count):

        @pl.when((block <= me) & (me < count - 1))
        def _():
            hand_on(block, True).wait_send()

        @pl.when((block >= me) & (me > 0))
        def _():
            hand_on(block, False).wait_send()


def moe(normed, cotangents, weights, gate_proj, up_proj, down_proj, bits, count):
    tokens, width = normed.shape
    experts, _, hidden = gate_proj.shape
    half = width // 2
    low = jnp.bfloat16
    final = (half // 2) >> len(bits)
    vmem = pl.BlockSpec(memory_space=pltpu.VMEM)
    anywhere = pl.BlockSpec(memory_space=pl.ANY)
    landings = [pltpu.VMEM((experts, 3, half, hidden), low)]
    for step in range(len(bits)):
        size = (half // 2) >> (step + 1)
        landings += [pltpu.VMEM((experts, 3, size, hidden), low)] * 2
    slots = len(landings)
    dma = pltpu.SemaphoreType.DMA
    return pl.pallas_call(
        functools.partial(moe_kernel, count, bits),
        in_specs=[vmem, vmem, vmem, anywhere, anywhere, anywhere],
        out_specs=[vmem, vmem, vmem],
        out_shape=[
            jax.ShapeDtypeStruct((count, tokens, width), low),
            jax.ShapeDtypeStruct((tokens, width), jnp.float32),
            jax.ShapeDtypeStruct((experts, 3, 2, final, hidden), low),
        ],
        scratch_shapes=[
            pltpu.VMEM((count, tokens, width), low),
            pltpu.VMEM((width, count * tokens), low),
            pltpu.VMEM((experts, 3, width, hidden), low),
            pltpu.VMEM((experts, hidden, count * tokens), low),
            pltpu.VMEM((experts, count * tokens, hidden), low),
            pltpu.VMEM((experts, count * tokens, hidden), low),
            pltpu.VMEM((count, tokens, width), low),
            pltpu.VMEM((count, tokens, width), low),
            pltpu.VMEM((tokens, width), jnp.float32),
            pltpu.VMEM((tokens, width), jnp.float32),
        ]
        + landings
        + [
            dma((4,)),
            dma((count,)),
            dma((count,)),
            dma((count,)),
            dma((count,)),
            dma((count,)),
            dma((slots, experts)),
            dma((slots, experts)),
            dma((experts, 3)),
            dma((experts, 3)),
        ],
        compiler_params=pltpu.CompilerParams(
            collective_id=1, has_side_effects=True, vmem_limit_bytes=63 * 1024 * 1024
        ),
        name="moe",
        cost_estimate=pl.CostEstimate(
            flops=39000000000, bytes_accessed=20000000, transcendentals=2000000
        ),
    )(normed, cotangents, weights, gate_proj, up_proj, down_proj)


def rep_bits(rep_count):
    bits = []
    bit = 2
    while bit < rep_count:
        bits.append(bit)
        bit = bit * 2
    return tuple(bits)


def spread_kernel(
    count,
    bits,
    share_ref,
    returned_ref,
    normed_ref,
    head_ref,
    weights_ref,
    small_ref,
    tokens_ref,
    cot_ref,
    second_ref,
    middle_ref,
    query_ref,
    pair_ref,
    total_ref,
    table_ref,
    row_ref,
    query_moment,
    key_moment,
    value_moment,
    out_moment,
    experts_hbm,
    dense_out,
    grads_out,
    gains_out,
    tokens_out,
    mixed_out,
    experts_out,
    got_ref,
    moment_piece,
    delta_ref,
    branch_ref,
    heads_ref,
    dense_ref,
    total,
    land_core,
    land_first,
    *rest,
):
    later = len(bits) - 1
    land_later = rest[:later]
    (
        piece_send,
        piece_land,
        piece,
        gains_send,
        gains_land,
        gains_all,
        local_sem,
        core_send,
        core_recv,
        half_send,
        half_recv,
        shard_send,
        shard_recv,
        grow_send,
        grow_recv,
        line_send,
        line_recv,
        join_send,
        join_recv,
        expert_send,
        expert_recv,
        gain_send,
        gain_recv,
        gain_line_send,
        gain_line_recv,
        back_send,
        back_recv,
        moment_sem,
        own_send,
        own_recv,
        own_join_send,
        own_join_recv,
    ) = rest[later:]
    rep = lax.axis_index("rep")
    me = lax.axis_index("shard")
    core = rep % 2
    rows = dense_ref.shape[2]
    expert_rows = experts_out.shape[2]
    steps = len(bits)
    streams = range(2)

    def remote(source, target, send_sem, recv_sem, peer):
        return pltpu.make_async_remote_copy(
            src_ref=source,
            dst_ref=target,
            send_sem=send_sem,
            recv_sem=recv_sem,
            device_id=peer,
            device_id_type=MESH,
        )

    def across(bit):
        return (flip(rep, bit), me)

    def order(stream):
        return [bits[(step + stream) % steps] for step in range(steps)]

    def side(bit):
        return (rep // bit) % 2

    plan = stream_plan(rep, bits, core * (expert_rows // 2), expert_rows // 4)
    base = [(core * (expert_rows // 2)) + stream * (expert_rows // 4) for stream in streams]

    def expert_copy(level, stream):
        if level == steps:
            place = rows_of(base[stream], expert_rows // 4)
            peer = across(1)
        else:
            bit, _, keep, _, size = plan[steps - 1 - level][stream]
            place = rows_of(keep, size)
            peer = across(bit)
        source = experts_out.at[:, :, place]
        if level == 0:
            source = share_ref.at[:, :, stream]
        return remote(
            source,
            experts_out.at[:, :, place],
            expert_send.at[level, stream],
            expert_recv.at[level, stream],
            peer,
        )

    def own_copy(stream):
        _, _, keep, _, size = plan[-1][stream]
        return pltpu.make_async_copy(
            share_ref.at[:, :, stream],
            experts_out.at[:, :, rows_of(keep, size)],
            local_sem.at[stream],
        )

    for stream in streams:
        own_copy(stream).start()
    peers = [(rep, lax.rem(me + k, count)) for k in range(1, count)]
    peers += [across(bit) for bit in (1,) + bits]
    greet(peers)

    def returning(peer, source):
        return remote(
            returned_ref.at[peer],
            got_ref.at[source],
            back_send.at[peer],
            back_recv.at[source],
            (rep, peer),
        )

    def core_copy(block):
        return remote(
            dense_ref.at[4 * (1 - core) + block],
            land_core.at[block],
            core_send.at[block],
            core_recv.at[block],
            across(1),
        )

    gain_bits = (1,) + bits

    def gain_copy(stage):
        return remote(
            gains_send.at[stage],
            gains_land.at[stage],
            gain_send.at[stage],
            gain_recv.at[stage],
            across(gain_bits[stage]),
        )

    for stream in streams:
        expert_copy(0, stream).start()

    for k in range(1, count):
        returning(lax.rem(me + k, count), me).start()

    def whole(index):
        return weights_ref[index].reshape(count * rows, -1)

    def gain(index):
        at = EXPERTS + index
        return jnp.concatenate([small_ref[z, at : at + 1, :rows] for z in range(count)], axis=1)

    scaled, inverse = normalize(middle_ref[...])
    middle_extra, midnorm_part = normalize_back(second_ref[...], gain(1), scaled, inverse)
    grad_middle = cot_ref[...].astype(jnp.float32) + middle_extra
    tokens_out[...] = grad_middle
    branch_ref[...] = grad_middle.astype(jnp.bfloat16)
    heads_ref[...] = dot_nt(branch_ref[...], whole(2)).astype(jnp.bfloat16)
    bias = allowed_pairs(row_ref[...])
    attend_backward(query_ref, pair_ref, bias, total_ref, heads_ref, table_ref, delta_ref)

    part = dense_ref.shape[3] // 3
    normed_turned = normed_ref[...].T
    head_turned = head_ref[...].T

    def make_block(block):
        def columns(ref, offset):
            return ref[:, pl.ds(pl.multiple_of(offset + block * part, part), part)]

        pair = jnp.concatenate([columns(delta_ref, 0), columns(delta_ref, 8 * part)], axis=1)
        left = jnp.dot(normed_turned, pair, preferred_element_type=jnp.float32)
        right = jnp.dot(head_turned, columns(branch_ref, 0), preferred_element_type=jnp.float32)
        for line in range(count):
            place = slice(line * rows, (line + 1) * rows)
            dense_ref[block, line, :, : 2 * part] = left[place].astype(jnp.bfloat16)
            dense_ref[block, line, :, 2 * part :] = right[place].astype(jnp.bfloat16)

    for block in range(4):
        make_block(4 * (1 - core) + block)
        core_copy(block).start()
    for block in range(4):
        make_block(4 * core + block)

    def gain_step(stage):
        gain_copy(stage).wait_recv()
        gains_send[stage + 1] = gains_send[stage] + gains_land[stage]
        if stage + 1 < len(gain_bits):
            gain_copy(stage + 1).start()

    first = [side(order(stream)[0]) for stream in streams]
    held = [2 * stream + first[stream] for stream in streams]
    given = [2 * stream + 1 - first[stream] for stream in streams]

    def first_copy(stream):
        return remote(
            total.at[given[stream]],
            land_first.at[stream],
            half_send.at[0, stream],
            half_recv.at[0, stream],
            across(order(stream)[0]),
        )

    def add_core(block):
        for line in range(count):
            total[block, line] = (
                dense_ref[4 * core + block, line].astype(jnp.float32)
                + land_core[block, line].astype(jnp.float32)
            ).astype(jnp.bfloat16)

    for block in range(4):
        core_copy(block).wait_recv()
    for stream in streams:
        add_core(given[stream])
        first_copy(stream).start()
    for stream in streams:
        add_core(held[stream])
    grad_first = dot_nt(delta_ref[:, : NHEADS * HEAD], whole(0)) + dot_nt(
        delta_ref[:, NHEADS * HEAD :], whole(1)
    )
    scaled, inverse = normalize(tokens_ref[...].astype(jnp.float32))
    input_extra, prenorm_part = normalize_back(grad_first, gain(0), scaled, inverse)
    tokens_out[...] = tokens_out[...] + input_extra
    gains_send[0] = jnp.concatenate(
        [prenorm_part, midnorm_part, jnp.zeros((6, prenorm_part.shape[1]), jnp.float32)], axis=0
    )
    gain_copy(0).start()
    gain_step(0)

    starts = []
    for stream in streams:
        start, size, line = 0, rows, []
        for step in range(1, steps):
            size = size // 2
            near = side(order(stream)[step])
            line.append((start + near * size, start + (1 - near) * size, size))
            start = start + near * size
        starts.append((start, size, line))

    last = starts[0][1]
    places = [rows_of(starts[stream][0], last) for stream in streams]
    inner = [slice(index * part, (index + 1) * part) for index in range(3)]

    def moment_copy(stream, index):
        block = 4 * core + held[stream]
        lanes = pl.ds(pl.multiple_of((held[stream] if index == 1 else block) * part, part), part)
        source = (query_moment, key_moment, out_moment)[index]
        return pltpu.make_async_copy(
            source.at[places[stream], lanes],
            moment_piece.at[stream, :, inner[index]],
            moment_sem.at[stream, index],
        )

    def moment_other(stream):
        lanes = pl.ds(pl.multiple_of(held[stream] * part, part), part)
        return pltpu.make_async_copy(
            value_moment.at[places[stream], lanes],
            moment_piece.at[stream, :, inner[1]],
            moment_sem.at[stream, 1],
        )

    for stream in streams:
        moment_copy(stream, 0).start()
        moment_copy(stream, 2).start()

        @pl.when(core == 0)
        def _():
            moment_copy(stream, 1).start()

        @pl.when(core == 1)
        def _():
            moment_other(stream).start()

    def later_copy(step, stream):
        keep, send, size = starts[stream][2][step - 1]
        return remote(
            total.at[held[stream], :, rows_of(send, size)],
            land_later[step - 1].at[stream],
            half_send.at[step, stream],
            half_recv.at[step, stream],
            across(order(stream)[step]),
        )

    for stream in streams:
        first_copy(stream).wait_recv()
        for line in range(count):
            total[held[stream], line] = (
                total[held[stream], line].astype(jnp.float32)
                + land_first[stream, line].astype(jnp.float32)
            ).astype(jnp.bfloat16)
        if steps > 1:
            later_copy(1, stream).start()
    gain_step(1)

    for step in range(1, steps):
        for stream in streams:
            later_copy(step, stream).wait_recv()
            keep, _, size = starts[stream][2][step - 1]
            for line in range(count):
                place = rows_of(keep, size)
                total[held[stream], line, place] = (
                    total[held[stream], line, place].astype(jnp.float32)
                    + land_later[step - 1][stream, line].astype(jnp.float32)
                ).astype(jnp.bfloat16)
            if step + 1 < steps:
                later_copy(step + 1, stream).start()
        gain_step(step + 1)

    for stream in streams:
        own_copy(stream).wait()
        expert_copy(0, stream).wait_recv()
        if steps > 1:
            expert_copy(1, stream).start()

    for stream in streams:
        for line in range(count):
            piece_send[line, stream] = total[held[stream], line, places[stream]]

    def shard_copy(k):
        target = lax.rem(me + k, count)
        return remote(
            piece_send.at[target],
            piece_land.at[me],
            shard_send.at[target],
            shard_recv.at[me],
            (rep, target),
        )

    def shard_arrival(source):
        return remote(
            piece_send.at[source],
            piece_land.at[source],
            shard_send.at[source],
            shard_recv.at[source],
            (rep, source),
        )

    def gain_line(k):
        target = lax.rem(me + k, count)
        return remote(
            gains_send.at[len(gain_bits)],
            gains_all.at[me],
            gain_line_send.at[target],
            gain_line_recv.at[me],
            (rep, target),
        )

    def gain_arrival(source):
        return remote(
            gains_send.at[len(gain_bits)],
            gains_all.at[source],
            gain_line_send.at[source],
            gain_line_recv.at[source],
            (rep, source),
        )

    def own_grow(step, stream):
        block = 4 * core + held[stream]
        if step == 0:
            part_ref = grads_out.at[block]
        else:
            keep, _, size = starts[stream][2][step - 1]
            part_ref = grads_out.at[block, rows_of(keep, size)]
        return remote(
            part_ref,
            part_ref,
            own_send.at[step, stream],
            own_recv.at[step, stream],
            across(order(stream)[step]),
        )

    def own_join(stream):
        part_ref = grads_out.at[pl.ds(4 * core + 2 * stream, 2)]
        return remote(
            part_ref, part_ref, own_join_send.at[stream], own_join_recv.at[stream], across(1)
        )

    for k in range(1, count):
        shard_copy(k).start()
        gain_line(k).start()
    summed = piece_send[me].astype(jnp.float32)
    for k in range(1, count):
        source = lax.rem(me + k, count)
        shard_arrival(source).wait_recv()
        summed = summed + piece_land[source].astype(jnp.float32)
    for stream in streams:
        for index in range(3):
            moment_copy(stream, index).wait()
        grads_out[4 * core + held[stream], places[stream]] = summed[stream].astype(jnp.bfloat16)
        own_grow(steps - 1, stream).start()
    piece[...] = (momentum_keep * moment_piece[...] + summed).astype(jnp.bfloat16)

    def line_copy(k, stream):
        target = lax.rem(me + k, count)
        return remote(
            piece.at[stream],
            dense_out.at[4 * core + held[stream], me, places[stream]],
            line_send.at[stream, target],
            line_recv.at[stream, me],
            (rep, target),
        )

    def line_arrival(source, stream):
        return remote(
            piece.at[stream],
            dense_out.at[4 * core + held[stream], source, places[stream]],
            line_send.at[stream, source],
            line_recv.at[stream, source],
            (rep, source),
        )

    def own_piece(stream):
        return pltpu.make_async_copy(
            piece.at[stream],
            dense_out.at[4 * core + held[stream], me, places[stream]],
            local_sem.at[2 + stream],
        )

    for stream in streams:
        own_piece(stream).start()
        for k in range(1, count):
            line_copy(k, stream).start()
    gained = gains_send[len(gain_bits)]
    for k in range(1, count):
        source = lax.rem(me + k, count)
        gain_arrival(source).wait_recv()
        gained = gained + gains_all[source]
    gains_out[...] = gained

    for level in range(1, steps):
        for stream in streams:
            expert_copy(level, stream).wait_recv()
            expert_copy(level + 1, stream).start()
    if steps == 1:
        for stream in streams:
            expert_copy(1, stream).start()

    def grow_copy(step, stream):
        if step == 0:
            place = dense_out.at[4 * core + held[stream]]
        else:
            keep, _, size = starts[stream][2][step - 1]
            place = dense_out.at[4 * core + held[stream], :, rows_of(keep, size)]
        return remote(
            place,
            place,
            grow_send.at[step, stream],
            grow_recv.at[step, stream],
            across(order(stream)[step]),
        )

    for stream in streams:
        own_piece(stream).wait()
        for k in range(1, count):
            line_arrival(lax.rem(me + k, count), stream).wait_recv()
        grow_copy(steps - 1, stream).start()
    for step in reversed(range(steps)):
        for stream in streams:
            own_grow(step, stream).wait_recv()
            if step > 0:
                own_grow(step - 1, stream).start()
            else:
                own_join(stream).start()
    mixed = middle_ref[...] + returned_ref[me].astype(jnp.float32)
    for k in range(1, count):
        source = lax.rem(me + k, count)
        returning(source, source).wait_recv()
        mixed = mixed + got_ref[source].astype(jnp.float32)
    mixed_out[...] = mixed.astype(mixed_out.dtype)
    for stream in streams:
        expert_copy(steps, stream).wait()
    leave = pltpu.make_async_copy(experts_out, experts_hbm, local_sem.at[0])
    leave.start()
    for step in reversed(range(steps)):
        for stream in streams:
            grow_copy(step, stream).wait_recv()
            if step > 0:
                grow_copy(step - 1, stream).start()

    def join_copy(stream):
        place = dense_out.at[pl.ds(4 * core + 2 * stream, 2)]
        return remote(place, place, join_send.at[stream], join_recv.at[stream], across(1))

    for stream in streams:
        join_copy(stream).start()
    for stream in streams:
        join_copy(stream).wait()
        own_join(stream).wait()
        for step in range(steps):
            own_grow(step, stream).wait_send()
        for level in range(steps):
            expert_copy(level, stream).wait_send()
        first_copy(stream).wait_send()
        for step in range(1, steps):
            later_copy(step, stream).wait_send()
        for k in range(1, count):
            line_copy(k, stream).wait_send()
        for step in range(steps):
            grow_copy(step, stream).wait_send()
    for block in range(4):
        core_copy(block).wait_send()
    for stage in range(len(gain_bits)):
        gain_copy(stage).wait_send()
    for k in range(1, count):
        shard_copy(k).wait_send()
        gain_line(k).wait_send()
        returning(lax.rem(me + k, count), me).wait_send()
    leave.wait()


def spread(
    share, returned, normed, head_low, weights, small, tokens, cotangent, second, middle, *rest, bits, count
):
    query, pair, log_total, tables, starts, moments = rest
    experts, _, _, final, hidden = share.shape
    token_count, features = normed.shape
    rows = features // count
    width = 3 * features // 8
    dense_shape = (8, count, rows, width)
    gains_shape = (8, features)
    steps = len(bits)
    last = rows >> (steps - 1)
    low = jnp.bfloat16
    vmem = pl.BlockSpec(memory_space=pltpu.VMEM)
    dma = pltpu.SemaphoreType.DMA
    return pl.pallas_call(
        functools.partial(spread_kernel, count, bits),
        in_specs=[vmem] * 15 + [pl.BlockSpec(memory_space=pl.ANY)] * 4,
        out_specs=[pl.BlockSpec(memory_space=pl.ANY)] + [vmem] * 5,
        out_shape=[
            jax.ShapeDtypeStruct((experts, 3, 4 * (final << steps), hidden), low),
            jax.ShapeDtypeStruct(dense_shape, low),
            jax.ShapeDtypeStruct((8, rows, width), low),
            jax.ShapeDtypeStruct(gains_shape, jnp.float32),
            jax.ShapeDtypeStruct((token_count, features), jnp.float32),
            jax.ShapeDtypeStruct((token_count, features), low),
        ],
        scratch_shapes=[
            pltpu.VMEM((experts, 3, 4 * (final << steps), hidden), low),
            pltpu.VMEM((count, token_count, features), low),
            pltpu.VMEM((2, last, width), jnp.float32),
            pltpu.VMEM((token_count, 2 * features), low),
            pltpu.VMEM((token_count, features), low),
            pltpu.VMEM((token_count, features), low),
            pltpu.VMEM(dense_shape, low),
            pltpu.VMEM((4, count, rows, width), low),
            pltpu.VMEM((4, count, rows, width), low),
            pltpu.VMEM((2, count, rows, width), low),
        ]
        + [pltpu.VMEM((2, count, rows >> step, width), low) for step in range(1, steps)]
        + [
            pltpu.VMEM((count, 2, last, width), low),
            pltpu.VMEM((count, 2, last, width), low),
            pltpu.VMEM((2, last, width), low),
            pltpu.VMEM((steps + 2,) + gains_shape, jnp.float32),
            pltpu.VMEM((steps + 1,) + gains_shape, jnp.float32),
            pltpu.VMEM((count,) + gains_shape, jnp.float32),
            dma((4,)),
            dma((4,)),
            dma((4,)),
            dma((steps, 2)),
            dma((steps, 2)),
            dma((count,)),
            dma((count,)),
            dma((steps, 2)),
            dma((steps, 2)),
            dma((2, count)),
            dma((2, count)),
            dma((2,)),
            dma((2,)),
            dma((steps + 1, 2)),
            dma((steps + 1, 2)),
            dma((steps + 1,)),
            dma((steps + 1,)),
            dma((count,)),
            dma((count,)),
            dma((count,)),
            dma((count,)),
            dma((2, 3)),
            dma((steps, 2)),
            dma((steps, 2)),
            dma((2,)),
            dma((2,)),
        ],
        compiler_params=pltpu.CompilerParams(
            collective_id=2, has_side_effects=True, vmem_limit_bytes=63 * 1024 * 1024
        ),
        name="spread",
    )(
        share,
        returned,
        normed,
        head_low,
        weights,
        small,
        tokens,
        cotangent,
        second,
        middle,
        query,
        pair,
        log_total,
        tables,
        starts[None, :],
        *moments,
    )


def gather_kernel(
    count,
    bits,
    query_weight,
    key_weight,
    value_weight,
    out_weight,
    small_ref,
    tokens_ref,
    cot_ref,
    table_ref,
    row_ref,
    weights_hbm,
    small_out,
    cot_out,
    middle_out,
    first_out,
    second_out,
    query_out,
    pair_out,
    head_out,
    total_out,
    weights_out,
    weights_ref,
    local_sem,
    line_send,
    line_recv,
    grow_send,
    grow_recv,
    join_send,
    join_recv,
    small_send,
    small_recv,
    right_sem,
    left_sem,
    arrive_sem,
):
    rep = lax.axis_index("rep")
    me = lax.axis_index("shard")
    core = rep % 2
    steps = len(bits)
    streams = range(2)
    rows, width = weights_ref.shape[1:]
    half = width // 2
    fine = half // 4
    others = [lax.rem(me + k, count) for k in range(1, count)]

    def columns_of(start, size):
        return pl.ds(pl.multiple_of(start, 128), size)

    def order(stream):
        return [bits[(step + stream) % steps] for step in range(steps)]

    def side(bit):
        return (rep // bit) % 2

    narrow = width // 2
    weights_ref[0] = query_weight[...]
    weights_ref[1, :, :narrow] = key_weight[...]
    weights_ref[1, :, narrow:] = value_weight[...]
    weights_ref[2] = out_weight[...]
    own_copy = pltpu.make_async_copy(weights_ref, weights_out.at[:, me], local_sem.at[0])
    own_copy.start()
    small_out[me] = small_ref[...]
    cot_out[me] = cot_ref[...]
    peers = [(rep, other) for other in others]
    peers += [(flip(rep, bit), me) for bit in (1,) + bits]
    greet(peers)

    regions = []
    for stream in streams:
        column = core * half + stream * 2 * fine
        narrow = columns_of(column + side(order(stream)[0]) * fine, fine)
        start, size = 0, rows
        held = [(pl.ds(0, rows), narrow)]
        for step in range(1, steps):
            size = size // 2
            start = start + side(order(stream)[step]) * size
            held.append((rows_of(start, size), narrow))
        regions.append((held, columns_of(column, 2 * fine)))

    def remote(source, target, send_sem, recv_sem, peer):
        return pltpu.make_async_remote_copy(
            src_ref=source,
            dst_ref=target,
            send_sem=send_sem,
            recv_sem=recv_sem,
            device_id=peer,
            device_id_type=MESH,
        )

    def line_copy(stream, source, peer):
        place, columns = regions[stream][0][-1]
        return remote(
            weights_ref.at[:, place, columns],
            weights_out.at[:, source, place, columns],
            line_send.at[stream, peer],
            line_recv.at[stream, source],
            (rep, peer),
        )

    def grow_copy(step, stream, source):
        place, columns = regions[stream][0][step]
        part = weights_out.at[:, source, place, columns]
        return remote(
            part,
            part,
            grow_send.at[step, stream, source],
            grow_recv.at[step, stream, source],
            (flip(rep, order(stream)[step]), me),
        )

    def join_copy(stream, source):
        part = weights_out.at[:, source, :, regions[stream][1]]
        return remote(
            part,
            part,
            join_send.at[stream, source],
            join_recv.at[stream, source],
            (flip(rep, 1), me),
        )

    def small_copy(source, peer):
        return remote(
            small_ref,
            small_out.at[source],
            small_send.at[peer],
            small_recv.at[source],
            (rep, peer),
        )

    def hand_on(block, to_right):
        peer = jnp.minimum(me + 1, count - 1) if to_right else jnp.maximum(me - 1, 0)
        return remote(
            cot_out.at[block],
            cot_out.at[block],
            (right_sem if to_right else left_sem).at[block],
            arrive_sem.at[block],
            (rep, peer),
        )

    def line_start():
        @pl.when(me < count - 1)
        def _():
            hand_on(me, True).start()

        @pl.when(me > 0)
        def _():
            hand_on(me, False).start()

    def line_step(step):
        lower = me - step
        upper = me + step

        @pl.when(lower >= 0)
        def _():
            hand_on(jnp.maximum(lower, 0), True).wait_recv()

            @pl.when(me < count - 1)
            def _():
                hand_on(jnp.maximum(lower, 0), True).start()

        @pl.when(upper < count)
        def _():
            hand_on(jnp.minimum(upper, count - 1), False).wait_recv()

            @pl.when(me > 0)
            def _():
                hand_on(jnp.minimum(upper, count - 1), False).start()

    def line_send_all():
        for other in others:
            for stream in streams:
                line_copy(stream, me, other).start()

    def advance(level):
        for other in others:
            for stream in streams:
                if level == 0:
                    line_copy(stream, other, other).wait_recv()
                else:
                    grow_copy(steps - level, stream, other).wait_recv()
                if level < steps:
                    grow_copy(steps - 1 - level, stream, other).start()
                else:
                    join_copy(stream, other).start()

    for other in others:
        small_copy(me, other).start()
    line_send_all()
    for other in others:
        small_copy(other, other).wait_recv()

    def gain(index):
        at = EXPERTS + index
        return jnp.concatenate([small_out[z, at : at + 1, :rows] for z in range(count)], axis=1)

    inputs = tokens_ref[...].astype(jnp.float32)
    first_out[...] = (normalize(inputs)[0] * gain(0)).astype(jnp.bfloat16)
    advance(0)
    line_start()
    for level in range(1, steps + 1):
        advance(level)
        if level == 1:
            line_step(1)
    for other in others:
        for stream in streams:
            join_copy(stream, other).wait_recv()
    own_copy.wait()
    leave = pltpu.make_async_copy(weights_out, weights_hbm, local_sem.at[2])
    leave.start()

    def whole(index):
        return weights_out[index].reshape(count * rows, width)

    project_inputs(first_out[...], whole, query_out, pair_out, table_ref)
    bias = allowed_pairs(row_ref[...])
    if count > 2:
        line_step(2)
    attend_forward(range(KVHEADS // 2), query_out, pair_out, bias, head_out, total_out)
    for step in range(3, count - 1):
        line_step(step)
    attend_forward(range(KVHEADS // 2, KVHEADS), query_out, pair_out, bias, head_out, total_out)
    middle = inputs + dot_nn(head_out[...], whole(2))
    middle_out[...] = middle
    second_out[...] = (normalize(middle)[0] * gain(1)).astype(jnp.bfloat16)
    if count > 3:
        line_step(count - 1)
    for other in others:
        for stream in streams:
            join_copy(stream, other).wait_send()
            line_copy(stream, me, other).wait_send()
            for step in range(steps):
                grow_copy(step, stream, other).wait_send()
    for other in others:
        small_copy(me, other).wait_send()
    for block in range(count):

        @pl.when((block <= me) & (me < count - 1))
        def _():
            hand_on(block, True).wait_send()

        @pl.when((block >= me) & (me > 0))
        def _():
            hand_on(block, False).wait_send()

    leave.wait()


def gather(weights, small, tokens, cotangent, tables, starts, bits, count):
    rows, width = weights[0].shape
    depth = 3
    token_count = tokens.shape[0]
    steps = len(bits)
    low = jnp.bfloat16
    vmem = pl.BlockSpec(memory_space=pltpu.VMEM)
    dma = pltpu.SemaphoreType.DMA
    whole = jax.ShapeDtypeStruct((depth, count, rows, width), low)
    features = jax.ShapeDtypeStruct((token_count, width), low)
    return pl.pallas_call(
        functools.partial(gather_kernel, count, bits),
        in_specs=[vmem] * 9,
        out_specs=[pl.BlockSpec(memory_space=pl.ANY)] + [vmem] * 9,
        out_shape=[
            whole,
            jax.ShapeDtypeStruct((count,) + small.shape, small.dtype),
            jax.ShapeDtypeStruct((count, token_count, width), low),
            jax.ShapeDtypeStruct((token_count, width), jnp.float32),
            features,
            features,
            features,
            features,
            features,
            jax.ShapeDtypeStruct((2 * token_count, KVHEADS), jnp.float32),
        ],
        scratch_shapes=[
            pltpu.VMEM(whole.shape, low),
            pltpu.VMEM((depth, rows, width), low),
            dma((3,)),
            dma((2, count)),
            dma((2, count)),
            dma((steps, 2, count)),
            dma((steps, 2, count)),
            dma((2, count)),
            dma((2, count)),
            dma((count,)),
            dma((count,)),
            dma((count,)),
            dma((count,)),
            dma((count,)),
        ],
        compiler_params=pltpu.CompilerParams(
            collective_id=3, has_side_effects=True, vmem_limit_bytes=56 * 1024 * 1024
        ),
        name="gather",
    )(
        *weights,
        small,
        tokens,
        cotangent,
        tables,
        starts[None, :],
    )


def local(
    tokens,
    sequence_start,
    routes,
    route_weights,
    cotangent,
    query_proj,
    key_proj,
    value_proj,
    out_proj,
    prenorm,
    midnorm,
    gate_proj,
    up_proj,
    down_proj,
    query_moment,
    key_moment,
    value_moment,
    out_moment,
    prenorm_moment,
    midnorm_moment,
    gate_moment,
    up_moment,
    down_moment,
):
    shard_index = lax.axis_index("shard")
    rep_count = lax.axis_size("rep")
    shard_count = lax.axis_size("shard")
    row_block = query_proj.shape[0]
    bits = rep_bits(rep_count)
    experts_here = gate_proj.shape[0]
    dense_weights = jnp.sum(
        jnp.where(
            routes.T[None, :, :] == jnp.arange(EXPERTS, dtype=jnp.int32)[:, None, None],
            route_weights.T[None, :, :],
            0.0,
        ),
        axis=1,
    )
    gain_rows = jnp.pad(
        jnp.stack([prenorm, midnorm]).astype(jnp.float32),
        ((0, 6), (0, tokens.shape[0] - row_block)),
    )
    tables = rotary_tables(jnp.arange(tokens.shape[0], dtype=jnp.int32) - sequence_start)
    (
        weights,
        small,
        cotangent_all,
        middle,
        normed_first,
        normed_second,
        query,
        pair,
        head_low,
        log_total,
    ) = gather(
        (query_proj, key_proj, value_proj, out_proj),
        jnp.concatenate([dense_weights, gain_rows], axis=0),
        tokens,
        cotangent,
        tables,
        sequence_start,
        bits,
        shard_count,
    )
    expert_weights = lax.dynamic_slice_in_dim(
        small, shard_index * experts_here, experts_here, 1
    ).transpose(0, 2, 1)
    returned, grad_second, expert_share = moe(
        normed_second,
        cotangent_all,
        expert_weights,
        gate_proj,
        up_proj,
        down_proj,
        bits,
        shard_count,
    )
    own_moments = (query_moment, key_moment, value_moment, out_moment)
    expert_grads, dense_next, dense_grads, gains_grad, grad_tokens, mixed = spread(
        expert_share,
        returned,
        normed_first,
        head_low,
        weights,
        small,
        tokens,
        cotangent,
        grad_second,
        middle,
        query,
        pair,
        log_total,
        tables,
        sequence_start,
        own_moments,
        bits=bits,
        count=shard_count,
    )
    gains_here = lax.dynamic_slice_in_dim(gains_grad, shard_index * row_block, row_block, 1)
    prenorm_grad = gains_here[0]
    midnorm_grad = gains_here[1]
    prenorm_next = momentum_keep * prenorm_moment + prenorm_grad
    midnorm_next = momentum_keep * midnorm_moment + midnorm_grad
    prenorm_update = -rate_gain * prenorm_next
    midnorm_update = -rate_gain * midnorm_next
    rep_index = lax.axis_index("rep")
    (
        query_grad,
        query_next,
        key_grad,
        key_next,
        value_grad,
        value_next,
        out_grad,
        out_next,
        own_wide,
        own_narrow,
    ) = dense_update(
        dense_next,
        dense_grads,
        own_moments,
        LAYOUT,
        shard_index,
        rep_index,
    )
    pairs = [(index, index + 1 - 2 * (index % 2)) for index in range(rep_count)]
    other_wide = lax.ppermute(own_wide, "rep", pairs)
    other_narrow = lax.ppermute(own_narrow, "rep", pairs)
    gate_grad, gate_next, gate_update, up_grad, up_next, up_update = expert_update(
        expert_grads, (0, 1), (gate_moment, up_moment)
    )
    (
        down_grad,
        down_next,
        down_update,
        query_update,
        out_update,
        key_update,
        value_update,
        grad_tokens,
        mixed,
    ) = expert_update(
        expert_grads,
        (2,),
        (down_moment,),
        (own_wide, other_wide, own_narrow, other_narrow, grad_tokens, mixed),
    )
    return (
        mixed,
        grad_tokens,
        query_grad,
        query_next,
        query_update,
        key_grad,
        key_next,
        key_update,
        value_grad,
        value_next,
        value_update,
        out_grad,
        out_next,
        out_update,
        prenorm_grad,
        prenorm_next,
        prenorm_update,
        midnorm_grad,
        midnorm_next,
        midnorm_update,
        gate_grad,
        gate_next,
        gate_update,
        up_grad,
        up_next,
        up_update,
        down_grad,
        down_next,
        down_update,
    )


def solution(mesh):
    return jax.shard_map(
        local,
        mesh=mesh,
        in_specs=(
            P(("rep", "shard"), None),
            P(("rep", "shard")),
            P(("rep", "shard"), None),
            P(("rep", "shard"), None),
            P(("rep", "shard"), None),
            P("shard", None),
            P("shard", None),
            P("shard", None),
            P("shard", None),
            P("shard"),
            P("shard"),
            P("shard", None, None),
            P("shard", None, None),
            P("shard", None, None),
            P("shard", None),
            P("shard", None),
            P("shard", None),
            P("shard", None),
            P("shard"),
            P("shard"),
            P("shard", None, None),
            P("shard", None, None),
            P("shard", None, None),
        ),
        out_specs=(
            P(("rep", "shard"), None),
            P(("rep", "shard"), None),
            P("shard", None),
            P("shard", None),
            P("shard", None),
            P("shard", None),
            P("shard", None),
            P("shard", None),
            P("shard", None),
            P("shard", None),
            P("shard", None),
            P("shard", None),
            P("shard", None),
            P("shard", None),
            P("shard"),
            P("shard"),
            P("shard"),
            P("shard"),
            P("shard"),
            P("shard"),
            P("shard", None, None),
            P("shard", None, None),
            P("shard", None, None),
            P("shard", None, None),
            P("shard", None, None),
            P("shard", None, None),
            P("shard", None, None),
            P("shard", None, None),
            P("shard", None, None),
        ),
        check_vma=False,
    )
```

```python
import functools
import math

import jax
import jax.numpy as jnp
from jax import lax
from jax.experimental import pallas as pl
from jax.experimental.pallas import tpu as pltpu
from jax.sharding import PartitionSpec as P

NHEADS = 16
KVHEADS = 8
HEAD = 64
EXPERTS = 16
NS_ITERS = 2


norm_epsilon = 1e-06
rotary_base = 10000.0
momentum_keep = 0.9
rate_matrix = 0.5
rate_gain = 0.0002
newton_first = 3.4445
newton_second = -4.775
newton_third = 2.0315
masked_score = -1e30


def normalize(values):
    inverse = lax.rsqrt(jnp.mean(values * values, axis=-1, keepdims=True) + norm_epsilon)
    return (values * inverse, inverse)


def normalize_back(grad_normed, scaling, scaled, inverse):
    grad_scaled = grad_normed * scaling
    inner_mean = jnp.mean(grad_scaled * scaled, axis=-1, keepdims=True)
    return (
        inverse * (grad_scaled - scaled * inner_mean),
        jnp.sum(grad_normed * scaled, axis=0, keepdims=True),
    )


def dot_nn(left, right):
    return jnp.dot(left, right, preferred_element_type=jnp.float32)


def dot_nt(left, right):
    return lax.dot_general(
        left, right, (((1,), (1,)), ((), ())), preferred_element_type=jnp.float32
    )


def dot_tn(left, right):
    return lax.dot_general(
        left, right, (((0,), (0,)), ((), ())), preferred_element_type=jnp.float32
    )


def rotate(values, table_ref, sign):
    return (
        values * table_ref[0]
        + sign * pltpu.roll(values, 96, 1) * table_ref[1]
        + sign * pltpu.roll(values, 32, 1) * table_ref[2]
    )


def lane_low(shape):
    return lax.broadcasted_iota(jnp.int32, shape, 1) < HEAD


def twice(pair, upper):
    wide = pair.astype(jnp.float32)
    turned = pltpu.roll(wide, HEAD, 1)
    first = lane_low(pair.shape)
    return jnp.where(first != upper, wide, turned).astype(pair.dtype)


def stacked(pair):
    first = lane_low(pair.shape)
    zero = jnp.zeros_like(pair)
    return jnp.concatenate([jnp.where(first, pair, zero), jnp.where(first, zero, pair)], axis=0)


def unstacked(rows):
    half = rows.shape[0] // 2
    return jnp.where(lane_low((half, rows.shape[1])), rows[:half], rows[half:])


def allowed_pairs(start_row):
    shape = (start_row.shape[1], start_row.shape[1])
    keys = jnp.broadcast_to(start_row.astype(jnp.float32), shape)
    query_places = lax.broadcasted_iota(jnp.int32, shape, 0)
    key_places = lax.broadcasted_iota(jnp.int32, shape, 1)
    one = (keys.T == keys) & (key_places <= query_places)
    return jnp.where(jnp.concatenate([one, one], axis=0), 0.0, masked_score)


def block_lanes(ref, block):
    return ref[:, block * 2 * HEAD : (block + 1) * 2 * HEAD]


def attend_pair(block, query_ref, pair_ref, bias):
    key = twice(block_lanes(pair_ref, block // 2), block % 2 == 1)
    value = twice(block_lanes(pair_ref, KVHEADS // 2 + block // 2), block % 2 == 1)
    queries = stacked(block_lanes(query_ref, block))
    scores = dot_nt(queries, key) * (1.0 / math.sqrt(HEAD)) + bias
    return (queries, key, value, scores)


def project_inputs(normed, weights, query_ref, pair_ref, table_ref):
    queries = dot_nn(normed, weights(0))
    for block in range(NHEADS // 2):
        lanes = slice(block * 2 * HEAD, (block + 1) * 2 * HEAD)
        query_ref[:, lanes] = rotate(queries[:, lanes], table_ref, 1.0).astype(jnp.bfloat16)
    pairs = dot_nn(normed, weights(1))
    for block in range(KVHEADS):
        lanes = slice(block * 2 * HEAD, (block + 1) * 2 * HEAD)
        value = pairs[:, lanes]
        if block < KVHEADS // 2:
            value = rotate(value, table_ref, 1.0)
        pair_ref[:, lanes] = value.astype(jnp.bfloat16)


def attend_forward(blocks, query_ref, pair_ref, bias, head_ref, total_ref):
    for block in blocks:
        _, _, value, scores = attend_pair(block, query_ref, pair_ref, bias)
        row_max = jnp.max(scores, axis=-1, keepdims=True)
        exponents = jnp.exp(scores - row_max)
        totals = jnp.sum(exponents, axis=-1, keepdims=True)
        softmax_low = (exponents * (1.0 / totals)).astype(jnp.bfloat16)
        head_ref[:, block * 2 * HEAD : (block + 1) * 2 * HEAD] = unstacked(
            dot_nn(softmax_low, value)
        ).astype(jnp.bfloat16)
        total_ref[:, block : block + 1] = row_max + jnp.log(totals)


def attend_backward(query_ref, pair_ref, bias, total_ref, grad_ref, table_ref, delta_ref):
    folded = []
    for block in range(KVHEADS):
        queries, key, value, scores = attend_pair(block, query_ref, pair_ref, bias)
        grads = stacked(block_lanes(grad_ref, block))
        softmax_full = jnp.exp(scores - total_ref[:, block : block + 1])
        grad_softmax = dot_nt(grads, value)
        inner = jnp.sum(softmax_full * grad_softmax, axis=-1, keepdims=True)
        grad_scores = (softmax_full * (grad_softmax - inner)).astype(jnp.bfloat16)
        scale = 1.0 / math.sqrt(HEAD)
        grad_query = unstacked(dot_nn(grad_scores, key)) * scale
        lanes = slice(block * 2 * HEAD, (block + 1) * 2 * HEAD)
        delta_ref[:, lanes] = rotate(grad_query, table_ref, -1.0).astype(jnp.bfloat16)
        grad_key = dot_tn(grad_scores, queries) * scale
        grad_value = dot_tn(softmax_full.astype(jnp.bfloat16), grads)
        folded.append(
            (
                grad_key + pltpu.roll(grad_key, HEAD, 1),
                grad_value + pltpu.roll(grad_value, HEAD, 1),
            )
        )
        if block % 2 == 1:
            first = lane_low(grad_key.shape)
            both = [jnp.where(first, low, high) for low, high in zip(*folded)]
            folded = []
            base = NHEADS * HEAD + (block // 2) * 2 * HEAD
            delta_ref[:, base : base + 2 * HEAD] = rotate(both[0], table_ref, -1.0).astype(
                jnp.bfloat16
            )
            base = base + KVHEADS * HEAD
            delta_ref[:, base : base + 2 * HEAD] = both[1].astype(jnp.bfloat16)


def rotary_tables(positions):
    half_size = HEAD // 2
    frequency = rotary_base ** (-(jnp.arange(half_size, dtype=jnp.float32) * 2.0) / HEAD)
    angles = positions.astype(jnp.float32)[:, None] * frequency[None, :]
    cosine, sine = (jnp.cos(angles), jnp.sin(angles))
    zero = jnp.zeros_like(sine)
    return jnp.stack(
        [
            jnp.concatenate([cosine] * 4, axis=1),
            jnp.concatenate([-sine, zero] * 2, axis=1),
            jnp.concatenate([zero, sine] * 2, axis=1),
        ]
    )


def newton_parts(grams):
    a, b, c = newton_first, newton_second, newton_third

    def times(left, right):
        return jnp.dot(left, right, preferred_element_type=jnp.float32)

    lows = [gram.astype(jnp.bfloat16) for gram in grams]
    firsts = [b * gram + c * times(low, low) for gram, low in zip(grams, lows)]
    first_lows = [first.astype(jnp.bfloat16) for first in firsts]
    mixes = [times(low, first) for low, first in zip(lows, first_lows)]
    nexts = [
        (a * a) * gram + (2.0 * a) * mix + times(mix.astype(jnp.bfloat16), first)
        for gram, mix, first in zip(grams, mixes, first_lows)
    ]
    next_lows = [gram.astype(jnp.bfloat16) for gram in nexts]
    seconds = [b * gram + c * times(low, low) for gram, low in zip(nexts, next_lows)]
    second_lows = [second.astype(jnp.bfloat16) for second in seconds]
    return list(zip(firsts, first_lows, seconds, second_lows))


def scaled_gram(gram):
    shape = gram.shape
    rows = lax.broadcasted_iota(jnp.int32, shape, 0)
    diagonal = rows == lax.broadcasted_iota(jnp.int32, shape, 1)
    inverse = 1.0 / (jnp.sqrt(jnp.sum(jnp.where(diagonal, gram, 0.0))) + 1e-07)
    return (gram * (inverse * inverse), inverse)


def expert_update_kernel(kinds, scale, carried, *refs):
    a = newton_first
    grads_ref = refs[0]
    moments = refs[1 : 1 + len(kinds)]
    given = refs[1 + len(kinds) : 1 + len(kinds) + carried]
    outs = refs[1 + len(kinds) + carried :]
    if carried:
        taken = outs[3 * len(kinds) : 3 * len(kinds) + carried]
        held = outs[3 * len(kinds) + carried : -2]
        load_sem, store_sem = outs[-2:]
        core = lax.axis_index("rep") % 2

        def load(index):
            return pltpu.make_async_copy(given[index], held[index], load_sem.at[index])

        def store(source, target):
            return pltpu.make_async_copy(held[source], taken[target], store_sem.at[target])

        @pl.when(pl.program_id(0) == 0)
        def _():
            for index in range(carried):
                load(index).start()

    half = grads_ref.shape[3]
    tall = kinds[0] < 2
    states = []
    for index in range(len(kinds)):
        for e in range(grads_ref.shape[0]):
            grad = grads_ref[e, index].astype(jnp.float32)
            if not tall:
                grad = jnp.concatenate([grad[:half], grad[half:]], axis=1)
            moment = momentum_keep * moments[index][e] + grad
            outs[3 * index][e] = grad
            outs[3 * index + 1][e] = moment
            low = moment.astype(jnp.bfloat16)
            sides = (((0,), (0,)), ((), ())) if tall else (((1,), (1,)), ((), ()))
            gram, inverse = scaled_gram(
                lax.dot_general(low, low, sides, preferred_element_type=jnp.float32)
            )
            states.append((index, e, inverse, low, gram))
    parts = newton_parts([state[-1] for state in states])
    for (index, e, inverse, low, _), (first, first_low, second, second_low) in zip(states, parts):
        rest = a * (first + second) + jnp.dot(
            first_low, second_low, preferred_element_type=jnp.float32
        )
        rest = ((-scale * inverse) * rest).astype(jnp.bfloat16)
        if tall:
            step = jnp.dot(low, rest, preferred_element_type=jnp.float32)
        else:
            step = jnp.dot(rest, low, preferred_element_type=jnp.float32)
        outs[3 * index + 2][e] = (-scale * a * a * inverse) * outs[3 * index + 1][e] + step
    if carried:

        @pl.when(pl.program_id(0) == 0)
        def _():
            for index in range(carried):
                load(index).wait()
            for pair in (0, 2):

                @pl.when(core == 0)
                def _():
                    store(pair, pair).start()
                    store(pair + 1, pair + 1).start()

                @pl.when(core == 1)
                def _():
                    store(pair + 1, pair).start()
                    store(pair, pair + 1).start()

            for index in range(4, carried):
                store(index, index).start()

        @pl.when(pl.program_id(0) == pl.num_programs(0) - 1)
        def _():
            for index in range(carried):
                store(index, index).wait()


def expert_update(grads, kinds, moments, carried=()):
    count, rows, columns = moments[0].shape
    group = 2 // len(kinds)
    scale = rate_matrix * math.sqrt(max(1.0, columns / rows))
    block = pl.BlockSpec((group, rows, columns), lambda i: (i, 0, 0))
    place = kinds[0] // len(kinds)
    taken = pl.BlockSpec((group, len(kinds)) + grads.shape[2:], lambda i: (i, place, 0, 0))
    shape = jax.ShapeDtypeStruct(moments[0].shape, jnp.float32)
    hand_on = [pl.BlockSpec(memory_space=pl.ANY)] * len(carried)
    return pl.pallas_call(
        functools.partial(expert_update_kernel, kinds, scale, len(carried)),
        grid=(count // group,),
        in_specs=[taken] + [block] * len(kinds) + hand_on,
        out_specs=[block] * (3 * len(kinds)) + hand_on,
        out_shape=[shape] * (3 * len(kinds))
        + [jax.ShapeDtypeStruct(array.shape, array.dtype) for array in carried],
        scratch_shapes=[pltpu.VMEM(array.shape, array.dtype) for array in carried]
        + [pltpu.SemaphoreType.DMA((len(carried),))] * (2 if carried else 0),
        compiler_params=pltpu.CompilerParams(vmem_limit_bytes=60 * 1024 * 1024),
        name="expert_update",
        cost_estimate=pl.CostEstimate(
            flops=count * len(kinds) * 2500000000,
            bytes_accessed=moments[0].size * len(kinds) * 18,
            transcendentals=0,
        ),
    )(grads, *moments, *carried)


def dense_update_kernel(layout, place_ref, next_ref, grads_ref, *refs):
    a = newton_first
    amount = len(layout)
    own_moments = refs[:amount]
    outs = refs[amount : 3 * amount]
    updates = refs[3 * amount : 3 * amount + 2]
    matrices = refs[3 * amount + 2 : 3 * amount + 4]
    own_grads, own_next, sem = refs[3 * amount + 4 :]
    blocks, count, block_rows, width = next_ref.shape
    part = width // 3
    me = place_ref[0]
    core = place_ref[1]
    start = pl.multiple_of(me * block_rows, block_rows)
    loads = [
        pltpu.make_async_copy(
            own_moments[index], own_next.at[:, begin : begin + size], sem.at[2 * index]
        )
        for index, (begin, size) in enumerate(layout)
    ]
    for load in loads:
        load.start()

    for block in range(blocks):
        outer = slice(block * part, (block + 1) * part)
        lanes = pl.ds(pl.multiple_of(2 * core * part, part), part)
        matrices[0][:, outer] = next_ref[block, :, :, lanes].reshape(count * block_rows, part)
        for index in range(3):
            columns = slice(8 * part * index + block * part, 8 * part * index + (block + 1) * part)
            inner = slice(index * part, (index + 1) * part)
            own_grads[:, columns] = grads_ref[block, :, inner].astype(jnp.float32)
    for block in range(blocks // 2):
        outer = slice(block * part, (block + 1) * part)
        matrices[1][:, outer] = next_ref[
            core * (blocks // 2) + block, :, :, part : 2 * part
        ].reshape(count * block_rows, part)
    leaving = []
    for index, (begin, size) in enumerate(layout):
        loads[index].wait()
        lanes = slice(begin, begin + size)
        own_next[:, lanes] = momentum_keep * own_next[:, lanes] + own_grads[:, lanes]
        leaving += [
            pltpu.make_async_copy(own_grads.at[:, lanes], outs[2 * index], sem.at[2 * index]),
            pltpu.make_async_copy(own_next.at[:, lanes], outs[2 * index + 1], sem.at[2 * index + 1]),
        ]
        leaving[-2].start()
        leaving[-1].start()
    states = []
    for matrix in matrices:
        low = matrix[...]
        states.append(
            scaled_gram(
                lax.dot_general(
                    low, low, (((0,), (0,)), ((), ())), preferred_element_type=jnp.float32
                )
            )
        )
    parts = newton_parts([state[0] for state in states])
    for matrix, update, (_, inverse), (_, first_low, _, second_low) in zip(
        matrices, updates, states, parts
    ):
        rows, columns = matrix.shape
        scale = rate_matrix * math.sqrt(max(1.0, columns / rows))
        own = matrix[pl.ds(start, block_rows)]
        once = a * own.astype(jnp.float32) + jnp.dot(
            own, first_low, preferred_element_type=jnp.float32
        )
        update[...] = (-scale * inverse) * (
            a * once
            + jnp.dot(once.astype(jnp.bfloat16), second_low, preferred_element_type=jnp.float32)
        )
    for copy in leaving:
        copy.wait()


def dense_update(nexts, grads, own_moments, layout, shard_index, rep_index):
    _, count, block_rows, _ = nexts.shape
    width = own_moments[0].shape[1]
    whole = lambda shape: pl.BlockSpec(shape, lambda i: (0,) * len(shape))
    anywhere = pl.BlockSpec(memory_space=pl.ANY)
    shapes = []
    for _, size in layout:
        shapes += [jax.ShapeDtypeStruct((block_rows, size), jnp.float32)] * 2
    shapes += [
        jax.ShapeDtypeStruct((block_rows, width), jnp.float32),
        jax.ShapeDtypeStruct((block_rows, width // 2), jnp.float32),
    ]
    place = jnp.stack([shard_index, rep_index % 2]).astype(jnp.int32)
    return pl.pallas_call(
        functools.partial(dense_update_kernel, layout),
        grid=(1,),
        in_specs=[pl.BlockSpec(memory_space=pltpu.SMEM), whole(nexts.shape), whole(grads.shape)]
        + [anywhere] * len(own_moments),
        out_specs=[anywhere] * (2 * len(layout)) + [whole(shape.shape) for shape in shapes[-2:]],
        out_shape=shapes,
        scratch_shapes=[
            pltpu.VMEM((count * block_rows, width), jnp.bfloat16),
            pltpu.VMEM((count * block_rows, width // 2), jnp.bfloat16),
            pltpu.VMEM((block_rows, 3 * width), jnp.float32),
            pltpu.VMEM((block_rows, 3 * width), jnp.float32),
            pltpu.SemaphoreType.DMA((2 * len(layout),)),
        ],
        compiler_params=pltpu.CompilerParams(vmem_limit_bytes=63 * 1024 * 1024),
        name="dense_update",
        cost_estimate=pl.CostEstimate(
            flops=14000000000, bytes_accessed=24 * width * width, transcendentals=0
        ),
    )(place, nexts, grads, *own_moments)


LAYOUT = ((0, 1024), (1024, 512), (1536, 512), (2048, 1024))


MESH = pl.DeviceIdType.MESH


def flip(index, bit):
    return index + bit - 2 * bit * ((index // bit) % 2)


def greet(peers):
    barrier = pltpu.get_barrier_semaphore()
    for peer in peers:
        pl.semaphore_signal(barrier, inc=1, device_id=peer, device_id_type=MESH)
    pl.semaphore_wait(barrier, len(peers))


def stream_plan(rep, bits, base, size):
    stages = []
    starts = [base, base + size]
    for step in range(len(bits)):
        size = size // 2
        stage = []
        for stream in range(2):
            bit = bits[(step + stream) % len(bits)]
            side = (rep // bit) % 2
            keep = starts[stream] + side * size
            send = starts[stream] + (1 - side) * size
            starts[stream] = keep
            stage.append((bit, stream, keep, send, size))
        stages.append(stage)
    return stages


def rows_of(start, size):
    return pl.ds(pl.multiple_of(start, 16), size)


def moe_kernel(
    count,
    bits,
    own_ref,
    cot_ref,
    weight_ref,
    gate_hbm,
    up_hbm,
    down_hbm,
    stage_out,
    back_ref,
    share_ref,
    tok,
    turned,
    mats,
    hid,
    gate_delta,
    up_delta,
    stage_back,
    got_back,
    sum_back,
    sum_out,
    *rest,
):
    landing = rest[: 1 + 2 * len(bits)]
    (
        load_sem,
        right_sem,
        left_sem,
        arrive_sem,
        back_send,
        back_recv,
        sum_send,
        sum_recv,
        core_send,
        core_recv,
    ) = rest[1 + 2 * len(bits) :]
    rep = lax.axis_index("rep")
    me = lax.axis_index("shard")
    experts = mats.shape[0]
    tokens = own_ref.shape[0]
    half = mats.shape[2] // 2
    core = rep % 2

    loads = [
        pltpu.make_async_copy(gate_hbm, mats.at[:, 0], load_sem.at[0]),
        pltpu.make_async_copy(up_hbm, mats.at[:, 1], load_sem.at[1]),
        pltpu.make_async_copy(
            down_hbm.at[:, :, pl.ds(0, half)], mats.at[:, 2, pl.ds(0, half)], load_sem.at[2]
        ),
        pltpu.make_async_copy(
            down_hbm.at[:, :, pl.ds(half, half)], mats.at[:, 2, pl.ds(half, half)], load_sem.at[3]
        ),
    ]
    for load in loads:
        load.start()
    peers = [(rep, lax.rem(me + k, count)) for k in range(1, count)]
    peers += [(flip(rep, bit), me) for bit in (1,) + bits]
    greet(peers)

    right_peer = (rep, jnp.minimum(me + 1, count - 1))
    left_peer = (rep, jnp.maximum(me - 1, 0))

    def hand_on(block, to_right):
        return pltpu.make_async_remote_copy(
            src_ref=tok.at[block],
            dst_ref=tok.at[block],
            send_sem=(right_sem if to_right else left_sem).at[block],
            recv_sem=arrive_sem.at[block],
            device_id=right_peer if to_right else left_peer,
            device_id_type=MESH,
        )

    def returning(stage, got, send_sem, recv_sem, block):
        return pltpu.make_async_remote_copy(
            src_ref=stage.at[block],
            dst_ref=got.at[me],
            send_sem=send_sem.at[block],
            recv_sem=recv_sem.at[me],
            device_id=(rep, block),
            device_id_type=MESH,
        )

    tok[me] = own_ref[...]

    @pl.when(me < count - 1)
    def _():
        hand_on(me, True).start()

    @pl.when(me > 0)
    def _():
        hand_on(me, False).start()

    for load in loads:
        load.wait()

    margin = jnp.minimum(me, count - 1 - me)
    longer = jnp.where(me < count - 1 - me, 1, -1)
    inward = jnp.where(2 * me < count, 1, -1)
    nt = (((1,), (1,)), ((), ()))

    def dot(left, right):
        return jnp.dot(left, right, preferred_element_type=jnp.float32)

    def dot_nt(left, right):
        return lax.dot_general(left, right, nt, preferred_element_type=jnp.float32)

    def arrivals(j):
        lower = me - j
        upper = me + j

        @pl.when((j > 0) & (lower >= 0))
        def _():
            hand_on(jnp.maximum(lower, 0), True).wait_recv()

            @pl.when(me < count - 1)
            def _():
                hand_on(jnp.maximum(lower, 0), True).start()

        @pl.when((j > 0) & (upper < count))
        def _():
            hand_on(jnp.minimum(upper, count - 1), False).wait_recv()

            @pl.when(me > 0)
            def _():
                hand_on(jnp.minimum(upper, count - 1), False).start()

    def block_at(j):
        near = (j + 1) // 2
        alternating = me + near - 2 * near * (j % 2)
        return jnp.where(j <= 2 * margin, alternating, me + longer * (j - margin))

    def places_of(block):
        return pl.ds(pl.multiple_of(block * tokens, tokens), tokens)

    def factors(e, block):
        places = places_of(block)
        rows = tok[block]
        grads = cot_ref[block]
        weight = weight_ref[block, :, e : e + 1]
        u = dot(rows, mats[e, 0])
        w = dot(rows, mats[e, 1])
        gate = 1.0 / (1.0 + jnp.exp(-u))
        act = u * gate
        hidden = (weight * (act * w)).astype(jnp.bfloat16)
        hid[e, :, places] = hidden.T
        pulled = weight * (
            dot_nt(grads[:, :half], mats[e, 2, :half])
            + dot_nt(grads[:, half:], mats[e, 2, half:])
        )
        gate_delta[e, places] = (pulled * w * (gate + act * (1.0 - gate))).astype(jnp.bfloat16)
        up_delta[e, places] = (pulled * act).astype(jnp.bfloat16)
        return hidden

    def sums(block, e, hidden, place):
        places = places_of(block)
        for side in range(2):
            part = slice(side * half, (side + 1) * half)
            back = dot_nt(gate_delta[e, places], mats[e, 0, part]) + dot_nt(
                up_delta[e, places], mats[e, 1, part]
            )
            out = dot(hidden, mats[e, 2, part])
            if e > 0:
                back = place[0][:, part] + back
                out = place[1][:, part] + out
            place[0][:, part] = back
            place[1][:, part] = out

    def visit(j, carry):
        arrivals(j)
        block = block_at(j)
        places = places_of(block)
        turned[:, places] = tok[block].T
        hiddens = [factors(e, block) for e in range(experts)]
        for side in range(2):
            part = slice(side * half, (side + 1) * half)
            total_back = None
            total_out = None
            for e in range(experts):
                back = dot_nt(gate_delta[e, places], mats[e, 0, part]) + dot_nt(
                    up_delta[e, places], mats[e, 1, part]
                )
                out = dot(hiddens[e], mats[e, 2, part])
                total_back = back if e == 0 else total_back + back
                total_out = out if e == 0 else total_out + out
            stage_back[block, :, part] = total_back.astype(jnp.bfloat16)
            stage_out[block, :, part] = total_out.astype(jnp.bfloat16)

        @pl.when((j > 0) & ((block - me) * inward > 0))
        def _():
            returning(stage_back, got_back, back_send, back_recv, block).start()

        return carry

    lax.fori_loop(0, count - 1, visit, 0)
    arrivals(count - 1)
    last = block_at(count - 1)
    for k in range(1, count):
        block = block_at(k - 1)

        @pl.when((block - me) * inward < 0)
        def _():
            returning(stage_back, got_back, back_send, back_recv, block).start()

    turned[:, places_of(last)] = tok[last].T
    plan = stream_plan(rep, bits, core * half, half // 2)

    def sum_copy(stage, slot, e, start, size, bit):
        return pltpu.make_async_remote_copy(
            src_ref=mats.at[e, :, rows_of(start, size)],
            dst_ref=landing[slot].at[e],
            send_sem=sum_send.at[slot, e],
            recv_sem=sum_recv.at[slot, e],
            device_id=(flip(rep, bit), me),
            device_id_type=MESH,
        )

    def core_copy(e, kind):
        return pltpu.make_async_remote_copy(
            src_ref=mats.at[e, kind, rows_of((1 - core) * half, half)],
            dst_ref=landing[0].at[e, kind],
            send_sem=core_send.at[e, kind],
            recv_sem=core_recv.at[e, kind],
            device_id=(flip(rep, 1), me),
            device_id_type=MESH,
        )

    def copies(stage, e):
        return [
            (
                sum_copy(stage, 1 + 2 * (stage - 1) + stream, e, send, size, bit),
                1 + 2 * (stage - 1) + stream,
                keep,
                size,
            )
            for bit, stream, keep, send, size in plan[stage - 1]
        ]

    def finish(stage, e):
        if stage == 0:
            place = rows_of(core * half, half)
            for kind in range(3):
                core_copy(e, kind).wait_recv()
                mats[e, kind, place] = (
                    mats[e, kind, place].astype(jnp.float32)
                    + landing[0][e, kind].astype(jnp.float32)
                ).astype(jnp.bfloat16)
            return
        for copy, slot, keep, size in copies(stage, e):
            copy.wait_recv()
            place = rows_of(keep, size)
            for kind in range(3):
                mats[e, kind, place] = (
                    mats[e, kind, place].astype(jnp.float32)
                    + landing[slot][e, kind].astype(jnp.float32)
                ).astype(jnp.bfloat16)

    stages = 1 + len(bits)
    for turn in range(experts + stages):
        if turn < experts:
            e = turn
            sums(last, e, factors(e, last), (sum_back, sum_out))
            for kind in range(3):
                for side in range(2):
                    part = slice(side * half, (side + 1) * half)
                    if kind == 2:
                        values = dot(hid[e], cot_ref[:, :, part].reshape(count * tokens, half))
                    else:
                        values = dot(turned[part], (gate_delta, up_delta)[kind][e])
                    mats[e, kind, part] = values.astype(jnp.bfloat16)
                core_copy(e, kind).start()
            if e == experts - 1:
                stage_back[last] = sum_back[...].astype(jnp.bfloat16)
                stage_out[last] = sum_out[...].astype(jnp.bfloat16)
                returning(stage_back, got_back, back_send, back_recv, last).start()
        for stage in range(stages):
            e = turn - 1 - stage
            if 0 <= e < experts:
                finish(stage, e)
                if stage + 1 < stages:
                    for copy, _, _, _ in copies(stage + 1, e):
                        copy.start()
                else:
                    for _, stream, keep, _, size in plan[-1]:
                        share_ref[e, :, stream] = mats[e, :, rows_of(keep, size)]

    total = stage_back[me].astype(jnp.float32)
    for k in range(1, count):
        source = lax.rem(me + k, count)
        pltpu.make_async_remote_copy(
            src_ref=stage_back.at[source],
            dst_ref=got_back.at[source],
            send_sem=back_send.at[source],
            recv_sem=back_recv.at[source],
            device_id=(rep, source),
            device_id_type=MESH,
        ).wait_recv()
        total = total + got_back[source].astype(jnp.float32)
    back_ref[...] = total
    for k in range(1, count):
        block = lax.rem(me + k, count)
        returning(stage_back, got_back, back_send, back_recv, block).wait_send()
    for e in range(experts):
        for kind in range(3):
            core_copy(e, kind).wait_send()
        for stage in range(1, stages):
            for copy, _, _, _ in copies(stage, e):
                copy.wait_send()
    for block in range(count):

        @pl.when((block <= me) & (me < count - 1))
        def _():
            hand_on(block, True).wait_send()

        @pl.when((block >= me) & (me > 0))
        def _():
            hand_on(block, False).wait_send()


def moe(normed, cotangents, weights, gate_proj, up_proj, down_proj, bits, count):
    tokens, width = normed.shape
    experts, _, hidden = gate_proj.shape
    half = width // 2
    low = jnp.bfloat16
    final = (half // 2) >> len(bits)
    vmem = pl.BlockSpec(memory_space=pltpu.VMEM)
    anywhere = pl.BlockSpec(memory_space=pl.ANY)
    landings = [pltpu.VMEM((experts, 3, half, hidden), low)]
    for step in range(len(bits)):
        size = (half // 2) >> (step + 1)
        landings += [pltpu.VMEM((experts, 3, size, hidden), low)] * 2
    slots = len(landings)
    dma = pltpu.SemaphoreType.DMA
    return pl.pallas_call(
        functools.partial(moe_kernel, count, bits),
        in_specs=[vmem, vmem, vmem, anywhere, anywhere, anywhere],
        out_specs=[vmem, vmem, vmem],
        out_shape=[
            jax.ShapeDtypeStruct((count, tokens, width), low),
            jax.ShapeDtypeStruct((tokens, width), jnp.float32),
            jax.ShapeDtypeStruct((experts, 3, 2, final, hidden), low),
        ],
        scratch_shapes=[
            pltpu.VMEM((count, tokens, width), low),
            pltpu.VMEM((width, count * tokens), low),
            pltpu.VMEM((experts, 3, width, hidden), low),
            pltpu.VMEM((experts, hidden, count * tokens), low),
            pltpu.VMEM((experts, count * tokens, hidden), low),
            pltpu.VMEM((experts, count * tokens, hidden), low),
            pltpu.VMEM((count, tokens, width), low),
            pltpu.VMEM((count, tokens, width), low),
            pltpu.VMEM((tokens, width), jnp.float32),
            pltpu.VMEM((tokens, width), jnp.float32),
        ]
        + landings
        + [
            dma((4,)),
            dma((count,)),
            dma((count,)),
            dma((count,)),
            dma((count,)),
            dma((count,)),
            dma((slots, experts)),
            dma((slots, experts)),
            dma((experts, 3)),
            dma((experts, 3)),
        ],
        compiler_params=pltpu.CompilerParams(
            collective_id=1, has_side_effects=True, vmem_limit_bytes=63 * 1024 * 1024
        ),
        name="moe",
        cost_estimate=pl.CostEstimate(
            flops=39000000000, bytes_accessed=20000000, transcendentals=2000000
        ),
    )(normed, cotangents, weights, gate_proj, up_proj, down_proj)


def rep_bits(rep_count):
    bits = []
    bit = 2
    while bit < rep_count:
        bits.append(bit)
        bit = bit * 2
    return tuple(bits)


def spread_kernel(
    count,
    bits,
    share_ref,
    returned_ref,
    normed_ref,
    head_ref,
    weights_hbm,
    small_ref,
    tokens_ref,
    cot_ref,
    second_ref,
    middle_ref,
    query_ref,
    pair_ref,
    total_ref,
    table_ref,
    row_ref,
    query_moment,
    key_moment,
    value_moment,
    out_moment,
    experts_hbm,
    dense_out,
    grads_out,
    gains_out,
    tokens_out,
    mixed_out,
    experts_out,
    weights_ref,
    got_ref,
    moment_piece,
    delta_ref,
    branch_ref,
    heads_ref,
    dense_ref,
    total,
    land_core,
    land_first,
    *rest,
):
    later = len(bits) - 1
    land_later = rest[:later]
    (
        piece_send,
        piece_land,
        piece,
        gains_send,
        gains_land,
        gains_all,
        local_sem,
        core_send,
        core_recv,
        half_send,
        half_recv,
        shard_send,
        shard_recv,
        grow_send,
        grow_recv,
        line_send,
        line_recv,
        join_send,
        join_recv,
        expert_send,
        expert_recv,
        gain_send,
        gain_recv,
        gain_line_send,
        gain_line_recv,
        back_send,
        back_recv,
        moment_sem,
        own_send,
        own_recv,
        own_join_send,
        own_join_recv,
        weights_sem,
    ) = rest[later:]
    rep = lax.axis_index("rep")
    me = lax.axis_index("shard")
    core = rep % 2
    rows = dense_ref.shape[2]
    expert_rows = experts_out.shape[2]
    steps = len(bits)
    streams = range(2)

    def remote(source, target, send_sem, recv_sem, peer):
        return pltpu.make_async_remote_copy(
            src_ref=source,
            dst_ref=target,
            send_sem=send_sem,
            recv_sem=recv_sem,
            device_id=peer,
            device_id_type=MESH,
        )

    def across(bit):
        return (flip(rep, bit), me)

    def order(stream):
        return [bits[(step + stream) % steps] for step in range(steps)]

    def side(bit):
        return (rep // bit) % 2

    plan = stream_plan(rep, bits, core * (expert_rows // 2), expert_rows // 4)
    base = [(core * (expert_rows // 2)) + stream * (expert_rows // 4) for stream in streams]

    def expert_copy(level, stream):
        if level == steps:
            place = rows_of(base[stream], expert_rows // 4)
            peer = across(1)
        else:
            bit, _, keep, _, size = plan[steps - 1 - level][stream]
            place = rows_of(keep, size)
            peer = across(bit)
        source = experts_out.at[:, :, place]
        if level == 0:
            source = share_ref.at[:, :, stream]
        return remote(
            source,
            experts_out.at[:, :, place],
            expert_send.at[level, stream],
            expert_recv.at[level, stream],
            peer,
        )

    def own_copy(stream):
        _, _, keep, _, size = plan[-1][stream]
        return pltpu.make_async_copy(
            share_ref.at[:, :, stream],
            experts_out.at[:, :, rows_of(keep, size)],
            local_sem.at[stream],
        )

    weights_load = pltpu.make_async_copy(weights_hbm, weights_ref, weights_sem.at[0])
    weights_load.start()
    for stream in streams:
        own_copy(stream).start()
    peers = [(rep, lax.rem(me + k, count)) for k in range(1, count)]
    peers += [across(bit) for bit in (1,) + bits]
    greet(peers)

    def returning(peer, source):
        return remote(
            returned_ref.at[peer],
            got_ref.at[source],
            back_send.at[peer],
            back_recv.at[source],
            (rep, peer),
        )

    def core_copy(block):
        return remote(
            dense_ref.at[4 * (1 - core) + block],
            land_core.at[block],
            core_send.at[block],
            core_recv.at[block],
            across(1),
        )

    gain_bits = (1,) + bits

    def gain_copy(stage):
        return remote(
            gains_send.at[stage],
            gains_land.at[stage],
            gain_send.at[stage],
            gain_recv.at[stage],
            across(gain_bits[stage]),
        )

    for stream in streams:
        expert_copy(0, stream).start()

    for k in range(1, count):
        returning(lax.rem(me + k, count), me).start()

    def whole(index):
        return weights_ref[index].reshape(count * rows, -1)

    def gain(index):
        at = EXPERTS + index
        return jnp.concatenate([small_ref[z, at : at + 1, :rows] for z in range(count)], axis=1)

    scaled, inverse = normalize(middle_ref[...])
    middle_extra, midnorm_part = normalize_back(second_ref[...], gain(1), scaled, inverse)
    grad_middle = cot_ref[...].astype(jnp.float32) + middle_extra
    tokens_out[...] = grad_middle
    branch_ref[...] = grad_middle.astype(jnp.bfloat16)
    weights_load.wait()
    heads_ref[...] = dot_nt(branch_ref[...], whole(2)).astype(jnp.bfloat16)
    bias = allowed_pairs(row_ref[...])
    attend_backward(query_ref, pair_ref, bias, total_ref, heads_ref, table_ref, delta_ref)

    part = dense_ref.shape[3] // 3
    normed_turned = normed_ref[...].T
    head_turned = head_ref[...].T

    def make_block(block):
        def columns(ref, offset):
            return ref[:, pl.ds(pl.multiple_of(offset + block * part, part), part)]

        pair = jnp.concatenate([columns(delta_ref, 0), columns(delta_ref, 8 * part)], axis=1)
        left = jnp.dot(normed_turned, pair, preferred_element_type=jnp.float32)
        right = jnp.dot(head_turned, columns(branch_ref, 0), preferred_element_type=jnp.float32)
        for line in range(count):
            place = slice(line * rows, (line + 1) * rows)
            dense_ref[block, line, :, : 2 * part] = left[place].astype(jnp.bfloat16)
            dense_ref[block, line, :, 2 * part :] = right[place].astype(jnp.bfloat16)

    for block in range(4):
        make_block(4 * (1 - core) + block)
        core_copy(block).start()
    for block in range(4):
        make_block(4 * core + block)

    def gain_step(stage):
        gain_copy(stage).wait_recv()
        gains_send[stage + 1] = gains_send[stage] + gains_land[stage]
        if stage + 1 < len(gain_bits):
            gain_copy(stage + 1).start()

    first = [side(order(stream)[0]) for stream in streams]
    held = [2 * stream + first[stream] for stream in streams]
    given = [2 * stream + 1 - first[stream] for stream in streams]

    def first_copy(stream):
        return remote(
            total.at[given[stream]],
            land_first.at[stream],
            half_send.at[0, stream],
            half_recv.at[0, stream],
            across(order(stream)[0]),
        )

    def add_core(block):
        for line in range(count):
            total[block, line] = (
                dense_ref[4 * core + block, line].astype(jnp.float32)
                + land_core[block, line].astype(jnp.float32)
            ).astype(jnp.bfloat16)

    for block in range(4):
        core_copy(block).wait_recv()
    for stream in streams:
        add_core(given[stream])
        first_copy(stream).start()
    for stream in streams:
        add_core(held[stream])
    grad_first = dot_nt(delta_ref[:, : NHEADS * HEAD], whole(0)) + dot_nt(
        delta_ref[:, NHEADS * HEAD :], whole(1)
    )
    scaled, inverse = normalize(tokens_ref[...].astype(jnp.float32))
    input_extra, prenorm_part = normalize_back(grad_first, gain(0), scaled, inverse)
    tokens_out[...] = tokens_out[...] + input_extra
    gains_send[0] = jnp.concatenate(
        [prenorm_part, midnorm_part, jnp.zeros((6, prenorm_part.shape[1]), jnp.float32)], axis=0
    )
    gain_copy(0).start()
    gain_step(0)

    starts = []
    for stream in streams:
        start, size, line = 0, rows, []
        for step in range(1, steps):
            size = size // 2
            near = side(order(stream)[step])
            line.append((start + near * size, start + (1 - near) * size, size))
            start = start + near * size
        starts.append((start, size, line))

    last = starts[0][1]
    places = [rows_of(starts[stream][0], last) for stream in streams]
    inner = [slice(index * part, (index + 1) * part) for index in range(3)]

    def moment_copy(stream, index):
        block = 4 * core + held[stream]
        lanes = pl.ds(pl.multiple_of((held[stream] if index == 1 else block) * part, part), part)
        source = (query_moment, key_moment, out_moment)[index]
        return pltpu.make_async_copy(
            source.at[places[stream], lanes],
            moment_piece.at[stream, :, inner[index]],
            moment_sem.at[stream, index],
        )

    def moment_other(stream):
        lanes = pl.ds(pl.multiple_of(held[stream] * part, part), part)
        return pltpu.make_async_copy(
            value_moment.at[places[stream], lanes],
            moment_piece.at[stream, :, inner[1]],
            moment_sem.at[stream, 1],
        )

    for stream in streams:
        moment_copy(stream, 0).start()
        moment_copy(stream, 2).start()

        @pl.when(core == 0)
        def _():
            moment_copy(stream, 1).start()

        @pl.when(core == 1)
        def _():
            moment_other(stream).start()

    def later_copy(step, stream):
        keep, send, size = starts[stream][2][step - 1]
        return remote(
            total.at[held[stream], :, rows_of(send, size)],
            land_later[step - 1].at[stream],
            half_send.at[step, stream],
            half_recv.at[step, stream],
            across(order(stream)[step]),
        )

    for stream in streams:
        first_copy(stream).wait_recv()
        for line in range(count):
            total[held[stream], line] = (
                total[held[stream], line].astype(jnp.float32)
                + land_first[stream, line].astype(jnp.float32)
            ).astype(jnp.bfloat16)
        if steps > 1:
            later_copy(1, stream).start()
    gain_step(1)

    for step in range(1, steps):
        for stream in streams:
            later_copy(step, stream).wait_recv()
            keep, _, size = starts[stream][2][step - 1]
            for line in range(count):
                place = rows_of(keep, size)
                total[held[stream], line, place] = (
                    total[held[stream], line, place].astype(jnp.float32)
                    + land_later[step - 1][stream, line].astype(jnp.float32)
                ).astype(jnp.bfloat16)
            if step + 1 < steps:
                later_copy(step + 1, stream).start()
        gain_step(step + 1)

    for stream in streams:
        own_copy(stream).wait()
        expert_copy(0, stream).wait_recv()
        if steps > 1:
            expert_copy(1, stream).start()

    for stream in streams:
        for line in range(count):
            piece_send[line, stream] = total[held[stream], line, places[stream]]

    def shard_copy(k):
        target = lax.rem(me + k, count)
        return remote(
            piece_send.at[target],
            piece_land.at[me],
            shard_send.at[target],
            shard_recv.at[me],
            (rep, target),
        )

    def shard_arrival(source):
        return remote(
            piece_send.at[source],
            piece_land.at[source],
            shard_send.at[source],
            shard_recv.at[source],
            (rep, source),
        )

    def gain_line(k):
        target = lax.rem(me + k, count)
        return remote(
            gains_send.at[len(gain_bits)],
            gains_all.at[me],
            gain_line_send.at[target],
            gain_line_recv.at[me],
            (rep, target),
        )

    def gain_arrival(source):
        return remote(
            gains_send.at[len(gain_bits)],
            gains_all.at[source],
            gain_line_send.at[source],
            gain_line_recv.at[source],
            (rep, source),
        )

    def own_grow(step, stream):
        block = 4 * core + held[stream]
        if step == 0:
            part_ref = grads_out.at[block]
        else:
            keep, _, size = starts[stream][2][step - 1]
            part_ref = grads_out.at[block, rows_of(keep, size)]
        return remote(
            part_ref,
            part_ref,
            own_send.at[step, stream],
            own_recv.at[step, stream],
            across(order(stream)[step]),
        )

    def own_join(stream):
        part_ref = grads_out.at[pl.ds(4 * core + 2 * stream, 2)]
        return remote(
            part_ref, part_ref, own_join_send.at[stream], own_join_recv.at[stream], across(1)
        )

    for k in range(1, count):
        shard_copy(k).start()
        gain_line(k).start()
    summed = piece_send[me].astype(jnp.float32)
    for k in range(1, count):
        source = lax.rem(me + k, count)
        shard_arrival(source).wait_recv()
        summed = summed + piece_land[source].astype(jnp.float32)
    for stream in streams:
        for index in range(3):
            moment_copy(stream, index).wait()
        grads_out[4 * core + held[stream], places[stream]] = summed[stream].astype(jnp.bfloat16)
        own_grow(steps - 1, stream).start()
    piece[...] = (momentum_keep * moment_piece[...] + summed).astype(jnp.bfloat16)

    def line_copy(k, stream):
        target = lax.rem(me + k, count)
        return remote(
            piece.at[stream],
            dense_out.at[4 * core + held[stream], me, places[stream]],
            line_send.at[stream, target],
            line_recv.at[stream, me],
            (rep, target),
        )

    def line_arrival(source, stream):
        return remote(
            piece.at[stream],
            dense_out.at[4 * core + held[stream], source, places[stream]],
            line_send.at[stream, source],
            line_recv.at[stream, source],
            (rep, source),
        )

    def own_piece(stream):
        return pltpu.make_async_copy(
            piece.at[stream],
            dense_out.at[4 * core + held[stream], me, places[stream]],
            local_sem.at[2 + stream],
        )

    for stream in streams:
        own_piece(stream).start()
        for k in range(1, count):
            line_copy(k, stream).start()
    gained = gains_send[len(gain_bits)]
    for k in range(1, count):
        source = lax.rem(me + k, count)
        gain_arrival(source).wait_recv()
        gained = gained + gains_all[source]
    gains_out[...] = gained

    for level in range(1, steps):
        for stream in streams:
            expert_copy(level, stream).wait_recv()
            expert_copy(level + 1, stream).start()
    if steps == 1:
        for stream in streams:
            expert_copy(1, stream).start()

    def grow_copy(step, stream):
        if step == 0:
            place = dense_out.at[4 * core + held[stream]]
        else:
            keep, _, size = starts[stream][2][step - 1]
            place = dense_out.at[4 * core + held[stream], :, rows_of(keep, size)]
        return remote(
            place,
            place,
            grow_send.at[step, stream],
            grow_recv.at[step, stream],
            across(order(stream)[step]),
        )

    for stream in streams:
        own_piece(stream).wait()
        for k in range(1, count):
            line_arrival(lax.rem(me + k, count), stream).wait_recv()
        grow_copy(steps - 1, stream).start()
    for step in reversed(range(steps)):
        for stream in streams:
            own_grow(step, stream).wait_recv()
            if step > 0:
                own_grow(step - 1, stream).start()
            else:
                own_join(stream).start()
    mixed = middle_ref[...] + returned_ref[me].astype(jnp.float32)
    for k in range(1, count):
        source = lax.rem(me + k, count)
        returning(source, source).wait_recv()
        mixed = mixed + got_ref[source].astype(jnp.float32)
    mixed_out[...] = mixed.astype(mixed_out.dtype)
    for stream in streams:
        expert_copy(steps, stream).wait()
    leave = pltpu.make_async_copy(experts_out, experts_hbm, local_sem.at[0])
    leave.start()
    for step in reversed(range(steps)):
        for stream in streams:
            grow_copy(step, stream).wait_recv()
            if step > 0:
                grow_copy(step - 1, stream).start()

    def join_copy(stream):
        place = dense_out.at[pl.ds(4 * core + 2 * stream, 2)]
        return remote(place, place, join_send.at[stream], join_recv.at[stream], across(1))

    for stream in streams:
        join_copy(stream).start()
    for stream in streams:
        join_copy(stream).wait()
        own_join(stream).wait()
        for step in range(steps):
            own_grow(step, stream).wait_send()
        for level in range(steps):
            expert_copy(level, stream).wait_send()
        first_copy(stream).wait_send()
        for step in range(1, steps):
            later_copy(step, stream).wait_send()
        for k in range(1, count):
            line_copy(k, stream).wait_send()
        for step in range(steps):
            grow_copy(step, stream).wait_send()
    for block in range(4):
        core_copy(block).wait_send()
    for stage in range(len(gain_bits)):
        gain_copy(stage).wait_send()
    for k in range(1, count):
        shard_copy(k).wait_send()
        gain_line(k).wait_send()
        returning(lax.rem(me + k, count), me).wait_send()
    leave.wait()


def spread(
    share, returned, normed, head_low, weights, small, tokens, cotangent, second, middle, *rest, bits, count
):
    query, pair, log_total, tables, starts, moments = rest
    experts, _, _, final, hidden = share.shape
    token_count, features = normed.shape
    rows = features // count
    width = 3 * features // 8
    dense_shape = (8, count, rows, width)
    gains_shape = (8, features)
    steps = len(bits)
    last = rows >> (steps - 1)
    low = jnp.bfloat16
    vmem = pl.BlockSpec(memory_space=pltpu.VMEM)
    dma = pltpu.SemaphoreType.DMA
    return pl.pallas_call(
        functools.partial(spread_kernel, count, bits),
        in_specs=[vmem] * 4
        + [pl.BlockSpec(memory_space=pl.ANY)]
        + [vmem] * 10
        + [pl.BlockSpec(memory_space=pl.ANY)] * 4,
        out_specs=[pl.BlockSpec(memory_space=pl.ANY)] + [vmem] * 5,
        out_shape=[
            jax.ShapeDtypeStruct((experts, 3, 4 * (final << steps), hidden), low),
            jax.ShapeDtypeStruct(dense_shape, low),
            jax.ShapeDtypeStruct((8, rows, width), low),
            jax.ShapeDtypeStruct(gains_shape, jnp.float32),
            jax.ShapeDtypeStruct((token_count, features), jnp.float32),
            jax.ShapeDtypeStruct((token_count, features), low),
        ],
        scratch_shapes=[
            pltpu.VMEM((experts, 3, 4 * (final << steps), hidden), low),
            pltpu.VMEM(weights.shape, low),
            pltpu.VMEM((count, token_count, features), low),
            pltpu.VMEM((2, last, width), jnp.float32),
            pltpu.VMEM((token_count, 2 * features), low),
            pltpu.VMEM((token_count, features), low),
            pltpu.VMEM((token_count, features), low),
            pltpu.VMEM(dense_shape, low),
            pltpu.VMEM((4, count, rows, width), low),
            pltpu.VMEM((4, count, rows, width), low),
            pltpu.VMEM((2, count, rows, width), low),
        ]
        + [pltpu.VMEM((2, count, rows >> step, width), low) for step in range(1, steps)]
        + [
            pltpu.VMEM((count, 2, last, width), low),
            pltpu.VMEM((count, 2, last, width), low),
            pltpu.VMEM((2, last, width), low),
            pltpu.VMEM((steps + 2,) + gains_shape, jnp.float32),
            pltpu.VMEM((steps + 1,) + gains_shape, jnp.float32),
            pltpu.VMEM((count,) + gains_shape, jnp.float32),
            dma((4,)),
            dma((4,)),
            dma((4,)),
            dma((steps, 2)),
            dma((steps, 2)),
            dma((count,)),
            dma((count,)),
            dma((steps, 2)),
            dma((steps, 2)),
            dma((2, count)),
            dma((2, count)),
            dma((2,)),
            dma((2,)),
            dma((steps + 1, 2)),
            dma((steps + 1, 2)),
            dma((steps + 1,)),
            dma((steps + 1,)),
            dma((count,)),
            dma((count,)),
            dma((count,)),
            dma((count,)),
            dma((2, 3)),
            dma((steps, 2)),
            dma((steps, 2)),
            dma((2,)),
            dma((2,)),
            dma((1,)),
        ],
        compiler_params=pltpu.CompilerParams(
            collective_id=2, has_side_effects=True, vmem_limit_bytes=63 * 1024 * 1024
        ),
        name="spread",
    )(
        share,
        returned,
        normed,
        head_low,
        weights,
        small,
        tokens,
        cotangent,
        second,
        middle,
        query,
        pair,
        log_total,
        tables,
        starts[None, :],
        *moments,
    )


def gather_kernel(
    count,
    bits,
    query_weight,
    key_weight,
    value_weight,
    out_weight,
    small_ref,
    tokens_ref,
    cot_ref,
    table_ref,
    row_ref,
    weights_hbm,
    small_out,
    cot_out,
    middle_out,
    first_out,
    second_out,
    query_out,
    pair_out,
    head_out,
    total_out,
    weights_out,
    weights_ref,
    local_sem,
    line_send,
    line_recv,
    grow_send,
    grow_recv,
    join_send,
    join_recv,
    small_send,
    small_recv,
    right_sem,
    left_sem,
    arrive_sem,
):
    rep = lax.axis_index("rep")
    me = lax.axis_index("shard")
    core = rep % 2
    steps = len(bits)
    streams = range(2)
    rows, width = weights_ref.shape[1:]
    half = width // 2
    fine = half // 4
    others = [lax.rem(me + k, count) for k in range(1, count)]

    def columns_of(start, size):
        return pl.ds(pl.multiple_of(start, 128), size)

    def order(stream):
        return [bits[(step + stream) % steps] for step in range(steps)]

    def side(bit):
        return (rep // bit) % 2

    narrow = width // 2
    weights_ref[0] = query_weight[...]
    weights_ref[1, :, :narrow] = key_weight[...]
    weights_ref[1, :, narrow:] = value_weight[...]
    weights_ref[2] = out_weight[...]
    own_copy = pltpu.make_async_copy(weights_ref, weights_out.at[:, me], local_sem.at[0])
    own_copy.start()
    small_out[me] = small_ref[...]
    cot_out[me] = cot_ref[...]
    peers = [(rep, other) for other in others]
    peers += [(flip(rep, bit), me) for bit in (1,) + bits]
    greet(peers)

    regions = []
    for stream in streams:
        column = core * half + stream * 2 * fine
        narrow = columns_of(column + side(order(stream)[0]) * fine, fine)
        start, size = 0, rows
        held = [(pl.ds(0, rows), narrow)]
        for step in range(1, steps):
            size = size // 2
            start = start + side(order(stream)[step]) * size
            held.append((rows_of(start, size), narrow))
        regions.append((held, columns_of(column, 2 * fine)))

    def remote(source, target, send_sem, recv_sem, peer):
        return pltpu.make_async_remote_copy(
            src_ref=source,
            dst_ref=target,
            send_sem=send_sem,
            recv_sem=recv_sem,
            device_id=peer,
            device_id_type=MESH,
        )

    def line_copy(stream, source, peer):
        place, columns = regions[stream][0][-1]
        return remote(
            weights_ref.at[:, place, columns],
            weights_out.at[:, source, place, columns],
            line_send.at[stream, peer],
            line_recv.at[stream, source],
            (rep, peer),
        )

    def grow_copy(step, stream, source):
        place, columns = regions[stream][0][step]
        part = weights_out.at[:, source, place, columns]
        return remote(
            part,
            part,
            grow_send.at[step, stream, source],
            grow_recv.at[step, stream, source],
            (flip(rep, order(stream)[step]), me),
        )

    def join_copy(stream, source):
        part = weights_out.at[:, source, :, regions[stream][1]]
        return remote(
            part,
            part,
            join_send.at[stream, source],
            join_recv.at[stream, source],
            (flip(rep, 1), me),
        )

    def small_copy(source, peer):
        return remote(
            small_ref,
            small_out.at[source],
            small_send.at[peer],
            small_recv.at[source],
            (rep, peer),
        )

    def hand_on(block, to_right):
        peer = jnp.minimum(me + 1, count - 1) if to_right else jnp.maximum(me - 1, 0)
        return remote(
            cot_out.at[block],
            cot_out.at[block],
            (right_sem if to_right else left_sem).at[block],
            arrive_sem.at[block],
            (rep, peer),
        )

    def line_start():
        @pl.when(me < count - 1)
        def _():
            hand_on(me, True).start()

        @pl.when(me > 0)
        def _():
            hand_on(me, False).start()

    def line_step(step):
        lower = me - step
        upper = me + step

        @pl.when(lower >= 0)
        def _():
            hand_on(jnp.maximum(lower, 0), True).wait_recv()

            @pl.when(me < count - 1)
            def _():
                hand_on(jnp.maximum(lower, 0), True).start()

        @pl.when(upper < count)
        def _():
            hand_on(jnp.minimum(upper, count - 1), False).wait_recv()

            @pl.when(me > 0)
            def _():
                hand_on(jnp.minimum(upper, count - 1), False).start()

    def line_send_all():
        for other in others:
            for stream in streams:
                line_copy(stream, me, other).start()

    def advance(level):
        for other in others:
            for stream in streams:
                if level == 0:
                    line_copy(stream, other, other).wait_recv()
                else:
                    grow_copy(steps - level, stream, other).wait_recv()
                if level < steps:
                    grow_copy(steps - 1 - level, stream, other).start()
                else:
                    join_copy(stream, other).start()

    for other in others:
        small_copy(me, other).start()
    line_send_all()
    for other in others:
        small_copy(other, other).wait_recv()

    def gain(index):
        at = EXPERTS + index
        return jnp.concatenate([small_out[z, at : at + 1, :rows] for z in range(count)], axis=1)

    inputs = tokens_ref[...].astype(jnp.float32)
    first_out[...] = (normalize(inputs)[0] * gain(0)).astype(jnp.bfloat16)
    advance(0)
    line_start()
    for level in range(1, steps + 1):
        advance(level)
        if level == 1:
            line_step(1)
    for other in others:
        for stream in streams:
            join_copy(stream, other).wait_recv()
    own_copy.wait()
    leave = pltpu.make_async_copy(weights_out, weights_hbm, local_sem.at[2])
    leave.start()

    def whole(index):
        return weights_out[index].reshape(count * rows, width)

    project_inputs(first_out[...], whole, query_out, pair_out, table_ref)
    bias = allowed_pairs(row_ref[...])
    if count > 2:
        line_step(2)
    attend_forward(range(KVHEADS // 2), query_out, pair_out, bias, head_out, total_out)
    for step in range(3, count - 1):
        line_step(step)
    attend_forward(range(KVHEADS // 2, KVHEADS), query_out, pair_out, bias, head_out, total_out)
    middle = inputs + dot_nn(head_out[...], whole(2))
    middle_out[...] = middle
    second_out[...] = (normalize(middle)[0] * gain(1)).astype(jnp.bfloat16)
    if count > 3:
        line_step(count - 1)
    for other in others:
        for stream in streams:
            join_copy(stream, other).wait_send()
            line_copy(stream, me, other).wait_send()
            for step in range(steps):
                grow_copy(step, stream, other).wait_send()
    for other in others:
        small_copy(me, other).wait_send()
    for block in range(count):

        @pl.when((block <= me) & (me < count - 1))
        def _():
            hand_on(block, True).wait_send()

        @pl.when((block >= me) & (me > 0))
        def _():
            hand_on(block, False).wait_send()

    leave.wait()


def gather(weights, small, tokens, cotangent, tables, starts, bits, count):
    rows, width = weights[0].shape
    depth = 3
    token_count = tokens.shape[0]
    steps = len(bits)
    low = jnp.bfloat16
    vmem = pl.BlockSpec(memory_space=pltpu.VMEM)
    dma = pltpu.SemaphoreType.DMA
    whole = jax.ShapeDtypeStruct((depth, count, rows, width), low)
    features = jax.ShapeDtypeStruct((token_count, width), low)
    return pl.pallas_call(
        functools.partial(gather_kernel, count, bits),
        in_specs=[vmem] * 9,
        out_specs=[pl.BlockSpec(memory_space=pl.ANY)] + [vmem] * 9,
        out_shape=[
            whole,
            jax.ShapeDtypeStruct((count,) + small.shape, small.dtype),
            jax.ShapeDtypeStruct((count, token_count, width), low),
            jax.ShapeDtypeStruct((token_count, width), jnp.float32),
            features,
            features,
            features,
            features,
            features,
            jax.ShapeDtypeStruct((2 * token_count, KVHEADS), jnp.float32),
        ],
        scratch_shapes=[
            pltpu.VMEM(whole.shape, low),
            pltpu.VMEM((depth, rows, width), low),
            dma((3,)),
            dma((2, count)),
            dma((2, count)),
            dma((steps, 2, count)),
            dma((steps, 2, count)),
            dma((2, count)),
            dma((2, count)),
            dma((count,)),
            dma((count,)),
            dma((count,)),
            dma((count,)),
            dma((count,)),
        ],
        compiler_params=pltpu.CompilerParams(
            collective_id=3, has_side_effects=True, vmem_limit_bytes=56 * 1024 * 1024
        ),
        name="gather",
    )(
        *weights,
        small,
        tokens,
        cotangent,
        tables,
        starts[None, :],
    )


def local(
    tokens,
    sequence_start,
    routes,
    route_weights,
    cotangent,
    query_proj,
    key_proj,
    value_proj,
    out_proj,
    prenorm,
    midnorm,
    gate_proj,
    up_proj,
    down_proj,
    query_moment,
    key_moment,
    value_moment,
    out_moment,
    prenorm_moment,
    midnorm_moment,
    gate_moment,
    up_moment,
    down_moment,
):
    shard_index = lax.axis_index("shard")
    rep_count = lax.axis_size("rep")
    shard_count = lax.axis_size("shard")
    row_block = query_proj.shape[0]
    bits = rep_bits(rep_count)
    experts_here = gate_proj.shape[0]
    dense_weights = jnp.sum(
        jnp.where(
            routes.T[None, :, :] == jnp.arange(EXPERTS, dtype=jnp.int32)[:, None, None],
            route_weights.T[None, :, :],
            0.0,
        ),
        axis=1,
    )
    gain_rows = jnp.pad(
        jnp.stack([prenorm, midnorm]).astype(jnp.float32),
        ((0, 6), (0, tokens.shape[0] - row_block)),
    )
    tables = rotary_tables(jnp.arange(tokens.shape[0], dtype=jnp.int32) - sequence_start)
    (
        weights,
        small,
        cotangent_all,
        middle,
        normed_first,
        normed_second,
        query,
        pair,
        head_low,
        log_total,
    ) = gather(
        (query_proj, key_proj, value_proj, out_proj),
        jnp.concatenate([dense_weights, gain_rows], axis=0),
        tokens,
        cotangent,
        tables,
        sequence_start,
        bits,
        shard_count,
    )
    expert_weights = lax.dynamic_slice_in_dim(
        small, shard_index * experts_here, experts_here, 1
    ).transpose(0, 2, 1)
    returned, grad_second, expert_share = moe(
        normed_second,
        cotangent_all,
        expert_weights,
        gate_proj,
        up_proj,
        down_proj,
        bits,
        shard_count,
    )
    own_moments = (query_moment, key_moment, value_moment, out_moment)
    expert_grads, dense_next, dense_grads, gains_grad, grad_tokens, mixed = spread(
        expert_share,
        returned,
        normed_first,
        head_low,
        weights,
        small,
        tokens,
        cotangent,
        grad_second,
        middle,
        query,
        pair,
        log_total,
        tables,
        sequence_start,
        own_moments,
        bits=bits,
        count=shard_count,
    )
    gains_here = lax.dynamic_slice_in_dim(gains_grad, shard_index * row_block, row_block, 1)
    prenorm_grad = gains_here[0]
    midnorm_grad = gains_here[1]
    prenorm_next = momentum_keep * prenorm_moment + prenorm_grad
    midnorm_next = momentum_keep * midnorm_moment + midnorm_grad
    prenorm_update = -rate_gain * prenorm_next
    midnorm_update = -rate_gain * midnorm_next
    rep_index = lax.axis_index("rep")
    (
        query_grad,
        query_next,
        key_grad,
        key_next,
        value_grad,
        value_next,
        out_grad,
        out_next,
        own_wide,
        own_narrow,
    ) = dense_update(
        dense_next,
        dense_grads,
        own_moments,
        LAYOUT,
        shard_index,
        rep_index,
    )
    pairs = [(index, index + 1 - 2 * (index % 2)) for index in range(rep_count)]
    other_wide = lax.ppermute(own_wide, "rep", pairs)
    other_narrow = lax.ppermute(own_narrow, "rep", pairs)
    gate_grad, gate_next, gate_update, up_grad, up_next, up_update = expert_update(
        expert_grads, (0, 1), (gate_moment, up_moment)
    )
    (
        down_grad,
        down_next,
        down_update,
        query_update,
        out_update,
        key_update,
        value_update,
        grad_tokens,
        mixed,
    ) = expert_update(
        expert_grads,
        (2,),
        (down_moment,),
        (own_wide, other_wide, own_narrow, other_narrow, grad_tokens, mixed),
    )
    return (
        mixed,
        grad_tokens,
        query_grad,
        query_next,
        query_update,
        key_grad,
        key_next,
        key_update,
        value_grad,
        value_next,
        value_update,
        out_grad,
        out_next,
        out_update,
        prenorm_grad,
        prenorm_next,
        prenorm_update,
        midnorm_grad,
        midnorm_next,
        midnorm_update,
        gate_grad,
        gate_next,
        gate_update,
        up_grad,
        up_next,
        up_update,
        down_grad,
        down_next,
        down_update,
    )


def solution(mesh):
    return jax.shard_map(
        local,
        mesh=mesh,
        in_specs=(
            P(("rep", "shard"), None),
            P(("rep", "shard")),
            P(("rep", "shard"), None),
            P(("rep", "shard"), None),
            P(("rep", "shard"), None),
            P("shard", None),
            P("shard", None),
            P("shard", None),
            P("shard", None),
            P("shard"),
            P("shard"),
            P("shard", None, None),
            P("shard", None, None),
            P("shard", None, None),
            P("shard", None),
            P("shard", None),
            P("shard", None),
            P("shard", None),
            P("shard"),
            P("shard"),
            P("shard", None, None),
            P("shard", None, None),
            P("shard", None, None),
        ),
        out_specs=(
            P(("rep", "shard"), None),
            P(("rep", "shard"), None),
            P("shard", None),
            P("shard", None),
            P("shard", None),
            P("shard", None),
            P("shard", None),
            P("shard", None),
            P("shard", None),
            P("shard", None),
            P("shard", None),
            P("shard", None),
            P("shard", None),
            P("shard", None),
            P("shard"),
            P("shard"),
            P("shard"),
            P("shard"),
            P("shard"),
            P("shard"),
            P("shard", None, None),
            P("shard", None, None),
            P("shard", None, None),
            P("shard", None, None),
            P("shard", None, None),
            P("shard", None, None),
            P("shard", None, None),
            P("shard", None, None),
            P("shard", None, None),
        ),
        check_vma=False,
    )
```
